32 devices in a mesh: rep: 4 (over x, core), fsdp: 8 (over z, y).
Axes of the slice: x: 2, y: 2, z: 4, core: 2. Of those that a mesh axis runs over, the one named last changes fastest.
Arguments:
- normed: bfloat16 [12288, 4608], P(('rep', 'fsdp')), may hold values from -6 to 6
- key_grad: bfloat16 [12288, 1024], P(('rep', 'fsdp')), may hold values from -6 to 6
- master: float32 [4, 4608, 1024], P('rep', 'fsdp'), may hold values from -6 to 6
- first_moment: float32 [4, 4608, 1024], P('rep', 'fsdp'), may hold values from -6 to 6
- second_moment: float32 [4, 4608, 1024], P('rep', 'fsdp'), may hold values from 0.1 to 10
- anchor: float32 [4608, 1024], P('fsdp'), may hold values from -6 to 6
- momentum: float32 [4608, 1024], P('fsdp'), may hold values from -6 to 6
- inner_step: int32 [1], replicated, may hold values from 1 to 6
Outputs:
- keys: bfloat16 [12288, 1024], P(('rep', 'fsdp'))
- input_grad: bfloat16 [12288, 4608], P(('rep', 'fsdp'))
- merged: float32 [4, 4608, 1024], P('rep', 'fsdp')
- new_first: float32 [4, 4608, 1024], P('rep', 'fsdp')
- new_second: float32 [4, 4608, 1024], P('rep', 'fsdp')
- new_anchor: float32 [4608, 1024], P('fsdp')
- new_momentum: float32 [4608, 1024], P('fsdp')
The draws below stay inside these ranges and needn't reach their ends.
Inputs may be any that keep to these rules, and one draw needn't show every extreme that they name: `inner_step`: the 1-based count of inner steps taken by the inner optimizer.
All inputs are finite; a program needn't handle non-finite values.
Results may differ from the reference program's by a relative error of at most 0.0049.
Values may be sent and summed in bfloat16 or wider, within the bound.
No kernel may reach another device: no remote copies, remote signals or barrier semaphores. Data moves between devices by JAX's collectives and lax.ppermute only.
A program may use at most 128 MiB of HBM per device.

```python
import math
import jax
import jax.numpy as jnp
from jax import lax

D = 4608
TOK_DEV = 384
KD = 1024
TOKENS = 12288
N_REP = 4
N_FSDP = 8


def with_spikes(result, own_key, source, target, shards_of, factor):
    def block_of(axis_at):
        return (jnp.arange(result.shape[axis_at]) // (result.shape[axis_at] // shards_of)).reshape((-1,) + (1,) * (result.ndim - 1 - axis_at))

    first = jax.random.permutation(own_key, shards_of)[block_of(target)]
    far = (block_of(target) + shards_of // 2) % shards_of
    return jnp.where((block_of(source) == first) | (block_of(source) == far), factor * result, result)


def level_of(rng, dims, pieces, least, high):
    loudness = 1.0
    for axis_at, parts in pieces:
        draws = jax.random.uniform(jax.random.fold_in(jax.random.fold_in(rng, 6), axis_at), (parts,), jnp.float32, least / len(pieces), high / len(pieces))
        loudness = loudness * jnp.repeat(jnp.exp(draws), dims[axis_at] // parts).reshape((-1,) + (1,) * (len(dims) - 1 - axis_at))
    return loudness


def scatter_about(own_key, extent, spread, limit, split=(), held_as=jnp.bfloat16):
    entries = jax.random.normal(own_key, extent, jnp.float32) * spread
    if len(split) > 0:
        entries = level_of(own_key, extent, split, -0.22, 0.18) * entries
    return jnp.clip(entries, min=-limit, max=limit).astype(held_as)


def noise_with(stream_key, shape, deviation, most, pieces, heavy, held_as=jnp.bfloat16):
    entries = deviation * jax.random.normal(stream_key, shape, jnp.float32)
    if pieces:
        entries = entries * level_of(stream_key, shape, pieces, -0.22, 0.18)
    return jnp.clip(with_spikes(entries, jax.random.fold_in(stream_key, 3), *heavy), -most, most).astype(held_as)


def setup_inputs(seed: int = 0) -> dict:
    streams_of = jax.random.split(jax.random.key(seed), 9)
    normed = noise_with(streams_of[0], (TOKENS, D), 1.0, 6.0, ((0, 32),), (0, 1, 32, 2.75))
    key_grad = scatter_about(streams_of[1], (TOKENS, KD), 1.0, 6.0, ((0, 32),))
    master = scatter_about(streams_of[2], (N_REP, D, KD), 1.0, 6.0, ((0, 4), (1, 8)), jnp.float32)
    first_moment = scatter_about(streams_of[3], (N_REP, D, KD), 1.0, 6.0, ((0, 4), (1, 8)), jnp.float32)
    second_moment = jnp.clip(jnp.exp(math.log(10.0) - 4.6051702 * jax.random.uniform(streams_of[4], (N_REP, D, KD), jnp.float32) ** level_of(streams_of[4], (N_REP, D, KD), ((0, 4), (1, 8)), -0.2, 0.2)), 0.1, 10.0)
    anchor = scatter_about(streams_of[5], (D, KD), 1.0, 6.0, ((0, 8),), jnp.float32)
    momentum = scatter_about(streams_of[6], (D, KD), 0.5, 6.0, ((0, 8),), jnp.float32)
    inner_step = jax.random.randint(streams_of[7], (1,), 1, 7).astype(jnp.int32)
    return {"normed": normed, "key_grad": key_grad, "master": master, "first_moment": first_moment, "second_moment": second_moment, "anchor": anchor, "momentum": momentum, "inner_step": inner_step}


beta_first = 0.9
beta_second = 0.95
inner_rate = 0.1
weight_decay = 0.1
epsilon = 1e-08
outer_rate = 0.7
outer_mu = 0.9
mix_weight = 0.5

def reference(normed, key_grad, master, first_moment, second_moment, anchor, momentum, inner_step):
    scale = D ** (-0.5)
    count = inner_step[0].astype(jnp.float32)
    fix_first = 1.0 - jnp.power(jnp.float32(beta_first), count)
    fix_second = 1.0 - jnp.power(jnp.float32(beta_second), count)
    delta_sum = jnp.zeros((D, KD), jnp.float32)
    for index in range(N_REP):
        delta_sum = delta_sum + (anchor - master[index])
    outer_grad = delta_sum / N_REP
    new_momentum = outer_mu * momentum + outer_grad
    new_anchor = anchor - outer_rate * (outer_grad + outer_mu * new_momentum)
    span = TOK_DEV * N_FSDP
    key_parts, grad_parts, merged_parts, first_parts, second_parts = ([], [], [], [], [])
    for index in range(N_REP):
        inputs = normed[index * span:(index + 1) * span]
        cotangent = key_grad[index * span:(index + 1) * span]
        weight_half = master[index].astype(jnp.bfloat16)
        key_parts.append((jnp.dot(inputs, weight_half, preferred_element_type=jnp.float32) * scale).astype(jnp.bfloat16))
        grad_parts.append((jnp.dot(cotangent, weight_half.T, preferred_element_type=jnp.float32) * scale).astype(jnp.bfloat16))
        gradient = lax.dot_general(inputs, cotangent, (((0,), (0,)), ((), ())), preferred_element_type=jnp.float32) * scale
        first_new = beta_first * first_moment[index] + (1.0 - beta_first) * gradient
        second_new = beta_second * second_moment[index] + (1.0 - beta_second) * gradient * gradient
        direction = first_new / fix_first / (jnp.sqrt(second_new / fix_second) + epsilon)
        stepped = master[index] - inner_rate * (direction + weight_decay * master[index])
        merged_parts.append(mix_weight * stepped + (1.0 - mix_weight) * new_anchor)
        first_parts.append(first_new)
        second_parts.append(second_new)
    return (jnp.concatenate(key_parts, 0), jnp.concatenate(grad_parts, 0), jnp.stack(merged_parts), jnp.stack(first_parts), jnp.stack(second_parts), new_anchor, new_momentum)
```

```python
import jax
import jax.numpy as jnp
from jax import lax
from jax.sharding import PartitionSpec as P

beta_first = 0.9
beta_second = 0.95
inner_rate = 0.1
weight_decay = 0.1
epsilon = 1e-08
outer_rate = 0.7
outer_mu = 0.9
mix_weight = 0.5

f32 = jnp.float32
bf16 = jnp.bfloat16


def nesterov(outer_grad, anchor_rows, moment_rows):
    moment_new = outer_mu * moment_rows + outer_grad
    anchor_new = anchor_rows - outer_rate * (outer_grad + outer_mu * moment_new)
    return (anchor_new, moment_new)


def outer_update(local, anchor, momentum):
    delta = anchor - local
    replicas = lax.axis_size("rep")
    summed = lax.psum(delta, "rep")
    return nesterov(summed / replicas, anchor, momentum)


def adam(gradient, local, first_old, second_old, inner_step):
    count_float = inner_step[0].astype(f32)
    fix_first = 1.0 - jnp.power(f32(beta_first), count_float)
    fix_second = 1.0 - jnp.power(f32(beta_second), count_float)
    first_new = beta_first * first_old + (1.0 - beta_first) * gradient
    second_new = beta_second * second_old + (1.0 - beta_second) * gradient * gradient
    direction = first_new / fix_first / (jnp.sqrt(second_new / fix_second) + epsilon)
    stepped = local - inner_rate * (direction + weight_decay * local)
    return (stepped, first_new, second_new)


def whole_pass(normed, key_grad, local):
    scale = normed.shape[1] ** (-0.5)
    weight = lax.all_gather(local.astype(bf16), "fsdp", axis=0, tiled=True)
    keys = (jnp.dot(normed, weight, preferred_element_type=f32) * scale).astype(bf16)
    input_grad = (
        lax.dot_general(key_grad, weight, (((1,), (1,)), ((), ())), preferred_element_type=f32)
        * scale
    ).astype(bf16)
    gradient = lax.psum_scatter(
        lax.dot_general(normed, key_grad, (((0,), (0,)), ((), ())), preferred_element_type=f32)
        * scale,
        "fsdp",
        scatter_dimension=0,
        tiled=True,
    )
    return (keys, input_grad, gradient)


def after(value, *earlier):
    return lax.optimization_barrier((value,) + earlier)[0]


def pair_pass(normed, key_grad, local):
    tokens, width = normed.shape
    rows = local.shape[0]
    scale = width ** (-0.5)
    me = lax.axis_index("fsdp")
    y, z = me % 2, me // 2

    def along(links):
        pairs = [(2 * a + c, 2 * b + c) for a, b in links for c in (0, 1)]
        return lambda value: lax.ppermute(value, "fsdp", pairs)

    outer = along([(0, 1), (1, 0), (2, 3), (3, 2)])
    inner = along([(1, 2), (2, 1)])
    outward = along([(1, 0), (2, 3)])
    inward = along([(0, 1), (3, 2)])

    def swap(value):
        return lax.ppermute(value, "fsdp", [(i, i ^ 1) for i in range(8)])

    far = jnp.where(z < 2, 3, 0)
    middle = jnp.where(z < 2, 2, 1)
    beside = z ^ 1
    order = (far, middle, beside, z)

    def columns(block, half):
        both = lax.dynamic_slice_in_dim(normed, block * (2 * rows), 2 * rows, 1)
        return jnp.where(half == 0, both[:, :rows], both[:, rows:])

    weight = local.astype(bf16)

    w_beside = outer(weight)
    w_inner = inner(weight)
    key_grad_pair = swap(key_grad)
    theirs = [columns(block, 1 - y) for block in order]
    mine = [columns(block, y) for block in order]
    x0 = swap(theirs[0])
    x1 = swap(after(theirs[1], key_grad_pair))
    w_far_inner = inner(w_beside)
    w_middle_outer = outward(w_inner)

    def partial(block, other):
        dims = (((0,), (0,)), ((), ()))
        own = lax.dot_general(mine[block], key_grad, dims, preferred_element_type=f32)
        pair = lax.dot_general(other, key_grad_pair, dims, preferred_element_type=f32)
        return (own + pair) * scale

    def input_part(cotangent, block):
        return (
            lax.dot_general(
                cotangent, block, (((1,), (1,)), ((), ())), preferred_element_type=f32
            )
            * scale
        ).astype(bf16)

    p0 = partial(0, x0)
    r0 = inward(p0.astype(bf16))
    g0 = swap(input_part(key_grad_pair, weight))
    x2 = swap(after(theirs[2], x0))
    p1 = partial(1, x1)
    r1 = inward(after(p1.astype(bf16), r0))
    w_middle = w_inner + w_middle_outer
    w_far_outer = outward(w_far_inner)
    s0 = inner((p0 + r0.astype(f32)).astype(bf16))
    g1 = swap(input_part(key_grad_pair, w_beside))
    x3 = swap(after(theirs[3], x1))
    p2 = partial(2, x2)
    g2 = swap(input_part(key_grad_pair, w_middle))
    s1 = inner((p1 + r1.astype(f32)).astype(bf16))
    t = outer((p2 + s0.astype(f32)).astype(bf16))
    p3 = partial(3, x3)
    w_far = w_far_inner + w_far_outer
    g3 = swap(input_part(key_grad_pair, w_far))
    weights = (w_far, w_middle, w_beside, weight)
    others = (x0, x1, x2, x3)
    key_part = sum(jnp.dot(x, w, preferred_element_type=f32) for x, w in zip(others, weights))
    key_other = swap((key_part * scale).astype(bf16))
    key_own = sum(jnp.dot(x, w, preferred_element_type=f32) for x, w in zip(mine, weights))
    keys = (key_own * scale + key_other.astype(f32)).astype(bf16)
    gradient = p3 + t.astype(f32) + s1.astype(f32)

    input_grad = jnp.zeros((tokens, width), bf16)
    for block, w, other in zip(order, weights, (g3, g2, g1, g0)):
        own = input_part(key_grad, w)
        joined = jnp.where(
            y == 0, jnp.concatenate([own, other], 1), jnp.concatenate([other, own], 1)
        )
        input_grad = lax.dynamic_update_slice_in_dim(input_grad, joined, block * (2 * rows), 1)
    return (keys, input_grad, gradient)


def body(normed, key_grad, master, first_moment, second_moment, anchor, momentum, inner_step):
    local = master[0]
    inner_pass = pair_pass if lax.axis_size("fsdp") == 8 else whole_pass
    keys, input_grad, gradient = inner_pass(normed, key_grad, local)
    stepped, first_new, second_new = adam(
        gradient, local, first_moment[0], second_moment[0], inner_step
    )
    anchor_new, moment_new = outer_update(local, anchor, momentum)
    merged = mix_weight * stepped + (1.0 - mix_weight) * anchor_new
    return (
        keys,
        input_grad,
        merged[None],
        first_new[None],
        second_new[None],
        anchor_new,
        moment_new,
    )


def solution(mesh):
    in_specs = (
        P(("rep", "fsdp"), None),
        P(("rep", "fsdp"), None),
        P("rep", "fsdp", None),
        P("rep", "fsdp", None),
        P("rep", "fsdp", None),
        P("fsdp", None),
        P("fsdp", None),
        P(),
    )
    out_specs = (
        P(("rep", "fsdp"), None),
        P(("rep", "fsdp"), None),
        P("rep", "fsdp", None),
        P("rep", "fsdp", None),
        P("rep", "fsdp", None),
        P("fsdp", None),
        P("fsdp", None),
    )
    return jax.shard_map(body, mesh=mesh, in_specs=in_specs, out_specs=out_specs, check_vma=False)
```

```python
import jax
import jax.numpy as jnp
from jax import lax
from jax.experimental import pallas as pl
from jax.experimental.pallas import tpu as pltpu
from jax.sharding import PartitionSpec as P

beta_first = 0.9
beta_second = 0.95
inner_rate = 0.1
weight_decay = 0.1
epsilon = 1e-08
outer_rate = 0.7
outer_mu = 0.9
mix_weight = 0.5

f32 = jnp.float32
bf16 = jnp.bfloat16
vmem_bytes = 40 * 1024 * 1024


def corrections(inner_step):
    count_float = inner_step[0].astype(f32)
    fix_first = 1.0 - jnp.power(f32(beta_first), count_float)
    fix_second = 1.0 - jnp.power(f32(beta_second), count_float)
    return fix_first, fix_second


def adam(gradient, local, first_old, second_old, fix_first, fix_second):
    first_new = beta_first * first_old + (1.0 - beta_first) * gradient
    second_new = beta_second * second_old + (1.0 - beta_second) * gradient * gradient
    direction = first_new / fix_first / (jnp.sqrt(second_new / fix_second) + epsilon)
    stepped = local - inner_rate * (direction + weight_decay * local)
    return (stepped, first_new, second_new)


def nesterov(outer_grad, anchor_rows, moment_rows):
    moment_new = outer_mu * moment_rows + outer_grad
    anchor_new = anchor_rows - outer_rate * (outer_grad + outer_mu * moment_new)
    return (anchor_new, moment_new)


def outer_update(local, anchor, momentum):
    delta = anchor - local
    replicas = lax.axis_size("rep")
    summed = lax.psum(delta, "rep")
    return nesterov(summed / replicas, anchor, momentum)


def whole_pass(normed, key_grad, local, first_old, second_old, anchor_new, inner_step):
    scale = normed.shape[1] ** (-0.5)
    weight = lax.all_gather(local.astype(bf16), "fsdp", axis=0, tiled=True)
    keys = (jnp.dot(normed, weight, preferred_element_type=f32) * scale).astype(bf16)
    input_grad = (
        lax.dot_general(key_grad, weight, (((1,), (1,)), ((), ())), preferred_element_type=f32)
        * scale
    ).astype(bf16)
    gradient = lax.psum_scatter(
        lax.dot_general(normed, key_grad, (((0,), (0,)), ((), ())), preferred_element_type=f32)
        * scale,
        "fsdp",
        scatter_dimension=0,
        tiled=True,
    )
    stepped, first_new, second_new = adam(
        gradient, local, first_old, second_old, *corrections(inner_step)
    )
    merged = mix_weight * stepped + (1.0 - mix_weight) * anchor_new
    return (keys, input_grad, merged, first_new, second_new)


def after(value, *earlier):
    return lax.optimization_barrier((value,) + earlier)[0]


def call(kernel, out_shape, flops, nbytes, **options):
    return pl.pallas_call(
        kernel,
        out_shape=out_shape,
        compiler_params=pltpu.CompilerParams(vmem_limit_bytes=vmem_bytes),
        cost_estimate=pl.CostEstimate(flops=flops, bytes_accessed=nbytes, transcendentals=0),
        **options,
    )


def half_of(ref, half, rows):
    return jnp.where(half == 0, ref[:, :rows], ref[:, rows : 2 * rows])


def dot_t(a, b):
    return lax.dot_general(a, b, (((0,), (0,)), ((), ())), preferred_element_type=f32)


def dot_bt(a, b):
    return lax.dot_general(a, b, (((1,), (1,)), ((), ())), preferred_element_type=f32)


def gradient_part(place, normed, normed_pair, key_grad, key_grad_pair, scale, dtype):
    tokens, features = key_grad.shape
    rows = normed_pair.shape[1]
    tile = features // 2

    def kernel(place_ref, x_ref, xp_ref, g_ref, gp_ref, out_ref):
        own = half_of(x_ref, place_ref[1], rows)
        total = dot_t(own, g_ref[...]) + dot_t(xp_ref[...], gp_ref[...])
        out_ref[...] = (total * scale).astype(dtype)

    return call(
        kernel,
        jax.ShapeDtypeStruct((rows, features), dtype),
        4 * tokens * rows * features,
        6 * tokens * features,
        grid_spec=pltpu.PrefetchScalarGridSpec(
            num_scalar_prefetch=1,
            grid=(2,),
            in_specs=[
                pl.BlockSpec((tokens, 2 * rows), lambda i, s: (0, s[0])),
                pl.BlockSpec((tokens, rows), lambda i, s: (0, 0)),
                pl.BlockSpec((tokens, tile), lambda i, s: (0, i)),
                pl.BlockSpec((tokens, tile), lambda i, s: (0, i)),
            ],
            out_specs=pl.BlockSpec((rows, tile), lambda i, s: (0, i)),
        ),
    )(place, normed, normed_pair, key_grad, key_grad_pair)


def joined_sum(part, received):
    rows, features = part.shape

    def kernel(a_ref, b_ref, out_ref):
        out_ref[...] = (a_ref[...].astype(f32) + b_ref[...].astype(f32)).astype(bf16)

    block = pl.BlockSpec((rows // 3, features), lambda i: (i, 0))
    return call(
        kernel,
        jax.ShapeDtypeStruct((rows, features), bf16),
        rows * features,
        8 * rows * features,
        grid=(3,),
        in_specs=[block, block],
        out_specs=block,
    )(part, received)


def input_part(cotangent, weight, scale):
    tokens, features = cotangent.shape
    rows = weight.shape[0]
    tile = tokens // 2

    def kernel(g_ref, w_ref, out_ref):
        out_ref[...] = (dot_bt(g_ref[...], w_ref[...]) * scale).astype(bf16)

    return call(
        kernel,
        jax.ShapeDtypeStruct((tokens, rows), bf16),
        2 * tokens * rows * features,
        2 * rows * features + 2 * tokens * features,
        grid=(2,),
        in_specs=[
            pl.BlockSpec((tile, features), lambda i: (i, 0)),
            pl.BlockSpec((rows, features), lambda i: (0, 0)),
        ],
        out_specs=pl.BlockSpec((tile, rows), lambda i: (i, 0)),
    )(cotangent, weight)


def input_join(place, cotangent, weight, other, width, scale, target):
    tokens, features = cotangent.shape
    rows = weight.shape[0]
    tile = tokens // 2

    def kernel(place_ref, g_ref, w_ref, other_ref, *rest):
        out_ref = rest[-1]
        own = (dot_bt(g_ref[...], w_ref[...]) * scale).astype(bf16)

        @pl.when(place_ref[1] == 0)
        def _():
            out_ref[...] = jnp.concatenate([own, other_ref[...]], 1)

        @pl.when(place_ref[1] != 0)
        def _():
            out_ref[...] = jnp.concatenate([other_ref[...], own], 1)

    targets = [] if target is None else [target]
    return call(
        kernel,
        jax.ShapeDtypeStruct((tokens, width), bf16),
        2 * tokens * rows * features,
        2 * rows * features + 2 * tokens * features,
        grid_spec=pltpu.PrefetchScalarGridSpec(
            num_scalar_prefetch=1,
            grid=(2,),
            in_specs=[
                pl.BlockSpec((tile, features), lambda i, s: (i, 0)),
                pl.BlockSpec((rows, features), lambda i, s: (0, 0)),
                pl.BlockSpec((tile, rows), lambda i, s: (i, 0)),
            ]
            + [pl.BlockSpec(memory_space=pl.ANY)] * len(targets),
            out_specs=pl.BlockSpec((tile, 2 * rows), lambda i, s: (i, s[0])),
        ),
        input_output_aliases={4: 0} if targets else {},
    )(place, cotangent, weight, other, *targets)


def key_sums(places, normed, pairs, weights):
    tokens, rows = pairs[0].shape
    features = weights[0].shape[1]
    tile = features // 2
    count = len(weights)

    def kernel(place_ref, *refs):
        xs, xps, ws = refs[:count], refs[count : 2 * count], refs[2 * count : 3 * count]
        own_ref, pair_ref = refs[3 * count :]
        own = pair = 0.0
        for x_ref, xp_ref, w_ref in zip(xs, xps, ws):
            w = w_ref[...]
            half = half_of(x_ref, place_ref[count], rows)
            own += jnp.dot(half, w, preferred_element_type=f32)
            pair += jnp.dot(xp_ref[...], w, preferred_element_type=f32)
        own_ref[...] = own
        pair_ref[...] = pair

    def block_of(k):
        return pl.BlockSpec((tokens, 2 * rows), lambda i, s: (0, s[k]))

    out = pl.BlockSpec((tokens, tile), lambda i, s: (0, i))
    return call(
        kernel,
        [jax.ShapeDtypeStruct((tokens, features), f32)] * 2,
        4 * count * tokens * rows * features,
        2 * count * rows * features + 8 * tokens * features,
        grid_spec=pltpu.PrefetchScalarGridSpec(
            num_scalar_prefetch=1,
            grid=(2,),
            in_specs=[block_of(k) for k in range(count)]
            + [pl.BlockSpec((tokens, rows), lambda i, s: (0, 0))] * count
            + [pl.BlockSpec((rows, tile), lambda i, s: (0, i))] * count,
            out_specs=[out, out],
        ),
    )(places, *([normed] * count), *pairs, *weights)


def key_last(total, inputs, weight, scale):
    tokens, features = total.shape
    rows = weight.shape[0]
    tile = features // 2

    def kernel(total_ref, x_ref, w_ref, out_ref):
        value = total_ref[...] + jnp.dot(x_ref[...], w_ref[...], preferred_element_type=f32)
        out_ref[...] = (value * scale).astype(bf16)

    column = pl.BlockSpec((tokens, tile), lambda i: (0, i))
    return call(
        kernel,
        jax.ShapeDtypeStruct((tokens, features), bf16),
        2 * tokens * rows * features,
        2 * rows * features + 6 * tokens * features,
        grid=(2,),
        in_specs=[
            column,
            pl.BlockSpec((tokens, rows), lambda i: (0, 0)),
            pl.BlockSpec((rows, tile), lambda i: (0, i)),
        ],
        out_specs=column,
    )(total, inputs, weight)


def key_own(place, total, normed, weight, received, scale):
    tokens, features = total.shape
    rows = weight.shape[0]
    tile = features // 2

    def kernel(place_ref, total_ref, x_ref, w_ref, other_ref, out_ref):
        half = half_of(x_ref, place_ref[1], rows)
        value = total_ref[...] + jnp.dot(half, w_ref[...], preferred_element_type=f32)
        out_ref[...] = (value * scale + other_ref[...].astype(f32)).astype(bf16)

    column = pl.BlockSpec((tokens, tile), lambda i, s: (0, i))
    return call(
        kernel,
        jax.ShapeDtypeStruct((tokens, features), bf16),
        2 * tokens * rows * features,
        2 * rows * features + 8 * tokens * features,
        grid_spec=pltpu.PrefetchScalarGridSpec(
            num_scalar_prefetch=1,
            grid=(2,),
            in_specs=[
                column,
                pl.BlockSpec((tokens, 2 * rows), lambda i, s: (0, s[0])),
                pl.BlockSpec((rows, tile), lambda i, s: (0, i)),
                column,
            ],
            out_specs=column,
        ),
    )(place, total, normed, weight, received)


def final_update(fixes, parts, local, first_old, second_old, anchor_new):
    rows, features = local.shape
    count = len(parts)
    tile = rows // 6

    def kernel(fix_ref, *refs):
        gradient = sum(ref[...].astype(f32) for ref in refs[:count])
        local_ref, first_ref, second_ref, anchor_ref, merged_ref, m_ref, v_ref = refs[count:]
        stepped, first_new, second_new = adam(
            gradient, local_ref[...], first_ref[...], second_ref[...], fix_ref[0], fix_ref[1]
        )
        merged_ref[...] = mix_weight * stepped + (1.0 - mix_weight) * anchor_ref[...]
        m_ref[...] = first_new
        v_ref[...] = second_new

    block = pl.BlockSpec((tile, features), lambda i, s: (i, 0))
    return call(
        kernel,
        [jax.ShapeDtypeStruct((rows, features), f32)] * 3,
        20 * rows * features,
        36 * rows * features,
        grid_spec=pltpu.PrefetchScalarGridSpec(
            num_scalar_prefetch=1,
            grid=(6,),
            in_specs=[block] * (count + 4),
            out_specs=[block] * 3,
        ),
    )(fixes, *parts, local, first_old, second_old, anchor_new)


def pair_pass(normed, key_grad, local, first_old, second_old, anchor_new, inner_step):
    tokens, width = normed.shape
    rows = local.shape[0]
    scale = width ** (-0.5)
    me = lax.axis_index("fsdp")
    y, z = me % 2, me // 2

    def along(links):
        pairs = [(2 * a + c, 2 * b + c) for a, b in links for c in (0, 1)]
        return lambda value: lax.ppermute(value, "fsdp", pairs)

    outer = along([(0, 1), (1, 0), (2, 3), (3, 2)])
    inner = along([(1, 2), (2, 1)])
    outward = along([(1, 0), (2, 3)])
    inward = along([(0, 1), (3, 2)])

    def swap(value):
        return lax.ppermute(value, "fsdp", [(i, i ^ 1) for i in range(8)])

    far = jnp.where(z < 2, 3, 0)
    middle = jnp.where(z < 2, 2, 1)
    beside = z ^ 1
    order = (far, middle, beside, z)
    places = [jnp.stack([block, y]).astype(jnp.int32) for block in order]

    def theirs(block):
        both = lax.dynamic_slice_in_dim(normed, block * (2 * rows), 2 * rows, 1)
        return jnp.where(y == 0, both[:, rows:], both[:, :rows])

    weight = local.astype(bf16)

    w_beside = outer(weight)
    w_inner = inner(weight)
    key_grad_pair = swap(key_grad)
    pieces = [theirs(block) for block in order]
    x0 = swap(pieces[0])
    x1 = swap(after(pieces[1], key_grad_pair))
    w_far_inner = inner(w_beside)
    w_middle_outer = outward(w_inner)

    def partial(k, other, dtype):
        return gradient_part(
            places[k], normed, other, key_grad, key_grad_pair, scale, dtype
        )

    p0 = partial(0, x0, bf16)
    r0 = inward(p0)
    g0 = swap(input_part(key_grad_pair, weight, scale))
    x2 = swap(after(pieces[2], x0))
    p1 = partial(1, x1, bf16)
    r1 = inward(after(p1, r0))
    w_middle = w_inner + w_middle_outer
    w_far_outer = outward(w_far_inner)
    s0 = inner(joined_sum(p0, r0))
    g1 = swap(input_part(key_grad_pair, w_beside, scale))
    x3 = swap(after(pieces[3], x1))
    p2 = partial(2, x2, f32)
    g2 = swap(input_part(key_grad_pair, w_middle, scale))
    s1 = inner(joined_sum(p1, r1))
    t = outer(joined_sum(p2, s0))
    p3 = partial(3, x3, f32)
    w_far = w_far_inner + w_far_outer
    own_total, pair_total = key_sums(
        jnp.stack([z, beside, middle, y]).astype(jnp.int32),
        normed,
        (x3, x2, x1),
        (weight, w_beside, w_middle),
    )
    key_pair = swap(key_last(pair_total, x0, w_far, scale))
    g3 = swap(input_part(key_grad_pair, w_far, scale))
    keys = key_own(places[0], own_total, normed, w_far, key_pair, scale)

    input_grad = None
    for k, w, other in ((3, weight, g0), (2, w_beside, g1), (1, w_middle, g2), (0, w_far, g3)):
        input_grad = input_join(places[k], key_grad, w, other, width, scale, input_grad)

    merged, first_new, second_new = final_update(
        jnp.stack(corrections(inner_step)), (p3, t, s1), local, first_old, second_old, anchor_new
    )
    return (keys, input_grad, merged, first_new, second_new)


def body(normed, key_grad, master, first_moment, second_moment, anchor, momentum, inner_step):
    local = master[0]
    anchor_new, moment_new = outer_update(local, anchor, momentum)
    inner_pass = pair_pass if lax.axis_size("fsdp") == 8 else whole_pass
    keys, input_grad, merged, first_new, second_new = inner_pass(
        normed, key_grad, local, first_moment[0], second_moment[0], anchor_new, inner_step
    )
    return (
        keys,
        input_grad,
        merged[None],
        first_new[None],
        second_new[None],
        anchor_new,
        moment_new,
    )


def solution(mesh):
    in_specs = (
        P(("rep", "fsdp"), None),
        P(("rep", "fsdp"), None),
        P("rep", "fsdp", None),
        P("rep", "fsdp", None),
        P("rep", "fsdp", None),
        P("fsdp", None),
        P("fsdp", None),
        P(),
    )
    out_specs = (
        P(("rep", "fsdp"), None),
        P(("rep", "fsdp"), None),
        P("rep", "fsdp", None),
        P("rep", "fsdp", None),
        P("rep", "fsdp", None),
        P("fsdp", None),
        P("fsdp", None),
    )
    return jax.shard_map(body, mesh=mesh, in_specs=in_specs, out_specs=out_specs, check_vma=False)
```

```python
import jax
import jax.numpy as jnp
from jax import lax
from jax.experimental import pallas as pl
from jax.experimental.pallas import tpu as pltpu
from jax.sharding import PartitionSpec as P

beta_first = 0.9
beta_second = 0.95
inner_rate = 0.1
weight_decay = 0.1
epsilon = 1e-08
outer_rate = 0.7
outer_mu = 0.9
mix_weight = 0.5

f32 = jnp.float32
bf16 = jnp.bfloat16
vmem_bytes = 16 * 1024 * 1024


def corrections(inner_step):
    count_float = inner_step[0].astype(f32)
    fix_first = 1.0 - jnp.power(f32(beta_first), count_float)
    fix_second = 1.0 - jnp.power(f32(beta_second), count_float)
    return fix_first, fix_second


def adam(gradient, local, first_old, second_old, fix_first, fix_second):
    first_new = beta_first * first_old + (1.0 - beta_first) * gradient
    second_new = beta_second * second_old + (1.0 - beta_second) * gradient * gradient
    direction = first_new / fix_first / (jnp.sqrt(second_new / fix_second) + epsilon)
    stepped = local - inner_rate * (direction + weight_decay * local)
    return (stepped, first_new, second_new)


def nesterov(outer_grad, anchor_rows, moment_rows):
    moment_new = outer_mu * moment_rows + outer_grad
    anchor_new = anchor_rows - outer_rate * (outer_grad + outer_mu * moment_new)
    return (anchor_new, moment_new)


def outer_update(local, anchor, momentum):
    summed = lax.psum(local, "rep")
    return nesterov(anchor - summed / lax.axis_size("rep"), anchor, momentum)


def whole_pass(normed, key_grad, local, first_old, second_old, anchor_new, inner_step):
    scale = normed.shape[1] ** (-0.5)
    weight = lax.all_gather(local.astype(bf16), "fsdp", axis=0, tiled=True)
    keys = (jnp.dot(normed, weight, preferred_element_type=f32) * scale).astype(bf16)
    input_grad = (
        lax.dot_general(key_grad, weight, (((1,), (1,)), ((), ())), preferred_element_type=f32)
        * scale
    ).astype(bf16)
    gradient = lax.psum_scatter(
        lax.dot_general(normed, key_grad, (((0,), (0,)), ((), ())), preferred_element_type=f32)
        * scale,
        "fsdp",
        scatter_dimension=0,
        tiled=True,
    )
    stepped, first_new, second_new = adam(
        gradient, local, first_old, second_old, *corrections(inner_step)
    )
    merged = mix_weight * stepped + (1.0 - mix_weight) * anchor_new
    return (keys, input_grad, merged, first_new, second_new)


def after(value, *earlier):
    return lax.optimization_barrier((value,) + earlier)[0]


def call(kernel, out_shape, flops, nbytes, **options):
    return pl.pallas_call(
        kernel,
        out_shape=out_shape,
        compiler_params=pltpu.CompilerParams(vmem_limit_bytes=vmem_bytes),
        cost_estimate=pl.CostEstimate(flops=flops, bytes_accessed=nbytes, transcendentals=0),
        **options,
    )


def dot_t(a, b):
    return lax.dot_general(a, b, (((0,), (0,)), ((), ())), preferred_element_type=f32)


def dot_bt(a, b):
    return lax.dot_general(a, b, (((1,), (1,)), ((), ())), preferred_element_type=f32)


def chosen(flag_ref, yes, no):
    return jnp.where(flag_ref[0] != 0, yes, no)


def gradient_part(mine, theirs, key_grad, key_grad_pair, scale, dtype, outer=None, inner_sends=None):
    tokens, rows = mine.shape
    features = key_grad.shape[1]
    tile = features // 2
    extra = inner_sends is not None

    def kernel(flag_ref, x_ref, xp_ref, g_ref, gp_ref, *rest):
        total = dot_t(x_ref[...], g_ref[...]) + dot_t(xp_ref[...], gp_ref[...])
        value = (total * scale).astype(dtype)
        if extra:
            w_ref, out_ref, send_ref = rest
            out_ref[...] = value
            send_ref[...] = chosen(flag_ref, value, w_ref[...])
        else:
            rest[0][...] = value

    whole = pl.BlockSpec((tokens, rows), lambda i, s: (0, 0))
    column = pl.BlockSpec((tokens, tile), lambda i, s: (0, i))
    out = pl.BlockSpec((rows, tile), lambda i, s: (0, i))
    shape = jax.ShapeDtypeStruct((rows, features), dtype)
    flag = jnp.zeros((1,), jnp.int32) if outer is None else outer
    return call(
        kernel,
        [shape, shape] if extra else shape,
        4 * tokens * rows * features,
        6 * tokens * features,
        grid_spec=pltpu.PrefetchScalarGridSpec(
            num_scalar_prefetch=1,
            grid=(2,),
            in_specs=[whole, whole, column, column] + [out] * extra,
            out_specs=[out, out] if extra else out,
        ),
    )(flag, mine, theirs, key_grad, key_grad_pair, *([inner_sends] if extra else []))


def rowwise(kernel, flag, dtype, *arrays):
    rows, features = arrays[0].shape
    steps = 3 if rows % 48 == 0 else 1
    block = pl.BlockSpec((rows // steps, features), lambda i, s: (i, 0))
    return call(
        kernel,
        jax.ShapeDtypeStruct((rows, features), dtype),
        rows * features,
        8 * rows * features,
        grid_spec=pltpu.PrefetchScalarGridSpec(
            num_scalar_prefetch=1,
            grid=(steps,),
            in_specs=[block] * len(arrays),
            out_specs=block,
        ),
    )(flag, *arrays)


def choose(flag, yes, no):
    def kernel(flag_ref, a_ref, b_ref, out_ref):
        out_ref[...] = chosen(flag_ref, a_ref[...], b_ref[...])

    return rowwise(kernel, flag, yes.dtype, yes, no)


def joined_sum(flag, part, received):
    def kernel(flag_ref, a_ref, b_ref, out_ref):
        a = a_ref[...].astype(f32)
        out_ref[...] = chosen(flag_ref, a + b_ref[...].astype(f32), a).astype(bf16)

    return rowwise(kernel, flag, bf16, part, received)


def key_join(flag, total, received, scale):
    def kernel(flag_ref, a_ref, b_ref, out_ref):
        out_ref[...] = (a_ref[...] * scale + b_ref[...].astype(f32)).astype(bf16)

    return rowwise(kernel, flag, bf16, total, received)


def input_part(cotangent, weight, scale):
    tokens, features = cotangent.shape
    rows = weight.shape[0]
    tile = tokens // 2

    def kernel(g_ref, w_ref, out_ref):
        out_ref[...] = (dot_bt(g_ref[...], w_ref[...]) * scale).astype(bf16)

    return call(
        kernel,
        jax.ShapeDtypeStruct((tokens, rows), bf16),
        2 * tokens * rows * features,
        2 * rows * features + 2 * tokens * features,
        grid=(2,),
        in_specs=[
            pl.BlockSpec((tile, features), lambda i: (i, 0)),
            pl.BlockSpec((rows, features), lambda i: (0, 0)),
        ],
        out_specs=pl.BlockSpec((tile, rows), lambda i: (i, 0)),
    )(cotangent, weight)


def input_part_of(flag, cotangent, yes, no, scale):
    tokens, features = cotangent.shape
    rows = yes.shape[0]

    def kernel(flag_ref, g_ref, a_ref, b_ref, out_ref, w_ref):
        weight = chosen(flag_ref, a_ref[...], b_ref[...])
        w_ref[...] = weight
        out_ref[...] = (dot_bt(g_ref[...], weight) * scale).astype(bf16)

    def whole(shape):
        return pl.BlockSpec(shape, lambda i, s: (0, 0))

    return call(
        kernel,
        [
            jax.ShapeDtypeStruct((tokens, rows), bf16),
            jax.ShapeDtypeStruct((rows, features), bf16),
        ],
        2 * tokens * rows * features,
        8 * rows * features + 2 * tokens * features,
        grid_spec=pltpu.PrefetchScalarGridSpec(
            num_scalar_prefetch=1,
            grid=(1,),
            in_specs=[
                whole((tokens, features)),
                whole((rows, features)),
                whole((rows, features)),
            ],
            out_specs=[whole((tokens, rows)), whole((rows, features))],
        ),
    )(flag, cotangent, yes, no)


def input_join(place, cotangent, weight, other, width, scale, target):
    tokens, features = cotangent.shape
    rows = weight.shape[0]
    tile = tokens // 2

    def kernel(place_ref, g_ref, w_ref, other_ref, *rest):
        out_ref = rest[-1]
        own = (dot_bt(g_ref[...], w_ref[...]) * scale).astype(bf16)

        @pl.when(place_ref[1] == 0)
        def _():
            out_ref[...] = jnp.concatenate([own, other_ref[...]], 1)

        @pl.when(place_ref[1] != 0)
        def _():
            out_ref[...] = jnp.concatenate([other_ref[...], own], 1)

    targets = [] if target is None else [target]
    return call(
        kernel,
        jax.ShapeDtypeStruct((tokens, width), bf16),
        2 * tokens * rows * features,
        2 * rows * features + 2 * tokens * features,
        grid_spec=pltpu.PrefetchScalarGridSpec(
            num_scalar_prefetch=1,
            grid=(2,),
            in_specs=[
                pl.BlockSpec((tile, features), lambda i, s: (i, 0)),
                pl.BlockSpec((rows, features), lambda i, s: (0, 0)),
                pl.BlockSpec((tile, rows), lambda i, s: (i, 0)),
            ]
            + [pl.BlockSpec(memory_space=pl.ANY)] * len(targets),
            out_specs=pl.BlockSpec((tile, 2 * rows), lambda i, s: (i, s[0])),
        ),
        input_output_aliases={4: 0} if targets else {},
    )(place, cotangent, weight, other, *targets)


def key_sums(mine, theirs, weights):
    tokens, rows = mine[0].shape
    features = weights[0].shape[1]
    tile = features // 2
    count = len(weights)

    def kernel(*refs):
        xs, xps, ws = refs[:count], refs[count : 2 * count], refs[2 * count : 3 * count]
        own_ref, pair_ref = refs[3 * count :]
        own = pair = 0.0
        for x_ref, xp_ref, w_ref in zip(xs, xps, ws):
            w = w_ref[...]
            own += jnp.dot(x_ref[...], w, preferred_element_type=f32)
            pair += jnp.dot(xp_ref[...], w, preferred_element_type=f32)
        own_ref[...] = own
        pair_ref[...] = pair

    out = pl.BlockSpec((tokens, tile), lambda i: (0, i))
    return call(
        kernel,
        [jax.ShapeDtypeStruct((tokens, features), f32)] * 2,
        4 * count * tokens * rows * features,
        2 * count * rows * features + 8 * tokens * features,
        grid=(2,),
        in_specs=[pl.BlockSpec((tokens, rows), lambda i: (0, 0))] * (2 * count)
        + [pl.BlockSpec((rows, tile), lambda i: (0, i))] * count,
        out_specs=[out, out],
    )(*mine, *theirs, *weights)


def key_last(total, inputs, weight, scale, dtype):
    tokens, features = total.shape
    rows = weight.shape[0]
    tile = features // 2

    def kernel(total_ref, x_ref, w_ref, out_ref):
        value = total_ref[...] + jnp.dot(x_ref[...], w_ref[...], preferred_element_type=f32)
        out_ref[...] = (value * scale).astype(dtype)

    column = pl.BlockSpec((tokens, tile), lambda i: (0, i))
    return call(
        kernel,
        jax.ShapeDtypeStruct((tokens, features), dtype),
        2 * tokens * rows * features,
        2 * rows * features + 6 * tokens * features,
        grid=(2,),
        in_specs=[
            column,
            pl.BlockSpec((tokens, rows), lambda i: (0, 0)),
            pl.BlockSpec((rows, tile), lambda i: (0, i)),
        ],
        out_specs=column,
    )(total, inputs, weight)


def final_update(flag, fixes, part, received, inner_received, local, first_old, second_old, anchor_new):
    rows, features = local.shape
    tile = rows // 6

    def kernel(flag_ref, fix_ref, p_ref, t_ref, s_ref, local_ref, first_ref, second_ref, anchor_ref, *out):
        merged_ref, m_ref, v_ref = out
        gradient = p_ref[...] + t_ref[...].astype(f32)
        gradient = chosen(flag_ref, gradient + s_ref[...].astype(f32), gradient)
        stepped, first_new, second_new = adam(
            gradient, local_ref[...], first_ref[...], second_ref[...], fix_ref[0], fix_ref[1]
        )
        merged_ref[...] = mix_weight * stepped + (1.0 - mix_weight) * anchor_ref[...]
        m_ref[...] = first_new
        v_ref[...] = second_new

    block = pl.BlockSpec((tile, features), lambda i, s, c: (i, 0))
    return call(
        kernel,
        [jax.ShapeDtypeStruct((rows, features), f32)] * 3,
        20 * rows * features,
        36 * rows * features,
        grid_spec=pltpu.PrefetchScalarGridSpec(
            num_scalar_prefetch=2,
            grid=(6,),
            in_specs=[block] * 7,
            out_specs=[block] * 3,
        ),
    )(flag, fixes, part, received, inner_received, local, first_old, second_old, anchor_new)


def pair_pass(normed, key_grad, local, first_old, second_old, anchor_new, inner_step):
    tokens, width = normed.shape
    rows = local.shape[0]
    scale = width ** (-0.5)
    me = lax.axis_index("fsdp")
    y, z = me % 2, me // 2
    inside = ((z == 1) | (z == 2)).astype(jnp.int32)[None]
    at_end = 1 - inside

    def along(partner):
        pairs = [(2 * a + c, 2 * partner[a] + c) for a in range(4) for c in (0, 1)]
        return lambda value: lax.ppermute(value, "fsdp", pairs)

    outer = along((1, 0, 3, 2))
    inner = along((0, 2, 1, 3))

    def swap(value):
        return lax.ppermute(value, "fsdp", [(i, i ^ 1) for i in range(8)])

    far = jnp.where(z < 2, 3, 0)
    middle = jnp.where(z < 2, 2, 1)
    beside = z ^ 1
    order = (far, middle, beside, z)
    places = [jnp.stack([block, y]).astype(jnp.int32) for block in order]

    def columns(block, half):
        both = lax.dynamic_slice_in_dim(normed, block * (2 * rows), 2 * rows, 1)
        return jnp.where(half == 0, both[:, :rows], both[:, rows:])

    g_pair = swap(key_grad)
    weight = local.astype(bf16)
    w_beside = outer(weight)
    w_inner = inner(weight)
    pieces = [columns(block, 1 - y) for block in order]
    x0 = swap(pieces[0])
    mine = [columns(block, y) for block in order]

    def partial(k, other, dtype, **sends):
        return gradient_part(mine[k], other, key_grad, g_pair, scale, dtype, **sends)

    i0 = input_part(g_pair, weight, scale)
    g0 = swap(i0)
    mine[0] = after(mine[0], i0)
    p0, send = partial(0, x0, bf16, outer=at_end, inner_sends=w_inner)
    c1 = outer(send)
    w_across = inner(w_beside)
    x1 = swap(after(pieces[1], x0))
    i1 = input_part(g_pair, w_beside, scale)
    x2 = swap(after(pieces[2], g0))
    p1 = partial(1, x1, bf16)
    g1 = swap(after(i1, x1))
    x3 = swap(after(pieces[3], x2))
    p2 = partial(2, x2, f32)

    q2 = inner(joined_sum(inside, after(p0, p2), c1))
    c2 = outer(choose(at_end, p1, w_across))
    i2, w_middle = input_part_of(inside, g_pair, w_inner, c1, scale)
    g2 = swap(after(i2, g1))
    p3 = partial(3, x3, f32)
    own_total, pair_total = key_sums(mine[1:], (x1, x2, x3), (w_middle, w_beside, weight))
    input_grad = input_join(places[3], key_grad, weight, g0, width, scale, None)
    input_grad = input_join(places[2], key_grad, w_beside, g1, width, scale, input_grad)

    qa = outer(joined_sum(inside, after(p2, own_total, p3, input_grad), q2))
    qb = inner(joined_sum(inside, p1, c2))
    i3, w_far = input_part_of(inside, g_pair, w_across, c2, scale)
    key_pair = swap(key_last(pair_total, x0, w_far, scale, bf16))
    g3 = swap(after(i3, g2))
    own_total = key_last(own_total, mine[0], w_far, 1.0, f32)
    input_grad = input_join(places[1], key_grad, w_middle, g2, width, scale, input_grad)
    keys = key_join(inside, after(own_total, input_grad, anchor_new), key_pair, scale)
    input_grad = input_join(places[0], key_grad, w_far, g3, width, scale, input_grad)

    merged, first_new, second_new = final_update(
        inside, jnp.stack(corrections(inner_step)), p3, qa, qb, local, first_old, second_old, anchor_new
    )
    return (keys, input_grad, merged, first_new, second_new)


def body(normed, key_grad, master, first_moment, second_moment, anchor, momentum, inner_step):
    local = master[0]
    anchor_new, moment_new = outer_update(local, anchor, momentum)
    inner_pass = pair_pass if lax.axis_size("fsdp") == 8 else whole_pass
    keys, input_grad, merged, first_new, second_new = inner_pass(
        normed, key_grad, local, first_moment[0], second_moment[0], anchor_new, inner_step
    )
    return (
        keys,
        input_grad,
        merged[None],
        first_new[None],
        second_new[None],
        anchor_new,
        moment_new,
    )


def solution(mesh):
    in_specs = (
        P(("rep", "fsdp"), None),
        P(("rep", "fsdp"), None),
        P("rep", "fsdp", None),
        P("rep", "fsdp", None),
        P("rep", "fsdp", None),
        P("fsdp", None),
        P("fsdp", None),
        P(),
    )
    out_specs = (
        P(("rep", "fsdp"), None),
        P(("rep", "fsdp"), None),
        P("rep", "fsdp", None),
        P("rep", "fsdp", None),
        P("rep", "fsdp", None),
        P("fsdp", None),
        P("fsdp", None),
    )
    return jax.shard_map(body, mesh=mesh, in_specs=in_specs, out_specs=out_specs, check_vma=False)
```

```python
import jax
import jax.numpy as jnp
from jax import lax
from jax.experimental import pallas as pl
from jax.experimental.pallas import tpu as pltpu
from jax.sharding import PartitionSpec as P

beta_first = 0.9
beta_second = 0.95
inner_rate = 0.1
weight_decay = 0.1
epsilon = 1e-08
outer_rate = 0.7
outer_mu = 0.9
mix_weight = 0.5

f32 = jnp.float32
bf16 = jnp.bfloat16
vmem_bytes = 16 * 1024 * 1024
wait_factor = 40


def corrections(inner_step):
    count_float = inner_step[0].astype(f32)
    fix_first = 1.0 - jnp.power(f32(beta_first), count_float)
    fix_second = 1.0 - jnp.power(f32(beta_second), count_float)
    return fix_first, fix_second


def adam(gradient, local, first_old, second_old, fix_first, fix_second):
    first_new = beta_first * first_old + (1.0 - beta_first) * gradient
    second_new = beta_second * second_old + (1.0 - beta_second) * gradient * gradient
    direction = first_new / fix_first / (jnp.sqrt(second_new / fix_second) + epsilon)
    stepped = local - inner_rate * (direction + weight_decay * local)
    return (stepped, first_new, second_new)


def nesterov(outer_grad, anchor_rows, moment_rows):
    moment_new = outer_mu * moment_rows + outer_grad
    anchor_new = anchor_rows - outer_rate * (outer_grad + outer_mu * moment_new)
    return (anchor_new, moment_new)


def outer_update(local, anchor, momentum):
    summed = lax.psum(local, "rep")
    return nesterov(anchor - summed / lax.axis_size("rep"), anchor, momentum)


def whole_pass(normed, key_grad, local, first_old, second_old, anchor, momentum, inner_step):
    scale = normed.shape[1] ** (-0.5)
    weight = lax.all_gather(local.astype(bf16), "fsdp", axis=0, tiled=True)
    keys = (jnp.dot(normed, weight, preferred_element_type=f32) * scale).astype(bf16)
    input_grad = (
        lax.dot_general(key_grad, weight, (((1,), (1,)), ((), ())), preferred_element_type=f32)
        * scale
    ).astype(bf16)
    gradient = lax.psum_scatter(
        lax.dot_general(normed, key_grad, (((0,), (0,)), ((), ())), preferred_element_type=f32)
        * scale,
        "fsdp",
        scatter_dimension=0,
        tiled=True,
    )
    stepped, first_new, second_new = adam(
        gradient, local, first_old, second_old, *corrections(inner_step)
    )
    anchor_new, moment_new = outer_update(local, anchor, momentum)
    merged = mix_weight * stepped + (1.0 - mix_weight) * anchor_new
    return (keys, input_grad, merged, first_new, second_new, anchor_new, moment_new)


FAR, MIDDLE, BESIDE, OWN, Y, INNER, END = range(7)


class Order:
    def __init__(self, place):
        self.place = place
        self.token = None

    def call(self, kernel, inputs, outputs, grid, flops=0, aliases=None, fixes=None):
        scalars = [self.place] + ([] if fixes is None else [fixes])
        tokens = [] if self.token is None else [self.token]
        before = len(scalars) + len(inputs)

        def wrapped(*refs):
            refs[-1][...] = jnp.zeros_like(refs[-1])
            kernel(*refs[:before], *refs[before + len(tokens) : -1])

        outputs = outputs + [whole(shaped(jnp.int32, 8, 128))]
        shapes = [shape for shape, _, _ in outputs]
        nbytes = sum(a.size * a.dtype.itemsize for a, _, _ in inputs) + sum(
            a.size * a.dtype.itemsize for a in shapes
        )
        keep = pl.BlockSpec(memory_space=pl.ANY)
        out = pl.pallas_call(
            wrapped,
            out_shape=shapes,
            grid_spec=pltpu.PrefetchScalarGridSpec(
                num_scalar_prefetch=len(scalars),
                grid=grid,
                in_specs=[
                    keep if block is None else pl.BlockSpec(block, index)
                    for _, block, index in inputs
                ]
                + [keep] * len(tokens),
                out_specs=[pl.BlockSpec(block, index) for _, block, index in outputs],
            ),
            input_output_aliases=aliases or {},
            compiler_params=pltpu.CompilerParams(vmem_limit_bytes=vmem_bytes),
            cost_estimate=pl.CostEstimate(flops=flops, bytes_accessed=nbytes, transcendentals=0),
        )(*scalars, *[a for a, _, _ in inputs], *tokens)
        self.token = out[-1]
        return out[0] if len(out) == 2 else out[:-1]


def shaped(dtype, *shape):
    return jax.ShapeDtypeStruct(shape, dtype)


def whole(array):
    zeros = (0,) * len(array.shape)
    return (array, array.shape, lambda *_: zeros)


def rowwise(array, steps):
    return (array, (array.shape[0] // steps, array.shape[1]), lambda i, *_: (i, 0))


def columnwise(array, steps):
    return (array, (array.shape[0], array.shape[1] // steps), lambda i, *_: (0, i))


def stacked(array, k, rows):
    return (array, (rows, array.shape[1]), lambda *_: (k, 0))


def dot_t(a, b):
    return lax.dot_general(a, b, (((0,), (0,)), ((), ())), preferred_element_type=f32)


def dot_bt(a, b):
    return lax.dot_general(a, b, (((1,), (1,)), ((), ())), preferred_element_type=f32)


def dot(a, b):
    return jnp.dot(a, b, preferred_element_type=f32)


def chosen(flag, yes, no):
    return jnp.where(flag != 0, yes, no)


def halves(x_ref, rows):
    turned = x_ref[...].T
    return turned[:rows], turned[rows:]


def prepare(order, normed, local):
    tokens = normed.shape[0]
    rows = local.shape[0]

    def kernel(s_ref, x_ref, a_ref, piece_ref, out_ref):
        out_ref[...] = a_ref[...].astype(bf16)

        @pl.when(pl.program_id(0) == 0)
        def _():
            low, high = halves(x_ref, rows)
            piece_ref[...] = chosen(s_ref[Y], low, high)

    return order.call(
        kernel,
        [(normed, (tokens, 2 * rows), lambda i, s: (0, s[FAR])), rowwise(local, 3)],
        [whole(shaped(bf16, rows, tokens)), rowwise(shaped(bf16, *local.shape), 3)],
        (3,),
    )


def split(order, normed, rows, g_pair):
    tokens = normed.shape[0]

    def kernel(s_ref, x_ref, g_ref, one_ref, two_ref, own_ref):
        i = pl.program_id(0)
        low, high = halves(x_ref, rows)
        own_ref[...] = chosen(s_ref[Y], high, low)

        @pl.when(i == 0)
        def _():
            one_ref[...] = chosen(s_ref[Y], low, high)

        @pl.when((i == 1) | (i == 2))
        def _():
            two_ref[...] = chosen(s_ref[Y], low, high)

    return order.call(
        kernel,
        [
            (normed, (tokens, 2 * rows), lambda i, s: (0, s[(i + 1) % 4])),
            (g_pair, None, None),
        ],
        [
            whole(shaped(bf16, rows, tokens)),
            (
                shaped(bf16, 2 * rows, tokens),
                (rows, tokens),
                lambda i, s: (jnp.clip(i - 1, 0, 1), 0),
            ),
            (shaped(bf16, 4 * rows, tokens), (rows, tokens), lambda i, s: ((i + 1) % 4, 0)),
        ],
        (4,),
    )


def gradient_part(order, mine, k, theirs, key_grad, g_pair, scale, weights=()):
    rows, tokens = theirs.shape
    features = key_grad.shape[1]

    def kernel(s_ref, x_ref, xp_ref, g_ref, gp_ref, *rest):
        total = dot(x_ref[...], g_ref[...]) + dot(xp_ref[...], gp_ref[...])
        value = (total * scale).astype(bf16)
        if not weights:
            rest[0][...] = value
        else:
            inner_ref, beside_ref, out_ref, send_ref, across_ref = rest
            out_ref[...] = value
            send_ref[...] = chosen(s_ref[END], value, inner_ref[...])
            across_ref[...] = beside_ref[...]

    extra = [columnwise(w, 2) for w in weights]
    out = columnwise(shaped(bf16, rows, features), 2)
    return order.call(
        kernel,
        [stacked(mine, k, rows), whole(theirs), columnwise(key_grad, 2), columnwise(g_pair, 2)]
        + extra,
        [out] + [out] * len(extra),
        (2,),
        4 * tokens * rows * features * (1 if weights else wait_factor),
    )


def gradient_rest(order, mine, theirs, key_grad, g_pair, scale):
    rows, tokens = theirs.shape
    rows //= 2
    features = key_grad.shape[1]
    tile = features // 2

    def kernel(s_ref, x_ref, xp_ref, g_ref, gp_ref, out_ref):
        total = dot(x_ref[...], g_ref[...]) + dot(xp_ref[...], gp_ref[...])
        out_ref[...] = total * scale

    return order.call(
        kernel,
        [
            (mine, (rows, tokens), lambda k, i, s: (k + 2, 0)),
            (theirs, (rows, tokens), lambda k, i, s: (k, 0)),
            (key_grad, (tokens, tile), lambda k, i, s: (0, i)),
            (g_pair, (tokens, tile), lambda k, i, s: (0, i)),
        ],
        [(shaped(f32, 2 * rows, features), (rows, tile), lambda k, i, s: (k, i))],
        (2, 2),
        8 * tokens * rows * features,
    )


def input_parts(order, cotangent, first, second, scale):
    tokens, features = cotangent.shape
    rows = first.shape[0]

    def kernel(s_ref, g_ref, a_ref, b_ref, out_ref):
        @pl.when(pl.program_id(0) == 0)
        def _():
            out_ref[...] = (dot_bt(a_ref[...], g_ref[...]) * scale).astype(bf16)

        @pl.when(pl.program_id(0) == 1)
        def _():
            out_ref[...] = (dot_bt(b_ref[...], g_ref[...]) * scale).astype(bf16)

    return order.call(
        kernel,
        [whole(cotangent), whole(first), whole(second)],
        [(shaped(bf16, 2 * rows, tokens), (rows, tokens), lambda i, s: (i, 0))],
        (2,),
        4 * tokens * rows * features,
    )


def input_part_of(order, cotangent, yes, no, scale):
    tokens, features = cotangent.shape
    rows = yes.shape[0]

    def kernel(s_ref, g_ref, a_ref, b_ref, out_ref, w_ref):
        weight = chosen(s_ref[INNER], a_ref[...], b_ref[...])
        w_ref[...] = weight
        out_ref[...] = (dot_bt(weight, g_ref[...]) * scale).astype(bf16)

    return order.call(
        kernel,
        [whole(cotangent), whole(yes), whole(no)],
        [whole(shaped(bf16, rows, tokens)), whole(shaped(bf16, rows, features))],
        (1,),
        2 * tokens * rows * features,
    )


def store_joined(y, out_ref, own, other):
    @pl.when(y == 0)
    def _():
        out_ref[...] = jnp.concatenate([own, other], 0).T

    @pl.when(y != 0)
    def _():
        out_ref[...] = jnp.concatenate([other, own], 0).T


def input_join(order, slot, cotangent, weight, other, scale, target):
    tokens, features = cotangent.shape
    rows = weight.shape[0]

    def kernel(s_ref, g_ref, w_ref, other_ref, target_ref, out_ref):
        own = (dot_bt(w_ref[...], g_ref[...]) * scale).astype(bf16)
        store_joined(s_ref[Y], out_ref, own, other_ref[...])

    return order.call(
        kernel,
        [rowwise(cotangent, 3), whole(weight), columnwise(other, 3), (target, None, None)],
        [(target, (tokens // 3, 2 * rows), lambda i, s: (i, s[slot]))],
        (3,),
        2 * tokens * rows * features,
        {4: 0},
    )


def input_join_two(order, cotangent, first, second, others, width, scale):
    tokens, features = cotangent.shape
    rows = first.shape[0]
    tile = tokens // 3

    def kernel(s_ref, g_ref, a_ref, b_ref, other_ref, out_ref):
        weight = chosen(pl.program_id(0), b_ref[...], a_ref[...])
        own = (dot_bt(weight, g_ref[...]) * scale).astype(bf16)
        store_joined(s_ref[Y], out_ref, own, other_ref[...])

    return order.call(
        kernel,
        [
            (cotangent, (tile, features), lambda k, i, s: (i, 0)),
            whole(first),
            whole(second),
            (others, (rows, tile), lambda k, i, s: (k, i)),
        ],
        [
            (
                shaped(bf16, tokens, width),
                (tile, 2 * rows),
                lambda k, i, s: (i, s[OWN - k]),
            )
        ],
        (2, 3),
        4 * tokens * rows * features,
    )


def key_sums(order, mine, theirs_one, theirs_two, weights):
    rows, tokens = theirs_one.shape
    features = weights[0].shape[1]

    def kernel(s_ref, x_ref, one_ref, two_ref, *refs):
        own_ref, pair_ref = refs[3:]
        own = pair = 0.0
        for k in range(3):
            w = refs[k][...]
            theirs = one_ref[...] if k == 0 else two_ref[(k - 1) * rows : k * rows]
            own += dot_t(x_ref[(k + 1) * rows : (k + 2) * rows], w)
            pair += dot_t(theirs, w)
        own_ref[...] = own
        pair_ref[...] = pair

    out = columnwise(shaped(f32, tokens, features), 2)
    return order.call(
        kernel,
        [whole(mine), whole(theirs_one), whole(theirs_two)] + [columnwise(w, 2) for w in weights],
        [out, out],
        (2,),
        12 * tokens * rows * features,
    )


def key_last(order, total, inputs, weight, scale, dtype):
    tokens, features = total.shape
    rows = weight.shape[0]

    def kernel(s_ref, total_ref, x_ref, w_ref, out_ref):
        value = total_ref[...] + dot_t(x_ref[...], w_ref[...])
        out_ref[...] = (value * scale).astype(dtype)

    return order.call(
        kernel,
        [columnwise(total, 2), stacked(inputs, 0, rows), columnwise(weight, 2)],
        [columnwise(shaped(dtype, tokens, features), 2)],
        (2,),
        2 * tokens * rows * features,
    )


def add(order, dtype, a, b):
    def kernel(s_ref, a_ref, b_ref, out_ref):
        out_ref[...] = (a_ref[...].astype(f32) + b_ref[...].astype(f32)).astype(dtype)

    return order.call(
        kernel, [rowwise(a, 3), rowwise(b, 3)], [rowwise(shaped(dtype, *a.shape), 3)], (3,), a.size
    )


def first_handoff(order, p0, c1, p1, w_across):
    def kernel(s_ref, p0_ref, c1_ref, p1_ref, w_ref, sum_ref, send_ref):
        sum_ref[...] = (p0_ref[...].astype(f32) + c1_ref[...].astype(f32)).astype(bf16)
        send_ref[...] = chosen(s_ref[END], p1_ref[...], w_ref[...])

    out = rowwise(shaped(bf16, *p0.shape), 3)
    return order.call(
        kernel, [rowwise(a, 3) for a in (p0, c1, p1, w_across)], [out, out], (3,), p0.size
    )


def second_handoff(order, p1, c2, p23, q2, g2):
    def kernel(s_ref, p1_ref, c2_ref, p2_ref, q2_ref, g2_ref, s1_ref, t_ref):
        s1_ref[...] = (p1_ref[...].astype(f32) + c2_ref[...].astype(f32)).astype(bf16)
        t_ref[...] = (p2_ref[...] + q2_ref[...].astype(f32)).astype(bf16)

    out = rowwise(shaped(bf16, *p1.shape), 3)
    return order.call(
        kernel,
        [rowwise(p1, 3), rowwise(c2, 3), rowwise(p23, 6), rowwise(q2, 3), (g2, None, None)],
        [out, out],
        (3,),
        p1.size,
    )


def nesterov_pass(order, chip_sum, other_chip, anchor, momentum):
    def kernel(s_ref, a_ref, b_ref, anchor_ref, momentum_ref, anchor_new_ref, moment_new_ref):
        outer_grad = anchor_ref[...] - (a_ref[...] + b_ref[...]) / 4
        anchor_new, moment_new = nesterov(outer_grad, anchor_ref[...], momentum_ref[...])
        anchor_new_ref[...] = anchor_new
        moment_new_ref[...] = moment_new

    out = rowwise(shaped(f32, *anchor.shape), 6)
    return order.call(
        kernel,
        [rowwise(a, 6) for a in (chip_sum, other_chip, anchor, momentum)],
        [out, out],
        (6,),
        8 * anchor.size,
    )


def key_join(order, total, received, scale):
    def kernel(s_ref, a_ref, b_ref, out_ref):
        out_ref[...] = (a_ref[...] * scale + b_ref[...].astype(f32)).astype(bf16)

    return order.call(
        kernel,
        [rowwise(total, 3), rowwise(received, 3)],
        [rowwise(shaped(bf16, *total.shape), 3)],
        (3,),
        total.size,
    )


def final_update(order, fixes, p23, t, s1, local, first_old, second_old, anchor_new):
    rows, features = local.shape
    tile = rows // 6

    def kernel(s_ref, fix_ref, p_ref, t_ref, s1_ref, local_ref, first_ref, second_ref, anchor_ref, *out):
        merged_ref, m_ref, v_ref = out
        gradient = p_ref[...] + t_ref[...].astype(f32) + s1_ref[...].astype(f32)
        stepped, first_new, second_new = adam(
            gradient, local_ref[...], first_ref[...], second_ref[...], fix_ref[0], fix_ref[1]
        )
        merged_ref[...] = mix_weight * stepped + (1.0 - mix_weight) * anchor_ref[...]
        m_ref[...] = first_new
        v_ref[...] = second_new

    out = rowwise(shaped(f32, *local.shape), 6)
    return order.call(
        kernel,
        [(p23, (tile, features), lambda i, *_: (i + 6, 0))]
        + [rowwise(a, 6) for a in (t, s1, local, first_old, second_old, anchor_new)],
        [out, out, out],
        (6,),
        20 * local.size,
        fixes=fixes,
    )


def pair_pass(normed, key_grad, local, first_old, second_old, anchor, momentum, inner_step):
    width = normed.shape[1]
    rows = local.shape[0]
    scale = width ** (-0.5)
    me = lax.axis_index("fsdp")
    y, z = me % 2, me // 2
    inside = (z == 1) | (z == 2)
    far = jnp.where(z < 2, 3, 0)
    middle = jnp.where(z < 2, 2, 1)
    order = Order(jnp.stack([far, middle, z ^ 1, z, y, inside, ~inside]).astype(jnp.int32))

    def along(links):
        pairs = [(2 * a + c, 2 * b + c) for a, b in links for c in (0, 1)]
        return lambda value: lax.ppermute(value, "fsdp", pairs)

    outer = along([(0, 1), (1, 0), (2, 3), (3, 2)])
    inner = along([(1, 2), (2, 1)])

    def swap(value):
        return lax.ppermute(value, "fsdp", [(i, i ^ 1) for i in range(8)])

    def replica(value, bit):
        return lax.ppermute(value, "rep", [(i, i ^ bit) for i in range(4)])

    g_pair = swap(key_grad)
    piece, weight = prepare(order, normed, local)
    x0 = swap(piece)
    w_beside = outer(weight)
    w_inner = inner(weight)
    chip_sum = add(order, f32, local, replica(local, 1))
    other_chip = replica(chip_sum, 2)
    one, two, mine = split(order, normed, rows, g_pair)
    x1 = swap(one)

    p0, send, across = gradient_part(
        order, mine, 0, x0, key_grad, g_pair, scale, (w_inner, w_beside)
    )
    c1 = outer(send)
    w_across = inner(across)
    x23 = swap(two)
    i01 = input_parts(order, g_pair, weight, w_beside, scale)
    g01 = swap(i01)
    p1 = gradient_part(order, mine, 1, x1, key_grad, g_pair, scale)

    s0, send = first_handoff(order, p0, c1, p1, w_across)
    c2 = outer(send)
    q2 = inner(s0)
    i2, w_middle = input_part_of(order, g_pair, w_inner, c1, scale)
    g2 = swap(i2)
    p23 = gradient_rest(order, mine, x23, key_grad, g_pair, scale)
    own_total, pair_total = key_sums(order, mine, x1, x23, (w_middle, w_beside, weight))
    input_grad = input_join_two(order, key_grad, weight, w_beside, g01, width, scale)

    i3, w_far = input_part_of(order, g_pair, w_across, c2, scale)
    g3 = swap(i3)
    s1, t = second_handoff(order, p1, c2, p23, q2, g2)
    qa = outer(t)
    qb = inner(s1)
    key_pair = swap(key_last(order, pair_total, x0, w_far, scale, bf16))
    own_total = key_last(order, own_total, mine, w_far, 1.0, f32)
    input_grad = input_join(order, MIDDLE, key_grad, w_middle, g2, scale, input_grad)
    anchor_new, moment_new = nesterov_pass(order, chip_sum, other_chip, anchor, momentum)
    input_grad = input_join(order, FAR, key_grad, w_far, g3, scale, input_grad)
    keys = key_join(order, own_total, key_pair, scale)

    merged, first_new, second_new = final_update(
        order,
        jnp.stack(corrections(inner_step)),
        p23,
        qa,
        qb,
        local,
        first_old,
        second_old,
        anchor_new,
    )
    return (keys, input_grad, merged, first_new, second_new, anchor_new, moment_new)


def body(normed, key_grad, master, first_moment, second_moment, anchor, momentum, inner_step):
    local = master[0]
    sizes = (lax.axis_size("rep"), lax.axis_size("fsdp"))
    inner_pass = pair_pass if sizes == (4, 8) else whole_pass
    keys, input_grad, merged, first_new, second_new, anchor_new, moment_new = inner_pass(
        normed, key_grad, local, first_moment[0], second_moment[0], anchor, momentum, inner_step
    )
    return (
        keys,
        input_grad,
        merged[None],
        first_new[None],
        second_new[None],
        anchor_new,
        moment_new,
    )


def solution(mesh):
    in_specs = (
        P(("rep", "fsdp"), None),
        P(("rep", "fsdp"), None),
        P("rep", "fsdp", None),
        P("rep", "fsdp", None),
        P("rep", "fsdp", None),
        P("fsdp", None),
        P("fsdp", None),
        P(),
    )
    out_specs = (
        P(("rep", "fsdp"), None),
        P(("rep", "fsdp"), None),
        P("rep", "fsdp", None),
        P("rep", "fsdp", None),
        P("rep", "fsdp", None),
        P("fsdp", None),
        P("fsdp", None),
    )
    return jax.shard_map(body, mesh=mesh, in_specs=in_specs, out_specs=out_specs, check_vma=False)
```

```python
import jax
import jax.numpy as jnp
from jax import lax
from jax.experimental import pallas as pl
from jax.experimental.pallas import tpu as pltpu
from jax.sharding import PartitionSpec as P

beta_first = 0.9
beta_second = 0.95
inner_rate = 0.1
weight_decay = 0.1
epsilon = 1e-08
outer_rate = 0.7
outer_mu = 0.9
mix_weight = 0.5

f32 = jnp.float32
bf16 = jnp.bfloat16
vmem_bytes = 16 * 1024 * 1024


def corrections(inner_step):
    count_float = inner_step[0].astype(f32)
    fix_first = 1.0 - jnp.power(f32(beta_first), count_float)
    fix_second = 1.0 - jnp.power(f32(beta_second), count_float)
    return fix_first, fix_second


def adam(gradient, local, first_old, second_old, fix_first, fix_second):
    first_new = beta_first * first_old + (1.0 - beta_first) * gradient
    second_new = beta_second * second_old + (1.0 - beta_second) * gradient * gradient
    direction = first_new / fix_first / (jnp.sqrt(second_new / fix_second) + epsilon)
    stepped = local - inner_rate * (direction + weight_decay * local)
    return (stepped, first_new, second_new)


def nesterov(outer_grad, anchor_rows, moment_rows):
    moment_new = outer_mu * moment_rows + outer_grad
    anchor_new = anchor_rows - outer_rate * (outer_grad + outer_mu * moment_new)
    return (anchor_new, moment_new)


def outer_update(local, anchor, momentum):
    summed = lax.psum(local, "rep")
    return nesterov(anchor - summed / lax.axis_size("rep"), anchor, momentum)


def whole_pass(normed, key_grad, local, first_old, second_old, anchor, momentum, inner_step):
    scale = normed.shape[1] ** (-0.5)
    weight = lax.all_gather(local.astype(bf16), "fsdp", axis=0, tiled=True)
    keys = (jnp.dot(normed, weight, preferred_element_type=f32) * scale).astype(bf16)
    input_grad = (
        lax.dot_general(key_grad, weight, (((1,), (1,)), ((), ())), preferred_element_type=f32)
        * scale
    ).astype(bf16)
    gradient = lax.psum_scatter(
        lax.dot_general(normed, key_grad, (((0,), (0,)), ((), ())), preferred_element_type=f32)
        * scale,
        "fsdp",
        scatter_dimension=0,
        tiled=True,
    )
    stepped, first_new, second_new = adam(
        gradient, local, first_old, second_old, *corrections(inner_step)
    )
    anchor_new, moment_new = outer_update(local, anchor, momentum)
    merged = mix_weight * stepped + (1.0 - mix_weight) * anchor_new
    return (keys, input_grad, merged, first_new, second_new, anchor_new, moment_new)


FAR, MIDDLE, BESIDE, OWN, Y, INNER, END = range(7)


class Order:
    def __init__(self, place):
        self.place = place
        self.token = None

    def call(self, kernel, inputs, outputs, grid, span=1, aliases=None, fixes=None):
        scalars = [self.place] + ([] if fixes is None else [fixes])
        tokens = [] if self.token is None else [self.token]
        before = len(scalars) + len(inputs)

        def wrapped(*refs):
            refs[-1][...] = jnp.zeros_like(refs[-1])
            kernel(*refs[:before], *refs[before + len(tokens) : -1])

        outputs = outputs + [whole(shaped(jnp.int32, 8, 128))]
        shapes = [shape for shape, _, _ in outputs]
        keep = pl.BlockSpec(memory_space=pl.ANY)
        out = pl.pallas_call(
            wrapped,
            out_shape=shapes,
            grid_spec=pltpu.PrefetchScalarGridSpec(
                num_scalar_prefetch=len(scalars),
                grid=grid,
                in_specs=[
                    keep if block is None else pl.BlockSpec(block, index)
                    for _, block, index in inputs
                ]
                + [keep] * len(tokens),
                out_specs=[pl.BlockSpec(block, index) for _, block, index in outputs],
            ),
            input_output_aliases=aliases or {},
            compiler_params=pltpu.CompilerParams(vmem_limit_bytes=vmem_bytes),
            cost_estimate=pl.CostEstimate(
                flops=int(span * 1e9), bytes_accessed=0, transcendentals=0
            ),
        )(*scalars, *[a for a, _, _ in inputs], *tokens)
        self.token = out[-1]
        return out[0] if len(out) == 2 else out[:-1]


def shaped(dtype, *shape):
    return jax.ShapeDtypeStruct(shape, dtype)


def whole(array):
    zeros = (0,) * len(array.shape)
    return (array, array.shape, lambda *_: zeros)


def rowwise(array, steps):
    return (array, (array.shape[0] // steps, array.shape[1]), lambda i, *_: (i, 0))


def columnwise(array, steps):
    return (array, (array.shape[0], array.shape[1] // steps), lambda i, *_: (0, i))


def stacked(array, k, rows):
    return (array, (rows, array.shape[1]), lambda *_: (k, 0))


def dot_t(a, b):
    return lax.dot_general(a, b, (((0,), (0,)), ((), ())), preferred_element_type=f32)


def dot_bt(a, b):
    return lax.dot_general(a, b, (((1,), (1,)), ((), ())), preferred_element_type=f32)


def dot(a, b):
    return jnp.dot(a, b, preferred_element_type=f32)


def chosen(flag, yes, no):
    return jnp.where(flag != 0, yes, no)


def halves(x_ref, rows):
    turned = x_ref[...].T
    return turned[:rows], turned[rows:]


def rounded(order, local):
    def kernel(s_ref, a_ref, out_ref):
        out_ref[...] = a_ref[...].astype(bf16)

    return order.call(
        kernel, [rowwise(local, 3)], [rowwise(shaped(bf16, *local.shape), 3)], (3,)
    )


def first_piece(order, normed, rows):
    tokens = normed.shape[0]

    def kernel(s_ref, x_ref, piece_ref):
        low, high = halves(x_ref, rows)
        piece_ref[...] = chosen(s_ref[Y], low, high)

    return order.call(
        kernel,
        [(normed, (tokens, 2 * rows), lambda i, s: (0, s[FAR]))],
        [whole(shaped(bf16, rows, tokens))],
        (1,),
    )


def split(order, normed, rows, g_pair):
    tokens = normed.shape[0]

    def kernel(s_ref, x_ref, g_ref, rest_ref, own_ref):
        low, high = halves(x_ref, rows)
        own_ref[...] = chosen(s_ref[Y], high, low)

        @pl.when(pl.program_id(0) < 3)
        def _():
            rest_ref[...] = chosen(s_ref[Y], low, high)

    return order.call(
        kernel,
        [
            (normed, (tokens, 2 * rows), lambda i, s: (0, s[(i + 1) % 4])),
            (g_pair, None, None),
        ],
        [
            (
                shaped(bf16, 3 * rows, tokens),
                (rows, tokens),
                lambda i, s: (jnp.minimum(i, 2), 0),
            ),
            (shaped(bf16, 4 * rows, tokens), (rows, tokens), lambda i, s: ((i + 1) % 4, 0)),
        ],
        (4,),
        30,
    )


def gradient_part(order, mine, k, theirs, key_grad, g_pair, scale, weights=()):
    tokens, features = key_grad.shape
    rows = mine.shape[0] // 4

    def kernel(s_ref, x_ref, xp_ref, g_ref, gp_ref, *rest):
        total = dot(x_ref[...], g_ref[...]) + dot(xp_ref[...], gp_ref[...])
        value = (total * scale).astype(bf16)
        if not weights:
            rest[0][...] = value
        else:
            inner_ref, beside_ref, out_ref, send_ref, across_ref = rest
            out_ref[...] = value
            send_ref[...] = chosen(s_ref[END], value, inner_ref[...])
            across_ref[...] = beside_ref[...]

    extra = [columnwise(w, 2) for w in weights]
    out = columnwise(shaped(bf16, rows, features), 2)
    return order.call(
        kernel,
        [
            stacked(mine, k, rows),
            stacked(theirs, 0, rows),
            columnwise(key_grad, 2),
            columnwise(g_pair, 2),
        ]
        + extra,
        [out] + [out] * len(extra),
        (2,),
        1 if weights else 30,
    )


def gradient_rest(order, mine, theirs, key_grad, g_pair, scale):
    tokens, features = key_grad.shape
    rows = mine.shape[0] // 4
    tile = features // 2

    def kernel(s_ref, x_ref, xp_ref, g_ref, gp_ref, out_ref):
        total = dot(x_ref[...], g_ref[...]) + dot(xp_ref[...], gp_ref[...])
        out_ref[...] = total * scale

    return order.call(
        kernel,
        [
            (mine, (rows, tokens), lambda k, i, s: (k + 2, 0)),
            (theirs, (rows, tokens), lambda k, i, s: (k + 1, 0)),
            (key_grad, (tokens, tile), lambda k, i, s: (0, i)),
            (g_pair, (tokens, tile), lambda k, i, s: (0, i)),
        ],
        [(shaped(f32, 2 * rows, features), (rows, tile), lambda k, i, s: (k, i))],
        (2, 2),
        0,
    )


def input_parts(order, cotangent, first, second, scale):
    tokens, features = cotangent.shape
    rows = first.shape[0]

    def kernel(s_ref, g_ref, a_ref, b_ref, out_ref):
        @pl.when(pl.program_id(0) == 0)
        def _():
            out_ref[...] = (dot_bt(a_ref[...], g_ref[...]) * scale).astype(bf16)

        @pl.when(pl.program_id(0) == 1)
        def _():
            out_ref[...] = (dot_bt(b_ref[...], g_ref[...]) * scale).astype(bf16)

    return order.call(
        kernel,
        [whole(cotangent), whole(first), whole(second)],
        [(shaped(bf16, 2 * rows, tokens), (rows, tokens), lambda i, s: (i, 0))],
        (2,),
        30,
    )


def input_part_of(order, cotangent, yes, no, scale):
    tokens, features = cotangent.shape
    rows = yes.shape[0]

    def kernel(s_ref, g_ref, a_ref, b_ref, out_ref, w_ref):
        weight = chosen(s_ref[INNER], a_ref[...], b_ref[...])
        w_ref[...] = weight
        out_ref[...] = (dot_bt(weight, g_ref[...]) * scale).astype(bf16)

    return order.call(
        kernel,
        [whole(cotangent), whole(yes), whole(no)],
        [whole(shaped(bf16, rows, tokens)), whole(shaped(bf16, rows, features))],
        (1,),
        0,
    )


def store_joined(y, out_ref, own, other):
    @pl.when(y == 0)
    def _():
        out_ref[...] = jnp.concatenate([own, other], 0).T

    @pl.when(y != 0)
    def _():
        out_ref[...] = jnp.concatenate([other, own], 0).T


def input_join(order, slot, cotangent, weight, other, scale, target):
    tokens, features = cotangent.shape
    rows = weight.shape[0]

    def kernel(s_ref, g_ref, w_ref, other_ref, target_ref, out_ref):
        own = (dot_bt(w_ref[...], g_ref[...]) * scale).astype(bf16)
        store_joined(s_ref[Y], out_ref, own, other_ref[...])

    return order.call(
        kernel,
        [rowwise(cotangent, 3), whole(weight), columnwise(other, 3), (target, None, None)],
        [(target, (tokens // 3, 2 * rows), lambda i, s: (i, s[slot]))],
        (3,),
        10 if slot == FAR else 0,
        {4: 0},
    )


def input_join_two(order, cotangent, first, second, others, width, scale):
    tokens, features = cotangent.shape
    rows = first.shape[0]
    tile = tokens // 3

    def kernel(s_ref, g_ref, a_ref, b_ref, other_ref, out_ref):
        weight = chosen(pl.program_id(0), b_ref[...], a_ref[...])
        own = (dot_bt(weight, g_ref[...]) * scale).astype(bf16)
        store_joined(s_ref[Y], out_ref, own, other_ref[...])

    return order.call(
        kernel,
        [
            (cotangent, (tile, features), lambda k, i, s: (i, 0)),
            whole(first),
            whole(second),
            (others, (rows, tile), lambda k, i, s: (k, i)),
        ],
        [
            (
                shaped(bf16, tokens, width),
                (tile, 2 * rows),
                lambda k, i, s: (i, s[OWN - k]),
            )
        ],
        (2, 3),
        8,
    )


def key_sums(order, mine, theirs, weights):
    rows, tokens = mine.shape[0] // 4, mine.shape[1]
    features = weights[0].shape[1]

    def kernel(s_ref, x_ref, xp_ref, *refs):
        own_ref, pair_ref = refs[3:]
        own = pair = 0.0
        for k in range(3):
            w = refs[k][...]
            own += dot_t(x_ref[(k + 1) * rows : (k + 2) * rows], w)
            pair += dot_t(xp_ref[k * rows : (k + 1) * rows], w)
        own_ref[...] = own
        pair_ref[...] = pair

    out = columnwise(shaped(f32, tokens, features), 2)
    return order.call(
        kernel,
        [whole(mine), whole(theirs)] + [columnwise(w, 2) for w in weights],
        [out, out],
        (2,),
        0,
    )


def key_last(order, total, inputs, weight, scale, dtype):
    tokens, features = total.shape
    rows = weight.shape[0]

    def kernel(s_ref, total_ref, x_ref, w_ref, out_ref):
        value = total_ref[...] + dot_t(x_ref[...], w_ref[...])
        out_ref[...] = (value * scale).astype(dtype)

    return order.call(
        kernel,
        [columnwise(total, 2), stacked(inputs, 0, rows), columnwise(weight, 2)],
        [columnwise(shaped(dtype, tokens, features), 2)],
        (2,),
        0,
    )


def add(order, dtype, a, b):
    def kernel(s_ref, a_ref, b_ref, out_ref):
        out_ref[...] = (a_ref[...].astype(f32) + b_ref[...].astype(f32)).astype(dtype)

    return order.call(
        kernel, [rowwise(a, 3), rowwise(b, 3)], [rowwise(shaped(dtype, *a.shape), 3)], (3,)
    )


def first_handoff(order, p0, c1, p1, w_across):
    def kernel(s_ref, p0_ref, c1_ref, p1_ref, w_ref, sum_ref, send_ref):
        sum_ref[...] = (p0_ref[...].astype(f32) + c1_ref[...].astype(f32)).astype(bf16)
        send_ref[...] = chosen(s_ref[END], p1_ref[...], w_ref[...])

    out = rowwise(shaped(bf16, *p0.shape), 3)
    return order.call(
        kernel, [rowwise(a, 3) for a in (p0, c1, p1, w_across)], [out, out], (3,)
    )


def second_handoff(order, p1, c2, p23, q2, g2):
    def kernel(s_ref, p1_ref, c2_ref, p2_ref, q2_ref, g2_ref, s1_ref, t_ref):
        s1_ref[...] = (p1_ref[...].astype(f32) + c2_ref[...].astype(f32)).astype(bf16)
        t_ref[...] = (p2_ref[...] + q2_ref[...].astype(f32)).astype(bf16)

    out = rowwise(shaped(bf16, *p1.shape), 3)
    return order.call(
        kernel,
        [rowwise(p1, 3), rowwise(c2, 3), rowwise(p23, 6), rowwise(q2, 3), (g2, None, None)],
        [out, out],
        (3,),
    )


def nesterov_pass(order, chip_sum, other_chip, anchor, momentum):
    def kernel(s_ref, a_ref, b_ref, anchor_ref, momentum_ref, anchor_new_ref, moment_new_ref):
        outer_grad = anchor_ref[...] - (a_ref[...] + b_ref[...]) / 4
        anchor_new, moment_new = nesterov(outer_grad, anchor_ref[...], momentum_ref[...])
        anchor_new_ref[...] = anchor_new
        moment_new_ref[...] = moment_new

    out = rowwise(shaped(f32, *anchor.shape), 6)
    return order.call(
        kernel,
        [rowwise(a, 6) for a in (chip_sum, other_chip, anchor, momentum)],
        [out, out],
        (6,),
    )


def key_join(order, total, received, scale):
    def kernel(s_ref, a_ref, b_ref, out_ref):
        out_ref[...] = (a_ref[...] * scale + b_ref[...].astype(f32)).astype(bf16)

    return order.call(
        kernel,
        [rowwise(total, 3), rowwise(received, 3)],
        [rowwise(shaped(bf16, *total.shape), 3)],
        (3,),
    )


def final_update(order, fixes, p23, t, s1, local, first_old, second_old, anchor_new):
    rows, features = local.shape
    tile = rows // 6

    def kernel(s_ref, fix_ref, p_ref, t_ref, s1_ref, local_ref, first_ref, second_ref, anchor_ref, *out):
        merged_ref, m_ref, v_ref = out
        gradient = p_ref[...] + t_ref[...].astype(f32) + s1_ref[...].astype(f32)
        stepped, first_new, second_new = adam(
            gradient, local_ref[...], first_ref[...], second_ref[...], fix_ref[0], fix_ref[1]
        )
        merged_ref[...] = mix_weight * stepped + (1.0 - mix_weight) * anchor_ref[...]
        m_ref[...] = first_new
        v_ref[...] = second_new

    out = rowwise(shaped(f32, *local.shape), 6)
    return order.call(
        kernel,
        [(p23, (tile, features), lambda i, *_: (i + 6, 0))]
        + [rowwise(a, 6) for a in (t, s1, local, first_old, second_old, anchor_new)],
        [out, out, out],
        (6,),
        fixes=fixes,
    )


def pair_pass(normed, key_grad, local, first_old, second_old, anchor, momentum, inner_step):
    width = normed.shape[1]
    rows = local.shape[0]
    scale = width ** (-0.5)
    me = lax.axis_index("fsdp")
    y, z = me % 2, me // 2
    inside = (z == 1) | (z == 2)
    far = jnp.where(z < 2, 3, 0)
    middle = jnp.where(z < 2, 2, 1)
    order = Order(jnp.stack([far, middle, z ^ 1, z, y, inside, ~inside]).astype(jnp.int32))

    def along(links):
        pairs = [(2 * a + c, 2 * b + c) for a, b in links for c in (0, 1)]
        return lambda value: lax.ppermute(value, "fsdp", pairs)

    outer = along([(0, 1), (1, 0), (2, 3), (3, 2)])
    inner = along([(1, 2), (2, 1)])

    def swap(value):
        return lax.ppermute(value, "fsdp", [(i, i ^ 1) for i in range(8)])

    def replica(value, bit):
        return lax.ppermute(value, "rep", [(i, i ^ bit) for i in range(4)])

    g_pair = swap(key_grad)
    weight = rounded(order, local)
    w_beside = outer(weight)
    w_inner = inner(weight)
    x0 = swap(first_piece(order, normed, rows))
    chip_sum = add(order, f32, local, replica(local, 1))
    other_chip = replica(chip_sum, 2)
    rest, mine = split(order, normed, rows, g_pair)
    x123 = swap(rest)

    p0, send, across = gradient_part(
        order, mine, 0, x0, key_grad, g_pair, scale, (w_inner, w_beside)
    )
    c1 = outer(send)
    w_across = inner(across)
    i01 = input_parts(order, g_pair, weight, w_beside, scale)
    g01 = swap(i01)
    p1 = gradient_part(order, mine, 1, x123, key_grad, g_pair, scale)

    s0, send = first_handoff(order, p0, c1, p1, w_across)
    c2 = outer(send)
    q2 = inner(s0)
    i2, w_middle = input_part_of(order, g_pair, w_inner, c1, scale)
    g2 = swap(i2)
    p23 = gradient_rest(order, mine, x123, key_grad, g_pair, scale)
    own_total, pair_total = key_sums(order, mine, x123, (w_middle, w_beside, weight))
    input_grad = input_join_two(order, key_grad, weight, w_beside, g01, width, scale)

    i3, w_far = input_part_of(order, g_pair, w_across, c2, scale)
    g3 = swap(i3)
    s1, t = second_handoff(order, p1, c2, p23, q2, g2)
    qa = outer(t)
    qb = inner(s1)
    key_pair = swap(key_last(order, pair_total, x0, w_far, scale, bf16))
    own_total = key_last(order, own_total, mine, w_far, 1.0, f32)
    input_grad = input_join(order, MIDDLE, key_grad, w_middle, g2, scale, input_grad)
    anchor_new, moment_new = nesterov_pass(order, chip_sum, other_chip, anchor, momentum)
    input_grad = input_join(order, FAR, key_grad, w_far, g3, scale, input_grad)
    keys = key_join(order, own_total, key_pair, scale)

    merged, first_new, second_new = final_update(
        order,
        jnp.stack(corrections(inner_step)),
        p23,
        qa,
        qb,
        local,
        first_old,
        second_old,
        anchor_new,
    )
    return (keys, input_grad, merged, first_new, second_new, anchor_new, moment_new)


def body(normed, key_grad, master, first_moment, second_moment, anchor, momentum, inner_step):
    local = master[0]
    sizes = (lax.axis_size("rep"), lax.axis_size("fsdp"))
    inner_pass = pair_pass if sizes == (4, 8) else whole_pass
    keys, input_grad, merged, first_new, second_new, anchor_new, moment_new = inner_pass(
        normed, key_grad, local, first_moment[0], second_moment[0], anchor, momentum, inner_step
    )
    return (
        keys,
        input_grad,
        merged[None],
        first_new[None],
        second_new[None],
        anchor_new,
        moment_new,
    )


def solution(mesh):
    in_specs = (
        P(("rep", "fsdp"), None),
        P(("rep", "fsdp"), None),
        P("rep", "fsdp", None),
        P("rep", "fsdp", None),
        P("rep", "fsdp", None),
        P("fsdp", None),
        P("fsdp", None),
        P(),
    )
    out_specs = (
        P(("rep", "fsdp"), None),
        P(("rep", "fsdp"), None),
        P("rep", "fsdp", None),
        P("rep", "fsdp", None),
        P("rep", "fsdp", None),
        P("fsdp", None),
        P("fsdp", None),
    )
    return jax.shard_map(body, mesh=mesh, in_specs=in_specs, out_specs=out_specs, check_vma=False)
```

```python
import jax
import jax.numpy as jnp
from jax import lax
from jax.experimental import pallas as pl
from jax.experimental.pallas import tpu as pltpu
from jax.sharding import PartitionSpec as P

beta_first = 0.9
beta_second = 0.95
inner_rate = 0.1
weight_decay = 0.1
epsilon = 1e-08
outer_rate = 0.7
outer_mu = 0.9
mix_weight = 0.5

f32 = jnp.float32
bf16 = jnp.bfloat16
vmem_bytes = 16 * 1024 * 1024


def corrections(inner_step):
    count_float = inner_step[0].astype(f32)
    fix_first = 1.0 - jnp.power(f32(beta_first), count_float)
    fix_second = 1.0 - jnp.power(f32(beta_second), count_float)
    return fix_first, fix_second


def adam(gradient, local, first_old, second_old, fix_first, fix_second):
    first_new = beta_first * first_old + (1.0 - beta_first) * gradient
    second_new = beta_second * second_old + (1.0 - beta_second) * gradient * gradient
    direction = first_new / fix_first / (jnp.sqrt(second_new / fix_second) + epsilon)
    stepped = local - inner_rate * (direction + weight_decay * local)
    return (stepped, first_new, second_new)


def nesterov(outer_grad, anchor_rows, moment_rows):
    moment_new = outer_mu * moment_rows + outer_grad
    anchor_new = anchor_rows - outer_rate * (outer_grad + outer_mu * moment_new)
    return (anchor_new, moment_new)


def outer_update(local, anchor, momentum):
    summed = lax.psum(anchor - local, "rep")
    return nesterov(summed / lax.axis_size("rep"), anchor, momentum)


def whole_pass(normed, key_grad, local, first_old, second_old, anchor, momentum, inner_step):
    scale = normed.shape[1] ** (-0.5)
    weight = lax.all_gather(local.astype(bf16), "fsdp", axis=0, tiled=True)
    keys = (jnp.dot(normed, weight, preferred_element_type=f32) * scale).astype(bf16)
    input_grad = (
        lax.dot_general(key_grad, weight, (((1,), (1,)), ((), ())), preferred_element_type=f32)
        * scale
    ).astype(bf16)
    gradient = lax.psum_scatter(
        lax.dot_general(normed, key_grad, (((0,), (0,)), ((), ())), preferred_element_type=f32)
        * scale,
        "fsdp",
        scatter_dimension=0,
        tiled=True,
    )
    stepped, first_new, second_new = adam(
        gradient, local, first_old, second_old, *corrections(inner_step)
    )
    anchor_new, moment_new = outer_update(local, anchor, momentum)
    merged = mix_weight * stepped + (1.0 - mix_weight) * anchor_new
    return (keys, input_grad, merged, first_new, second_new, anchor_new, moment_new)


FAR, MIDDLE, BESIDE, OWN, Y, INNER, END = range(7)


class Order:
    def __init__(self, place):
        self.place = place
        self.token = None

    def call(self, kernel, inputs, outputs, grid, span=1, aliases=None, fixes=None):
        scalars = [self.place] + ([] if fixes is None else [fixes])
        tokens = [] if self.token is None else [self.token]
        before = len(scalars) + len(inputs)

        def wrapped(*refs):
            refs[-1][...] = jnp.zeros_like(refs[-1])
            kernel(*refs[:before], *refs[before + len(tokens) : -1])

        outputs = outputs + [whole(shaped(jnp.int32, 8, 128))]
        shapes = [shape for shape, _, _ in outputs]
        keep = pl.BlockSpec(memory_space=pl.ANY)
        out = pl.pallas_call(
            wrapped,
            out_shape=shapes,
            grid_spec=pltpu.PrefetchScalarGridSpec(
                num_scalar_prefetch=len(scalars),
                grid=grid,
                in_specs=[
                    keep if block is None else pl.BlockSpec(block, index)
                    for _, block, index in inputs
                ]
                + [keep] * len(tokens),
                out_specs=[pl.BlockSpec(block, index) for _, block, index in outputs],
            ),
            input_output_aliases=aliases or {},
            compiler_params=pltpu.CompilerParams(vmem_limit_bytes=vmem_bytes),
            cost_estimate=pl.CostEstimate(
                flops=int(span * 1e9), bytes_accessed=0, transcendentals=0
            ),
        )(*scalars, *[a for a, _, _ in inputs], *tokens)
        self.token = out[-1]
        return out[0] if len(out) == 2 else out[:-1]


def shaped(dtype, *shape):
    return jax.ShapeDtypeStruct(shape, dtype)


def whole(array):
    zeros = (0,) * len(array.shape)
    return (array, array.shape, lambda *_: zeros)


def rowwise(array, steps):
    return (array, (array.shape[0] // steps, array.shape[1]), lambda i, *_: (i, 0))


def columnwise(array, steps):
    return (array, (array.shape[0], array.shape[1] // steps), lambda i, *_: (0, i))


def stacked(array, k, rows):
    return (array, (rows, array.shape[1]), lambda *_: (k, 0))


def dot_t(a, b):
    return lax.dot_general(a, b, (((0,), (0,)), ((), ())), preferred_element_type=f32)


def dot_bt(a, b):
    return lax.dot_general(a, b, (((1,), (1,)), ((), ())), preferred_element_type=f32)


def dot(a, b):
    return jnp.dot(a, b, preferred_element_type=f32)


def chosen(flag, yes, no):
    return jnp.where(flag != 0, yes, no)


def halves(x_ref, rows):
    turned = x_ref[...].T
    return turned[:rows], turned[rows:]


def rounded(order, local):
    def kernel(s_ref, a_ref, out_ref):
        out_ref[...] = a_ref[...].astype(bf16)

    return order.call(
        kernel, [rowwise(local, 3)], [rowwise(shaped(bf16, *local.shape), 3)], (3,)
    )


def first_piece(order, normed, rows):
    tokens = normed.shape[0]

    def kernel(s_ref, x_ref, piece_ref):
        low, high = halves(x_ref, rows)
        piece_ref[...] = chosen(s_ref[Y], low, high)

    return order.call(
        kernel,
        [(normed, (tokens, 2 * rows), lambda i, s: (0, s[FAR]))],
        [whole(shaped(bf16, rows, tokens))],
        (1,),
    )


def split(order, normed, rows, g_pair, fixes):
    tokens = normed.shape[0]

    def kernel(s_ref, fix_ref, x_ref, g_ref, rest_ref, own_ref):
        low, high = halves(x_ref, rows)
        own_ref[...] = chosen(s_ref[Y], high, low)

        @pl.when(pl.program_id(0) < 3)
        def _():
            rest_ref[...] = chosen(s_ref[Y], low, high)

    return order.call(
        kernel,
        [
            (normed, (tokens, 2 * rows), lambda i, s, f: (0, s[(i + 1) % 4])),
            (g_pair, None, None),
        ],
        [
            (
                shaped(bf16, 3 * rows, tokens),
                (rows, tokens),
                lambda i, s, f: (jnp.minimum(i, 2), 0),
            ),
            (shaped(bf16, 4 * rows, tokens), (rows, tokens), lambda i, s, f: ((i + 1) % 4, 0)),
        ],
        (4,),
        30,
        fixes=fixes,
    )


def gradient_part(order, mine, k, theirs, key_grad, g_pair, scale, span=0):
    tokens, features = key_grad.shape
    rows = mine.shape[0] // 4

    def kernel(s_ref, x_ref, xp_ref, g_ref, gp_ref, out_ref):
        total = dot(x_ref[...], g_ref[...]) + dot(xp_ref[...], gp_ref[...])
        out_ref[...] = (total * scale).astype(bf16)

    return order.call(
        kernel,
        [
            stacked(mine, k, rows),
            stacked(theirs, 0, rows),
            columnwise(key_grad, 2),
            columnwise(g_pair, 2),
        ],
        [columnwise(shaped(bf16, rows, features), 2)],
        (2,),
        span,
    )


def gradient_rest(order, mine, theirs, key_grad, g_pair, scale):
    tokens, features = key_grad.shape
    rows = mine.shape[0] // 4
    tile = features // 2

    def kernel(s_ref, x_ref, xp_ref, g_ref, gp_ref, out_ref):
        total = dot(x_ref[...], g_ref[...]) + dot(xp_ref[...], gp_ref[...])
        out_ref[...] = total * scale

    return order.call(
        kernel,
        [
            (mine, (rows, tokens), lambda k, i, s: (k + 2, 0)),
            (theirs, (rows, tokens), lambda k, i, s: (k + 1, 0)),
            (key_grad, (tokens, tile), lambda k, i, s: (0, i)),
            (g_pair, (tokens, tile), lambda k, i, s: (0, i)),
        ],
        [(shaped(f32, 2 * rows, features), (rows, tile), lambda k, i, s: (k, i))],
        (2, 2),
        0,
    )


def input_parts(order, cotangent, first, second, scale):
    tokens, features = cotangent.shape
    rows = first.shape[0]

    def kernel(s_ref, g_ref, a_ref, b_ref, out_ref):
        @pl.when(pl.program_id(0) == 0)
        def _():
            out_ref[...] = (dot_bt(a_ref[...], g_ref[...]) * scale).astype(bf16)

        @pl.when(pl.program_id(0) == 1)
        def _():
            out_ref[...] = (dot_bt(b_ref[...], g_ref[...]) * scale).astype(bf16)

    return order.call(
        kernel,
        [whole(cotangent), whole(first), whole(second)],
        [(shaped(bf16, 2 * rows, tokens), (rows, tokens), lambda i, s: (i, 0))],
        (2,),
        30,
    )


def input_part_of(order, cotangent, yes, no, scale):
    tokens, features = cotangent.shape
    rows = yes.shape[0]

    def kernel(s_ref, g_ref, a_ref, b_ref, out_ref, w_ref):
        weight = chosen(s_ref[INNER], a_ref[...], b_ref[...])
        w_ref[...] = weight
        out_ref[...] = (dot_bt(weight, g_ref[...]) * scale).astype(bf16)

    return order.call(
        kernel,
        [whole(cotangent), whole(yes), whole(no)],
        [whole(shaped(bf16, rows, tokens)), whole(shaped(bf16, rows, features))],
        (1,),
        0,
    )


def store_joined(y, out_ref, own, other):
    @pl.when(y == 0)
    def _():
        out_ref[...] = jnp.concatenate([own, other], 0).T

    @pl.when(y != 0)
    def _():
        out_ref[...] = jnp.concatenate([other, own], 0).T


def input_join(order, slot, cotangent, weight, other, scale, target):
    tokens, features = cotangent.shape
    rows = weight.shape[0]

    def kernel(s_ref, g_ref, w_ref, other_ref, target_ref, out_ref):
        own = (dot_bt(w_ref[...], g_ref[...]) * scale).astype(bf16)
        store_joined(s_ref[Y], out_ref, own, other_ref[...])

    return order.call(
        kernel,
        [rowwise(cotangent, 3), whole(weight), columnwise(other, 3), (target, None, None)],
        [(target, (tokens // 3, 2 * rows), lambda i, s: (i, s[slot]))],
        (3,),
        10 if slot == FAR else 0,
        {4: 0},
    )


def input_join_two(order, cotangent, first, second, others, width, scale):
    tokens, features = cotangent.shape
    rows = first.shape[0]
    tile = tokens // 3

    def kernel(s_ref, g_ref, a_ref, b_ref, other_ref, out_ref):
        weight = chosen(pl.program_id(0), b_ref[...], a_ref[...])
        own = (dot_bt(weight, g_ref[...]) * scale).astype(bf16)
        store_joined(s_ref[Y], out_ref, own, other_ref[...])

    return order.call(
        kernel,
        [
            (cotangent, (tile, features), lambda k, i, s: (i, 0)),
            whole(first),
            whole(second),
            (others, (rows, tile), lambda k, i, s: (k, i)),
        ],
        [
            (
                shaped(bf16, tokens, width),
                (tile, 2 * rows),
                lambda k, i, s: (i, s[OWN - k]),
            )
        ],
        (2, 3),
        8,
    )


def key_sums(order, mine, theirs, weights):
    rows, tokens = mine.shape[0] // 4, mine.shape[1]
    features = weights[0].shape[1]

    def kernel(s_ref, x_ref, xp_ref, *refs):
        own_ref, pair_ref = refs[3:]
        own = pair = 0.0
        for k in range(3):
            w = refs[k][...]
            own += dot_t(x_ref[(k + 1) * rows : (k + 2) * rows], w)
            pair += dot_t(xp_ref[k * rows : (k + 1) * rows], w)
        own_ref[...] = own
        pair_ref[...] = pair

    out = columnwise(shaped(f32, tokens, features), 2)
    return order.call(
        kernel,
        [whole(mine), whole(theirs)] + [columnwise(w, 2) for w in weights],
        [out, out],
        (2,),
        0,
    )


def key_last(order, total, inputs, weight, scale, dtype):
    tokens, features = total.shape
    rows = weight.shape[0]

    def kernel(s_ref, total_ref, x_ref, w_ref, out_ref):
        value = total_ref[...] + dot_t(x_ref[...], w_ref[...])
        out_ref[...] = (value * scale).astype(dtype)

    return order.call(
        kernel,
        [columnwise(total, 2), stacked(inputs, 0, rows), columnwise(weight, 2)],
        [columnwise(shaped(dtype, tokens, features), 2)],
        (2,),
        0,
    )


def add(order, a, b):
    def kernel(s_ref, a_ref, b_ref, out_ref):
        out_ref[...] = (a_ref[...].astype(f32) + b_ref[...].astype(f32)).astype(bf16)

    return order.call(
        kernel, [rowwise(a, 3), rowwise(b, 3)], [rowwise(shaped(bf16, *a.shape), 3)], (3,)
    )


def chip_delta(order, anchor, local, other):
    def kernel(s_ref, anchor_ref, a_ref, b_ref, out_ref):
        anchor_rows = anchor_ref[...]
        out_ref[...] = (anchor_rows - a_ref[...]) + (anchor_rows - b_ref[...])

    return order.call(
        kernel,
        [rowwise(a, 6) for a in (anchor, local, other)],
        [rowwise(shaped(f32, *local.shape), 6)],
        (6,),
    )


def second_handoff(order, p1, c2, p23, q2, g2):
    def kernel(s_ref, p1_ref, c2_ref, p2_ref, q2_ref, g2_ref, s1_ref, t_ref):
        s1_ref[...] = (p1_ref[...].astype(f32) + c2_ref[...].astype(f32)).astype(bf16)
        t_ref[...] = (p2_ref[...] + q2_ref[...].astype(f32)).astype(bf16)

    out = rowwise(shaped(bf16, *p1.shape), 3)
    return order.call(
        kernel,
        [rowwise(p1, 3), rowwise(c2, 3), rowwise(p23, 6), rowwise(q2, 3), (g2, None, None)],
        [out, out],
        (3,),
    )


def nesterov_pass(order, here, there, anchor, momentum):
    def kernel(s_ref, a_ref, b_ref, anchor_ref, momentum_ref, anchor_new_ref, moment_new_ref):
        outer_grad = (a_ref[...] + b_ref[...]) / 4
        anchor_new, moment_new = nesterov(outer_grad, anchor_ref[...], momentum_ref[...])
        anchor_new_ref[...] = anchor_new
        moment_new_ref[...] = moment_new

    out = rowwise(shaped(f32, *anchor.shape), 6)
    return order.call(
        kernel,
        [rowwise(a, 6) for a in (here, there, anchor, momentum)],
        [out, out],
        (6,),
    )


def key_join(order, total, received, scale):
    def kernel(s_ref, a_ref, b_ref, out_ref):
        out_ref[...] = (a_ref[...] * scale + b_ref[...].astype(f32)).astype(bf16)

    return order.call(
        kernel,
        [rowwise(total, 3), rowwise(received, 3)],
        [rowwise(shaped(bf16, *total.shape), 3)],
        (3,),
    )


def final_update(order, fixes, p23, t, s1, local, first_old, second_old, anchor_new):
    rows, features = local.shape
    tile = rows // 6

    def kernel(s_ref, fix_ref, p_ref, t_ref, s1_ref, local_ref, first_ref, second_ref, anchor_ref, *out):
        merged_ref, m_ref, v_ref = out
        gradient = p_ref[...] + t_ref[...].astype(f32) + s1_ref[...].astype(f32)
        stepped, first_new, second_new = adam(
            gradient, local_ref[...], first_ref[...], second_ref[...], fix_ref[0], fix_ref[1]
        )
        merged_ref[...] = mix_weight * stepped + (1.0 - mix_weight) * anchor_ref[...]
        m_ref[...] = first_new
        v_ref[...] = second_new

    out = rowwise(shaped(f32, *local.shape), 6)
    return order.call(
        kernel,
        [(p23, (tile, features), lambda i, *_: (i + 6, 0))]
        + [rowwise(a, 6) for a in (t, s1, local, first_old, second_old, anchor_new)],
        [out, out, out],
        (6,),
        fixes=fixes,
    )


def pair_pass(normed, key_grad, local, first_old, second_old, anchor, momentum, inner_step):
    width = normed.shape[1]
    rows = local.shape[0]
    scale = width ** (-0.5)
    me = lax.axis_index("fsdp")
    y, z = me % 2, me // 2
    inside = (z == 1) | (z == 2)
    far = jnp.where(z < 2, 3, 0)
    middle = jnp.where(z < 2, 2, 1)
    order = Order(jnp.stack([far, middle, z ^ 1, z, y, inside, ~inside]).astype(jnp.int32))

    def along(links):
        pairs = [(2 * a + c, 2 * b + c) for a, b in links for c in (0, 1)]
        return lambda value: lax.ppermute(value, "fsdp", pairs)

    outer = along([(0, 1), (1, 0), (2, 3), (3, 2)])
    inner = along([(1, 2), (2, 1)])
    outward = along([(1, 0), (2, 3)])
    inward = along([(0, 1), (3, 2)])

    def swap(value):
        return lax.ppermute(value, "fsdp", [(i, i ^ 1) for i in range(8)])

    def replica(value, bit):
        return lax.ppermute(value, "rep", [(i, i ^ bit) for i in range(4)])

    g_pair = swap(key_grad)
    weight = rounded(order, local)
    w_beside = outer(weight)
    w_inner = inner(weight)
    x0 = swap(first_piece(order, normed, rows))
    fixes = jnp.stack(corrections(inner_step))
    rest, mine = split(order, normed, rows, g_pair, fixes)
    x123 = swap(rest)

    p0 = gradient_part(order, mine, 0, x0, key_grad, g_pair, scale)
    r0 = inward(p0)
    w_across = inner(w_beside)
    w_middle_end = outward(w_inner)
    delta = chip_delta(order, anchor, local, replica(local, 1))
    delta_there = replica(delta, 2)
    i01 = input_parts(order, g_pair, weight, w_beside, scale)
    g01 = swap(i01)

    p1 = gradient_part(order, mine, 1, x123, key_grad, g_pair, scale, 30)
    r1 = inward(p1)
    w_far_end = outward(w_across)
    q2 = inner(add(order, p0, r0))
    i2, w_middle = input_part_of(order, g_pair, w_inner, w_middle_end, scale)
    g2 = swap(i2)
    p23 = gradient_rest(order, mine, x123, key_grad, g_pair, scale)
    own_total, pair_total = key_sums(order, mine, x123, (w_middle, w_beside, weight))
    input_grad = input_join_two(order, key_grad, weight, w_beside, g01, width, scale)

    i3, w_far = input_part_of(order, g_pair, w_across, w_far_end, scale)
    g3 = swap(i3)
    s1, t = second_handoff(order, p1, r1, p23, q2, g2)
    qa = outer(t)
    qb = inner(s1)
    key_pair = swap(key_last(order, pair_total, x0, w_far, scale, bf16))
    own_total = key_last(order, own_total, mine, w_far, 1.0, f32)
    input_grad = input_join(order, MIDDLE, key_grad, w_middle, g2, scale, input_grad)
    anchor_new, moment_new = nesterov_pass(order, delta, delta_there, anchor, momentum)
    input_grad = input_join(order, FAR, key_grad, w_far, g3, scale, input_grad)
    keys = key_join(order, own_total, key_pair, scale)

    merged, first_new, second_new = final_update(
        order,
        fixes,
        p23,
        qa,
        qb,
        local,
        first_old,
        second_old,
        anchor_new,
    )
    return (keys, input_grad, merged, first_new, second_new, anchor_new, moment_new)


def body(normed, key_grad, master, first_moment, second_moment, anchor, momentum, inner_step):
    local = master[0]
    sizes = (lax.axis_size("rep"), lax.axis_size("fsdp"))
    inner_pass = pair_pass if sizes == (4, 8) else whole_pass
    keys, input_grad, merged, first_new, second_new, anchor_new, moment_new = inner_pass(
        normed, key_grad, local, first_moment[0], second_moment[0], anchor, momentum, inner_step
    )
    return (
        keys,
        input_grad,
        merged[None],
        first_new[None],
        second_new[None],
        anchor_new,
        moment_new,
    )


def solution(mesh):
    in_specs = (
        P(("rep", "fsdp"), None),
        P(("rep", "fsdp"), None),
        P("rep", "fsdp", None),
        P("rep", "fsdp", None),
        P("rep", "fsdp", None),
        P("fsdp", None),
        P("fsdp", None),
        P(),
    )
    out_specs = (
        P(("rep", "fsdp"), None),
        P(("rep", "fsdp"), None),
        P("rep", "fsdp", None),
        P("rep", "fsdp", None),
        P("rep", "fsdp", None),
        P("fsdp", None),
        P("fsdp", None),
    )
    return jax.shard_map(body, mesh=mesh, in_specs=in_specs, out_specs=out_specs, check_vma=False)
```

```python
import jax
import jax.numpy as jnp
from jax import lax
from jax.experimental import pallas as pl
from jax.experimental.pallas import tpu as pltpu
from jax.sharding import PartitionSpec as P

beta_first = 0.9
beta_second = 0.95
inner_rate = 0.1
weight_decay = 0.1
epsilon = 1e-08
outer_rate = 0.7
outer_mu = 0.9
mix_weight = 0.5

f32 = jnp.float32
bf16 = jnp.bfloat16
vmem_bytes = 16 * 1024 * 1024


def corrections(inner_step):
    count_float = inner_step[0].astype(f32)
    fix_first = 1.0 - jnp.power(f32(beta_first), count_float)
    fix_second = 1.0 - jnp.power(f32(beta_second), count_float)
    return fix_first, fix_second


def adam(gradient, local, first_old, second_old, fix_first, fix_second):
    first_new = beta_first * first_old + (1.0 - beta_first) * gradient
    second_new = beta_second * second_old + (1.0 - beta_second) * gradient * gradient
    direction = first_new / fix_first / (jnp.sqrt(second_new / fix_second) + epsilon)
    stepped = local - inner_rate * (direction + weight_decay * local)
    return (stepped, first_new, second_new)


def nesterov(outer_grad, anchor_rows, moment_rows):
    moment_new = outer_mu * moment_rows + outer_grad
    anchor_new = anchor_rows - outer_rate * (outer_grad + outer_mu * moment_new)
    return (anchor_new, moment_new)


def outer_update(local, anchor, momentum):
    summed = lax.psum(anchor - local, "rep")
    return nesterov(summed / lax.axis_size("rep"), anchor, momentum)


def whole_pass(normed, key_grad, local, first_old, second_old, anchor, momentum, inner_step):
    scale = normed.shape[1] ** (-0.5)
    weight = lax.all_gather(local.astype(bf16), "fsdp", axis=0, tiled=True)
    keys = (jnp.dot(normed, weight, preferred_element_type=f32) * scale).astype(bf16)
    input_grad = (
        lax.dot_general(key_grad, weight, (((1,), (1,)), ((), ())), preferred_element_type=f32)
        * scale
    ).astype(bf16)
    gradient = lax.psum_scatter(
        lax.dot_general(normed, key_grad, (((0,), (0,)), ((), ())), preferred_element_type=f32)
        * scale,
        "fsdp",
        scatter_dimension=0,
        tiled=True,
    )
    stepped, first_new, second_new = adam(
        gradient, local, first_old, second_old, *corrections(inner_step)
    )
    anchor_new, moment_new = outer_update(local, anchor, momentum)
    merged = mix_weight * stepped + (1.0 - mix_weight) * anchor_new
    return (keys, input_grad, merged, first_new, second_new, anchor_new, moment_new)


FAR, MIDDLE, BESIDE, OWN, Y, INNER, END = range(7)


class Order:
    def __init__(self, place):
        self.place = place
        self.token = None

    def call(self, kernel, inputs, outputs, grid, span=1, aliases=None, fixes=None):
        scalars = [self.place] + ([] if fixes is None else [fixes])
        tokens = [] if self.token is None else [self.token]
        before = len(scalars) + len(inputs)

        def wrapped(*refs):
            refs[-1][...] = jnp.zeros_like(refs[-1])
            kernel(*refs[:before], *refs[before + len(tokens) : -1])

        outputs = outputs + [whole(shaped(jnp.int32, 8, 128))]
        shapes = [shape for shape, _, _ in outputs]
        keep = pl.BlockSpec(memory_space=pl.ANY)
        out = pl.pallas_call(
            wrapped,
            out_shape=shapes,
            grid_spec=pltpu.PrefetchScalarGridSpec(
                num_scalar_prefetch=len(scalars),
                grid=grid,
                in_specs=[
                    keep if block is None else pl.BlockSpec(block, index)
                    for _, block, index in inputs
                ]
                + [keep] * len(tokens),
                out_specs=[pl.BlockSpec(block, index) for _, block, index in outputs],
            ),
            input_output_aliases=aliases or {},
            compiler_params=pltpu.CompilerParams(vmem_limit_bytes=vmem_bytes),
            cost_estimate=pl.CostEstimate(
                flops=int(span * 1e9), bytes_accessed=0, transcendentals=0
            ),
        )(*scalars, *[a for a, _, _ in inputs], *tokens)
        self.token = out[-1]
        return out[0] if len(out) == 2 else out[:-1]


def shaped(dtype, *shape):
    return jax.ShapeDtypeStruct(shape, dtype)


def whole(array):
    zeros = (0,) * len(array.shape)
    return (array, array.shape, lambda *_: zeros)


def rowwise(array, steps):
    return (array, (array.shape[0] // steps, array.shape[1]), lambda i, *_: (i, 0))


def columnwise(array, steps):
    return (array, (array.shape[0], array.shape[1] // steps), lambda i, *_: (0, i))


def stacked(array, k, rows):
    return (array, (rows, array.shape[1]), lambda *_: (k, 0))


def dot_t(a, b):
    return lax.dot_general(a, b, (((0,), (0,)), ((), ())), preferred_element_type=f32)


def dot_bt(a, b):
    return lax.dot_general(a, b, (((1,), (1,)), ((), ())), preferred_element_type=f32)


def dot(a, b):
    return jnp.dot(a, b, preferred_element_type=f32)


def chosen(flag, yes, no):
    return jnp.where(flag != 0, yes, no)


def halves(x_ref, rows):
    turned = x_ref[...].T
    return turned[:rows], turned[rows:]


def rounded(order, local):
    def kernel(s_ref, a_ref, out_ref):
        out_ref[...] = a_ref[...].astype(bf16)

    return order.call(
        kernel, [rowwise(local, 3)], [rowwise(shaped(bf16, *local.shape), 3)], (3,)
    )


def first_piece(order, normed, rows):
    tokens = normed.shape[0]

    def kernel(s_ref, x_ref, piece_ref):
        low, high = halves(x_ref, rows)
        piece_ref[...] = chosen(s_ref[Y], low, high)

    return order.call(
        kernel,
        [(normed, (tokens, 2 * rows), lambda i, s: (0, s[FAR]))],
        [whole(shaped(bf16, rows, tokens))],
        (1,),
    )


def split(order, normed, rows, g_pair, fixes):
    tokens = normed.shape[0]

    def kernel(s_ref, fix_ref, x_ref, g_ref, rest_ref, own_ref):
        low, high = halves(x_ref, rows)
        own_ref[...] = chosen(s_ref[Y], high, low)

        @pl.when(pl.program_id(0) < 3)
        def _():
            rest_ref[...] = chosen(s_ref[Y], low, high)

    return order.call(
        kernel,
        [
            (normed, (tokens, 2 * rows), lambda i, s, f: (0, s[(i + 1) % 4])),
            (g_pair, None, None),
        ],
        [
            (
                shaped(bf16, 3 * rows, tokens),
                (rows, tokens),
                lambda i, s, f: (jnp.minimum(i, 2), 0),
            ),
            (shaped(bf16, 4 * rows, tokens), (rows, tokens), lambda i, s, f: ((i + 1) % 4, 0)),
        ],
        (4,),
        30,
        fixes=fixes,
    )


def gradient_part(order, mine, k, theirs, key_grad, g_pair, scale, span=0):
    tokens, features = key_grad.shape
    rows = mine.shape[0] // 4

    def kernel(s_ref, x_ref, xp_ref, g_ref, gp_ref, out_ref):
        total = dot(x_ref[...], g_ref[...]) + dot(xp_ref[...], gp_ref[...])
        out_ref[...] = (total * scale).astype(bf16)

    return order.call(
        kernel,
        [
            stacked(mine, k, rows),
            stacked(theirs, 0, rows),
            columnwise(key_grad, 2),
            columnwise(g_pair, 2),
        ],
        [columnwise(shaped(bf16, rows, features), 2)],
        (2,),
        span,
    )


def gradient_rest(order, mine, theirs, key_grad, g_pair, scale):
    tokens, features = key_grad.shape
    rows = mine.shape[0] // 4
    tile = features // 2

    def kernel(s_ref, x_ref, xp_ref, g_ref, gp_ref, out_ref):
        total = dot(x_ref[...], g_ref[...]) + dot(xp_ref[...], gp_ref[...])
        out_ref[...] = total * scale

    return order.call(
        kernel,
        [
            (mine, (rows, tokens), lambda k, i, s: (k + 2, 0)),
            (theirs, (rows, tokens), lambda k, i, s: (k + 1, 0)),
            (key_grad, (tokens, tile), lambda k, i, s: (0, i)),
            (g_pair, (tokens, tile), lambda k, i, s: (0, i)),
        ],
        [(shaped(f32, 2 * rows, features), (rows, tile), lambda k, i, s: (k, i))],
        (2, 2),
        0,
    )


def input_parts(order, cotangent, first, second, scale):
    tokens, features = cotangent.shape
    rows = first.shape[0]

    def kernel(s_ref, g_ref, a_ref, b_ref, out_ref):
        @pl.when(pl.program_id(0) == 0)
        def _():
            out_ref[...] = (dot_bt(a_ref[...], g_ref[...]) * scale).astype(bf16)

        @pl.when(pl.program_id(0) == 1)
        def _():
            out_ref[...] = (dot_bt(b_ref[...], g_ref[...]) * scale).astype(bf16)

    return order.call(
        kernel,
        [whole(cotangent), whole(first), whole(second)],
        [(shaped(bf16, 2 * rows, tokens), (rows, tokens), lambda i, s: (i, 0))],
        (2,),
        30,
    )


def input_part_of(order, cotangent, yes, no, scale):
    tokens, features = cotangent.shape
    rows = yes.shape[0]

    def kernel(s_ref, g_ref, a_ref, b_ref, out_ref, w_ref):
        weight = chosen(s_ref[INNER], a_ref[...], b_ref[...])
        w_ref[...] = weight
        out_ref[...] = (dot_bt(weight, g_ref[...]) * scale).astype(bf16)

    return order.call(
        kernel,
        [whole(cotangent), whole(yes), whole(no)],
        [whole(shaped(bf16, rows, tokens)), whole(shaped(bf16, rows, features))],
        (1,),
        0,
    )


def store_joined(y, out_ref, own, other):
    @pl.when(y == 0)
    def _():
        out_ref[...] = jnp.concatenate([own, other], 0).T

    @pl.when(y != 0)
    def _():
        out_ref[...] = jnp.concatenate([other, own], 0).T


def input_join(order, slot, cotangent, weight, other, scale, target):
    tokens, features = cotangent.shape
    rows = weight.shape[0]

    def kernel(s_ref, g_ref, w_ref, other_ref, target_ref, out_ref):
        own = (dot_bt(w_ref[...], g_ref[...]) * scale).astype(bf16)
        store_joined(s_ref[Y], out_ref, own, other_ref[...])

    return order.call(
        kernel,
        [rowwise(cotangent, 3), whole(weight), columnwise(other, 3), (target, None, None)],
        [(target, (tokens // 3, 2 * rows), lambda i, s: (i, s[slot]))],
        (3,),
        10 if slot == FAR else 0,
        {4: 0},
    )


def input_join_two(order, cotangent, first, second, others, width, scale):
    tokens, features = cotangent.shape
    rows = first.shape[0]
    tile = tokens // 3

    def kernel(s_ref, g_ref, a_ref, b_ref, other_ref, out_ref):
        weight = chosen(pl.program_id(0), b_ref[...], a_ref[...])
        own = (dot_bt(weight, g_ref[...]) * scale).astype(bf16)
        store_joined(s_ref[Y], out_ref, own, other_ref[...])

    return order.call(
        kernel,
        [
            (cotangent, (tile, features), lambda k, i, s: (i, 0)),
            whole(first),
            whole(second),
            (others, (rows, tile), lambda k, i, s: (k, i)),
        ],
        [
            (
                shaped(bf16, tokens, width),
                (tile, 2 * rows),
                lambda k, i, s: (i, s[OWN - k]),
            )
        ],
        (2, 3),
        8,
    )


def key_sums(order, mine, theirs, weights):
    rows, tokens = mine.shape[0] // 4, mine.shape[1]
    features = weights[0].shape[1]

    def kernel(s_ref, x_ref, xp_ref, *refs):
        own_ref, pair_ref = refs[3:]
        own = pair = 0.0
        for k in range(3):
            w = refs[k][...]
            own += dot_t(x_ref[(k + 1) * rows : (k + 2) * rows], w)
            pair += dot_t(xp_ref[k * rows : (k + 1) * rows], w)
        own_ref[...] = own
        pair_ref[...] = pair

    out = columnwise(shaped(f32, tokens, features), 2)
    return order.call(
        kernel,
        [whole(mine), whole(theirs)] + [columnwise(w, 2) for w in weights],
        [out, out],
        (2,),
        0,
    )


def key_last(order, total, inputs, weight, scale, dtype):
    tokens, features = total.shape
    rows = weight.shape[0]

    def kernel(s_ref, total_ref, x_ref, w_ref, out_ref):
        value = total_ref[...] + dot_t(x_ref[...], w_ref[...])
        out_ref[...] = (value * scale).astype(dtype)

    return order.call(
        kernel,
        [columnwise(total, 2), stacked(inputs, 0, rows), columnwise(weight, 2)],
        [columnwise(shaped(dtype, tokens, features), 2)],
        (2,),
        0,
    )


def chip_delta(order, anchor, local, other):
    def kernel(s_ref, anchor_ref, a_ref, b_ref, out_ref):
        anchor_rows = anchor_ref[...]
        out_ref[...] = (anchor_rows - a_ref[...]) + (anchor_rows - b_ref[...])

    return order.call(
        kernel,
        [rowwise(a, 6) for a in (anchor, local, other)],
        [rowwise(shaped(f32, *local.shape), 6)],
        (6,),
    )


def choose_send(order, at_end, inside):
    def kernel(s_ref, a_ref, b_ref, out_ref):
        out_ref[...] = chosen(s_ref[END], a_ref[...], b_ref[...])

    return order.call(
        kernel,
        [rowwise(at_end, 3), rowwise(inside, 3)],
        [rowwise(shaped(bf16, *inside.shape), 3)],
        (3,),
    )


def first_handoff(order, p0, c1, p1, w_across):
    def kernel(s_ref, p0_ref, c1_ref, p1_ref, w_ref, sum_ref, send_ref):
        sum_ref[...] = (p0_ref[...].astype(f32) + c1_ref[...].astype(f32)).astype(bf16)
        send_ref[...] = chosen(s_ref[END], p1_ref[...], w_ref[...])

    out = rowwise(shaped(bf16, *p0.shape), 3)
    return order.call(kernel, [rowwise(a, 3) for a in (p0, c1, p1, w_across)], [out, out], (3,))


def second_handoff(order, p1, c2, p23, q2, g2):
    def kernel(s_ref, p1_ref, c2_ref, p2_ref, q2_ref, g2_ref, s1_ref, t_ref):
        s1_ref[...] = (p1_ref[...].astype(f32) + c2_ref[...].astype(f32)).astype(bf16)
        t_ref[...] = (p2_ref[...] + q2_ref[...].astype(f32)).astype(bf16)

    out = rowwise(shaped(bf16, *p1.shape), 3)
    return order.call(
        kernel,
        [rowwise(p1, 3), rowwise(c2, 3), rowwise(p23, 6), rowwise(q2, 3), (g2, None, None)],
        [out, out],
        (3,),
    )


def nesterov_pass(order, here, there, anchor, momentum):
    def kernel(s_ref, a_ref, b_ref, anchor_ref, momentum_ref, anchor_new_ref, moment_new_ref):
        outer_grad = (a_ref[...] + b_ref[...]) / 4
        anchor_new, moment_new = nesterov(outer_grad, anchor_ref[...], momentum_ref[...])
        anchor_new_ref[...] = anchor_new
        moment_new_ref[...] = moment_new

    out = rowwise(shaped(f32, *anchor.shape), 6)
    return order.call(
        kernel,
        [rowwise(a, 6) for a in (here, there, anchor, momentum)],
        [out, out],
        (6,),
    )


def final_update(
    order, fixes, p23, t, s1, local, first_old, second_old, anchor_new, total, received, scale
):
    def kernel(
        s_ref,
        fix_ref,
        p_ref,
        t_ref,
        s1_ref,
        local_ref,
        first_ref,
        second_ref,
        anchor_ref,
        total_ref,
        received_ref,
        merged_ref,
        m_ref,
        v_ref,
        keys_ref,
    ):
        gradient = p_ref[...] + t_ref[...].astype(f32) + s1_ref[...].astype(f32)
        stepped, first_new, second_new = adam(
            gradient, local_ref[...], first_ref[...], second_ref[...], fix_ref[0], fix_ref[1]
        )
        merged_ref[...] = mix_weight * stepped + (1.0 - mix_weight) * anchor_ref[...]
        m_ref[...] = first_new
        v_ref[...] = second_new
        keys_ref[...] = (total_ref[...] * scale + received_ref[...].astype(f32)).astype(bf16)

    rows, features = local.shape
    out = rowwise(shaped(f32, rows, features), 6)
    return order.call(
        kernel,
        [(p23, (rows // 6, features), lambda i, *_: (i + 6, 0))]
        + [
            rowwise(a, 6)
            for a in (t, s1, local, first_old, second_old, anchor_new, total, received)
        ],
        [out, out, out, rowwise(shaped(bf16, *total.shape), 6)],
        (6,),
        fixes=fixes,
    )


def pair_pass(normed, key_grad, local, first_old, second_old, anchor, momentum, inner_step):
    width = normed.shape[1]
    rows = local.shape[0]
    scale = width ** (-0.5)
    me = lax.axis_index("fsdp")
    y, z = me % 2, me // 2
    inside = (z == 1) | (z == 2)
    far = jnp.where(z < 2, 3, 0)
    middle = jnp.where(z < 2, 2, 1)
    order = Order(jnp.stack([far, middle, z ^ 1, z, y, inside, ~inside]).astype(jnp.int32))

    def along(links):
        pairs = [(2 * a + c, 2 * b + c) for a, b in links for c in (0, 1)]
        return lambda value: lax.ppermute(value, "fsdp", pairs)

    outer = along([(0, 1), (1, 0), (2, 3), (3, 2)])
    inner = along([(1, 2), (2, 1)])

    def swap(value):
        return lax.ppermute(value, "fsdp", [(i, i ^ 1) for i in range(8)])

    def replica(value, bit):
        return lax.ppermute(value, "rep", [(i, i ^ bit) for i in range(4)])

    g_pair = swap(key_grad)
    weight = rounded(order, local)
    w_beside = outer(weight)
    w_inner = inner(weight)
    x0 = swap(first_piece(order, normed, rows))
    fixes = jnp.stack(corrections(inner_step))
    rest, mine = split(order, normed, rows, g_pair, fixes)
    x123 = swap(rest)

    p0 = gradient_part(order, mine, 0, x0, key_grad, g_pair, scale)
    w_across = inner(w_beside)
    c1 = outer(choose_send(order, p0, w_inner))
    i01 = input_parts(order, g_pair, weight, w_beside, scale)
    g01 = swap(i01)
    delta = chip_delta(order, anchor, local, replica(local, 1))
    delta_there = replica(delta, 2)

    p1 = gradient_part(order, mine, 1, x123, key_grad, g_pair, scale, 5)
    s0, send = first_handoff(order, p0, c1, p1, w_across)
    c2 = outer(send)
    q2 = inner(s0)
    i2, w_middle = input_part_of(order, g_pair, w_inner, c1, scale)
    g2 = swap(i2)
    p23 = gradient_rest(order, mine, x123, key_grad, g_pair, scale)
    own_total, pair_total = key_sums(order, mine, x123, (w_middle, w_beside, weight))
    input_grad = input_join_two(order, key_grad, weight, w_beside, g01, width, scale)

    i3, w_far = input_part_of(order, g_pair, w_across, c2, scale)
    g3 = swap(i3)
    s1, t = second_handoff(order, p1, c2, p23, q2, g2)
    qa = outer(t)
    qb = inner(s1)
    key_pair = swap(key_last(order, pair_total, x0, w_far, scale, bf16))
    own_total = key_last(order, own_total, mine, w_far, 1.0, f32)
    input_grad = input_join(order, MIDDLE, key_grad, w_middle, g2, scale, input_grad)
    anchor_new, moment_new = nesterov_pass(order, delta, delta_there, anchor, momentum)
    input_grad = input_join(order, FAR, key_grad, w_far, g3, scale, input_grad)

    merged, first_new, second_new, keys = final_update(
        order,
        fixes,
        p23,
        qa,
        qb,
        local,
        first_old,
        second_old,
        anchor_new,
        own_total,
        key_pair,
        scale,
    )
    return (keys, input_grad, merged, first_new, second_new, anchor_new, moment_new)


def body(normed, key_grad, master, first_moment, second_moment, anchor, momentum, inner_step):
    local = master[0]
    sizes = (lax.axis_size("rep"), lax.axis_size("fsdp"))
    inner_pass = pair_pass if sizes == (4, 8) else whole_pass
    keys, input_grad, merged, first_new, second_new, anchor_new, moment_new = inner_pass(
        normed, key_grad, local, first_moment[0], second_moment[0], anchor, momentum, inner_step
    )
    return (
        keys,
        input_grad,
        merged[None],
        first_new[None],
        second_new[None],
        anchor_new,
        moment_new,
    )


def solution(mesh):
    in_specs = (
        P(("rep", "fsdp"), None),
        P(("rep", "fsdp"), None),
        P("rep", "fsdp", None),
        P("rep", "fsdp", None),
        P("rep", "fsdp", None),
        P("fsdp", None),
        P("fsdp", None),
        P(),
    )
    out_specs = (
        P(("rep", "fsdp"), None),
        P(("rep", "fsdp"), None),
        P("rep", "fsdp", None),
        P("rep", "fsdp", None),
        P("rep", "fsdp", None),
        P("fsdp", None),
        P("fsdp", None),
    )
    return jax.shard_map(body, mesh=mesh, in_specs=in_specs, out_specs=out_specs, check_vma=False)
```

```python
import jax
import jax.numpy as jnp
from jax import lax
from jax.experimental import pallas as pl
from jax.experimental.pallas import tpu as pltpu
from jax.sharding import PartitionSpec as P

beta_first = 0.9
beta_second = 0.95
inner_rate = 0.1
weight_decay = 0.1
epsilon = 1e-08
outer_rate = 0.7
outer_mu = 0.9
mix_weight = 0.5

f32 = jnp.float32
bf16 = jnp.bfloat16
vmem_bytes = 16 * 1024 * 1024

expected = {
    "split": 30,
    "first part": 0,
    "second part": 5,
    "input own": 6,
    "third": 5,
    "input two": 0,
    "rest": 8,
    "key sums": 0,
    "join own": 1,
    "input far": 0,
    "join two": 0,
    "join far": 10,
}


def corrections(inner_step):
    count_float = inner_step[0].astype(f32)
    fix_first = 1.0 - jnp.power(f32(beta_first), count_float)
    fix_second = 1.0 - jnp.power(f32(beta_second), count_float)
    return fix_first, fix_second


def adam(gradient, local, first_old, second_old, fix_first, fix_second):
    first_new = beta_first * first_old + (1.0 - beta_first) * gradient
    second_new = beta_second * second_old + (1.0 - beta_second) * gradient * gradient
    direction = first_new / fix_first / (jnp.sqrt(second_new / fix_second) + epsilon)
    stepped = local - inner_rate * (direction + weight_decay * local)
    return (stepped, first_new, second_new)


def nesterov(outer_grad, anchor_rows, moment_rows):
    moment_new = outer_mu * moment_rows + outer_grad
    anchor_new = anchor_rows - outer_rate * (outer_grad + outer_mu * moment_new)
    return (anchor_new, moment_new)


def outer_update(local, anchor, momentum):
    summed = lax.psum(anchor - local, "rep")
    return nesterov(summed / lax.axis_size("rep"), anchor, momentum)


def whole_pass(normed, key_grad, local, first_old, second_old, anchor, momentum, inner_step):
    scale = normed.shape[1] ** (-0.5)
    weight = lax.all_gather(local.astype(bf16), "fsdp", axis=0, tiled=True)
    keys = (jnp.dot(normed, weight, preferred_element_type=f32) * scale).astype(bf16)
    input_grad = (
        lax.dot_general(key_grad, weight, (((1,), (1,)), ((), ())), preferred_element_type=f32)
        * scale
    ).astype(bf16)
    gradient = lax.psum_scatter(
        lax.dot_general(normed, key_grad, (((0,), (0,)), ((), ())), preferred_element_type=f32)
        * scale,
        "fsdp",
        scatter_dimension=0,
        tiled=True,
    )
    stepped, first_new, second_new = adam(
        gradient, local, first_old, second_old, *corrections(inner_step)
    )
    anchor_new, moment_new = outer_update(local, anchor, momentum)
    merged = mix_weight * stepped + (1.0 - mix_weight) * anchor_new
    return (keys, input_grad, merged, first_new, second_new, anchor_new, moment_new)


FAR, MIDDLE, BESIDE, OWN, Y, INNER, END, CORE, END_0, END_1 = range(10)


class Order:
    def __init__(self, place):
        self.place = place
        self.token = None

    def call(self, kernel, inputs, outputs, grid, span=1, aliases=None, fixes=None):
        scalars = [self.place] + ([] if fixes is None else [fixes])
        tokens = [] if self.token is None else [self.token]
        before = len(scalars) + len(inputs)

        def wrapped(*refs):
            refs[-1][...] = jnp.zeros_like(refs[-1])
            kernel(*refs[:before], *refs[before + len(tokens) : -1])

        outputs = outputs + [whole(shaped(jnp.int32, 8, 128))]
        shapes = [shape for shape, _, _ in outputs]
        keep = pl.BlockSpec(memory_space=pl.ANY)
        out = pl.pallas_call(
            wrapped,
            out_shape=shapes,
            grid_spec=pltpu.PrefetchScalarGridSpec(
                num_scalar_prefetch=len(scalars),
                grid=grid,
                in_specs=[
                    keep if block is None else pl.BlockSpec(block, index)
                    for _, block, index in inputs
                ]
                + [keep] * len(tokens),
                out_specs=[pl.BlockSpec(block, index) for _, block, index in outputs],
            ),
            input_output_aliases=aliases or {},
            compiler_params=pltpu.CompilerParams(vmem_limit_bytes=vmem_bytes),
            cost_estimate=pl.CostEstimate(
                flops=int(span * 1e9), bytes_accessed=0, transcendentals=0
            ),
        )(*scalars, *[a for a, _, _ in inputs], *tokens)
        self.token = out[-1]
        return out[0] if len(out) == 2 else out[:-1]


def shaped(dtype, *shape):
    return jax.ShapeDtypeStruct(shape, dtype)


def whole(array):
    zeros = (0,) * len(array.shape)
    return (array, array.shape, lambda *_: zeros)


def rowwise(array, steps):
    return (array, (array.shape[0] // steps, array.shape[1]), lambda i, *_: (i, 0))


def columnwise(array, steps):
    return (array, (array.shape[0], array.shape[1] // steps), lambda i, *_: (0, i))


def stacked(array, k, rows):
    return (array, (rows, array.shape[1]), lambda *_: (k, 0))


def dot_t(a, b):
    return lax.dot_general(a, b, (((0,), (0,)), ((), ())), preferred_element_type=f32)


def dot_bt(a, b):
    return lax.dot_general(a, b, (((1,), (1,)), ((), ())), preferred_element_type=f32)


def dot(a, b):
    return jnp.dot(a, b, preferred_element_type=f32)


def chosen(flag, yes, no):
    return jnp.where(flag != 0, yes, no)


def halves(x_ref, rows):
    turned = x_ref[...].T
    return turned[:rows], turned[rows:]


def rounded(order, local):
    def kernel(s_ref, a_ref, out_ref):
        out_ref[...] = a_ref[...].astype(bf16)

    return order.call(
        kernel, [rowwise(local, 3)], [rowwise(shaped(bf16, *local.shape), 3)], (3,)
    )


def first_piece(order, normed, rows):
    tokens = normed.shape[0]

    def kernel(s_ref, x_ref, piece_ref):
        low, high = halves(x_ref, rows)
        piece_ref[...] = chosen(s_ref[Y], low, high)

    return order.call(
        kernel,
        [(normed, (tokens, 2 * rows), lambda i, s: (0, s[FAR]))],
        [whole(shaped(bf16, rows, tokens))],
        (1,),
    )


def split(order, normed, rows, g_pair, fixes):
    tokens = normed.shape[0]

    def kernel(s_ref, fix_ref, x_ref, g_ref, one_ref, two_ref, own_ref):
        i = pl.program_id(0)
        low, high = halves(x_ref, rows)
        own_ref[...] = chosen(s_ref[Y], high, low)

        @pl.when(i == 0)
        def _():
            one_ref[...] = chosen(s_ref[Y], low, high)

        @pl.when((i == 1) | (i == 2))
        def _():
            two_ref[...] = chosen(s_ref[Y], low, high)

    return order.call(
        kernel,
        [
            (normed, (tokens, 2 * rows), lambda i, s, f: (0, s[(i + 1) % 4])),
            (g_pair, None, None),
        ],
        [
            whole(shaped(bf16, rows, tokens)),
            (
                shaped(bf16, 2 * rows, tokens),
                (rows, tokens),
                lambda i, s, f: (jnp.clip(i - 1, 0, 1), 0),
            ),
            (shaped(bf16, 4 * rows, tokens), (rows, tokens), lambda i, s, f: ((i + 1) % 4, 0)),
        ],
        (4,),
        expected["split"],
        fixes=fixes,
    )


def gradient_part(order, mine, k, theirs, key_grad, g_pair, scale, inside=None, flag=END_1):
    tokens, features = key_grad.shape
    rows = theirs.shape[0]

    def kernel(s_ref, x_ref, xp_ref, g_ref, gp_ref, *rest):
        total = dot(x_ref[...], g_ref[...]) + dot(xp_ref[...], gp_ref[...])
        value = (total * scale).astype(bf16)
        if inside is None:
            rest[0][...] = value
        else:
            w_ref, out_ref, send_ref = rest
            out_ref[...] = value
            send_ref[...] = chosen(s_ref[flag], value, w_ref[...])

    extra = [] if inside is None else [columnwise(inside, 2)]
    out = columnwise(shaped(bf16, rows, features), 2)
    return order.call(
        kernel,
        [stacked(mine, k, rows), whole(theirs), columnwise(key_grad, 2), columnwise(g_pair, 2)]
        + extra,
        [out] + [out] * len(extra),
        (2,),
        expected["first part" if extra else "second part"],
    )


def gradient_rest(order, mine, theirs, key_grad, g_pair, scale):
    tokens, features = key_grad.shape
    rows = mine.shape[0] // 4
    tile = features // 2

    def kernel(s_ref, x_ref, xp_ref, g_ref, gp_ref, out_ref):
        total = dot(x_ref[...], g_ref[...]) + dot(xp_ref[...], gp_ref[...])
        out_ref[...] = total * scale

    return order.call(
        kernel,
        [
            (mine, (rows, tokens), lambda k, i, s: (k + 2, 0)),
            (theirs, (rows, tokens), lambda k, i, s: (k, 0)),
            (key_grad, (tokens, tile), lambda k, i, s: (0, i)),
            (g_pair, (tokens, tile), lambda k, i, s: (0, i)),
        ],
        [(shaped(f32, 2 * rows, features), (rows, tile), lambda k, i, s: (k, i))],
        (2, 2),
        expected["rest"],
    )


def input_part(order, cotangent, weight, scale):
    tokens, features = cotangent.shape
    rows = weight.shape[0]

    def kernel(s_ref, g_ref, w_ref, out_ref):
        out_ref[...] = (dot_bt(w_ref[...], g_ref[...]) * scale).astype(bf16)

    return order.call(
        kernel,
        [whole(cotangent), whole(weight)],
        [whole(shaped(bf16, rows, tokens))],
        (1,),
        expected["input own"],
    )


def input_parts(order, cotangent, beside_0, beside_1, end_0, end_1, scale):
    tokens, features = cotangent.shape
    rows = beside_0.shape[0]

    def kernel(s_ref, g_ref, a_ref, b_ref, c_ref, d_ref, out_ref, middle_ref, beside_ref):
        @pl.when(pl.program_id(0) == 0)
        def _():
            inner = chosen(s_ref[CORE], a_ref[...], b_ref[...])
            end = chosen(s_ref[CORE], d_ref[...], c_ref[...])
            middle_ref[...] = chosen(s_ref[INNER], inner, end)
            out_ref[...] = (dot_bt(middle_ref[...], g_ref[...]) * scale).astype(bf16)

        @pl.when(pl.program_id(0) == 1)
        def _():
            beside_ref[...] = chosen(s_ref[CORE], b_ref[...], a_ref[...])
            out_ref[...] = (dot_bt(beside_ref[...], g_ref[...]) * scale).astype(bf16)

    block = whole(shaped(bf16, rows, features))
    return order.call(
        kernel,
        [whole(cotangent)] + [whole(w) for w in (beside_0, beside_1, end_0, end_1)],
        [(shaped(bf16, 2 * rows, tokens), (rows, tokens), lambda i, s: (i, 0)), block, block],
        (2,),
        expected["input two"],
    )


def input_part_of(order, cotangent, inner_0, inner_1, end_0, end_1, scale):
    tokens, features = cotangent.shape
    rows = inner_0.shape[0]

    def kernel(s_ref, g_ref, a_ref, b_ref, c_ref, d_ref, out_ref, w_ref):
        inner = chosen(s_ref[CORE], b_ref[...], a_ref[...])
        end = chosen(s_ref[CORE], d_ref[...], c_ref[...])
        weight = chosen(s_ref[INNER], inner, end)
        w_ref[...] = weight
        out_ref[...] = (dot_bt(weight, g_ref[...]) * scale).astype(bf16)

    return order.call(
        kernel,
        [whole(cotangent)] + [whole(w) for w in (inner_0, inner_1, end_0, end_1)],
        [whole(shaped(bf16, rows, tokens)), whole(shaped(bf16, rows, features))],
        (1,),
        expected["input far"],
    )


def store_joined(y, out_ref, own, other):
    @pl.when(y == 0)
    def _():
        out_ref[...] = jnp.concatenate([own, other], 0).T

    @pl.when(y != 0)
    def _():
        out_ref[...] = jnp.concatenate([other, own], 0).T


def input_join(order, slots, cotangent, weights, others, shape, scale, target=None, before=()):
    tokens, features = cotangent.shape
    rows = weights[0].shape[0]
    count, tile = len(slots), tokens // 3
    kept = [a for a in (target, *before) if a is not None]

    def kernel(s_ref, g_ref, *refs):
        other_ref, out_ref = refs[count], refs[-1]
        weight = refs[0][...]
        if count == 2:
            weight = jnp.where(pl.program_id(0) == 0, weight, refs[1][...])
        own = (dot_bt(weight, g_ref[...]) * scale).astype(bf16)
        store_joined(s_ref[Y], out_ref, own, other_ref[...])

    return order.call(
        kernel,
        [(cotangent, (tile, features), lambda k, i, s: (i, 0))]
        + [whole(w) for w in weights]
        + [(others, (rows, tile), lambda k, i, s: (k, i))]
        + [(a, None, None) for a in kept],
        [(shaped(bf16, *shape), (tile, 2 * rows), lambda k, i, s: (i, s[slots[0] + k]))],
        (count, 3),
        expected["join far" if FAR in slots else "join own" if OWN in slots else "join two"],
        None if target is None else {count + 3: 0},
    )


def key_sums(order, mine, theirs_one, theirs_two, weights):
    rows, tokens = theirs_one.shape
    features = weights[0].shape[1]

    def kernel(s_ref, x_ref, one_ref, two_ref, *refs):
        own_ref, pair_ref = refs[3:]
        own = pair = 0.0
        for k in range(3):
            w = refs[k][...]
            theirs = one_ref[...] if k == 0 else two_ref[(k - 1) * rows : k * rows]
            own += dot_t(x_ref[(k + 1) * rows : (k + 2) * rows], w)
            pair += dot_t(theirs, w)
        own_ref[...] = own
        pair_ref[...] = pair

    out = columnwise(shaped(f32, tokens, features), 2)
    return order.call(
        kernel,
        [whole(mine), whole(theirs_one), whole(theirs_two)] + [columnwise(w, 2) for w in weights],
        [out, out],
        (2,),
        expected["key sums"],
    )


def key_last(order, total, inputs, weight, scale, dtype):
    tokens, features = total.shape
    rows = weight.shape[0]

    def kernel(s_ref, total_ref, x_ref, w_ref, out_ref):
        value = total_ref[...] + dot_t(x_ref[...], w_ref[...])
        out_ref[...] = (value * scale).astype(dtype)

    return order.call(
        kernel,
        [columnwise(total, 2), stacked(inputs, 0, rows), columnwise(weight, 2)],
        [columnwise(shaped(dtype, tokens, features), 2)],
        (2,),
        0,
    )


def chip_delta(order, anchor, local, other):
    rows, features = local.shape

    def kernel(s_ref, anchor_ref, a_ref, b_ref, out_ref):
        anchor_rows = anchor_ref[...]
        out_ref[...] = (anchor_rows - a_ref[...]) + (anchor_rows - b_ref[...])

    def half(array):
        return (array, (rows // 6, features), lambda i, s: (3 * s[CORE] + i, 0))

    return order.call(
        kernel,
        [half(anchor), half(local), half(other)],
        [rowwise(shaped(f32, rows // 2, features), 3)],
        (3,),
    )


def total_of(order, here, there):
    def kernel(s_ref, a_ref, b_ref, out_ref):
        out_ref[...] = a_ref[...] + b_ref[...]

    return order.call(
        kernel, [rowwise(here, 3), rowwise(there, 3)], [rowwise(shaped(f32, *here.shape), 3)], (3,)
    )


def handoff(order, pick, *arrays, span=1, before=()):
    def kernel(s_ref, *refs):
        refs[-1][...] = pick(s_ref, *[ref[...] for ref in refs[: len(arrays)]])

    rows, features = arrays[0].shape
    block = (rows // 3, features)
    return order.call(
        kernel,
        [(a, block, lambda i, s: (i, 0)) for a in arrays] + [(a, None, None) for a in before],
        [rowwise(shaped(bf16, rows, features), 3)],
        (3,),
        span,
    )


def sum_of(a, b):
    return (a.astype(f32) + b.astype(f32)).astype(bf16)


def second_send(s, p0, received):
    return chosen(s[END_0], p0, received)


def third_send(core):
    def pick(s, p0, p1, received):
        on_core = s[CORE] == core
        return jnp.where(on_core, sum_of(p0, received), chosen(s[END], p1, received))

    return pick


def fourth_send(core):
    def pick(s, p1, p2, received):
        part = jnp.where(s[CORE] == core, p2, p1.astype(f32))
        return (part + received.astype(f32)).astype(bf16)

    return pick


def nesterov_pass(order, own, other, anchor, momentum, local):
    rows, features = local.shape

    def kernel(s_ref, own_ref, other_ref, anchor_ref, momentum_ref, local_ref, *out):
        anchor_new_ref, moment_new_ref, base_ref = out
        in_own = pl.program_id(0) // 3 == s_ref[CORE]
        outer_grad = jnp.where(in_own, own_ref[...], other_ref[...]) / 4
        anchor_new, moment_new = nesterov(outer_grad, anchor_ref[...], momentum_ref[...])
        anchor_new_ref[...] = anchor_new
        moment_new_ref[...] = moment_new
        kept = mix_weight * (1.0 - inner_rate * weight_decay)
        base_ref[...] = kept * local_ref[...] + (1.0 - mix_weight) * anchor_new

    def half(array):
        return (array, (rows // 6, features), lambda i, s: (i % 3, 0))

    out = rowwise(shaped(f32, rows, features), 6)
    return order.call(
        kernel,
        [half(own), half(other)] + [rowwise(a, 6) for a in (anchor, momentum, local)],
        [out, out, out],
        (6,),
    )


def final_update(order, fixes, p23, sum_a, sum_b, first_old, second_old, base):
    rows, features = base.shape

    def kernel(s_ref, fix_ref, p_ref, a_ref, b_ref, first_ref, second_ref, base_ref, *out):
        merged_ref, m_ref, v_ref = out
        gradient = p_ref[...] + a_ref[...].astype(f32) + b_ref[...].astype(f32)
        first_new = beta_first * first_ref[...] + (1.0 - beta_first) * gradient
        second_new = beta_second * second_ref[...] + (1.0 - beta_second) * gradient * gradient
        root = jnp.sqrt(second_new * fix_ref[1]) + epsilon
        step = (mix_weight * inner_rate) * fix_ref[0]
        merged_ref[...] = base_ref[...] - step * first_new / root
        m_ref[...] = first_new
        v_ref[...] = second_new

    out = rowwise(shaped(f32, rows, features), 6)
    return order.call(
        kernel,
        [(p23, (rows // 6, features), lambda i, *_: (i + 6, 0))]
        + [rowwise(a, 6) for a in (sum_a, sum_b, first_old, second_old, base)],
        [out, out, out],
        (6,),
        fixes=fixes,
    )


def key_join(order, total, received, scale):
    def kernel(s_ref, a_ref, b_ref, out_ref):
        out_ref[...] = (a_ref[...] * scale + b_ref[...].astype(f32)).astype(bf16)

    return order.call(
        kernel,
        [rowwise(total, 3), rowwise(received, 3)],
        [rowwise(shaped(bf16, *total.shape), 3)],
        (3,),
    )


def pair_pass(normed, key_grad, local, first_old, second_old, anchor, momentum, inner_step):
    width = normed.shape[1]
    rows = local.shape[0]
    scale = width ** (-0.5)
    me = lax.axis_index("fsdp")
    core = lax.axis_index("rep") % 2
    y, z = me % 2, me // 2
    inside = (z == 1) | (z == 2)
    far = jnp.where(z < 2, 3, 0)
    middle = jnp.where(z < 2, 2, 1)
    flags = [inside, ~inside, core, ~inside & (core == 0), ~inside & (core == 1)]
    order = Order(jnp.stack([far, middle, z ^ 1, z, y] + flags).astype(jnp.int32))

    outer = [(0, 1), (1, 0), (2, 3), (3, 2)]
    inner = [(1, 2), (2, 1)]

    def turn(kind):
        pairs = [
            (8 * r + 2 * a + c, 8 * r + 2 * b + c)
            for r in range(4)
            for a, b in (outer if r % 2 == kind else inner)
            for c in (0, 1)
        ]
        return lambda value: lax.ppermute(value, ("rep", "fsdp"), pairs)

    turn_a, turn_b = turn(0), turn(1)

    def swap(value):
        return lax.ppermute(value, "fsdp", [(i, i ^ 1) for i in range(8)])

    def replica(value, bit):
        return lax.ppermute(value, "rep", [(i, i ^ bit) for i in range(4)])

    g_pair = swap(key_grad)
    weight = rounded(order, local)
    b1 = turn_b(weight)
    a1 = turn_a(weight)
    x0 = swap(first_piece(order, normed, rows))
    fixes = 1.0 / jnp.stack(corrections(inner_step))
    one, two, mine = split(order, normed, rows, g_pair, fixes)
    x1 = swap(one)
    delta = chip_delta(order, anchor, local, replica(local, 1))
    delta_there = replica(delta, 2)

    p0, send = gradient_part(order, mine, 0, x0, key_grad, g_pair, scale, a1)
    b2 = turn_b(send)
    a2 = turn_a(handoff(order, second_send, p0, b1))
    x23 = swap(two)
    p1 = gradient_part(order, mine, 1, x1, key_grad, g_pair, scale)
    g0 = swap(input_part(order, g_pair, weight, scale))

    a3 = turn_a(handoff(order, third_send(1), p0, p1, b2, span=expected["third"]))
    b3 = turn_b(handoff(order, third_send(0), p0, p1, a2))
    i12, w_middle, w_beside = input_parts(order, g_pair, a1, b1, a2, b2, scale)
    g12 = swap(i12)
    p23 = gradient_rest(order, mine, x23, key_grad, g_pair, scale)
    own_total, pair_total = key_sums(order, mine, x1, x23, (w_middle, w_beside, weight))
    total = total_of(order, delta, delta_there)
    total_there = replica(total, 1)
    input_grad = input_join(order, [OWN], key_grad, [weight], g0, normed.shape, scale)

    b4 = turn_b(handoff(order, fourth_send(1), p1, p23, a3))
    i3, w_far = input_part_of(order, g_pair, b2, a2, a3, b3, scale)
    g3 = swap(i3)
    a4 = turn_a(handoff(order, fourth_send(0), p1, p23, b3, before=[g12]))
    key_pair = swap(key_last(order, pair_total, x0, w_far, scale, bf16))
    own_total = key_last(order, own_total, mine, w_far, 1.0, f32)
    input_grad = input_join(
        order,
        [MIDDLE, BESIDE],
        key_grad,
        [w_middle, w_beside],
        g12,
        normed.shape,
        scale,
        input_grad,
    )
    anchor_new, moment_new, base = nesterov_pass(
        order, total, total_there, anchor, momentum, local
    )
    input_grad = input_join(
        order, [FAR], key_grad, [w_far], g3, normed.shape, scale, input_grad, [b4]
    )
    merged, first_new, second_new = final_update(
        order, fixes, p23, a4, b4, first_old, second_old, base
    )
    keys = key_join(order, own_total, key_pair, scale)
    return (keys, input_grad, merged, first_new, second_new, anchor_new, moment_new)


def body(normed, key_grad, master, first_moment, second_moment, anchor, momentum, inner_step):
    local = master[0]
    sizes = (lax.axis_size("rep"), lax.axis_size("fsdp"))
    inner_pass = pair_pass if sizes == (4, 8) else whole_pass
    keys, input_grad, merged, first_new, second_new, anchor_new, moment_new = inner_pass(
        normed, key_grad, local, first_moment[0], second_moment[0], anchor, momentum, inner_step
    )
    return (
        keys,
        input_grad,
        merged[None],
        first_new[None],
        second_new[None],
        anchor_new,
        moment_new,
    )


def solution(mesh):
    in_specs = (
        P(("rep", "fsdp"), None),
        P(("rep", "fsdp"), None),
        P("rep", "fsdp", None),
        P("rep", "fsdp", None),
        P("rep", "fsdp", None),
        P("fsdp", None),
        P("fsdp", None),
        P(),
    )
    out_specs = (
        P(("rep", "fsdp"), None),
        P(("rep", "fsdp"), None),
        P("rep", "fsdp", None),
        P("rep", "fsdp", None),
        P("rep", "fsdp", None),
        P("fsdp", None),
        P("fsdp", None),
    )
    return jax.shard_map(body, mesh=mesh, in_specs=in_specs, out_specs=out_specs, check_vma=False)
```

```python
import jax
import jax.numpy as jnp
from jax import lax
from jax.experimental import pallas as pl
from jax.experimental.pallas import tpu as pltpu
from jax.sharding import PartitionSpec as P

beta_first = 0.9
beta_second = 0.95
inner_rate = 0.1
weight_decay = 0.1
epsilon = 1e-08
outer_rate = 0.7
outer_mu = 0.9
mix_weight = 0.5

f32 = jnp.float32
bf16 = jnp.bfloat16
vmem_bytes = 16 * 1024 * 1024

expected = {
    "split": 30,
    "first part": 0,
    "second part": 5,
    "input own": 2,
    "third": 20,
    "input two": 0,
    "rest": 8,
    "key sums": 0,
    "join own": 1,
    "input far": 0,
    "join two": 0,
    "join far": 10,
}


def corrections(inner_step):
    count_float = inner_step[0].astype(f32)
    fix_first = 1.0 - jnp.power(f32(beta_first), count_float)
    fix_second = 1.0 - jnp.power(f32(beta_second), count_float)
    return fix_first, fix_second


def adam(gradient, local, first_old, second_old, fix_first, fix_second):
    first_new = beta_first * first_old + (1.0 - beta_first) * gradient
    second_new = beta_second * second_old + (1.0 - beta_second) * gradient * gradient
    direction = first_new / fix_first / (jnp.sqrt(second_new / fix_second) + epsilon)
    stepped = local - inner_rate * (direction + weight_decay * local)
    return (stepped, first_new, second_new)


def nesterov(outer_grad, anchor_rows, moment_rows):
    moment_new = outer_mu * moment_rows + outer_grad
    anchor_new = anchor_rows - outer_rate * (outer_grad + outer_mu * moment_new)
    return (anchor_new, moment_new)


def outer_update(local, anchor, momentum):
    summed = lax.psum(anchor - local, "rep")
    return nesterov(summed / lax.axis_size("rep"), anchor, momentum)


def whole_pass(normed, key_grad, local, first_old, second_old, anchor, momentum, inner_step):
    scale = normed.shape[1] ** (-0.5)
    weight = lax.all_gather(local.astype(bf16), "fsdp", axis=0, tiled=True)
    keys = (jnp.dot(normed, weight, preferred_element_type=f32) * scale).astype(bf16)
    input_grad = (
        lax.dot_general(key_grad, weight, (((1,), (1,)), ((), ())), preferred_element_type=f32)
        * scale
    ).astype(bf16)
    gradient = lax.psum_scatter(
        lax.dot_general(normed, key_grad, (((0,), (0,)), ((), ())), preferred_element_type=f32)
        * scale,
        "fsdp",
        scatter_dimension=0,
        tiled=True,
    )
    stepped, first_new, second_new = adam(
        gradient, local, first_old, second_old, *corrections(inner_step)
    )
    anchor_new, moment_new = outer_update(local, anchor, momentum)
    merged = mix_weight * stepped + (1.0 - mix_weight) * anchor_new
    return (keys, input_grad, merged, first_new, second_new, anchor_new, moment_new)


FAR, MIDDLE, BESIDE, OWN, Y, INNER, END, CORE, END_0, END_1 = range(10)


class Order:
    def __init__(self, place):
        self.place = place
        self.token = None

    def call(self, kernel, inputs, outputs, grid, span=1, aliases=None, fixes=None):
        scalars = [self.place] + ([] if fixes is None else [fixes])
        tokens = [] if self.token is None else [self.token]
        before = len(scalars) + len(inputs)

        def wrapped(*refs):
            refs[-1][...] = jnp.zeros_like(refs[-1])
            kernel(*refs[:before], *refs[before + len(tokens) : -1])

        outputs = outputs + [whole(shaped(jnp.int32, 8, 128))]
        shapes = [shape for shape, _, _ in outputs]
        keep = pl.BlockSpec(memory_space=pl.ANY)
        out = pl.pallas_call(
            wrapped,
            out_shape=shapes,
            grid_spec=pltpu.PrefetchScalarGridSpec(
                num_scalar_prefetch=len(scalars),
                grid=grid,
                in_specs=[
                    keep if block is None else pl.BlockSpec(block, index)
                    for _, block, index in inputs
                ]
                + [keep] * len(tokens),
                out_specs=[pl.BlockSpec(block, index) for _, block, index in outputs],
            ),
            input_output_aliases=aliases or {},
            compiler_params=pltpu.CompilerParams(vmem_limit_bytes=vmem_bytes),
            cost_estimate=pl.CostEstimate(
                flops=int(span * 1e9), bytes_accessed=0, transcendentals=0
            ),
        )(*scalars, *[a for a, _, _ in inputs], *tokens)
        self.token = out[-1]
        return out[0] if len(out) == 2 else out[:-1]


def shaped(dtype, *shape):
    return jax.ShapeDtypeStruct(shape, dtype)


def whole(array):
    zeros = (0,) * len(array.shape)
    return (array, array.shape, lambda *_: zeros)


def rowwise(array, steps):
    return (array, (array.shape[0] // steps, array.shape[1]), lambda i, *_: (i, 0))


def columnwise(array, steps):
    return (array, (array.shape[0], array.shape[1] // steps), lambda i, *_: (0, i))


def stacked(array, k, rows):
    return (array, (rows, array.shape[1]), lambda *_: (k, 0))


def dot_t(a, b):
    return lax.dot_general(a, b, (((0,), (0,)), ((), ())), preferred_element_type=f32)


def dot_bt(a, b):
    return lax.dot_general(a, b, (((1,), (1,)), ((), ())), preferred_element_type=f32)


def dot(a, b):
    return jnp.dot(a, b, preferred_element_type=f32)


def chosen(flag, yes, no):
    return jnp.where(flag != 0, yes, no)


def halves(x_ref, rows):
    turned = x_ref[...].T
    return turned[:rows], turned[rows:]


def rounded(order, local):
    def kernel(s_ref, a_ref, out_ref):
        out_ref[...] = a_ref[...].astype(bf16)

    return order.call(
        kernel, [rowwise(local, 3)], [rowwise(shaped(bf16, *local.shape), 3)], (3,)
    )


def first_piece(order, normed, rows):
    tokens = normed.shape[0]

    def kernel(s_ref, x_ref, piece_ref):
        low, high = halves(x_ref, rows)
        piece_ref[...] = chosen(s_ref[Y], low, high)

    return order.call(
        kernel,
        [(normed, (tokens, 2 * rows), lambda i, s: (0, s[FAR]))],
        [whole(shaped(bf16, rows, tokens))],
        (1,),
    )


def split(order, normed, rows, g_pair, fixes):
    tokens = normed.shape[0]

    def kernel(s_ref, fix_ref, x_ref, g_ref, one_ref, two_ref, own_ref):
        i = pl.program_id(0)
        low, high = halves(x_ref, rows)
        own_ref[...] = chosen(s_ref[Y], high, low)

        @pl.when(i == 0)
        def _():
            one_ref[...] = chosen(s_ref[Y], low, high)

        @pl.when((i == 1) | (i == 2))
        def _():
            two_ref[...] = chosen(s_ref[Y], low, high)

    return order.call(
        kernel,
        [
            (normed, (tokens, 2 * rows), lambda i, s, f: (0, s[(i + 1) % 4])),
            (g_pair, None, None),
        ],
        [
            whole(shaped(bf16, rows, tokens)),
            (
                shaped(bf16, 2 * rows, tokens),
                (rows, tokens),
                lambda i, s, f: (jnp.clip(i - 1, 0, 1), 0),
            ),
            (shaped(bf16, 4 * rows, tokens), (rows, tokens), lambda i, s, f: ((i + 1) % 4, 0)),
        ],
        (4,),
        expected["split"],
        fixes=fixes,
    )


def gradient_part(order, mine, k, theirs, key_grad, g_pair, scale, inside=None, flag=END_1):
    tokens, features = key_grad.shape
    rows = theirs.shape[0]

    def kernel(s_ref, x_ref, xp_ref, g_ref, gp_ref, *rest):
        total = dot(x_ref[...], g_ref[...]) + dot(xp_ref[...], gp_ref[...])
        value = (total * scale).astype(bf16)
        if inside is None:
            rest[0][...] = value
        else:
            w_ref, out_ref, send_ref = rest
            out_ref[...] = value
            send_ref[...] = chosen(s_ref[flag], value, w_ref[...])

    extra = [] if inside is None else [columnwise(inside, 2)]
    out = columnwise(shaped(bf16, rows, features), 2)
    return order.call(
        kernel,
        [stacked(mine, k, rows), whole(theirs), columnwise(key_grad, 2), columnwise(g_pair, 2)]
        + extra,
        [out] + [out] * len(extra),
        (2,),
        expected["first part" if extra else "second part"],
    )


def gradient_rest(order, mine, theirs, key_grad, g_pair, scale):
    tokens, features = key_grad.shape
    rows = mine.shape[0] // 4
    tile = features // 2

    def kernel(s_ref, x_ref, xp_ref, g_ref, gp_ref, out_ref):
        total = dot(x_ref[...], g_ref[...]) + dot(xp_ref[...], gp_ref[...])
        out_ref[...] = total * scale

    return order.call(
        kernel,
        [
            (mine, (rows, tokens), lambda k, i, s: (k + 2, 0)),
            (theirs, (rows, tokens), lambda k, i, s: (k, 0)),
            (key_grad, (tokens, tile), lambda k, i, s: (0, i)),
            (g_pair, (tokens, tile), lambda k, i, s: (0, i)),
        ],
        [(shaped(f32, 2 * rows, features), (rows, tile), lambda k, i, s: (k, i))],
        (2, 2),
        expected["rest"],
    )


def input_part(order, cotangent, weight, scale):
    tokens, features = cotangent.shape
    rows = weight.shape[0]

    def kernel(s_ref, g_ref, w_ref, out_ref):
        out_ref[...] = (dot_bt(w_ref[...], g_ref[...]) * scale).astype(bf16)

    return order.call(
        kernel,
        [whole(cotangent), whole(weight)],
        [whole(shaped(bf16, rows, tokens))],
        (1,),
        expected["input own"],
    )


def input_parts(order, cotangent, beside_0, beside_1, end_0, end_1, scale):
    tokens, features = cotangent.shape
    rows = beside_0.shape[0]

    def kernel(s_ref, g_ref, a_ref, b_ref, c_ref, d_ref, out_ref, middle_ref, beside_ref):
        @pl.when(pl.program_id(0) == 0)
        def _():
            inner = chosen(s_ref[CORE], a_ref[...], b_ref[...])
            end = chosen(s_ref[CORE], d_ref[...], c_ref[...])
            middle_ref[...] = chosen(s_ref[INNER], inner, end)
            out_ref[...] = (dot_bt(middle_ref[...], g_ref[...]) * scale).astype(bf16)

        @pl.when(pl.program_id(0) == 1)
        def _():
            beside_ref[...] = chosen(s_ref[CORE], b_ref[...], a_ref[...])
            out_ref[...] = (dot_bt(beside_ref[...], g_ref[...]) * scale).astype(bf16)

    block = whole(shaped(bf16, rows, features))
    return order.call(
        kernel,
        [whole(cotangent)] + [whole(w) for w in (beside_0, beside_1, end_0, end_1)],
        [(shaped(bf16, 2 * rows, tokens), (rows, tokens), lambda i, s: (i, 0)), block, block],
        (2,),
        expected["input two"],
    )


def input_part_of(order, cotangent, inner_0, inner_1, end_0, end_1, scale):
    tokens, features = cotangent.shape
    rows = inner_0.shape[0]

    def kernel(s_ref, g_ref, a_ref, b_ref, c_ref, d_ref, out_ref, w_ref):
        inner = chosen(s_ref[CORE], b_ref[...], a_ref[...])
        end = chosen(s_ref[CORE], d_ref[...], c_ref[...])
        weight = chosen(s_ref[INNER], inner, end)
        w_ref[...] = weight
        out_ref[...] = (dot_bt(weight, g_ref[...]) * scale).astype(bf16)

    return order.call(
        kernel,
        [whole(cotangent)] + [whole(w) for w in (inner_0, inner_1, end_0, end_1)],
        [whole(shaped(bf16, rows, tokens)), whole(shaped(bf16, rows, features))],
        (1,),
        expected["input far"],
    )


def store_joined(y, out_ref, own, other):
    @pl.when(y == 0)
    def _():
        out_ref[...] = jnp.concatenate([own, other], 0).T

    @pl.when(y != 0)
    def _():
        out_ref[...] = jnp.concatenate([other, own], 0).T


def input_join(order, slots, cotangent, weights, others, shape, scale, target=None, before=()):
    tokens, features = cotangent.shape
    rows = weights[0].shape[0]
    count, tile = len(slots), tokens // 3
    kept = [a for a in (target, *before) if a is not None]

    def kernel(s_ref, g_ref, *refs):
        other_ref, out_ref = refs[count], refs[-1]
        weight = refs[0][...]
        if count == 2:
            weight = jnp.where(pl.program_id(0) == 0, weight, refs[1][...])
        own = (dot_bt(weight, g_ref[...]) * scale).astype(bf16)
        store_joined(s_ref[Y], out_ref, own, other_ref[...])

    return order.call(
        kernel,
        [(cotangent, (tile, features), lambda k, i, s: (i, 0))]
        + [whole(w) for w in weights]
        + [(others, (rows, tile), lambda k, i, s: (k, i))]
        + [(a, None, None) for a in kept],
        [(shaped(bf16, *shape), (tile, 2 * rows), lambda k, i, s: (i, s[slots[0] + k]))],
        (count, 3),
        expected["join far" if FAR in slots else "join own" if OWN in slots else "join two"],
        None if target is None else {count + 3: 0},
    )


def key_sums(order, mine, theirs_one, theirs_two, weights):
    rows, tokens = theirs_one.shape
    features = weights[0].shape[1]

    def kernel(s_ref, x_ref, one_ref, two_ref, *refs):
        own_ref, pair_ref = refs[3:]
        own = pair = 0.0
        for k in range(3):
            w = refs[k][...]
            theirs = one_ref[...] if k == 0 else two_ref[(k - 1) * rows : k * rows]
            own += dot_t(x_ref[(k + 1) * rows : (k + 2) * rows], w)
            pair += dot_t(theirs, w)
        own_ref[...] = own
        pair_ref[...] = pair

    out = columnwise(shaped(f32, tokens, features), 2)
    return order.call(
        kernel,
        [whole(mine), whole(theirs_one), whole(theirs_two)] + [columnwise(w, 2) for w in weights],
        [out, out],
        (2,),
        expected["key sums"],
    )


def key_last(order, total, inputs, weight, scale, dtype):
    tokens, features = total.shape
    rows = weight.shape[0]

    def kernel(s_ref, total_ref, x_ref, w_ref, out_ref):
        value = total_ref[...] + dot_t(x_ref[...], w_ref[...])
        out_ref[...] = (value * scale).astype(dtype)

    return order.call(
        kernel,
        [columnwise(total, 2), stacked(inputs, 0, rows), columnwise(weight, 2)],
        [columnwise(shaped(dtype, tokens, features), 2)],
        (2,),
        0,
    )


def chip_delta(order, anchor, local, other):
    rows, features = local.shape

    def kernel(s_ref, anchor_ref, a_ref, b_ref, out_ref):
        anchor_rows = anchor_ref[...]
        out_ref[...] = (anchor_rows - a_ref[...]) + (anchor_rows - b_ref[...])

    def half(array):
        return (array, (rows // 6, features), lambda i, s: (3 * s[CORE] + i, 0))

    return order.call(
        kernel,
        [half(anchor), half(local), half(other)],
        [rowwise(shaped(f32, rows // 2, features), 3)],
        (3,),
    )


def total_of(order, here, there):
    def kernel(s_ref, a_ref, b_ref, out_ref):
        out_ref[...] = a_ref[...] + b_ref[...]

    return order.call(
        kernel, [rowwise(here, 3), rowwise(there, 3)], [rowwise(shaped(f32, *here.shape), 3)], (3,)
    )


def handoff(order, pick, *arrays, span=1, before=()):
    def kernel(s_ref, *refs):
        refs[-1][...] = pick(s_ref, *[ref[...] for ref in refs[: len(arrays)]])

    rows, features = arrays[0].shape
    block = (rows // 3, features)
    return order.call(
        kernel,
        [(a, block, lambda i, s: (i, 0)) for a in arrays] + [(a, None, None) for a in before],
        [rowwise(shaped(bf16, rows, features), 3)],
        (3,),
        span,
    )


def sum_of(a, b):
    return (a.astype(f32) + b.astype(f32)).astype(bf16)


def second_send(s, p0, received):
    return chosen(s[END_0], p0, received)


def third_send(core):
    def pick(s, p0, p1, received):
        on_core = s[CORE] == core
        return jnp.where(on_core, sum_of(p0, received), chosen(s[END], p1, received))

    return pick


def fourth_send(core):
    def pick(s, p1, p2, received):
        part = jnp.where(s[CORE] == core, p2, p1.astype(f32))
        return (part + received.astype(f32)).astype(bf16)

    return pick


def nesterov_pass(order, own, other, anchor, momentum, local):
    rows, features = local.shape

    def kernel(s_ref, own_ref, other_ref, anchor_ref, momentum_ref, local_ref, *out):
        anchor_new_ref, moment_new_ref, base_ref = out
        in_own = pl.program_id(0) // 3 == s_ref[CORE]
        outer_grad = jnp.where(in_own, own_ref[...], other_ref[...]) / 4
        anchor_new, moment_new = nesterov(outer_grad, anchor_ref[...], momentum_ref[...])
        anchor_new_ref[...] = anchor_new
        moment_new_ref[...] = moment_new
        kept = mix_weight * (1.0 - inner_rate * weight_decay)
        base_ref[...] = kept * local_ref[...] + (1.0 - mix_weight) * anchor_new

    def half(array):
        return (array, (rows // 6, features), lambda i, s: (i % 3, 0))

    out = rowwise(shaped(f32, rows, features), 6)
    return order.call(
        kernel,
        [half(own), half(other)] + [rowwise(a, 6) for a in (anchor, momentum, local)],
        [out, out, out],
        (6,),
    )


def final_update(order, fixes, p23, sum_a, sum_b, first_old, second_old, base):
    rows, features = base.shape

    def kernel(s_ref, fix_ref, p_ref, a_ref, b_ref, first_ref, second_ref, base_ref, *out):
        merged_ref, m_ref, v_ref = out
        gradient = p_ref[...] + a_ref[...].astype(f32) + b_ref[...].astype(f32)
        first_new = beta_first * first_ref[...] + (1.0 - beta_first) * gradient
        second_new = beta_second * second_ref[...] + (1.0 - beta_second) * gradient * gradient
        root = jnp.sqrt(second_new * fix_ref[1]) + epsilon
        step = (mix_weight * inner_rate) * fix_ref[0]
        merged_ref[...] = base_ref[...] - step * first_new / root
        m_ref[...] = first_new
        v_ref[...] = second_new

    out = rowwise(shaped(f32, rows, features), 6)
    return order.call(
        kernel,
        [(p23, (rows // 6, features), lambda i, *_: (i + 6, 0))]
        + [rowwise(a, 6) for a in (sum_a, sum_b, first_old, second_old, base)],
        [out, out, out],
        (6,),
        fixes=fixes,
    )


def key_join(order, total, received, scale):
    def kernel(s_ref, a_ref, b_ref, out_ref):
        out_ref[...] = (a_ref[...] * scale + b_ref[...].astype(f32)).astype(bf16)

    return order.call(
        kernel,
        [rowwise(total, 3), rowwise(received, 3)],
        [rowwise(shaped(bf16, *total.shape), 3)],
        (3,),
    )


def pair_pass(normed, key_grad, local, first_old, second_old, anchor, momentum, inner_step):
    width = normed.shape[1]
    rows = local.shape[0]
    scale = width ** (-0.5)
    me = lax.axis_index("fsdp")
    core = lax.axis_index("rep") % 2
    y, z = me % 2, me // 2
    inside = (z == 1) | (z == 2)
    far = jnp.where(z < 2, 3, 0)
    middle = jnp.where(z < 2, 2, 1)
    flags = [inside, ~inside, core, ~inside & (core == 0), ~inside & (core == 1)]
    order = Order(jnp.stack([far, middle, z ^ 1, z, y] + flags).astype(jnp.int32))

    outer = [(0, 1), (1, 0), (2, 3), (3, 2)]
    inner = [(1, 2), (2, 1)]

    def turn(kind):
        pairs = [
            (8 * r + 2 * a + c, 8 * r + 2 * b + c)
            for r in range(4)
            for a, b in (outer if r % 2 == kind else inner)
            for c in (0, 1)
        ]
        return lambda value: lax.ppermute(value, ("rep", "fsdp"), pairs)

    turn_a, turn_b = turn(0), turn(1)

    def swap(value):
        return lax.ppermute(value, "fsdp", [(i, i ^ 1) for i in range(8)])

    def replica(value, bit):
        return lax.ppermute(value, "rep", [(i, i ^ bit) for i in range(4)])

    g_pair = swap(key_grad)
    weight = rounded(order, local)
    b1 = turn_b(weight)
    a1 = turn_a(weight)
    x0 = swap(first_piece(order, normed, rows))
    fixes = 1.0 / jnp.stack(corrections(inner_step))
    one, two, mine = split(order, normed, rows, g_pair, fixes)
    x1 = swap(one)
    delta = chip_delta(order, anchor, local, replica(local, 1))
    delta_there = replica(delta, 2)

    p0, send = gradient_part(order, mine, 0, x0, key_grad, g_pair, scale, a1)
    b2 = turn_b(send)
    x23 = swap(two)
    p1 = gradient_part(order, mine, 1, x1, key_grad, g_pair, scale)
    g0 = swap(input_part(order, g_pair, weight, scale))
    a2 = turn_a(handoff(order, second_send, p0, b1))

    a3 = turn_a(handoff(order, third_send(1), p0, p1, b2, span=expected["third"]))
    b3 = turn_b(handoff(order, third_send(0), p0, p1, a2))
    i12, w_middle, w_beside = input_parts(order, g_pair, a1, b1, a2, b2, scale)
    g12 = swap(i12)
    p23 = gradient_rest(order, mine, x23, key_grad, g_pair, scale)
    own_total, pair_total = key_sums(order, mine, x1, x23, (w_middle, w_beside, weight))
    total = total_of(order, delta, delta_there)
    total_there = replica(total, 1)
    input_grad = input_join(order, [OWN], key_grad, [weight], g0, normed.shape, scale)

    b4 = turn_b(handoff(order, fourth_send(1), p1, p23, a3))
    i3, w_far = input_part_of(order, g_pair, b2, a2, a3, b3, scale)
    g3 = swap(i3)
    a4 = turn_a(handoff(order, fourth_send(0), p1, p23, b3, before=[g12]))
    key_pair = swap(key_last(order, pair_total, x0, w_far, scale, bf16))
    own_total = key_last(order, own_total, mine, w_far, 1.0, f32)
    input_grad = input_join(
        order,
        [MIDDLE, BESIDE],
        key_grad,
        [w_middle, w_beside],
        g12,
        normed.shape,
        scale,
        input_grad,
    )
    anchor_new, moment_new, base = nesterov_pass(
        order, total, total_there, anchor, momentum, local
    )
    input_grad = input_join(
        order, [FAR], key_grad, [w_far], g3, normed.shape, scale, input_grad, [b4]
    )
    merged, first_new, second_new = final_update(
        order, fixes, p23, a4, b4, first_old, second_old, base
    )
    keys = key_join(order, own_total, key_pair, scale)
    return (keys, input_grad, merged, first_new, second_new, anchor_new, moment_new)


def body(normed, key_grad, master, first_moment, second_moment, anchor, momentum, inner_step):
    local = master[0]
    sizes = (lax.axis_size("rep"), lax.axis_size("fsdp"))
    inner_pass = pair_pass if sizes == (4, 8) else whole_pass
    keys, input_grad, merged, first_new, second_new, anchor_new, moment_new = inner_pass(
        normed, key_grad, local, first_moment[0], second_moment[0], anchor, momentum, inner_step
    )
    return (
        keys,
        input_grad,
        merged[None],
        first_new[None],
        second_new[None],
        anchor_new,
        moment_new,
    )


def solution(mesh):
    in_specs = (
        P(("rep", "fsdp"), None),
        P(("rep", "fsdp"), None),
        P("rep", "fsdp", None),
        P("rep", "fsdp", None),
        P("rep", "fsdp", None),
        P("fsdp", None),
        P("fsdp", None),
        P(),
    )
    out_specs = (
        P(("rep", "fsdp"), None),
        P(("rep", "fsdp"), None),
        P("rep", "fsdp", None),
        P("rep", "fsdp", None),
        P("rep", "fsdp", None),
        P("fsdp", None),
        P("fsdp", None),
    )
    return jax.shard_map(body, mesh=mesh, in_specs=in_specs, out_specs=out_specs, check_vma=False)
```

```python
import jax
import jax.numpy as jnp
from jax import lax
from jax.experimental import pallas as pl
from jax.experimental.pallas import tpu as pltpu
from jax.sharding import PartitionSpec as P

beta_first = 0.9
beta_second = 0.95
inner_rate = 0.1
weight_decay = 0.1
epsilon = 1e-08
outer_rate = 0.7
outer_mu = 0.9
mix_weight = 0.5

f32 = jnp.float32
bf16 = jnp.bfloat16
vmem_bytes = 16 * 1024 * 1024

expected = {
    "split": 30,
    "first part": 0,
    "input two": 12,
    "second part": 30,
    "nesterov": 1,
    "handoff": 1,
    "input middle": 0,
    "own sums": 0,
    "early sums": 1,
    "input far": 0,
    "pair sums": 0,
    "late sums": 1,
    "join middle": 0,
    "first half": 5,
    "join far": 0,
}


def corrections(inner_step):
    count_float = inner_step[0].astype(f32)
    fix_first = 1.0 - jnp.power(f32(beta_first), count_float)
    fix_second = 1.0 - jnp.power(f32(beta_second), count_float)
    return fix_first, fix_second


def adam(gradient, local, first_old, second_old, fix_first, fix_second):
    first_new = beta_first * first_old + (1.0 - beta_first) * gradient
    second_new = beta_second * second_old + (1.0 - beta_second) * gradient * gradient
    direction = first_new / fix_first / (jnp.sqrt(second_new / fix_second) + epsilon)
    stepped = local - inner_rate * (direction + weight_decay * local)
    return (stepped, first_new, second_new)


def nesterov(outer_grad, anchor_rows, moment_rows):
    moment_new = outer_mu * moment_rows + outer_grad
    anchor_new = anchor_rows - outer_rate * (outer_grad + outer_mu * moment_new)
    return (anchor_new, moment_new)


def outer_update(local, anchor, momentum):
    summed = lax.psum(anchor - local, "rep")
    return nesterov(summed / lax.axis_size("rep"), anchor, momentum)


def whole_pass(normed, key_grad, local, first_old, second_old, anchor, momentum, inner_step):
    scale = normed.shape[1] ** (-0.5)
    weight = lax.all_gather(local.astype(bf16), "fsdp", axis=0, tiled=True)
    keys = (jnp.dot(normed, weight, preferred_element_type=f32) * scale).astype(bf16)
    input_grad = (
        lax.dot_general(key_grad, weight, (((1,), (1,)), ((), ())), preferred_element_type=f32)
        * scale
    ).astype(bf16)
    gradient = lax.psum_scatter(
        lax.dot_general(normed, key_grad, (((0,), (0,)), ((), ())), preferred_element_type=f32)
        * scale,
        "fsdp",
        scatter_dimension=0,
        tiled=True,
    )
    stepped, first_new, second_new = adam(
        gradient, local, first_old, second_old, *corrections(inner_step)
    )
    anchor_new, moment_new = outer_update(local, anchor, momentum)
    merged = mix_weight * stepped + (1.0 - mix_weight) * anchor_new
    return (keys, input_grad, merged, first_new, second_new, anchor_new, moment_new)


FAR, MIDDLE, BESIDE, OWN, Y, INNER, END, CORE = range(8)


class Order:
    def __init__(self, place):
        self.place = place
        self.token = None

    def call(self, kernel, inputs, outputs, grid, span=1, aliases=None, fixes=None):
        scalars = [self.place] + ([] if fixes is None else [fixes])
        tokens = [] if self.token is None else [self.token]
        before = len(scalars) + len(inputs)

        def wrapped(*refs):
            refs[-1][...] = jnp.zeros_like(refs[-1])
            kernel(*refs[:before], *refs[before + len(tokens) : -1])

        outputs = outputs + [whole(shaped(jnp.int32, 8, 128))]
        shapes = [shape for shape, _, _ in outputs]
        keep = pl.BlockSpec(memory_space=pl.ANY)
        out = pl.pallas_call(
            wrapped,
            out_shape=shapes,
            grid_spec=pltpu.PrefetchScalarGridSpec(
                num_scalar_prefetch=len(scalars),
                grid=grid,
                in_specs=[
                    keep if block is None else pl.BlockSpec(block, index)
                    for _, block, index in inputs
                ]
                + [keep] * len(tokens),
                out_specs=[pl.BlockSpec(block, index) for _, block, index in outputs],
            ),
            input_output_aliases=aliases or {},
            compiler_params=pltpu.CompilerParams(vmem_limit_bytes=vmem_bytes),
            cost_estimate=pl.CostEstimate(
                flops=int(span * 1e9), bytes_accessed=0, transcendentals=0
            ),
        )(*scalars, *[a for a, _, _ in inputs], *tokens)
        self.token = out[-1]
        return out[0] if len(out) == 2 else out[:-1]


def shaped(dtype, *shape):
    return jax.ShapeDtypeStruct(shape, dtype)


def whole(array):
    zeros = (0,) * len(array.shape)
    return (array, array.shape, lambda *_: zeros)


def rowwise(array, steps):
    return (array, (array.shape[0] // steps, array.shape[1]), lambda i, *_: (i, 0))


def columnwise(array, steps):
    return (array, (array.shape[0], array.shape[1] // steps), lambda i, *_: (0, i))


def stacked(array, k, rows):
    return (array, (rows, array.shape[1]), lambda *_: (k, 0))


def dot_t(a, b):
    return lax.dot_general(a, b, (((0,), (0,)), ((), ())), preferred_element_type=f32)


def dot_bt(a, b):
    return lax.dot_general(a, b, (((1,), (1,)), ((), ())), preferred_element_type=f32)


def dot(a, b):
    return jnp.dot(a, b, preferred_element_type=f32)


def chosen(flag, yes, no):
    return jnp.where(flag != 0, yes, no)


def halves(x_ref, rows):
    turned = x_ref[...].T
    return turned[:rows], turned[rows:]


def rounded(order, local):
    def kernel(s_ref, a_ref, out_ref):
        out_ref[...] = a_ref[...].astype(bf16)

    return order.call(
        kernel, [rowwise(local, 3)], [rowwise(shaped(bf16, *local.shape), 3)], (3,)
    )


def first_piece(order, normed, rows):
    tokens = normed.shape[0]

    def kernel(s_ref, x_ref, piece_ref):
        low, high = halves(x_ref, rows)
        piece_ref[...] = chosen(s_ref[Y], low, high)

    return order.call(
        kernel,
        [(normed, (tokens, 2 * rows), lambda i, s: (0, s[FAR]))],
        [whole(shaped(bf16, rows, tokens))],
        (1,),
    )


def split(order, normed, rows, g_pair, fixes):
    tokens = normed.shape[0]

    def kernel(s_ref, fix_ref, x_ref, g_ref, two_ref, last_ref, own_ref):
        i = pl.program_id(0)
        low, high = halves(x_ref, rows)
        own_ref[...] = chosen(s_ref[Y], high, low)

        @pl.when(i < 2)
        def _():
            two_ref[...] = chosen(s_ref[Y], low, high)

        @pl.when(i == 2)
        def _():
            last_ref[...] = chosen(s_ref[Y], low, high)

    return order.call(
        kernel,
        [
            (normed, (tokens, 2 * rows), lambda i, s, f: (0, s[(i + 1) % 4])),
            (g_pair, None, None),
        ],
        [
            (
                shaped(bf16, 2 * rows, tokens),
                (rows, tokens),
                lambda i, s, f: (jnp.minimum(i, 1), 0),
            ),
            (shaped(bf16, 3 * rows, tokens), (rows, tokens), lambda i, s, f: (0, 0)),
            (shaped(bf16, 4 * rows, tokens), (rows, tokens), lambda i, s, f: ((i + 1) % 4, 0)),
        ],
        (4,),
        expected["split"],
        fixes=fixes,
    )


def gradient_part(order, mine, k, theirs, at, key_grad, g_pair, scale, dtype, span):
    tokens, features = key_grad.shape
    rows = mine.shape[0] // 4

    def kernel(s_ref, x_ref, xp_ref, g_ref, gp_ref, out_ref):
        total = dot(x_ref[...], g_ref[...]) + dot(xp_ref[...], gp_ref[...])
        out_ref[...] = (total * scale).astype(dtype)

    return order.call(
        kernel,
        [
            stacked(mine, k, rows),
            stacked(theirs, at, rows),
            columnwise(key_grad, 2),
            columnwise(g_pair, 2),
        ],
        [columnwise(shaped(dtype, rows, features), 2)],
        (2,),
        span,
    )


def input_two(order, key_grad, g_pair, first, second, target, scale):
    tokens, features = key_grad.shape
    rows = first.shape[0]

    def kernel(s_ref, g_ref, gp_ref, a_ref, b_ref, target_ref, pair_ref, own_ref):
        weight = jnp.where(pl.program_id(0) == 0, a_ref[...], b_ref[...])
        pair_ref[...] = (dot_bt(weight, gp_ref[...]) * scale).astype(bf16)
        own_ref[...] = (dot_bt(weight, g_ref[...]) * scale).astype(bf16)

    return order.call(
        kernel,
        [whole(a) for a in (key_grad, g_pair, first, second)] + [(target, None, None)],
        [
            (target, (rows, tokens), lambda i, s: (1 + i, 0)),
            (shaped(bf16, 2 * rows, tokens), (rows, tokens), lambda i, s: (i, 0)),
        ],
        (2,),
        expected["input two"],
        {5: 0},
    )


def input_one(order, key_grad, g_pair, inner, half, end, scale, span, before=()):
    tokens, features = key_grad.shape
    rows = end.shape[0]

    def kernel(s_ref, g_ref, gp_ref, a_ref, b_ref, *rest):
        pair_ref, own_ref, w_ref = rest[len(before) :]
        weight = chosen(s_ref[INNER], a_ref[...], b_ref[...])
        w_ref[...] = weight
        pair_ref[...] = (dot_bt(weight, gp_ref[...]) * scale).astype(bf16)
        own_ref[...] = (dot_bt(weight, g_ref[...]) * scale).astype(bf16)

    out = whole(shaped(bf16, rows, tokens))
    return order.call(
        kernel,
        [whole(key_grad), whole(g_pair), stacked(inner, half, rows), whole(end)]
        + [(a, None, None) for a in before],
        [out, out, whole(shaped(bf16, rows, features))],
        (1,),
        span,
    )


def input_join(order, slot, own, others, shape, span, target=None, first=0):
    pieces = len(own)
    tokens = own[0].shape[1]
    tile = tokens // 3
    rows = shape[1] // 8
    count = sum(a.shape[0] for a in own) // rows

    def kernel(s_ref, *refs):
        mine = jnp.concatenate([ref[...] for ref in refs[:pieces]], 0)
        theirs = jnp.concatenate([ref[...] for ref in refs[pieces : 2 * pieces]], 0)
        out_ref = refs[-1]

        @pl.when(s_ref[Y] == 0)
        def _():
            out_ref[...] = jnp.concatenate([mine, theirs], 0).T

        @pl.when(s_ref[Y] != 0)
        def _():
            out_ref[...] = jnp.concatenate([theirs, mine], 0).T

    def tiled(array, height, offset=0):
        return (array, (height, tile), lambda k, i, s: (offset + k, i))

    heights = [a.shape[0] // count for a in own]
    inputs = [tiled(a, h) for a, h in zip(own, heights)]
    inputs += [tiled(a, h, first) for a, h in zip(others, heights)]

    return order.call(
        kernel,
        inputs + ([] if target is None else [(target, None, None)]),
        [(shaped(bf16, *shape), (tile, 2 * rows), lambda k, i, s: (i, s[slot - k]))],
        (count, 3),
        span,
        None if target is None else {2 * pieces + 1: 0},
    )


def key_sums(order, blocks, weights, span, before=()):
    rows, features = weights[0].shape
    tokens = blocks[0][0].shape[1]
    count = len(blocks)

    def kernel(s_ref, *refs):
        total = 0.0
        for x_ref, w_ref in zip(refs[:count], refs[count : 2 * count]):
            total += dot_t(x_ref[...], w_ref[...])
        refs[-1][...] = total

    return order.call(
        kernel,
        [stacked(x, k, rows) for x, k in blocks]
        + [columnwise(w, 2) for w in weights]
        + [(a, None, None) for a in before],
        [columnwise(shaped(f32, tokens, features), 2)],
        (2,),
        span,
    )


def key_last(order, total, inputs, weights, scale, dtype, before=()):
    tokens, features = total.shape
    rows = weights[0].shape[0]

    def kernel(s_ref, total_ref, x_ref, a_ref, b_ref, *rest):
        value = total_ref[...] + dot_t(x_ref[:rows], a_ref[...]) + dot_t(x_ref[rows:], b_ref[...])
        rest[-1][...] = (value * scale).astype(dtype)

    return order.call(
        kernel,
        [columnwise(total, 2), stacked(inputs, 0, 2 * rows)]
        + [columnwise(w, 2) for w in weights]
        + [(a, None, None) for a in before],
        [columnwise(shaped(dtype, tokens, features), 2)],
        (2,),
        0,
    )


def chip_delta(order, anchor, local, other):
    rows, features = local.shape

    def kernel(s_ref, anchor_ref, a_ref, b_ref, out_ref):
        anchor_rows = anchor_ref[...]
        out_ref[...] = (anchor_rows - a_ref[...]) + (anchor_rows - b_ref[...])

    def half(array):
        return (array, (rows // 6, features), lambda i, s: (3 * s[CORE] + i, 0))

    return order.call(
        kernel,
        [half(anchor), half(local), half(other)],
        [rowwise(shaped(f32, rows // 2, features), 3)],
        (3,),
    )


def total_of(order, here, there):
    def kernel(s_ref, a_ref, b_ref, out_ref):
        out_ref[...] = a_ref[...] + b_ref[...]

    return order.call(
        kernel, [rowwise(here, 3), rowwise(there, 3)], [rowwise(shaped(f32, *here.shape), 3)], (3,)
    )


def choose_sends(order, at_end, inside, beside):
    def kernel(s_ref, a_ref, b_ref, c_ref, out_ref, across_ref):
        out_ref[...] = chosen(s_ref[END], a_ref[...], b_ref[...])
        across_ref[...] = c_ref[...]

    out = rowwise(shaped(bf16, *inside.shape), 3)
    return order.call(
        kernel, [rowwise(a, 3) for a in (at_end, inside, beside)], [out, out], (3,), 0
    )


def first_handoff(order, p0, c1, p1, w_across):
    rows, features = p0.shape
    half = rows // 2

    def kernel(s_ref, p0_ref, c1_ref, p1_ref, w_ref, *out):
        total = (p0_ref[...].astype(f32) + c1_ref[...].astype(f32)).astype(bf16)
        send = chosen(s_ref[END], p1_ref[...], w_ref[...])
        for k in (0, 1):

            @pl.when(pl.program_id(0) == k)
            def _(k=k):
                out[2 * k][...] = total
                out[2 * k + 1][...] = send

    return order.call(
        kernel,
        [rowwise(a, 2) for a in (p0, c1, p1, w_across)],
        [whole(shaped(bf16, half, features))] * 4,
        (2,),
        expected["handoff"],
    )


def second_handoff(order, k, p1, c2, p2, q2, before, span):
    def kernel(s_ref, p1_ref, c2_ref, p2_ref, q2_ref, before_ref, s1_ref, t_ref):
        s1_ref[...] = (p1_ref[...].astype(f32) + c2_ref[...].astype(f32)).astype(bf16)
        t_ref[...] = (p2_ref[...] + q2_ref[...].astype(f32)).astype(bf16)

    rows, features = c2.shape
    block = (rows // 3, features)
    out = rowwise(shaped(bf16, rows, features), 3)
    return order.call(
        kernel,
        [
            (p1, block, lambda i, s: (3 * k + i, 0)),
            rowwise(c2, 3),
            (p2, block, lambda i, s: (3 * k + i, 0)),
            rowwise(q2, 3),
            (before, None, None),
        ],
        [out, out],
        (3,),
        span,
    )


def nesterov_pass(order, own, other, anchor, momentum, local):
    rows, features = local.shape

    def kernel(s_ref, own_ref, other_ref, anchor_ref, momentum_ref, local_ref, *out):
        anchor_new_ref, moment_new_ref, base_ref = out
        in_own = pl.program_id(0) // 3 == s_ref[CORE]
        outer_grad = jnp.where(in_own, own_ref[...], other_ref[...]) / 4
        anchor_new, moment_new = nesterov(outer_grad, anchor_ref[...], momentum_ref[...])
        anchor_new_ref[...] = anchor_new
        moment_new_ref[...] = moment_new
        kept = mix_weight * (1.0 - inner_rate * weight_decay)
        base_ref[...] = kept * local_ref[...] + (1.0 - mix_weight) * anchor_new

    def half(array):
        return (array, (rows // 6, features), lambda i, s: (i % 3, 0))

    out = rowwise(shaped(f32, rows, features), 6)
    return order.call(
        kernel,
        [half(own), half(other)] + [rowwise(a, 6) for a in (anchor, momentum, local)],
        [out, out, out],
        (6,),
        expected["nesterov"],
    )


def final_update(order, k, fixes, p3, qa, qb, first_old, second_old, base, made=(), keys=()):
    rows, features = base.shape
    block = (rows // 6, features)
    scale = keys[2] if keys else None

    def kernel(s_ref, fix_ref, p_ref, a_ref, b_ref, first_ref, second_ref, base_ref, *rest):
        outs = rest[len(keys[:2]) + len(made) :]
        gradient = p_ref[...] + a_ref[...].astype(f32) + b_ref[...].astype(f32)
        first_new = beta_first * first_ref[...] + (1.0 - beta_first) * gradient
        second_new = beta_second * second_ref[...] + (1.0 - beta_second) * gradient * gradient
        root = jnp.sqrt(second_new * fix_ref[1]) + epsilon
        step = (mix_weight * inner_rate) * fix_ref[0]
        outs[0][...] = base_ref[...] - step * first_new / root
        outs[1][...] = first_new
        outs[2][...] = second_new
        if keys:
            outs[3][...] = (rest[0][...] * scale + rest[1][...].astype(f32)).astype(bf16)

    def at(array, offset):
        return (array, block, lambda i, *_: (offset + i, 0))

    out = at(shaped(f32, rows, features), 3 * k)
    inputs = [at(p3, 3 * k), rowwise(qa, 3), rowwise(qb, 3)]
    inputs += [at(a, 3 * k) for a in (first_old, second_old, base)]
    inputs += [rowwise(a, 3) for a in keys[:2]]
    aliases = {2 + len(inputs) + i: i for i in range(len(made))}
    return order.call(
        kernel,
        inputs + [(a, None, None) for a in made],
        [out] * 3 + ([rowwise(shaped(bf16, *keys[0].shape), 3)] if keys else []),
        (3,),
        0 if keys else expected["first half"],
        aliases,
        fixes,
    )


def pair_pass(normed, key_grad, local, first_old, second_old, anchor, momentum, inner_step):
    width = normed.shape[1]
    rows = local.shape[0]
    scale = width ** (-0.5)
    me = lax.axis_index("fsdp")
    core = lax.axis_index("rep") % 2
    y, z = me % 2, me // 2
    inside = (z == 1) | (z == 2)
    far = jnp.where(z < 2, 3, 0)
    middle = jnp.where(z < 2, 2, 1)
    order = Order(jnp.stack([far, middle, z ^ 1, z, y, inside, ~inside, core]).astype(jnp.int32))

    def along(links):
        pairs = [(2 * a + c, 2 * b + c) for a, b in links for c in (0, 1)]
        return lambda value: lax.ppermute(value, "fsdp", pairs)

    outer = along([(0, 1), (1, 0), (2, 3), (3, 2)])
    inner = along([(1, 2), (2, 1)])

    def swap(value):
        return lax.ppermute(value, "fsdp", [(i, i ^ 1) for i in range(8)])

    def replica(value, bit):
        return lax.ppermute(value, "rep", [(i, i ^ bit) for i in range(4)])

    g_pair = swap(key_grad)
    weight = rounded(order, local)
    w_beside = outer(weight)
    w_inner = inner(weight)
    x0 = swap(first_piece(order, normed, rows))
    delta = chip_delta(order, anchor, local, replica(local, 1))
    delta_there = replica(delta, 2)
    fixes = 1.0 / jnp.stack(corrections(inner_step))
    two, three, mine = split(order, normed, rows, g_pair, fixes)
    x12 = swap(two)

    def partial(k, theirs, at, dtype, span):
        return gradient_part(order, mine, k, theirs, at, key_grad, g_pair, scale, dtype, span)

    p0 = partial(0, x0, 0, bf16, expected["first part"])
    send, across = choose_sends(order, p0, w_inner, w_beside)
    c1 = outer(send)
    w_across = inner(across)
    three, own01 = input_two(order, key_grad, g_pair, weight, w_beside, three, scale)
    x3 = swap(three)
    total = total_of(order, delta, delta_there)
    total_there = replica(total, 1)
    p1 = partial(1, x12, 0, bf16, expected["second part"])
    p2 = partial(2, x12, 1, f32, 1)
    anchor_new, moment_new, base = nesterov_pass(
        order, total, total_there, anchor, momentum, local
    )

    s0a, send_a, s0b, send_b = first_handoff(order, p0, c1, p1, w_across)
    c2a, q2a = outer(send_a), inner(s0a)
    c2b, q2b = outer(send_b), inner(s0b)
    i2, own2, w_middle = input_one(
        order, key_grad, g_pair, w_inner, 0, c1, scale, expected["input middle"]
    )
    g2 = swap(i2)
    near = (w_middle, w_beside, weight)
    own_total = key_sums(order, [(mine, 1), (mine, 2), (mine, 3)], near, expected["own sums"])
    i3, own3a, w_far_a = input_one(
        order, key_grad, g_pair, w_across, 0, c2a, scale, expected["input far"], [x3]
    )
    g3a = swap(i3)
    s1, t = second_handoff(order, 0, p1, c2a, p2, q2a, x3, expected["early sums"])
    qaa, qba = outer(t), inner(s1)
    pair_total = key_sums(
        order, [(x12, 0), (x12, 1), (x3, 0)], near, expected["pair sums"], [g2]
    )
    i3, own3b, w_far_b = input_one(
        order, key_grad, g_pair, w_across, 1, c2b, scale, expected["input far"]
    )
    g3b = swap(i3)
    w_far = (w_far_a, w_far_b)
    key_pair = swap(key_last(order, pair_total, x0, w_far, scale, bf16))
    s1, t = second_handoff(order, 1, p1, c2b, p2, q2b, g3a, expected["late sums"])
    qab, qbb = outer(t), inner(s1)
    p3 = partial(3, x3, 0, f32, 0)
    own_total = key_last(order, own_total, mine, w_far, 1.0, f32, [g3b])
    shape = normed.shape
    input_grad = input_join(order, OWN, [own01], [x3], shape, 0, None, 1)
    input_grad = input_join(order, MIDDLE, [own2], [g2], shape, expected["join middle"], input_grad)
    state = (first_old, second_old, base)
    made = final_update(order, 0, fixes, p3, qaa, qba, *state)
    input_grad = input_join(
        order, FAR, [own3a, own3b], [g3a, g3b], shape, expected["join far"], input_grad
    )
    merged, first_new, second_new, keys = final_update(
        order, 1, fixes, p3, qab, qbb, *state, made, (own_total, key_pair, scale)
    )
    return (keys, input_grad, merged, first_new, second_new, anchor_new, moment_new)


def body(normed, key_grad, master, first_moment, second_moment, anchor, momentum, inner_step):
    local = master[0]
    sizes = (lax.axis_size("rep"), lax.axis_size("fsdp"))
    inner_pass = pair_pass if sizes == (4, 8) else whole_pass
    keys, input_grad, merged, first_new, second_new, anchor_new, moment_new = inner_pass(
        normed, key_grad, local, first_moment[0], second_moment[0], anchor, momentum, inner_step
    )
    return (
        keys,
        input_grad,
        merged[None],
        first_new[None],
        second_new[None],
        anchor_new,
        moment_new,
    )


def solution(mesh):
    in_specs = (
        P(("rep", "fsdp"), None),
        P(("rep", "fsdp"), None),
        P("rep", "fsdp", None),
        P("rep", "fsdp", None),
        P("rep", "fsdp", None),
        P("fsdp", None),
        P("fsdp", None),
        P(),
    )
    out_specs = (
        P(("rep", "fsdp"), None),
        P(("rep", "fsdp"), None),
        P("rep", "fsdp", None),
        P("rep", "fsdp", None),
        P("rep", "fsdp", None),
        P("fsdp", None),
        P("fsdp", None),
    )
    return jax.shard_map(body, mesh=mesh, in_specs=in_specs, out_specs=out_specs, check_vma=False)
```

```python
import jax
import jax.numpy as jnp
from jax import lax
from jax.experimental import pallas as pl
from jax.experimental.pallas import tpu as pltpu
from jax.sharding import PartitionSpec as P

beta_first = 0.9
beta_second = 0.95
inner_rate = 0.1
weight_decay = 0.1
epsilon = 1e-08
outer_rate = 0.7
outer_mu = 0.9
mix_weight = 0.5

f32 = jnp.float32
bf16 = jnp.bfloat16
vmem_bytes = 16 * 1024 * 1024

expected = {
    "split": 30,
    "first part": 0,
    "input two": 12,
    "second part": 30,
    "nesterov": 1,
    "early own": 0,
    "early pair": 0,
    "handoff": 1,
    "input middle": 0,
    "join two": 0,
    "input far": 0,
    "early sums": 1,
    "pair sums": 0,
    "late sums": 1,
    "own sums": 0,
    "join last": 0,
    "first half": 5,
}


def corrections(inner_step):
    count_float = inner_step[0].astype(f32)
    fix_first = 1.0 - jnp.power(f32(beta_first), count_float)
    fix_second = 1.0 - jnp.power(f32(beta_second), count_float)
    return fix_first, fix_second


def adam(gradient, local, first_old, second_old, fix_first, fix_second):
    first_new = beta_first * first_old + (1.0 - beta_first) * gradient
    second_new = beta_second * second_old + (1.0 - beta_second) * gradient * gradient
    direction = first_new / fix_first / (jnp.sqrt(second_new / fix_second) + epsilon)
    stepped = local - inner_rate * (direction + weight_decay * local)
    return (stepped, first_new, second_new)


def nesterov(outer_grad, anchor_rows, moment_rows):
    moment_new = outer_mu * moment_rows + outer_grad
    anchor_new = anchor_rows - outer_rate * (outer_grad + outer_mu * moment_new)
    return (anchor_new, moment_new)


def outer_update(local, anchor, momentum):
    summed = lax.psum(anchor - local, "rep")
    return nesterov(summed / lax.axis_size("rep"), anchor, momentum)


def whole_pass(normed, key_grad, local, first_old, second_old, anchor, momentum, inner_step):
    scale = normed.shape[1] ** (-0.5)
    weight = lax.all_gather(local.astype(bf16), "fsdp", axis=0, tiled=True)
    keys = (jnp.dot(normed, weight, preferred_element_type=f32) * scale).astype(bf16)
    input_grad = (
        lax.dot_general(key_grad, weight, (((1,), (1,)), ((), ())), preferred_element_type=f32)
        * scale
    ).astype(bf16)
    gradient = lax.psum_scatter(
        lax.dot_general(normed, key_grad, (((0,), (0,)), ((), ())), preferred_element_type=f32)
        * scale,
        "fsdp",
        scatter_dimension=0,
        tiled=True,
    )
    stepped, first_new, second_new = adam(
        gradient, local, first_old, second_old, *corrections(inner_step)
    )
    anchor_new, moment_new = outer_update(local, anchor, momentum)
    merged = mix_weight * stepped + (1.0 - mix_weight) * anchor_new
    return (keys, input_grad, merged, first_new, second_new, anchor_new, moment_new)


FAR, MIDDLE, BESIDE, OWN, Y, INNER, END, CORE = range(8)


class Order:
    def __init__(self, place):
        self.place = place
        self.token = None

    def call(self, kernel, inputs, outputs, grid, span=1, aliases=None, fixes=None):
        scalars = [self.place] + ([] if fixes is None else [fixes])
        tokens = [] if self.token is None else [self.token]
        before = len(scalars) + len(inputs)

        def wrapped(*refs):
            refs[-1][...] = jnp.zeros_like(refs[-1])
            kernel(*refs[:before], *refs[before + len(tokens) : -1])

        outputs = outputs + [whole(shaped(jnp.int32, 8, 128))]
        shapes = [shape for shape, _, _ in outputs]
        keep = pl.BlockSpec(memory_space=pl.ANY)
        out = pl.pallas_call(
            wrapped,
            out_shape=shapes,
            grid_spec=pltpu.PrefetchScalarGridSpec(
                num_scalar_prefetch=len(scalars),
                grid=grid,
                in_specs=[
                    keep if block is None else pl.BlockSpec(block, index)
                    for _, block, index in inputs
                ]
                + [keep] * len(tokens),
                out_specs=[pl.BlockSpec(block, index) for _, block, index in outputs],
            ),
            input_output_aliases=aliases or {},
            compiler_params=pltpu.CompilerParams(vmem_limit_bytes=vmem_bytes),
            cost_estimate=pl.CostEstimate(
                flops=int(span * 1e9), bytes_accessed=0, transcendentals=0
            ),
        )(*scalars, *[a for a, _, _ in inputs], *tokens)
        self.token = out[-1]
        return out[0] if len(out) == 2 else out[:-1]


def shaped(dtype, *shape):
    return jax.ShapeDtypeStruct(shape, dtype)


def whole(array):
    zeros = (0,) * len(array.shape)
    return (array, array.shape, lambda *_: zeros)


def rowwise(array, steps):
    return (array, (array.shape[0] // steps, array.shape[1]), lambda i, *_: (i, 0))


def columnwise(array, steps):
    return (array, (array.shape[0], array.shape[1] // steps), lambda i, *_: (0, i))


def stacked(array, k, rows):
    return (array, (rows, array.shape[1]), lambda *_: (k, 0))


def dot_t(a, b):
    return lax.dot_general(a, b, (((0,), (0,)), ((), ())), preferred_element_type=f32)


def dot_bt(a, b):
    return lax.dot_general(a, b, (((1,), (1,)), ((), ())), preferred_element_type=f32)


def dot(a, b):
    return jnp.dot(a, b, preferred_element_type=f32)


def chosen(flag, yes, no):
    return jnp.where(flag != 0, yes, no)


def halves(x_ref, rows):
    turned = x_ref[...].T
    return turned[:rows], turned[rows:]


def rounded(order, local):
    def kernel(s_ref, a_ref, out_ref):
        out_ref[...] = a_ref[...].astype(bf16)

    return order.call(
        kernel, [rowwise(local, 3)], [rowwise(shaped(bf16, *local.shape), 3)], (3,)
    )


def first_piece(order, normed, rows):
    tokens = normed.shape[0]

    def kernel(s_ref, x_ref, piece_ref):
        low, high = halves(x_ref, rows)
        piece_ref[...] = chosen(s_ref[Y], low, high)

    return order.call(
        kernel,
        [(normed, (tokens, 2 * rows), lambda i, s: (0, s[FAR]))],
        [whole(shaped(bf16, rows, tokens))],
        (1,),
    )


def split(order, normed, rows, g_pair, fixes):
    tokens = normed.shape[0]

    def kernel(s_ref, fix_ref, x_ref, g_ref, two_ref, last_ref, own_ref):
        i = pl.program_id(0)
        low, high = halves(x_ref, rows)
        own_ref[...] = chosen(s_ref[Y], high, low)

        @pl.when(i < 2)
        def _():
            two_ref[...] = chosen(s_ref[Y], low, high)

        @pl.when(i == 2)
        def _():
            last_ref[...] = chosen(s_ref[Y], low, high)

    return order.call(
        kernel,
        [
            (normed, (tokens, 2 * rows), lambda i, s, f: (0, s[(i + 1) % 4])),
            (g_pair, None, None),
        ],
        [
            (
                shaped(bf16, 2 * rows, tokens),
                (rows, tokens),
                lambda i, s, f: (jnp.minimum(i, 1), 0),
            ),
            (shaped(bf16, 3 * rows, tokens), (rows, tokens), lambda i, s, f: (0, 0)),
            (shaped(bf16, 4 * rows, tokens), (rows, tokens), lambda i, s, f: ((i + 1) % 4, 0)),
        ],
        (4,),
        expected["split"],
        fixes=fixes,
    )


def gradient_part(order, mine, k, theirs, at, key_grad, g_pair, scale, dtype, span):
    tokens, features = key_grad.shape
    rows = mine.shape[0] // 4

    def kernel(s_ref, x_ref, xp_ref, g_ref, gp_ref, out_ref):
        total = dot(x_ref[...], g_ref[...]) + dot(xp_ref[...], gp_ref[...])
        out_ref[...] = (total * scale).astype(dtype)

    return order.call(
        kernel,
        [
            stacked(mine, k, rows),
            stacked(theirs, at, rows),
            columnwise(key_grad, 2),
            columnwise(g_pair, 2),
        ],
        [columnwise(shaped(dtype, rows, features), 2)],
        (2,),
        span,
    )


def input_two(order, key_grad, g_pair, first, second, target, scale):
    tokens, features = key_grad.shape
    rows = first.shape[0]

    def kernel(s_ref, g_ref, gp_ref, a_ref, b_ref, target_ref, pair_ref, own_ref):
        weight = jnp.where(pl.program_id(0) == 0, a_ref[...], b_ref[...])
        pair_ref[...] = (dot_bt(weight, gp_ref[...]) * scale).astype(bf16)
        own_ref[...] = (dot_bt(weight, g_ref[...]) * scale).astype(bf16)

    return order.call(
        kernel,
        [whole(a) for a in (key_grad, g_pair, first, second)] + [(target, None, None)],
        [
            (target, (rows, tokens), lambda i, s: (1 + i, 0)),
            (shaped(bf16, 2 * rows, tokens), (rows, tokens), lambda i, s: (i, 0)),
        ],
        (2,),
        expected["input two"],
        {5: 0},
    )


def input_one(order, key_grad, g_pair, inner, half, end, scale, span, before=()):
    tokens, features = key_grad.shape
    rows = end.shape[0]

    def kernel(s_ref, g_ref, gp_ref, a_ref, b_ref, *rest):
        pair_ref, own_ref, w_ref = rest[len(before) :]
        weight = chosen(s_ref[INNER], a_ref[...], b_ref[...])
        w_ref[...] = weight
        pair_ref[...] = (dot_bt(weight, gp_ref[...]) * scale).astype(bf16)
        own_ref[...] = (dot_bt(weight, g_ref[...]) * scale).astype(bf16)

    out = whole(shaped(bf16, rows, tokens))
    return order.call(
        kernel,
        [whole(key_grad), whole(g_pair), stacked(inner, half, rows), whole(end)]
        + [(a, None, None) for a in before],
        [out, out, whole(shaped(bf16, rows, features))],
        (1,),
        span,
    )


def input_join(order, slots, own, others, shape, span, target=None, before=()):
    tokens = own[0][0][0].shape[1]
    tile = tokens // 3
    rows = shape[1] // 8
    flat = [(a, k, rows // len(piece)) for piece in own + others for a, k in piece]
    kept = [a for a in (target, *before) if a is not None]

    def kernel(s_ref, *refs):
        values = iter([ref[...] for ref in refs[: len(flat)]])
        sides = [jnp.concatenate([next(values) for _ in piece], 0) for piece in own + others]
        first = pl.program_id(0) == 0
        mine = jnp.where(first, sides[0], sides[1])
        theirs = jnp.where(first, sides[2], sides[3])
        out_ref = refs[-1]

        @pl.when(s_ref[Y] == 0)
        def _():
            out_ref[...] = jnp.concatenate([mine, theirs], 0).T

        @pl.when(s_ref[Y] != 0)
        def _():
            out_ref[...] = jnp.concatenate([theirs, mine], 0).T

    def piece(array, k, height):
        return (array, (height, tile), lambda j, i, s: (k, i))

    return order.call(
        kernel,
        [piece(*p) for p in flat] + [(a, None, None) for a in kept],
        [(shaped(bf16, *shape), (tile, 2 * rows), lambda j, i, s: (i, s[slots[0] - j]))],
        (2, 3),
        span,
        None if target is None else {len(flat) + 1: 0},
    )


def key_sums(order, total, blocks, weights, span, scale=1.0, dtype=f32, before=()):
    features = weights[0].shape[1]
    tokens = blocks[0][0].shape[1]
    count = len(blocks)
    totals = [] if total is None else [columnwise(total, 2)]

    def kernel(s_ref, *refs):
        value = refs[2 * count][...] if totals else 0.0
        for x_ref, w_ref in zip(refs[:count], refs[count : 2 * count]):
            value += dot_t(x_ref[...], w_ref[...])
        refs[-1][...] = (value * scale).astype(dtype)

    return order.call(
        kernel,
        [stacked(x, k, w.shape[0]) for (x, k), w in zip(blocks, weights)]
        + [columnwise(w, 2) for w in weights]
        + totals
        + [(a, None, None) for a in before],
        [columnwise(shaped(dtype, tokens, features), 2)],
        (2,),
        span,
    )


def chip_delta(order, anchor, local, other):
    rows, features = local.shape

    def kernel(s_ref, anchor_ref, a_ref, b_ref, out_ref):
        anchor_rows = anchor_ref[...]
        out_ref[...] = (anchor_rows - a_ref[...]) + (anchor_rows - b_ref[...])

    def half(array):
        return (array, (rows // 6, features), lambda i, s: (3 * s[CORE] + i, 0))

    return order.call(
        kernel,
        [half(anchor), half(local), half(other)],
        [rowwise(shaped(f32, rows // 2, features), 3)],
        (3,),
    )


def total_of(order, here, there):
    def kernel(s_ref, a_ref, b_ref, out_ref):
        out_ref[...] = a_ref[...] + b_ref[...]

    return order.call(
        kernel, [rowwise(here, 3), rowwise(there, 3)], [rowwise(shaped(f32, *here.shape), 3)], (3,)
    )


def choose_sends(order, at_end, inside, beside):
    def kernel(s_ref, a_ref, b_ref, c_ref, out_ref, across_ref):
        out_ref[...] = chosen(s_ref[END], a_ref[...], b_ref[...])
        across_ref[...] = c_ref[...]

    out = rowwise(shaped(bf16, *inside.shape), 3)
    return order.call(
        kernel, [rowwise(a, 3) for a in (at_end, inside, beside)], [out, out], (3,), 0
    )


def first_handoff(order, p0, c1, p1, w_across):
    rows, features = p0.shape
    half = rows // 2

    def kernel(s_ref, p0_ref, c1_ref, p1_ref, w_ref, *out):
        total = (p0_ref[...].astype(f32) + c1_ref[...].astype(f32)).astype(bf16)
        send = chosen(s_ref[END], p1_ref[...], w_ref[...])
        for k in (0, 1):

            @pl.when(pl.program_id(0) == k)
            def _(k=k):
                out[2 * k][...] = total
                out[2 * k + 1][...] = send

    return order.call(
        kernel,
        [rowwise(a, 2) for a in (p0, c1, p1, w_across)],
        [whole(shaped(bf16, half, features))] * 4,
        (2,),
        expected["handoff"],
    )


def second_handoff(order, k, p1, c2, p2, q2, before, span):
    def kernel(s_ref, p1_ref, c2_ref, p2_ref, q2_ref, before_ref, s1_ref, t_ref):
        s1_ref[...] = (p1_ref[...].astype(f32) + c2_ref[...].astype(f32)).astype(bf16)
        t_ref[...] = (p2_ref[...] + q2_ref[...].astype(f32)).astype(bf16)

    rows, features = c2.shape
    block = (rows // 3, features)
    out = rowwise(shaped(bf16, rows, features), 3)
    return order.call(
        kernel,
        [
            (p1, block, lambda i, s: (3 * k + i, 0)),
            rowwise(c2, 3),
            (p2, block, lambda i, s: (3 * k + i, 0)),
            rowwise(q2, 3),
            (before, None, None),
        ],
        [out, out],
        (3,),
        span,
    )


def nesterov_pass(order, own, other, anchor, momentum, local):
    rows, features = local.shape

    def kernel(s_ref, own_ref, other_ref, anchor_ref, momentum_ref, local_ref, *out):
        anchor_new_ref, moment_new_ref, base_ref = out
        in_own = pl.program_id(0) // 3 == s_ref[CORE]
        outer_grad = jnp.where(in_own, own_ref[...], other_ref[...]) / 4
        anchor_new, moment_new = nesterov(outer_grad, anchor_ref[...], momentum_ref[...])
        anchor_new_ref[...] = anchor_new
        moment_new_ref[...] = moment_new
        kept = mix_weight * (1.0 - inner_rate * weight_decay)
        base_ref[...] = kept * local_ref[...] + (1.0 - mix_weight) * anchor_new

    def half(array):
        return (array, (rows // 6, features), lambda i, s: (i % 3, 0))

    out = rowwise(shaped(f32, rows, features), 6)
    return order.call(
        kernel,
        [half(own), half(other)] + [rowwise(a, 6) for a in (anchor, momentum, local)],
        [out, out, out],
        (6,),
        expected["nesterov"],
    )


def final_update(order, k, fixes, p3, qa, qb, first_old, second_old, base, made=(), keys=()):
    rows, features = base.shape
    block = (rows // 6, features)
    scale = keys[2] if keys else None

    def kernel(s_ref, fix_ref, p_ref, a_ref, b_ref, first_ref, second_ref, base_ref, *rest):
        outs = rest[len(keys[:2]) + len(made) :]
        gradient = p_ref[...] + a_ref[...].astype(f32) + b_ref[...].astype(f32)
        first_new = beta_first * first_ref[...] + (1.0 - beta_first) * gradient
        second_new = beta_second * second_ref[...] + (1.0 - beta_second) * gradient * gradient
        root = jnp.sqrt(second_new * fix_ref[1]) + epsilon
        step = (mix_weight * inner_rate) * fix_ref[0]
        outs[0][...] = base_ref[...] - step * first_new / root
        outs[1][...] = first_new
        outs[2][...] = second_new
        if keys:
            outs[3][...] = (rest[0][...] * scale + rest[1][...].astype(f32)).astype(bf16)

    def at(array, offset):
        return (array, block, lambda i, *_: (offset + i, 0))

    out = at(shaped(f32, rows, features), 3 * k)
    inputs = [at(p3, 3 * k), rowwise(qa, 3), rowwise(qb, 3)]
    inputs += [at(a, 3 * k) for a in (first_old, second_old, base)]
    inputs += [rowwise(a, 3) for a in keys[:2]]
    aliases = {2 + len(inputs) + i: i for i in range(len(made))}
    return order.call(
        kernel,
        inputs + [(a, None, None) for a in made],
        [out] * 3 + ([rowwise(shaped(bf16, *keys[0].shape), 3)] if keys else []),
        (3,),
        0 if keys else expected["first half"],
        aliases,
        fixes,
    )


def pair_pass(normed, key_grad, local, first_old, second_old, anchor, momentum, inner_step):
    width = normed.shape[1]
    rows = local.shape[0]
    scale = width ** (-0.5)
    me = lax.axis_index("fsdp")
    core = lax.axis_index("rep") % 2
    y, z = me % 2, me // 2
    inside = (z == 1) | (z == 2)
    far = jnp.where(z < 2, 3, 0)
    middle = jnp.where(z < 2, 2, 1)
    order = Order(jnp.stack([far, middle, z ^ 1, z, y, inside, ~inside, core]).astype(jnp.int32))

    def along(links):
        pairs = [(2 * a + c, 2 * b + c) for a, b in links for c in (0, 1)]
        return lambda value: lax.ppermute(value, "fsdp", pairs)

    outer = along([(0, 1), (1, 0), (2, 3), (3, 2)])
    inner = along([(1, 2), (2, 1)])

    def swap(value):
        return lax.ppermute(value, "fsdp", [(i, i ^ 1) for i in range(8)])

    def replica(value, bit):
        return lax.ppermute(value, "rep", [(i, i ^ bit) for i in range(4)])

    g_pair = swap(key_grad)
    weight = rounded(order, local)
    w_beside = outer(weight)
    w_inner = inner(weight)
    x0 = swap(first_piece(order, normed, rows))
    delta = chip_delta(order, anchor, local, replica(local, 1))
    delta_there = replica(delta, 2)
    fixes = 1.0 / jnp.stack(corrections(inner_step))
    two, three, mine = split(order, normed, rows, g_pair, fixes)
    x12 = swap(two)

    def partial(k, theirs, at, dtype, span):
        return gradient_part(order, mine, k, theirs, at, key_grad, g_pair, scale, dtype, span)

    p0 = partial(0, x0, 0, bf16, expected["first part"])
    send, across = choose_sends(order, p0, w_inner, w_beside)
    c1 = outer(send)
    w_across = inner(across)
    three, own01 = input_two(order, key_grad, g_pair, weight, w_beside, three, scale)
    x3 = swap(three)
    total = total_of(order, delta, delta_there)
    total_there = replica(total, 1)
    p1 = partial(1, x12, 0, bf16, expected["second part"])
    p2 = partial(2, x12, 1, f32, 1)
    anchor_new, moment_new, base = nesterov_pass(
        order, total, total_there, anchor, momentum, local
    )
    known = (w_beside, weight)
    own_total = key_sums(order, None, [(mine, 2), (mine, 3)], known, expected["early own"])
    pair_total = key_sums(order, None, [(x12, 1)], known[:1], expected["early pair"])

    s0a, send_a, s0b, send_b = first_handoff(order, p0, c1, p1, w_across)
    c2a, q2a = outer(send_a), inner(s0a)
    c2b, q2b = outer(send_b), inner(s0b)
    i2, own2, w_middle = input_one(
        order, key_grad, g_pair, w_inner, 0, c1, scale, expected["input middle"]
    )
    g2 = swap(i2)
    input_grad = input_join(
        order,
        (OWN, BESIDE),
        [[(own01, 0)], [(own01, 1)]],
        [[(x3, 1)], [(x3, 2)]],
        normed.shape,
        expected["join two"],
    )
    i3, own3a, w_far_a = input_one(
        order, key_grad, g_pair, w_across, 0, c2a, scale, expected["input far"], [x3]
    )
    g3a = swap(i3)
    s1, t = second_handoff(order, 0, p1, c2a, p2, q2a, x3, expected["early sums"])
    qaa, qba = outer(t), inner(s1)
    pair_total = key_sums(
        order,
        pair_total,
        [(x12, 0), (x3, 0)],
        (w_middle, weight),
        expected["pair sums"],
        before=[g2],
    )
    i3, own3b, w_far_b = input_one(
        order, key_grad, g_pair, w_across, 1, c2b, scale, expected["input far"]
    )
    g3b = swap(i3)
    w_far = (w_far_a, w_far_b)
    key_pair = swap(key_sums(order, pair_total, [(x0, 0), (x0, 1)], w_far, 0, scale, bf16))
    s1, t = second_handoff(order, 1, p1, c2b, p2, q2b, g3a, expected["late sums"])
    qab, qbb = outer(t), inner(s1)
    own_total = key_sums(
        order,
        own_total,
        [(mine, 1), (mine, 0), (mine, 1)],
        (w_middle, *w_far),
        expected["own sums"],
        before=[g3b],
    )
    p3 = partial(3, x3, 0, f32, 0)
    input_grad = input_join(
        order,
        (MIDDLE, FAR),
        [[(own2, 0)], [(own3a, 0), (own3b, 0)]],
        [[(g2, 0)], [(g3a, 0), (g3b, 0)]],
        normed.shape,
        expected["join last"],
        input_grad,
    )
    state = (first_old, second_old, base)
    made = final_update(order, 0, fixes, p3, qaa, qba, *state)
    merged, first_new, second_new, keys = final_update(
        order, 1, fixes, p3, qab, qbb, *state, made, (own_total, key_pair, scale)
    )
    return (keys, input_grad, merged, first_new, second_new, anchor_new, moment_new)


def body(normed, key_grad, master, first_moment, second_moment, anchor, momentum, inner_step):
    local = master[0]
    sizes = (lax.axis_size("rep"), lax.axis_size("fsdp"))
    inner_pass = pair_pass if sizes == (4, 8) else whole_pass
    keys, input_grad, merged, first_new, second_new, anchor_new, moment_new = inner_pass(
        normed, key_grad, local, first_moment[0], second_moment[0], anchor, momentum, inner_step
    )
    return (
        keys,
        input_grad,
        merged[None],
        first_new[None],
        second_new[None],
        anchor_new,
        moment_new,
    )


def solution(mesh):
    in_specs = (
        P(("rep", "fsdp"), None),
        P(("rep", "fsdp"), None),
        P("rep", "fsdp", None),
        P("rep", "fsdp", None),
        P("rep", "fsdp", None),
        P("fsdp", None),
        P("fsdp", None),
        P(),
    )
    out_specs = (
        P(("rep", "fsdp"), None),
        P(("rep", "fsdp"), None),
        P("rep", "fsdp", None),
        P("rep", "fsdp", None),
        P("rep", "fsdp", None),
        P("fsdp", None),
        P("fsdp", None),
    )
    return jax.shard_map(body, mesh=mesh, in_specs=in_specs, out_specs=out_specs, check_vma=False)
```

```python
import jax
import jax.numpy as jnp
from jax import lax
from jax.experimental import pallas as pl
from jax.experimental.pallas import tpu as pltpu
from jax.sharding import PartitionSpec as P

beta_first = 0.9
beta_second = 0.95
inner_rate = 0.1
weight_decay = 0.1
epsilon = 1e-08
outer_rate = 0.7
outer_mu = 0.9
mix_weight = 0.5

f32 = jnp.float32
bf16 = jnp.bfloat16
expected = {
    "split": 30,
    "first part": 0,
    "input two": 12,
    "second part": 30,
    "nesterov": 1,
    "early own": 0,
    "early pair": 0,
    "handoff": 1,
    "input middle": 0,
    "join two": 0,
    "input far": 0,
    "early sums": 1,
    "pair sums": 0,
    "late sums": 1,
    "own sums": 0,
    "join last": 0,
    "first half": 5,
}


def corrections(inner_step):
    count_float = inner_step[0].astype(f32)
    fix_first = 1.0 - jnp.power(f32(beta_first), count_float)
    fix_second = 1.0 - jnp.power(f32(beta_second), count_float)
    return fix_first, fix_second


def adam(gradient, local, first_old, second_old, fix_first, fix_second):
    first_new = beta_first * first_old + (1.0 - beta_first) * gradient
    second_new = beta_second * second_old + (1.0 - beta_second) * gradient * gradient
    direction = first_new / fix_first / (jnp.sqrt(second_new / fix_second) + epsilon)
    stepped = local - inner_rate * (direction + weight_decay * local)
    return (stepped, first_new, second_new)


def nesterov(outer_grad, anchor_rows, moment_rows):
    moment_new = outer_mu * moment_rows + outer_grad
    anchor_new = anchor_rows - outer_rate * (outer_grad + outer_mu * moment_new)
    return (anchor_new, moment_new)


def outer_update(local, anchor, momentum):
    summed = lax.psum(anchor - local, "rep")
    return nesterov(summed / lax.axis_size("rep"), anchor, momentum)


def whole_pass(normed, key_grad, local, first_old, second_old, anchor, momentum, inner_step):
    scale = normed.shape[1] ** (-0.5)
    weight = lax.all_gather(local.astype(bf16), "fsdp", axis=0, tiled=True)
    keys = (jnp.dot(normed, weight, preferred_element_type=f32) * scale).astype(bf16)
    input_grad = (
        lax.dot_general(key_grad, weight, (((1,), (1,)), ((), ())), preferred_element_type=f32)
        * scale
    ).astype(bf16)
    gradient = lax.psum_scatter(
        lax.dot_general(normed, key_grad, (((0,), (0,)), ((), ())), preferred_element_type=f32)
        * scale,
        "fsdp",
        scatter_dimension=0,
        tiled=True,
    )
    stepped, first_new, second_new = adam(
        gradient, local, first_old, second_old, *corrections(inner_step)
    )
    anchor_new, moment_new = outer_update(local, anchor, momentum)
    merged = mix_weight * stepped + (1.0 - mix_weight) * anchor_new
    return (keys, input_grad, merged, first_new, second_new, anchor_new, moment_new)


FAR, MIDDLE, BESIDE, OWN, Y, INNER, END, CORE = range(8)


class Order:
    def __init__(self, place):
        self.place = place
        self.token = None

    def call(self, kernel, inputs, outputs, grid, span=1, aliases=None, fixes=None, room=16):
        scalars = [self.place] + ([] if fixes is None else [fixes])
        tokens = [] if self.token is None else [self.token]
        before = len(scalars) + len(inputs)

        def wrapped(*refs):
            refs[-1][...] = jnp.zeros_like(refs[-1])
            kernel(*refs[:before], *refs[before + len(tokens) : -1])

        outputs = outputs + [whole(shaped(jnp.int32, 8, 128))]
        shapes = [shape for shape, _, _ in outputs]
        keep = pl.BlockSpec(memory_space=pl.ANY)
        out = pl.pallas_call(
            wrapped,
            out_shape=shapes,
            grid_spec=pltpu.PrefetchScalarGridSpec(
                num_scalar_prefetch=len(scalars),
                grid=grid,
                in_specs=[
                    keep if block is None else pl.BlockSpec(block, index)
                    for _, block, index in inputs
                ]
                + [keep] * len(tokens),
                out_specs=[pl.BlockSpec(block, index) for _, block, index in outputs],
            ),
            input_output_aliases=aliases or {},
            compiler_params=pltpu.CompilerParams(vmem_limit_bytes=room * 1024 * 1024),
            cost_estimate=pl.CostEstimate(
                flops=int(span * 1e9), bytes_accessed=0, transcendentals=0
            ),
        )(*scalars, *[a for a, _, _ in inputs], *tokens)
        self.token = out[-1]
        return out[0] if len(out) == 2 else out[:-1]


def shaped(dtype, *shape):
    return jax.ShapeDtypeStruct(shape, dtype)


def whole(array):
    zeros = (0,) * len(array.shape)
    return (array, array.shape, lambda *_: zeros)


def rowwise(array, steps):
    return (array, (array.shape[0] // steps, array.shape[1]), lambda i, *_: (i, 0))


def columnwise(array, steps):
    return (array, (array.shape[0], array.shape[1] // steps), lambda i, *_: (0, i))


def stacked(array, k, rows):
    return (array, (rows, array.shape[1]), lambda *_: (k, 0))


def dot_t(a, b):
    return lax.dot_general(a, b, (((0,), (0,)), ((), ())), preferred_element_type=f32)


def dot_bt(a, b):
    return lax.dot_general(a, b, (((1,), (1,)), ((), ())), preferred_element_type=f32)


def dot(a, b):
    return jnp.dot(a, b, preferred_element_type=f32)


def chosen(flag, yes, no):
    return jnp.where(flag != 0, yes, no)


def halves(x_ref, rows):
    turned = x_ref[...].T
    return turned[:rows], turned[rows:]


def rounded(order, local):
    def kernel(s_ref, a_ref, out_ref):
        out_ref[...] = a_ref[...].astype(bf16)

    return order.call(
        kernel, [rowwise(local, 3)], [rowwise(shaped(bf16, *local.shape), 3)], (3,), room=62
    )


def first_piece(order, normed, rows):
    tokens = normed.shape[0]

    def kernel(s_ref, x_ref, piece_ref):
        low, high = halves(x_ref, rows)
        piece_ref[...] = chosen(s_ref[Y], low, high)

    return order.call(
        kernel,
        [(normed, (tokens, 2 * rows), lambda i, s: (0, s[FAR]))],
        [whole(shaped(bf16, rows, tokens))],
        (1,),
    )


def split(order, normed, rows, g_pair, fixes):
    tokens = normed.shape[0]

    def kernel(s_ref, fix_ref, x_ref, g_ref, two_ref, last_ref, own_ref):
        i = pl.program_id(0)
        low, high = halves(x_ref, rows)
        own_ref[...] = chosen(s_ref[Y], high, low)

        @pl.when(i < 2)
        def _():
            two_ref[...] = chosen(s_ref[Y], low, high)

        @pl.when(i == 2)
        def _():
            last_ref[...] = chosen(s_ref[Y], low, high)

    return order.call(
        kernel,
        [
            (normed, (tokens, 2 * rows), lambda i, s, f: (0, s[(i + 1) % 4])),
            (g_pair, None, None),
        ],
        [
            (
                shaped(bf16, 2 * rows, tokens),
                (rows, tokens),
                lambda i, s, f: (jnp.minimum(i, 1), 0),
            ),
            (shaped(bf16, 3 * rows, tokens), (rows, tokens), lambda i, s, f: (0, 0)),
            (shaped(bf16, 4 * rows, tokens), (rows, tokens), lambda i, s, f: ((i + 1) % 4, 0)),
        ],
        (4,),
        expected["split"],
        fixes=fixes,
    )


def gradient_part(order, mine, k, theirs, at, key_grad, g_pair, scale, dtype, span):
    tokens, features = key_grad.shape
    rows = mine.shape[0] // 4

    def kernel(s_ref, x_ref, xp_ref, g_ref, gp_ref, out_ref):
        total = dot(x_ref[...], g_ref[...]) + dot(xp_ref[...], gp_ref[...])
        out_ref[...] = (total * scale).astype(dtype)

    return order.call(
        kernel,
        [
            stacked(mine, k, rows),
            stacked(theirs, at, rows),
            columnwise(key_grad, 2),
            columnwise(g_pair, 2),
        ],
        [columnwise(shaped(dtype, rows, features), 2)],
        (2,),
        span,
    )


def input_two(order, key_grad, g_pair, first, second, target, scale):
    tokens, features = key_grad.shape
    rows = first.shape[0]

    def kernel(s_ref, g_ref, gp_ref, a_ref, b_ref, target_ref, pair_ref, own_ref):
        weight = jnp.where(pl.program_id(0) == 0, a_ref[...], b_ref[...])
        pair_ref[...] = (dot_bt(weight, gp_ref[...]) * scale).astype(bf16)
        own_ref[...] = (dot_bt(weight, g_ref[...]) * scale).astype(bf16)

    return order.call(
        kernel,
        [whole(a) for a in (key_grad, g_pair, first, second)] + [(target, None, None)],
        [
            (target, (rows, tokens), lambda i, s: (1 + i, 0)),
            (shaped(bf16, 2 * rows, tokens), (rows, tokens), lambda i, s: (i, 0)),
        ],
        (2,),
        expected["input two"],
        {5: 0},
    )


def input_one(order, key_grad, g_pair, inner, half, end, scale, span, before=()):
    tokens, features = key_grad.shape
    rows = end.shape[0]

    def kernel(s_ref, g_ref, gp_ref, a_ref, b_ref, *rest):
        pair_ref, own_ref, w_ref = rest[len(before) :]
        weight = chosen(s_ref[INNER], a_ref[...], b_ref[...])
        w_ref[...] = weight
        pair_ref[...] = (dot_bt(weight, gp_ref[...]) * scale).astype(bf16)
        own_ref[...] = (dot_bt(weight, g_ref[...]) * scale).astype(bf16)

    out = whole(shaped(bf16, rows, tokens))
    return order.call(
        kernel,
        [whole(key_grad), whole(g_pair), stacked(inner, half, rows), whole(end)]
        + [(a, None, None) for a in before],
        [out, out, whole(shaped(bf16, rows, features))],
        (1,),
        span,
    )


def input_join(order, slots, own, others, shape, span, target=None, before=()):
    tokens = own[0][0][0].shape[1]
    tile = tokens // 3
    rows = shape[1] // 8
    flat = [(a, k, rows // len(piece)) for piece in own + others for a, k in piece]
    kept = [a for a in (target, *before) if a is not None]

    def kernel(s_ref, *refs):
        values = iter([ref[...] for ref in refs[: len(flat)]])
        sides = [jnp.concatenate([next(values) for _ in piece], 0) for piece in own + others]
        first = pl.program_id(0) == 0
        mine = jnp.where(first, sides[0], sides[1])
        theirs = jnp.where(first, sides[2], sides[3])
        out_ref = refs[-1]

        @pl.when(s_ref[Y] == 0)
        def _():
            out_ref[...] = jnp.concatenate([mine, theirs], 0).T

        @pl.when(s_ref[Y] != 0)
        def _():
            out_ref[...] = jnp.concatenate([theirs, mine], 0).T

    def piece(array, k, height):
        return (array, (height, tile), lambda j, i, s: (k, i))

    return order.call(
        kernel,
        [piece(*p) for p in flat] + [(a, None, None) for a in kept],
        [(shaped(bf16, *shape), (tile, 2 * rows), lambda j, i, s: (i, s[slots[0] - j]))],
        (2, 3),
        span,
        None if target is None else {len(flat) + 1: 0},
    )


def key_sums(order, total, blocks, weights, span, scale=1.0, dtype=f32, before=()):
    features = weights[0].shape[1]
    tokens = blocks[0][0].shape[1]
    count = len(blocks)
    totals = [] if total is None else [columnwise(total, 2)]

    def kernel(s_ref, *refs):
        value = refs[2 * count][...] if totals else 0.0
        for x_ref, w_ref in zip(refs[:count], refs[count : 2 * count]):
            value += dot_t(x_ref[...], w_ref[...])
        refs[-1][...] = (value * scale).astype(dtype)

    return order.call(
        kernel,
        [stacked(x, k, w.shape[0]) for (x, k), w in zip(blocks, weights)]
        + [columnwise(w, 2) for w in weights]
        + totals
        + [(a, None, None) for a in before],
        [columnwise(shaped(dtype, tokens, features), 2)],
        (2,),
        span,
    )


def chip_delta(order, anchor, local, other):
    rows, features = local.shape

    def kernel(s_ref, anchor_ref, a_ref, b_ref, out_ref):
        anchor_rows = anchor_ref[...]
        out_ref[...] = (anchor_rows - a_ref[...]) + (anchor_rows - b_ref[...])

    def half(array):
        return (array, (rows // 6, features), lambda i, s: (3 * s[CORE] + i, 0))

    return order.call(
        kernel,
        [half(anchor), half(local), half(other)],
        [rowwise(shaped(f32, rows // 2, features), 3)],
        (3,),
    )


def total_of(order, here, there):
    def kernel(s_ref, a_ref, b_ref, out_ref):
        out_ref[...] = a_ref[...] + b_ref[...]

    return order.call(
        kernel, [rowwise(here, 3), rowwise(there, 3)], [rowwise(shaped(f32, *here.shape), 3)], (3,)
    )


def choose_sends(order, at_end, inside, beside):
    def kernel(s_ref, a_ref, b_ref, c_ref, out_ref, across_ref):
        out_ref[...] = chosen(s_ref[END], a_ref[...], b_ref[...])
        across_ref[...] = c_ref[...]

    out = rowwise(shaped(bf16, *inside.shape), 3)
    return order.call(
        kernel, [rowwise(a, 3) for a in (at_end, inside, beside)], [out, out], (3,), 0
    )


def first_handoff(order, p0, c1, p1, w_across):
    rows, features = p0.shape
    half = rows // 2

    def kernel(s_ref, p0_ref, c1_ref, p1_ref, w_ref, *out):
        total = (p0_ref[...].astype(f32) + c1_ref[...].astype(f32)).astype(bf16)
        send = chosen(s_ref[END], p1_ref[...], w_ref[...])
        for k in (0, 1):

            @pl.when(pl.program_id(0) == k)
            def _(k=k):
                out[2 * k][...] = total
                out[2 * k + 1][...] = send

    return order.call(
        kernel,
        [rowwise(a, 2) for a in (p0, c1, p1, w_across)],
        [whole(shaped(bf16, half, features))] * 4,
        (2,),
        expected["handoff"],
    )


def second_handoff(order, k, p1, c2, p2, q2, before, span):
    def kernel(s_ref, p1_ref, c2_ref, p2_ref, q2_ref, before_ref, s1_ref, t_ref):
        s1_ref[...] = (p1_ref[...].astype(f32) + c2_ref[...].astype(f32)).astype(bf16)
        t_ref[...] = (p2_ref[...] + q2_ref[...].astype(f32)).astype(bf16)

    rows, features = c2.shape
    block = (rows // 3, features)
    out = rowwise(shaped(bf16, rows, features), 3)
    return order.call(
        kernel,
        [
            (p1, block, lambda i, s: (3 * k + i, 0)),
            rowwise(c2, 3),
            (p2, block, lambda i, s: (3 * k + i, 0)),
            rowwise(q2, 3),
            (before, None, None),
        ],
        [out, out],
        (3,),
        span,
    )


def nesterov_pass(order, own, other, anchor, momentum, local):
    rows, features = local.shape

    def kernel(s_ref, own_ref, other_ref, anchor_ref, momentum_ref, local_ref, *out):
        anchor_new_ref, moment_new_ref, base_ref = out
        in_own = pl.program_id(0) // 3 == s_ref[CORE]
        outer_grad = jnp.where(in_own, own_ref[...], other_ref[...]) / 4
        anchor_new, moment_new = nesterov(outer_grad, anchor_ref[...], momentum_ref[...])
        anchor_new_ref[...] = anchor_new
        moment_new_ref[...] = moment_new
        kept = mix_weight * (1.0 - inner_rate * weight_decay)
        base_ref[...] = kept * local_ref[...] + (1.0 - mix_weight) * anchor_new

    def half(array):
        return (array, (rows // 6, features), lambda i, s: (i % 3, 0))

    out = rowwise(shaped(f32, rows, features), 6)
    return order.call(
        kernel,
        [half(own), half(other)] + [rowwise(a, 6) for a in (anchor, momentum, local)],
        [out, out, out],
        (6,),
        expected["nesterov"],
    )


def final_update(order, k, fixes, p3, qa, qb, first_old, second_old, base, made=(), keys=()):
    rows, features = base.shape
    block = (rows // 6, features)
    scale = keys[2] if keys else None

    def kernel(s_ref, fix_ref, p_ref, a_ref, b_ref, first_ref, second_ref, base_ref, *rest):
        outs = rest[len(keys[:2]) + len(made) :]
        gradient = p_ref[...] + a_ref[...].astype(f32) + b_ref[...].astype(f32)
        first_new = beta_first * first_ref[...] + (1.0 - beta_first) * gradient
        second_new = beta_second * second_ref[...] + (1.0 - beta_second) * gradient * gradient
        root = jnp.sqrt(second_new * fix_ref[1]) + epsilon
        step = (mix_weight * inner_rate) * fix_ref[0]
        outs[0][...] = base_ref[...] - step * first_new / root
        outs[1][...] = first_new
        outs[2][...] = second_new
        if keys:
            outs[3][...] = (rest[0][...] * scale + rest[1][...].astype(f32)).astype(bf16)

    def at(array, offset):
        return (array, block, lambda i, *_: (offset + i, 0))

    out = at(shaped(f32, rows, features), 3 * k)
    inputs = [at(p3, 3 * k), rowwise(qa, 3), rowwise(qb, 3)]
    inputs += [at(a, 3 * k) for a in (first_old, second_old, base)]
    inputs += [rowwise(a, 3) for a in keys[:2]]
    aliases = {2 + len(inputs) + i: i for i in range(len(made))}
    return order.call(
        kernel,
        inputs + [(a, None, None) for a in made],
        [out] * 3 + ([rowwise(shaped(bf16, *keys[0].shape), 3)] if keys else []),
        (3,),
        0 if keys else expected["first half"],
        aliases,
        fixes,
    )


def pair_pass(normed, key_grad, local, first_old, second_old, anchor, momentum, inner_step):
    width = normed.shape[1]
    rows = local.shape[0]
    scale = width ** (-0.5)
    me = lax.axis_index("fsdp")
    core = lax.axis_index("rep") % 2
    y, z = me % 2, me // 2
    inside = (z == 1) | (z == 2)
    far = jnp.where(z < 2, 3, 0)
    middle = jnp.where(z < 2, 2, 1)
    order = Order(jnp.stack([far, middle, z ^ 1, z, y, inside, ~inside, core]).astype(jnp.int32))

    def along(links):
        pairs = [(2 * a + c, 2 * b + c) for a, b in links for c in (0, 1)]
        return lambda value: lax.ppermute(value, "fsdp", pairs)

    outer = along([(0, 1), (1, 0), (2, 3), (3, 2)])
    inner = along([(1, 2), (2, 1)])

    def swap(value):
        return lax.ppermute(value, "fsdp", [(i, i ^ 1) for i in range(8)])

    def replica(value, bit):
        return lax.ppermute(value, "rep", [(i, i ^ bit) for i in range(4)])

    g_pair = swap(key_grad)
    weight = rounded(order, local)
    w_beside = outer(weight)
    w_inner = inner(weight)
    x0 = swap(first_piece(order, normed, rows))
    delta = chip_delta(order, anchor, local, replica(local, 1))
    delta_there = replica(delta, 2)
    fixes = 1.0 / jnp.stack(corrections(inner_step))
    two, three, mine = split(order, normed, rows, g_pair, fixes)
    x12 = swap(two)

    def partial(k, theirs, at, dtype, span):
        return gradient_part(order, mine, k, theirs, at, key_grad, g_pair, scale, dtype, span)

    p0 = partial(0, x0, 0, bf16, expected["first part"])
    send, across = choose_sends(order, p0, w_inner, w_beside)
    c1 = outer(send)
    w_across = inner(across)
    three, own01 = input_two(order, key_grad, g_pair, weight, w_beside, three, scale)
    x3 = swap(three)
    total = total_of(order, delta, delta_there)
    total_there = replica(total, 1)
    p1 = partial(1, x12, 0, bf16, expected["second part"])
    p2 = partial(2, x12, 1, f32, 1)
    anchor_new, moment_new, base = nesterov_pass(
        order, total, total_there, anchor, momentum, local
    )
    known = (w_beside, weight)
    own_total = key_sums(order, None, [(mine, 2), (mine, 3)], known, expected["early own"])
    pair_total = key_sums(order, None, [(x12, 1)], known[:1], expected["early pair"])

    s0a, send_a, s0b, send_b = first_handoff(order, p0, c1, p1, w_across)
    c2a, q2a = outer(send_a), inner(s0a)
    c2b, q2b = outer(send_b), inner(s0b)
    i2, own2, w_middle = input_one(
        order, key_grad, g_pair, w_inner, 0, c1, scale, expected["input middle"]
    )
    g2 = swap(i2)
    input_grad = input_join(
        order,
        (OWN, BESIDE),
        [[(own01, 0)], [(own01, 1)]],
        [[(x3, 1)], [(x3, 2)]],
        normed.shape,
        expected["join two"],
    )
    i3, own3a, w_far_a = input_one(
        order, key_grad, g_pair, w_across, 0, c2a, scale, expected["input far"], [x3]
    )
    g3a = swap(i3)
    s1, t = second_handoff(order, 0, p1, c2a, p2, q2a, x3, expected["early sums"])
    qaa, qba = outer(t), inner(s1)
    pair_total = key_sums(
        order,
        pair_total,
        [(x12, 0), (x3, 0)],
        (w_middle, weight),
        expected["pair sums"],
        before=[g2],
    )
    i3, own3b, w_far_b = input_one(
        order, key_grad, g_pair, w_across, 1, c2b, scale, expected["input far"]
    )
    g3b = swap(i3)
    w_far = (w_far_a, w_far_b)
    key_pair = swap(key_sums(order, pair_total, [(x0, 0), (x0, 1)], w_far, 0, scale, bf16))
    s1, t = second_handoff(order, 1, p1, c2b, p2, q2b, g3a, expected["late sums"])
    qab, qbb = outer(t), inner(s1)
    own_total = key_sums(
        order,
        own_total,
        [(mine, 1), (mine, 0), (mine, 1)],
        (w_middle, *w_far),
        expected["own sums"],
        before=[g3b],
    )
    p3 = partial(3, x3, 0, f32, 0)
    input_grad = input_join(
        order,
        (MIDDLE, FAR),
        [[(own2, 0)], [(own3a, 0), (own3b, 0)]],
        [[(g2, 0)], [(g3a, 0), (g3b, 0)]],
        normed.shape,
        expected["join last"],
        input_grad,
    )
    state = (first_old, second_old, base)
    made = final_update(order, 0, fixes, p3, qaa, qba, *state)
    merged, first_new, second_new, keys = final_update(
        order, 1, fixes, p3, qab, qbb, *state, made, (own_total, key_pair, scale)
    )
    return (keys, input_grad, merged, first_new, second_new, anchor_new, moment_new)


def body(normed, key_grad, master, first_moment, second_moment, anchor, momentum, inner_step):
    local = master[0]
    sizes = (lax.axis_size("rep"), lax.axis_size("fsdp"))
    inner_pass = pair_pass if sizes == (4, 8) else whole_pass
    keys, input_grad, merged, first_new, second_new, anchor_new, moment_new = inner_pass(
        normed, key_grad, local, first_moment[0], second_moment[0], anchor, momentum, inner_step
    )
    return (
        keys,
        input_grad,
        merged[None],
        first_new[None],
        second_new[None],
        anchor_new,
        moment_new,
    )


def solution(mesh):
    in_specs = (
        P(("rep", "fsdp"), None),
        P(("rep", "fsdp"), None),
        P("rep", "fsdp", None),
        P("rep", "fsdp", None),
        P("rep", "fsdp", None),
        P("fsdp", None),
        P("fsdp", None),
        P(),
    )
    out_specs = (
        P(("rep", "fsdp"), None),
        P(("rep", "fsdp"), None),
        P("rep", "fsdp", None),
        P("rep", "fsdp", None),
        P("rep", "fsdp", None),
        P("fsdp", None),
        P("fsdp", None),
    )
    return jax.shard_map(body, mesh=mesh, in_specs=in_specs, out_specs=out_specs, check_vma=False)
```

```python
import jax
import jax.numpy as jnp
from jax import lax
from jax.experimental import pallas as pl
from jax.experimental.pallas import tpu as pltpu
from jax.sharding import PartitionSpec as P

beta_first = 0.9
beta_second = 0.95
inner_rate = 0.1
weight_decay = 0.1
epsilon = 1e-08
outer_rate = 0.7
outer_mu = 0.9
mix_weight = 0.5

f32 = jnp.float32
bf16 = jnp.bfloat16
vmem_bytes = 16 * 1024 * 1024

expected = {
    "split": 30,
    "first part": 0,
    "input two": 12,
    "second part": 30,
    "nesterov": 1,
    "early own": 0,
    "early pair": 0,
    "handoff": 1,
    "input middle": 0,
    "join two": 0,
    "input far": 0,
    "early sums": 1,
    "pair sums": 0,
    "late sums": 1,
    "own sums": 0,
    "join last": 0,
    "first half": 5,
}


def corrections(inner_step):
    count_float = inner_step[0].astype(f32)
    fix_first = 1.0 - jnp.power(f32(beta_first), count_float)
    fix_second = 1.0 - jnp.power(f32(beta_second), count_float)
    return fix_first, fix_second


def adam(gradient, local, first_old, second_old, fix_first, fix_second):
    first_new = beta_first * first_old + (1.0 - beta_first) * gradient
    second_new = beta_second * second_old + (1.0 - beta_second) * gradient * gradient
    direction = first_new / fix_first / (jnp.sqrt(second_new / fix_second) + epsilon)
    stepped = local - inner_rate * (direction + weight_decay * local)
    return (stepped, first_new, second_new)


def nesterov(outer_grad, anchor_rows, moment_rows):
    moment_new = outer_mu * moment_rows + outer_grad
    anchor_new = anchor_rows - outer_rate * (outer_grad + outer_mu * moment_new)
    return (anchor_new, moment_new)


def outer_update(local, anchor, momentum):
    summed = lax.psum(anchor - local, "rep")
    return nesterov(summed / lax.axis_size("rep"), anchor, momentum)


def whole_pass(normed, key_grad, local, first_old, second_old, anchor, momentum, inner_step):
    scale = normed.shape[1] ** (-0.5)
    weight = lax.all_gather(local.astype(bf16), "fsdp", axis=0, tiled=True)
    keys = (jnp.dot(normed, weight, preferred_element_type=f32) * scale).astype(bf16)
    input_grad = (
        lax.dot_general(key_grad, weight, (((1,), (1,)), ((), ())), preferred_element_type=f32)
        * scale
    ).astype(bf16)
    gradient = lax.psum_scatter(
        lax.dot_general(normed, key_grad, (((0,), (0,)), ((), ())), preferred_element_type=f32)
        * scale,
        "fsdp",
        scatter_dimension=0,
        tiled=True,
    )
    stepped, first_new, second_new = adam(
        gradient, local, first_old, second_old, *corrections(inner_step)
    )
    anchor_new, moment_new = outer_update(local, anchor, momentum)
    merged = mix_weight * stepped + (1.0 - mix_weight) * anchor_new
    return (keys, input_grad, merged, first_new, second_new, anchor_new, moment_new)


FAR, MIDDLE, BESIDE, OWN, Y, INNER, END, CORE = range(8)


class Order:
    def __init__(self, place):
        self.place = place
        self.token = None

    def call(self, kernel, inputs, outputs, grid, span=1, aliases=None, fixes=None):
        scalars = [self.place] + ([] if fixes is None else [fixes])
        tokens = [] if self.token is None else [self.token]
        before = len(scalars) + len(inputs)

        def wrapped(*refs):
            refs[-1][...] = jnp.zeros_like(refs[-1])
            kernel(*refs[:before], *refs[before + len(tokens) : -1])

        outputs = outputs + [whole(shaped(jnp.int32, 8, 128))]
        shapes = [shape for shape, _, _ in outputs]
        keep = pl.BlockSpec(memory_space=pl.ANY)
        out = pl.pallas_call(
            wrapped,
            out_shape=shapes,
            grid_spec=pltpu.PrefetchScalarGridSpec(
                num_scalar_prefetch=len(scalars),
                grid=grid,
                in_specs=[
                    keep if block is None else pl.BlockSpec(block, index)
                    for _, block, index in inputs
                ]
                + [keep] * len(tokens),
                out_specs=[pl.BlockSpec(block, index) for _, block, index in outputs],
            ),
            input_output_aliases=aliases or {},
            compiler_params=pltpu.CompilerParams(vmem_limit_bytes=vmem_bytes),
            cost_estimate=pl.CostEstimate(
                flops=int(span * 1e9), bytes_accessed=0, transcendentals=0
            ),
        )(*scalars, *[a for a, _, _ in inputs], *tokens)
        self.token = out[-1]
        return out[0] if len(out) == 2 else out[:-1]


def shaped(dtype, *shape):
    return jax.ShapeDtypeStruct(shape, dtype)


def whole(array):
    zeros = (0,) * len(array.shape)
    return (array, array.shape, lambda *_: zeros)


def rowwise(array, steps):
    return (array, (array.shape[0] // steps, array.shape[1]), lambda i, *_: (i, 0))


def columnwise(array, steps):
    return (array, (array.shape[0], array.shape[1] // steps), lambda i, *_: (0, i))


def stacked(array, k, rows):
    return (array, (rows, array.shape[1]), lambda *_: (k, 0))


def dot_t(a, b):
    return lax.dot_general(a, b, (((0,), (0,)), ((), ())), preferred_element_type=f32)


def dot_bt(a, b):
    return lax.dot_general(a, b, (((1,), (1,)), ((), ())), preferred_element_type=f32)


def dot(a, b):
    return jnp.dot(a, b, preferred_element_type=f32)


def chosen(flag, yes, no):
    return jnp.where(flag != 0, yes, no)


def halves(x_ref, rows):
    turned = x_ref[...].T
    return turned[:rows], turned[rows:]


def rounded(order, local):
    def kernel(s_ref, a_ref, out_ref):
        out_ref[...] = a_ref[...].astype(bf16)

    return order.call(
        kernel, [rowwise(local, 3)], [rowwise(shaped(bf16, *local.shape), 3)], (3,)
    )


def first_piece(order, normed, rows):
    tokens = normed.shape[0]

    def kernel(s_ref, x_ref, piece_ref):
        low, high = halves(x_ref, rows)
        piece_ref[...] = chosen(s_ref[Y], low, high)

    return order.call(
        kernel,
        [(normed, (tokens, 2 * rows), lambda i, s: (0, s[FAR]))],
        [whole(shaped(bf16, rows, tokens))],
        (1,),
    )


def split(order, normed, rows, g_pair, fixes):
    tokens = normed.shape[0]

    def kernel(s_ref, fix_ref, x_ref, g_ref, two_ref, last_ref, own_ref):
        i = pl.program_id(0)
        low, high = halves(x_ref, rows)
        own_ref[...] = chosen(s_ref[Y], high, low)

        @pl.when(i < 2)
        def _():
            two_ref[...] = chosen(s_ref[Y], low, high)

        @pl.when(i == 2)
        def _():
            last_ref[...] = chosen(s_ref[Y], low, high)

    return order.call(
        kernel,
        [
            (normed, (tokens, 2 * rows), lambda i, s, f: (0, s[(i + 1) % 4])),
            (g_pair, None, None),
        ],
        [
            (
                shaped(bf16, 2 * rows, tokens),
                (rows, tokens),
                lambda i, s, f: (jnp.minimum(i, 1), 0),
            ),
            (shaped(bf16, 3 * rows, tokens), (rows, tokens), lambda i, s, f: (0, 0)),
            (shaped(bf16, 4 * rows, tokens), (rows, tokens), lambda i, s, f: ((i + 1) % 4, 0)),
        ],
        (4,),
        expected["split"],
        fixes=fixes,
    )


def gradient_part(order, mine, k, theirs, at, key_grad, g_pair, scale, dtype, span):
    tokens, features = key_grad.shape
    rows = mine.shape[0] // 4

    def kernel(s_ref, x_ref, xp_ref, g_ref, gp_ref, out_ref):
        total = dot(x_ref[...], g_ref[...]) + dot(xp_ref[...], gp_ref[...])
        out_ref[...] = (total * scale).astype(dtype)

    return order.call(
        kernel,
        [
            stacked(mine, k, rows),
            stacked(theirs, at, rows),
            columnwise(key_grad, 2),
            columnwise(g_pair, 2),
        ],
        [columnwise(shaped(dtype, rows, features), 2)],
        (2,),
        span,
    )


def input_two(order, key_grad, g_pair, first, second, target, scale):
    tokens, features = key_grad.shape
    rows = first.shape[0]

    def kernel(s_ref, g_ref, gp_ref, a_ref, b_ref, target_ref, pair_ref, own_ref):
        weight = jnp.where(pl.program_id(0) == 0, a_ref[...], b_ref[...])
        pair_ref[...] = (dot_bt(weight, gp_ref[...]) * scale).astype(bf16)
        own_ref[...] = (dot_bt(weight, g_ref[...]) * scale).astype(bf16)

    return order.call(
        kernel,
        [whole(a) for a in (key_grad, g_pair, first, second)] + [(target, None, None)],
        [
            (target, (rows, tokens), lambda i, s: (1 + i, 0)),
            (shaped(bf16, 2 * rows, tokens), (rows, tokens), lambda i, s: (i, 0)),
        ],
        (2,),
        expected["input two"],
        {5: 0},
    )


def input_one(order, key_grad, g_pair, inner, half, end, scale, span, before=()):
    tokens, features = key_grad.shape
    rows = end.shape[0]

    def kernel(s_ref, g_ref, gp_ref, a_ref, b_ref, *rest):
        pair_ref, own_ref, w_ref = rest[len(before) :]
        weight = chosen(s_ref[INNER], a_ref[...], b_ref[...])
        w_ref[...] = weight
        pair_ref[...] = (dot_bt(weight, gp_ref[...]) * scale).astype(bf16)
        own_ref[...] = (dot_bt(weight, g_ref[...]) * scale).astype(bf16)

    out = whole(shaped(bf16, rows, tokens))
    return order.call(
        kernel,
        [whole(key_grad), whole(g_pair), stacked(inner, half, rows), whole(end)]
        + [(a, None, None) for a in before],
        [out, out, whole(shaped(bf16, rows, features))],
        (1,),
        span,
    )


def input_join(order, slots, own, others, shape, span, target=None, before=()):
    tokens = own[0][0][0].shape[1]
    tile = tokens // 3
    rows = shape[1] // 8
    flat = [(a, k, rows // len(piece)) for piece in own + others for a, k in piece]
    kept = [a for a in (target, *before) if a is not None]

    def kernel(s_ref, *refs):
        values = iter([ref[...] for ref in refs[: len(flat)]])
        sides = [jnp.concatenate([next(values) for _ in piece], 0) for piece in own + others]
        first = pl.program_id(0) == 0
        mine = jnp.where(first, sides[0], sides[1])
        theirs = jnp.where(first, sides[2], sides[3])
        out_ref = refs[-1]

        @pl.when(s_ref[Y] == 0)
        def _():
            out_ref[...] = jnp.concatenate([mine, theirs], 0).T

        @pl.when(s_ref[Y] != 0)
        def _():
            out_ref[...] = jnp.concatenate([theirs, mine], 0).T

    def piece(array, k, height):
        return (array, (height, tile), lambda j, i, s: (k, i))

    return order.call(
        kernel,
        [piece(*p) for p in flat] + [(a, None, None) for a in kept],
        [(shaped(bf16, *shape), (tile, 2 * rows), lambda j, i, s: (i, s[slots[0] - j]))],
        (2, 3),
        span,
        None if target is None else {len(flat) + 1: 0},
    )


def key_sums(order, total, blocks, weights, span, scale=1.0, dtype=f32, before=()):
    features = weights[0].shape[1]
    tokens = blocks[0][0].shape[1]
    count = len(blocks)
    totals = [] if total is None else [columnwise(total, 2)]

    def kernel(s_ref, *refs):
        value = refs[2 * count][...] if totals else 0.0
        for x_ref, w_ref in zip(refs[:count], refs[count : 2 * count]):
            value += dot_t(x_ref[...], w_ref[...])
        refs[-1][...] = (value * scale).astype(dtype)

    return order.call(
        kernel,
        [stacked(x, k, w.shape[0]) for (x, k), w in zip(blocks, weights)]
        + [columnwise(w, 2) for w in weights]
        + totals
        + [(a, None, None) for a in before],
        [columnwise(shaped(dtype, tokens, features), 2)],
        (2,),
        span,
    )


def delta_halves(order, anchor, local):
    rows, features = local.shape

    def kernel(s_ref, a_ref, b_ref, c_ref, d_ref, own_ref, other_ref):
        own_ref[...] = a_ref[...] - b_ref[...]
        other_ref[...] = c_ref[...] - d_ref[...]

    def half(array, turned):
        def index(i, s):
            core = 1 - s[CORE] if turned else s[CORE]
            return (3 * core + i, 0)

        return (array, (rows // 6, features), index)

    out = rowwise(shaped(f32, rows // 2, features), 3)
    return order.call(
        kernel,
        [half(anchor, False), half(local, False), half(anchor, True), half(local, True)],
        [out, out],
        (3,),
    )


def total_of(order, here, there):
    def kernel(s_ref, a_ref, b_ref, out_ref):
        out_ref[...] = a_ref[...] + b_ref[...]

    return order.call(
        kernel, [rowwise(here, 3), rowwise(there, 3)], [rowwise(shaped(f32, *here.shape), 3)], (3,)
    )


def choose_sends(order, at_end, inside, beside):
    def kernel(s_ref, a_ref, b_ref, c_ref, out_ref, across_ref):
        out_ref[...] = chosen(s_ref[END], a_ref[...], b_ref[...])
        across_ref[...] = c_ref[...]

    out = rowwise(shaped(bf16, *inside.shape), 3)
    return order.call(
        kernel, [rowwise(a, 3) for a in (at_end, inside, beside)], [out, out], (3,), 0
    )


def first_handoff(order, p0, c1, p1, w_across):
    rows, features = p0.shape
    half = rows // 2

    def kernel(s_ref, p0_ref, c1_ref, p1_ref, w_ref, *out):
        total = (p0_ref[...].astype(f32) + c1_ref[...].astype(f32)).astype(bf16)
        send = chosen(s_ref[END], p1_ref[...], w_ref[...])
        for k in (0, 1):

            @pl.when(pl.program_id(0) == k)
            def _(k=k):
                out[2 * k][...] = total
                out[2 * k + 1][...] = send

    return order.call(
        kernel,
        [rowwise(a, 2) for a in (p0, c1, p1, w_across)],
        [whole(shaped(bf16, half, features))] * 4,
        (2,),
        expected["handoff"],
    )


def second_handoff(order, k, p1, c2, p2, q2, before, span):
    def kernel(s_ref, p1_ref, c2_ref, p2_ref, q2_ref, before_ref, s1_ref, t_ref):
        s1_ref[...] = (p1_ref[...].astype(f32) + c2_ref[...].astype(f32)).astype(bf16)
        t_ref[...] = (p2_ref[...] + q2_ref[...].astype(f32)).astype(bf16)

    rows, features = c2.shape
    block = (rows // 3, features)
    out = rowwise(shaped(bf16, rows, features), 3)
    return order.call(
        kernel,
        [
            (p1, block, lambda i, s: (3 * k + i, 0)),
            rowwise(c2, 3),
            (p2, block, lambda i, s: (3 * k + i, 0)),
            rowwise(q2, 3),
            (before, None, None),
        ],
        [out, out],
        (3,),
        span,
    )


def nesterov_pass(order, own, other, anchor, momentum, local):
    rows, features = local.shape

    def kernel(s_ref, own_ref, other_ref, anchor_ref, momentum_ref, local_ref, *out):
        anchor_new_ref, moment_new_ref, base_ref = out
        in_own = pl.program_id(0) // 3 == s_ref[CORE]
        outer_grad = jnp.where(in_own, own_ref[...], other_ref[...]) / 4
        anchor_new, moment_new = nesterov(outer_grad, anchor_ref[...], momentum_ref[...])
        anchor_new_ref[...] = anchor_new
        moment_new_ref[...] = moment_new
        kept = mix_weight * (1.0 - inner_rate * weight_decay)
        base_ref[...] = kept * local_ref[...] + (1.0 - mix_weight) * anchor_new

    def half(array):
        return (array, (rows // 6, features), lambda i, s: (i % 3, 0))

    out = rowwise(shaped(f32, rows, features), 6)
    return order.call(
        kernel,
        [half(own), half(other)] + [rowwise(a, 6) for a in (anchor, momentum, local)],
        [out, out, out],
        (6,),
        expected["nesterov"],
    )


def final_update(order, k, fixes, p3, qa, qb, first_old, second_old, base, made=(), keys=()):
    rows, features = base.shape
    block = (rows // 6, features)
    scale = keys[2] if keys else None

    def kernel(s_ref, fix_ref, p_ref, a_ref, b_ref, first_ref, second_ref, base_ref, *rest):
        outs = rest[len(keys[:2]) + len(made) :]
        gradient = p_ref[...] + a_ref[...].astype(f32) + b_ref[...].astype(f32)
        first_new = beta_first * first_ref[...] + (1.0 - beta_first) * gradient
        second_new = beta_second * second_ref[...] + (1.0 - beta_second) * gradient * gradient
        root = jnp.sqrt(second_new * fix_ref[1]) + epsilon
        step = (mix_weight * inner_rate) * fix_ref[0]
        outs[0][...] = base_ref[...] - step * first_new / root
        outs[1][...] = first_new
        outs[2][...] = second_new
        if keys:
            outs[3][...] = (rest[0][...] * scale + rest[1][...].astype(f32)).astype(bf16)

    def at(array, offset):
        return (array, block, lambda i, *_: (offset + i, 0))

    out = at(shaped(f32, rows, features), 3 * k)
    inputs = [at(p3, 3 * k), rowwise(qa, 3), rowwise(qb, 3)]
    inputs += [at(a, 3 * k) for a in (first_old, second_old, base)]
    inputs += [rowwise(a, 3) for a in keys[:2]]
    aliases = {2 + len(inputs) + i: i for i in range(len(made))}
    return order.call(
        kernel,
        inputs + [(a, None, None) for a in made],
        [out] * 3 + ([rowwise(shaped(bf16, *keys[0].shape), 3)] if keys else []),
        (3,),
        0 if keys else expected["first half"],
        aliases,
        fixes,
    )


def pair_pass(normed, key_grad, local, first_old, second_old, anchor, momentum, inner_step):
    width = normed.shape[1]
    rows = local.shape[0]
    scale = width ** (-0.5)
    me = lax.axis_index("fsdp")
    core = lax.axis_index("rep") % 2
    y, z = me % 2, me // 2
    inside = (z == 1) | (z == 2)
    far = jnp.where(z < 2, 3, 0)
    middle = jnp.where(z < 2, 2, 1)
    order = Order(jnp.stack([far, middle, z ^ 1, z, y, inside, ~inside, core]).astype(jnp.int32))

    def along(links):
        pairs = [(2 * a + c, 2 * b + c) for a, b in links for c in (0, 1)]
        return lambda value: lax.ppermute(value, "fsdp", pairs)

    outer = along([(0, 1), (1, 0), (2, 3), (3, 2)])
    inner = along([(1, 2), (2, 1)])

    def swap(value):
        return lax.ppermute(value, "fsdp", [(i, i ^ 1) for i in range(8)])

    def replica(value, bit):
        return lax.ppermute(value, "rep", [(i, i ^ bit) for i in range(4)])

    g_pair = swap(key_grad)
    weight = rounded(order, local)
    w_beside = outer(weight)
    w_inner = inner(weight)
    x0 = swap(first_piece(order, normed, rows))
    own_delta, other_delta = delta_halves(order, anchor, local)
    delta_core = replica(other_delta, 1)
    fixes = 1.0 / jnp.stack(corrections(inner_step))
    two, three, mine = split(order, normed, rows, g_pair, fixes)
    x12 = swap(two)
    delta = total_of(order, own_delta, delta_core)
    delta_there = replica(delta, 2)

    def partial(k, theirs, at, dtype, span):
        return gradient_part(order, mine, k, theirs, at, key_grad, g_pair, scale, dtype, span)

    p0 = partial(0, x0, 0, bf16, expected["first part"])
    send, across = choose_sends(order, p0, w_inner, w_beside)
    c1 = outer(send)
    w_across = inner(across)
    three, own01 = input_two(order, key_grad, g_pair, weight, w_beside, three, scale)
    x3 = swap(three)
    known = (w_beside, weight)
    own_total = key_sums(order, None, [(mine, 2), (mine, 3)], known, expected["early own"])
    total = total_of(order, delta, delta_there)
    total_there = replica(total, 1)
    p1 = partial(1, x12, 0, bf16, expected["second part"])
    p2 = partial(2, x12, 1, f32, 1)
    anchor_new, moment_new, base = nesterov_pass(
        order, total, total_there, anchor, momentum, local
    )
    pair_total = key_sums(order, None, [(x12, 1)], known[:1], expected["early pair"])

    s0a, send_a, s0b, send_b = first_handoff(order, p0, c1, p1, w_across)
    c2a, q2a = outer(send_a), inner(s0a)
    c2b, q2b = outer(send_b), inner(s0b)
    i2, own2, w_middle = input_one(
        order, key_grad, g_pair, w_inner, 0, c1, scale, expected["input middle"]
    )
    g2 = swap(i2)
    input_grad = input_join(
        order,
        (OWN, BESIDE),
        [[(own01, 0)], [(own01, 1)]],
        [[(x3, 1)], [(x3, 2)]],
        normed.shape,
        expected["join two"],
    )
    i3, own3a, w_far_a = input_one(
        order, key_grad, g_pair, w_across, 0, c2a, scale, expected["input far"], [x3]
    )
    g3a = swap(i3)
    s1, t = second_handoff(order, 0, p1, c2a, p2, q2a, x3, expected["early sums"])
    qaa, qba = outer(t), inner(s1)
    pair_total = key_sums(
        order,
        pair_total,
        [(x12, 0), (x3, 0)],
        (w_middle, weight),
        expected["pair sums"],
        before=[g2],
    )
    p3 = partial(3, x3, 0, f32, 0)
    i3, own3b, w_far_b = input_one(
        order, key_grad, g_pair, w_across, 1, c2b, scale, expected["input far"]
    )
    g3b = swap(i3)
    w_far = (w_far_a, w_far_b)
    key_pair = swap(key_sums(order, pair_total, [(x0, 0), (x0, 1)], w_far, 0, scale, bf16))
    s1, t = second_handoff(order, 1, p1, c2b, p2, q2b, g3a, expected["late sums"])
    qab, qbb = outer(t), inner(s1)
    own_total = key_sums(
        order,
        own_total,
        [(mine, 1), (mine, 0), (mine, 1)],
        (w_middle, *w_far),
        expected["own sums"],
        before=[g3b],
    )
    input_grad = input_join(
        order,
        (MIDDLE, FAR),
        [[(own2, 0)], [(own3a, 0), (own3b, 0)]],
        [[(g2, 0)], [(g3a, 0), (g3b, 0)]],
        normed.shape,
        expected["join last"],
        input_grad,
    )
    state = (first_old, second_old, base)
    made = final_update(order, 0, fixes, p3, qaa, qba, *state)
    merged, first_new, second_new, keys = final_update(
        order, 1, fixes, p3, qab, qbb, *state, made, (own_total, key_pair, scale)
    )
    return (keys, input_grad, merged, first_new, second_new, anchor_new, moment_new)


def body(normed, key_grad, master, first_moment, second_moment, anchor, momentum, inner_step):
    local = master[0]
    sizes = (lax.axis_size("rep"), lax.axis_size("fsdp"))
    inner_pass = pair_pass if sizes == (4, 8) else whole_pass
    keys, input_grad, merged, first_new, second_new, anchor_new, moment_new = inner_pass(
        normed, key_grad, local, first_moment[0], second_moment[0], anchor, momentum, inner_step
    )
    return (
        keys,
        input_grad,
        merged[None],
        first_new[None],
        second_new[None],
        anchor_new,
        moment_new,
    )


def solution(mesh):
    in_specs = (
        P(("rep", "fsdp"), None),
        P(("rep", "fsdp"), None),
        P("rep", "fsdp", None),
        P("rep", "fsdp", None),
        P("rep", "fsdp", None),
        P("fsdp", None),
        P("fsdp", None),
        P(),
    )
    out_specs = (
        P(("rep", "fsdp"), None),
        P(("rep", "fsdp"), None),
        P("rep", "fsdp", None),
        P("rep", "fsdp", None),
        P("rep", "fsdp", None),
        P("fsdp", None),
        P("fsdp", None),
    )
    return jax.shard_map(body, mesh=mesh, in_specs=in_specs, out_specs=out_specs, check_vma=False)
```

```python
import jax
import jax.numpy as jnp
from jax import lax
from jax.experimental import pallas as pl
from jax.experimental.pallas import tpu as pltpu
from jax.sharding import PartitionSpec as P

beta_first = 0.9
beta_second = 0.95
inner_rate = 0.1
weight_decay = 0.1
epsilon = 1e-08
outer_rate = 0.7
outer_mu = 0.9
mix_weight = 0.5

f32 = jnp.float32
bf16 = jnp.bfloat16
vmem_bytes = 16 * 1024 * 1024

expected = {
    "split": 30,
    "first part": 0,
    "input two": 12,
    "second part": 30,
    "nesterov": 1,
    "early own": 0,
    "early pair": 0,
    "handoff": 1,
    "input middle": 0,
    "join two": 0,
    "input far": 0,
    "early sums": 1,
    "pair sums": 0,
    "late sums": 1,
    "own sums": 0,
    "join last": 0,
    "first half": 5,
}


def corrections(inner_step):
    count_float = inner_step[0].astype(f32)
    fix_first = 1.0 - jnp.power(f32(beta_first), count_float)
    fix_second = 1.0 - jnp.power(f32(beta_second), count_float)
    return fix_first, fix_second


def adam(gradient, local, first_old, second_old, fix_first, fix_second):
    first_new = beta_first * first_old + (1.0 - beta_first) * gradient
    second_new = beta_second * second_old + (1.0 - beta_second) * gradient * gradient
    direction = first_new / fix_first / (jnp.sqrt(second_new / fix_second) + epsilon)
    stepped = local - inner_rate * (direction + weight_decay * local)
    return (stepped, first_new, second_new)


def nesterov(outer_grad, anchor_rows, moment_rows):
    moment_new = outer_mu * moment_rows + outer_grad
    anchor_new = anchor_rows - outer_rate * (outer_grad + outer_mu * moment_new)
    return (anchor_new, moment_new)


def outer_update(local, anchor, momentum):
    summed = lax.psum(anchor - local, "rep")
    return nesterov(summed / lax.axis_size("rep"), anchor, momentum)


def whole_pass(normed, key_grad, local, first_old, second_old, anchor, momentum, inner_step):
    scale = normed.shape[1] ** (-0.5)
    weight = lax.all_gather(local.astype(bf16), "fsdp", axis=0, tiled=True)
    keys = (jnp.dot(normed, weight, preferred_element_type=f32) * scale).astype(bf16)
    input_grad = (
        lax.dot_general(key_grad, weight, (((1,), (1,)), ((), ())), preferred_element_type=f32)
        * scale
    ).astype(bf16)
    gradient = lax.psum_scatter(
        lax.dot_general(normed, key_grad, (((0,), (0,)), ((), ())), preferred_element_type=f32)
        * scale,
        "fsdp",
        scatter_dimension=0,
        tiled=True,
    )
    stepped, first_new, second_new = adam(
        gradient, local, first_old, second_old, *corrections(inner_step)
    )
    anchor_new, moment_new = outer_update(local, anchor, momentum)
    merged = mix_weight * stepped + (1.0 - mix_weight) * anchor_new
    return (keys, input_grad, merged, first_new, second_new, anchor_new, moment_new)


FAR, MIDDLE, BESIDE, OWN, Y, INNER, END, CORE = range(8)


class Order:
    def __init__(self, place):
        self.place = place
        self.token = None

    def call(self, kernel, inputs, outputs, grid, span=1, aliases=None, fixes=None):
        scalars = [self.place] + ([] if fixes is None else [fixes])
        tokens = [] if self.token is None else [self.token]
        before = len(scalars) + len(inputs)

        def wrapped(*refs):
            refs[-1][...] = jnp.zeros_like(refs[-1])
            kernel(*refs[:before], *refs[before + len(tokens) : -1])

        outputs = outputs + [whole(shaped(jnp.int32, 8, 128))]
        shapes = [shape for shape, _, _ in outputs]
        keep = pl.BlockSpec(memory_space=pl.ANY)
        out = pl.pallas_call(
            wrapped,
            out_shape=shapes,
            grid_spec=pltpu.PrefetchScalarGridSpec(
                num_scalar_prefetch=len(scalars),
                grid=grid,
                in_specs=[
                    keep if block is None else pl.BlockSpec(block, index)
                    for _, block, index in inputs
                ]
                + [keep] * len(tokens),
                out_specs=[pl.BlockSpec(block, index) for _, block, index in outputs],
            ),
            input_output_aliases=aliases or {},
            compiler_params=pltpu.CompilerParams(vmem_limit_bytes=vmem_bytes),
            cost_estimate=pl.CostEstimate(
                flops=int(span * 1e9), bytes_accessed=0, transcendentals=0
            ),
        )(*scalars, *[a for a, _, _ in inputs], *tokens)
        self.token = out[-1]
        return out[0] if len(out) == 2 else out[:-1]


def shaped(dtype, *shape):
    return jax.ShapeDtypeStruct(shape, dtype)


def whole(array):
    zeros = (0,) * len(array.shape)
    return (array, array.shape, lambda *_: zeros)


def rowwise(array, steps):
    return (array, (array.shape[0] // steps, array.shape[1]), lambda i, *_: (i, 0))


def columnwise(array, steps):
    return (array, (array.shape[0], array.shape[1] // steps), lambda i, *_: (0, i))


def stacked(array, k, rows):
    return (array, (rows, array.shape[1]), lambda *_: (k, 0))


def dot_t(a, b):
    return lax.dot_general(a, b, (((0,), (0,)), ((), ())), preferred_element_type=f32)


def dot_bt(a, b):
    return lax.dot_general(a, b, (((1,), (1,)), ((), ())), preferred_element_type=f32)


def dot(a, b):
    return jnp.dot(a, b, preferred_element_type=f32)


def chosen(flag, yes, no):
    return jnp.where(flag != 0, yes, no)


def halves(x_ref, rows):
    turned = x_ref[...].T
    return turned[:rows], turned[rows:]


def rounded(order, local):
    def kernel(s_ref, a_ref, out_ref):
        out_ref[...] = a_ref[...].astype(bf16)

    return order.call(
        kernel, [rowwise(local, 3)], [rowwise(shaped(bf16, *local.shape), 3)], (3,)
    )


def first_piece(order, normed, rows):
    tokens = normed.shape[0]

    def kernel(s_ref, x_ref, piece_ref):
        low, high = halves(x_ref, rows)
        piece_ref[...] = chosen(s_ref[Y], low, high)

    return order.call(
        kernel,
        [(normed, (tokens, 2 * rows), lambda i, s: (0, s[FAR]))],
        [whole(shaped(bf16, rows, tokens))],
        (1,),
    )


def split(order, normed, rows, g_pair, fixes):
    tokens = normed.shape[0]

    def kernel(s_ref, fix_ref, x_ref, g_ref, two_ref, last_ref, own_ref):
        i = pl.program_id(0)
        low, high = halves(x_ref, rows)
        own_ref[...] = chosen(s_ref[Y], high, low)

        @pl.when(i < 2)
        def _():
            two_ref[...] = chosen(s_ref[Y], low, high)

        @pl.when(i == 2)
        def _():
            last_ref[...] = chosen(s_ref[Y], low, high)

    return order.call(
        kernel,
        [
            (normed, (tokens, 2 * rows), lambda i, s, f: (0, s[(i + 1) % 4])),
            (g_pair, None, None),
        ],
        [
            (
                shaped(bf16, 2 * rows, tokens),
                (rows, tokens),
                lambda i, s, f: (jnp.minimum(i, 1), 0),
            ),
            (shaped(bf16, 3 * rows, tokens), (rows, tokens), lambda i, s, f: (0, 0)),
            (shaped(bf16, 4 * rows, tokens), (rows, tokens), lambda i, s, f: ((i + 1) % 4, 0)),
        ],
        (4,),
        expected["split"],
        fixes=fixes,
    )


def gradient_part(order, mine, k, theirs, at, key_grad, g_pair, scale, dtype, span):
    tokens, features = key_grad.shape
    rows = mine.shape[0] // 4

    def kernel(s_ref, x_ref, xp_ref, g_ref, gp_ref, out_ref):
        total = dot(x_ref[...], g_ref[...]) + dot(xp_ref[...], gp_ref[...])
        out_ref[...] = (total * scale).astype(dtype)

    return order.call(
        kernel,
        [
            stacked(mine, k, rows),
            stacked(theirs, at, rows),
            columnwise(key_grad, 2),
            columnwise(g_pair, 2),
        ],
        [columnwise(shaped(dtype, rows, features), 2)],
        (2,),
        span,
    )


def input_two(order, key_grad, g_pair, first, second, target, scale):
    tokens, features = key_grad.shape
    rows = first.shape[0]

    def kernel(s_ref, g_ref, gp_ref, a_ref, b_ref, target_ref, pair_ref, own_ref):
        weight = jnp.where(pl.program_id(0) == 0, a_ref[...], b_ref[...])
        pair_ref[...] = (dot_bt(weight, gp_ref[...]) * scale).astype(bf16)
        own_ref[...] = (dot_bt(weight, g_ref[...]) * scale).astype(bf16)

    return order.call(
        kernel,
        [whole(a) for a in (key_grad, g_pair, first, second)] + [(target, None, None)],
        [
            (target, (rows, tokens), lambda i, s: (1 + i, 0)),
            (shaped(bf16, 2 * rows, tokens), (rows, tokens), lambda i, s: (i, 0)),
        ],
        (2,),
        expected["input two"],
        {5: 0},
    )


def input_one(order, key_grad, g_pair, inner, half, end, scale, span, before=()):
    tokens, features = key_grad.shape
    rows = end.shape[0]

    def kernel(s_ref, g_ref, gp_ref, a_ref, b_ref, *rest):
        pair_ref, own_ref, w_ref = rest[len(before) :]
        weight = chosen(s_ref[INNER], a_ref[...], b_ref[...])
        w_ref[...] = weight
        pair_ref[...] = (dot_bt(weight, gp_ref[...]) * scale).astype(bf16)
        own_ref[...] = (dot_bt(weight, g_ref[...]) * scale).astype(bf16)

    out = whole(shaped(bf16, rows, tokens))
    return order.call(
        kernel,
        [whole(key_grad), whole(g_pair), stacked(inner, half, rows), whole(end)]
        + [(a, None, None) for a in before],
        [out, out, whole(shaped(bf16, rows, features))],
        (1,),
        span,
    )


def input_join(order, slots, own, others, shape, span, target=None, before=()):
    tokens = own[0][0][0].shape[1]
    tile = tokens // 3
    rows = shape[1] // 8
    flat = [(a, k, rows // len(piece)) for piece in own + others for a, k in piece]
    kept = [a for a in (target, *before) if a is not None]

    def kernel(s_ref, *refs):
        values = iter([ref[...] for ref in refs[: len(flat)]])
        sides = [jnp.concatenate([next(values) for _ in piece], 0) for piece in own + others]
        first = pl.program_id(0) == 0
        mine = jnp.where(first, sides[0], sides[1])
        theirs = jnp.where(first, sides[2], sides[3])
        out_ref = refs[-1]

        @pl.when(s_ref[Y] == 0)
        def _():
            out_ref[...] = jnp.concatenate([mine, theirs], 0).T

        @pl.when(s_ref[Y] != 0)
        def _():
            out_ref[...] = jnp.concatenate([theirs, mine], 0).T

    def piece(array, k, height):
        return (array, (height, tile), lambda j, i, s: (k, i))

    return order.call(
        kernel,
        [piece(*p) for p in flat] + [(a, None, None) for a in kept],
        [(shaped(bf16, *shape), (tile, 2 * rows), lambda j, i, s: (i, s[slots[0] - j]))],
        (2, 3),
        span,
        None if target is None else {len(flat) + 1: 0},
    )


def key_sums(order, total, blocks, weights, span, scale=1.0, dtype=f32, before=()):
    features = weights[0].shape[1]
    tokens = blocks[0][0].shape[1]
    count = len(blocks)
    totals = [] if total is None else [columnwise(total, 2)]

    def kernel(s_ref, *refs):
        value = refs[2 * count][...] if totals else 0.0
        for x_ref, w_ref in zip(refs[:count], refs[count : 2 * count]):
            value += dot_t(x_ref[...], w_ref[...])
        refs[-1][...] = (value * scale).astype(dtype)

    return order.call(
        kernel,
        [stacked(x, k, w.shape[0]) for (x, k), w in zip(blocks, weights)]
        + [columnwise(w, 2) for w in weights]
        + totals
        + [(a, None, None) for a in before],
        [columnwise(shaped(dtype, tokens, features), 2)],
        (2,),
        span,
    )


def delta_halves(order, anchor, local):
    rows, features = local.shape

    def kernel(s_ref, a_ref, b_ref, c_ref, d_ref, own_ref, other_ref):
        own_ref[...] = a_ref[...] - b_ref[...]
        other_ref[...] = c_ref[...] - d_ref[...]

    def half(array, turned):
        def index(i, s):
            core = 1 - s[CORE] if turned else s[CORE]
            return (3 * core + i, 0)

        return (array, (rows // 6, features), index)

    out = rowwise(shaped(f32, rows // 2, features), 3)
    return order.call(
        kernel,
        [half(anchor, False), half(local, False), half(anchor, True), half(local, True)],
        [out, out],
        (3,),
    )


def total_of(order, here, there):
    def kernel(s_ref, a_ref, b_ref, out_ref):
        out_ref[...] = a_ref[...] + b_ref[...]

    return order.call(
        kernel, [rowwise(here, 3), rowwise(there, 3)], [rowwise(shaped(f32, *here.shape), 3)], (3,)
    )


def choose_sends(order, at_end, inside, beside):
    def kernel(s_ref, a_ref, b_ref, c_ref, out_ref, across_ref):
        out_ref[...] = chosen(s_ref[END], a_ref[...], b_ref[...])
        across_ref[...] = c_ref[...]

    out = rowwise(shaped(bf16, *inside.shape), 3)
    return order.call(
        kernel, [rowwise(a, 3) for a in (at_end, inside, beside)], [out, out], (3,), 0
    )


def first_handoff(order, p0, c1, p1, w_across):
    rows, features = p0.shape
    half = rows // 2

    def kernel(s_ref, p0_ref, c1_ref, p1_ref, w_ref, *out):
        total = (p0_ref[...].astype(f32) + c1_ref[...].astype(f32)).astype(bf16)
        send = chosen(s_ref[END], p1_ref[...], w_ref[...])
        for k in (0, 1):

            @pl.when(pl.program_id(0) == k)
            def _(k=k):
                out[2 * k][...] = total
                out[2 * k + 1][...] = send

    return order.call(
        kernel,
        [rowwise(a, 2) for a in (p0, c1, p1, w_across)],
        [whole(shaped(bf16, half, features))] * 4,
        (2,),
        expected["handoff"],
    )


def second_handoff(order, k, p1, c2, p2, q2, before, span):
    def kernel(s_ref, p1_ref, c2_ref, p2_ref, q2_ref, before_ref, s1_ref, t_ref):
        s1_ref[...] = (p1_ref[...].astype(f32) + c2_ref[...].astype(f32)).astype(bf16)
        t_ref[...] = (p2_ref[...] + q2_ref[...].astype(f32)).astype(bf16)

    rows, features = c2.shape
    block = (rows // 3, features)
    out = rowwise(shaped(bf16, rows, features), 3)
    return order.call(
        kernel,
        [
            (p1, block, lambda i, s: (3 * k + i, 0)),
            rowwise(c2, 3),
            (p2, block, lambda i, s: (3 * k + i, 0)),
            rowwise(q2, 3),
            (before, None, None),
        ],
        [out, out],
        (3,),
        span,
    )


def nesterov_pass(order, own, other, anchor, momentum, local):
    rows, features = local.shape

    def kernel(s_ref, own_ref, other_ref, anchor_ref, momentum_ref, local_ref, *out):
        anchor_new_ref, moment_new_ref, base_ref = out
        in_own = pl.program_id(0) // 3 == s_ref[CORE]
        outer_grad = jnp.where(in_own, own_ref[...], other_ref[...]) / 4
        anchor_new, moment_new = nesterov(outer_grad, anchor_ref[...], momentum_ref[...])
        anchor_new_ref[...] = anchor_new
        moment_new_ref[...] = moment_new
        kept = mix_weight * (1.0 - inner_rate * weight_decay)
        base_ref[...] = kept * local_ref[...] + (1.0 - mix_weight) * anchor_new

    def half(array):
        return (array, (rows // 6, features), lambda i, s: (i % 3, 0))

    out = rowwise(shaped(f32, rows, features), 6)
    return order.call(
        kernel,
        [half(own), half(other)] + [rowwise(a, 6) for a in (anchor, momentum, local)],
        [out, out, out],
        (6,),
        expected["nesterov"],
    )


def final_update(order, k, fixes, p3, qa, qb, first_old, second_old, base, made=(), keys=()):
    rows, features = base.shape
    block = (rows // 12, features)
    scale = keys[2] if keys else None

    def kernel(s_ref, fix_ref, p_ref, a_ref, b_ref, first_ref, second_ref, base_ref, *rest):
        outs = rest[len(keys[:2]) + len(made) :]
        gradient = p_ref[...] + a_ref[...].astype(f32) + b_ref[...].astype(f32)
        first_new = beta_first * first_ref[...] + (1.0 - beta_first) * gradient
        second_new = beta_second * second_ref[...] + (1.0 - beta_second) * gradient * gradient
        root = jnp.sqrt(second_new * fix_ref[1]) + epsilon
        step = (mix_weight * inner_rate) * fix_ref[0]
        outs[0][...] = base_ref[...] - step * first_new / root
        outs[1][...] = first_new
        outs[2][...] = second_new
        if keys:
            outs[3][...] = (rest[0][...] * scale + rest[1][...].astype(f32)).astype(bf16)

    def at(array, offset):
        return (array, block, lambda i, *_: (offset + i, 0))

    out = at(shaped(f32, rows, features), 6 * k)
    inputs = [at(p3, 6 * k), rowwise(qa, 6), rowwise(qb, 6)]
    inputs += [at(a, 6 * k) for a in (first_old, second_old, base)]
    inputs += [rowwise(a, 6) for a in keys[:2]]
    aliases = {2 + len(inputs) + i: i for i in range(len(made))}
    return order.call(
        kernel,
        inputs + [(a, None, None) for a in made],
        [out] * 3 + ([rowwise(shaped(bf16, *keys[0].shape), 6)] if keys else []),
        (6,),
        0 if keys else expected["first half"],
        aliases,
        fixes,
    )


def pair_pass(normed, key_grad, local, first_old, second_old, anchor, momentum, inner_step):
    width = normed.shape[1]
    rows = local.shape[0]
    scale = width ** (-0.5)
    me = lax.axis_index("fsdp")
    core = lax.axis_index("rep") % 2
    y, z = me % 2, me // 2
    inside = (z == 1) | (z == 2)
    far = jnp.where(z < 2, 3, 0)
    middle = jnp.where(z < 2, 2, 1)
    order = Order(jnp.stack([far, middle, z ^ 1, z, y, inside, ~inside, core]).astype(jnp.int32))

    def along(links):
        pairs = [(2 * a + c, 2 * b + c) for a, b in links for c in (0, 1)]
        return lambda value: lax.ppermute(value, "fsdp", pairs)

    outer = along([(0, 1), (1, 0), (2, 3), (3, 2)])
    inner = along([(1, 2), (2, 1)])

    def swap(value):
        return lax.ppermute(value, "fsdp", [(i, i ^ 1) for i in range(8)])

    def replica(value, bit):
        return lax.ppermute(value, "rep", [(i, i ^ bit) for i in range(4)])

    g_pair = swap(key_grad)
    weight = rounded(order, local)
    w_beside = outer(weight)
    w_inner = inner(weight)
    x0 = swap(first_piece(order, normed, rows))
    own_delta, other_delta = delta_halves(order, anchor, local)
    delta_core = replica(other_delta, 1)
    fixes = 1.0 / jnp.stack(corrections(inner_step))
    two, three, mine = split(order, normed, rows, g_pair, fixes)
    x12 = swap(two)
    delta = total_of(order, own_delta, delta_core)
    delta_there = replica(delta, 2)

    def partial(k, theirs, at, dtype, span):
        return gradient_part(order, mine, k, theirs, at, key_grad, g_pair, scale, dtype, span)

    p0 = partial(0, x0, 0, bf16, expected["first part"])
    send, across = choose_sends(order, p0, w_inner, w_beside)
    c1 = outer(send)
    w_across = inner(across)
    three, own01 = input_two(order, key_grad, g_pair, weight, w_beside, three, scale)
    x3 = swap(three)
    known = (w_beside, weight)
    own_total = key_sums(order, None, [(mine, 2), (mine, 3)], known, expected["early own"])
    total = total_of(order, delta, delta_there)
    total_there = replica(total, 1)
    p1 = partial(1, x12, 0, bf16, expected["second part"])
    p2 = partial(2, x12, 1, f32, 1)
    anchor_new, moment_new, base = nesterov_pass(
        order, total, total_there, anchor, momentum, local
    )
    pair_total = key_sums(order, None, [(x12, 1)], known[:1], expected["early pair"])

    s0a, send_a, s0b, send_b = first_handoff(order, p0, c1, p1, w_across)
    c2a, q2a = outer(send_a), inner(s0a)
    c2b, q2b = outer(send_b), inner(s0b)
    i2, own2, w_middle = input_one(
        order, key_grad, g_pair, w_inner, 0, c1, scale, expected["input middle"]
    )
    g2 = swap(i2)
    input_grad = input_join(
        order,
        (OWN, BESIDE),
        [[(own01, 0)], [(own01, 1)]],
        [[(x3, 1)], [(x3, 2)]],
        normed.shape,
        expected["join two"],
    )
    i3, own3a, w_far_a = input_one(
        order, key_grad, g_pair, w_across, 0, c2a, scale, expected["input far"], [x3]
    )
    g3a = swap(i3)
    s1, t = second_handoff(order, 0, p1, c2a, p2, q2a, x3, expected["early sums"])
    qaa, qba = outer(t), inner(s1)
    pair_total = key_sums(
        order,
        pair_total,
        [(x12, 0), (x3, 0)],
        (w_middle, weight),
        expected["pair sums"],
        before=[g2],
    )
    i3, own3b, w_far_b = input_one(
        order, key_grad, g_pair, w_across, 1, c2b, scale, expected["input far"]
    )
    g3b = swap(i3)
    w_far = (w_far_a, w_far_b)
    key_pair = swap(key_sums(order, pair_total, [(x0, 0), (x0, 1)], w_far, 0, scale, bf16))
    s1, t = second_handoff(order, 1, p1, c2b, p2, q2b, g3a, expected["late sums"])
    qab, qbb = outer(t), inner(s1)
    p3 = partial(3, x3, 0, f32, 0)
    own_total = key_sums(
        order,
        own_total,
        [(mine, 1), (mine, 0), (mine, 1)],
        (w_middle, *w_far),
        expected["own sums"],
        before=[g3b],
    )
    input_grad = input_join(
        order,
        (MIDDLE, FAR),
        [[(own2, 0)], [(own3a, 0), (own3b, 0)]],
        [[(g2, 0)], [(g3a, 0), (g3b, 0)]],
        normed.shape,
        expected["join last"],
        input_grad,
    )
    state = (first_old, second_old, base)
    made = final_update(order, 0, fixes, p3, qaa, qba, *state)
    merged, first_new, second_new, keys = final_update(
        order, 1, fixes, p3, qab, qbb, *state, made, (own_total, key_pair, scale)
    )
    return (keys, input_grad, merged, first_new, second_new, anchor_new, moment_new)


def body(normed, key_grad, master, first_moment, second_moment, anchor, momentum, inner_step):
    local = master[0]
    sizes = (lax.axis_size("rep"), lax.axis_size("fsdp"))
    inner_pass = pair_pass if sizes == (4, 8) else whole_pass
    keys, input_grad, merged, first_new, second_new, anchor_new, moment_new = inner_pass(
        normed, key_grad, local, first_moment[0], second_moment[0], anchor, momentum, inner_step
    )
    return (
        keys,
        input_grad,
        merged[None],
        first_new[None],
        second_new[None],
        anchor_new,
        moment_new,
    )


def solution(mesh):
    in_specs = (
        P(("rep", "fsdp"), None),
        P(("rep", "fsdp"), None),
        P("rep", "fsdp", None),
        P("rep", "fsdp", None),
        P("rep", "fsdp", None),
        P("fsdp", None),
        P("fsdp", None),
        P(),
    )
    out_specs = (
        P(("rep", "fsdp"), None),
        P(("rep", "fsdp"), None),
        P("rep", "fsdp", None),
        P("rep", "fsdp", None),
        P("rep", "fsdp", None),
        P("fsdp", None),
        P("fsdp", None),
    )
    return jax.shard_map(body, mesh=mesh, in_specs=in_specs, out_specs=out_specs, check_vma=False)
```

```python
import jax
import jax.numpy as jnp
from jax import lax
from jax.experimental import pallas as pl
from jax.experimental.pallas import tpu as pltpu
from jax.sharding import PartitionSpec as P

beta_first = 0.9
beta_second = 0.95
inner_rate = 0.1
weight_decay = 0.1
epsilon = 1e-08
outer_rate = 0.7
outer_mu = 0.9
mix_weight = 0.5

f32 = jnp.float32
bf16 = jnp.bfloat16
vmem_bytes = 16 * 1024 * 1024

expected = {
    "split": 30,
    "first part": 0,
    "input two": 12,
    "second part": 30,
    "nesterov": 1,
    "early own": 0,
    "early pair": 0,
    "handoff": 1,
    "input middle": 0,
    "join two": 0,
    "input far": 0,
    "input last": 12,
    "early sums": 1,
    "pair sums": 0,
    "late sums": 1,
    "own sums": 0,
    "join last": 0,
    "first half": 12,
}


def corrections(inner_step):
    count_float = inner_step[0].astype(f32)
    fix_first = 1.0 - jnp.power(f32(beta_first), count_float)
    fix_second = 1.0 - jnp.power(f32(beta_second), count_float)
    return fix_first, fix_second


def adam(gradient, local, first_old, second_old, fix_first, fix_second):
    first_new = beta_first * first_old + (1.0 - beta_first) * gradient
    second_new = beta_second * second_old + (1.0 - beta_second) * gradient * gradient
    direction = first_new / fix_first / (jnp.sqrt(second_new / fix_second) + epsilon)
    stepped = local - inner_rate * (direction + weight_decay * local)
    return (stepped, first_new, second_new)


def nesterov(outer_grad, anchor_rows, moment_rows):
    moment_new = outer_mu * moment_rows + outer_grad
    anchor_new = anchor_rows - outer_rate * (outer_grad + outer_mu * moment_new)
    return (anchor_new, moment_new)


def outer_update(local, anchor, momentum):
    summed = lax.psum(anchor - local, "rep")
    return nesterov(summed / lax.axis_size("rep"), anchor, momentum)


def whole_pass(normed, key_grad, local, first_old, second_old, anchor, momentum, inner_step):
    scale = normed.shape[1] ** (-0.5)
    weight = lax.all_gather(local.astype(bf16), "fsdp", axis=0, tiled=True)
    keys = (jnp.dot(normed, weight, preferred_element_type=f32) * scale).astype(bf16)
    input_grad = (
        lax.dot_general(key_grad, weight, (((1,), (1,)), ((), ())), preferred_element_type=f32)
        * scale
    ).astype(bf16)
    gradient = lax.psum_scatter(
        lax.dot_general(normed, key_grad, (((0,), (0,)), ((), ())), preferred_element_type=f32)
        * scale,
        "fsdp",
        scatter_dimension=0,
        tiled=True,
    )
    stepped, first_new, second_new = adam(
        gradient, local, first_old, second_old, *corrections(inner_step)
    )
    anchor_new, moment_new = outer_update(local, anchor, momentum)
    merged = mix_weight * stepped + (1.0 - mix_weight) * anchor_new
    return (keys, input_grad, merged, first_new, second_new, anchor_new, moment_new)


FAR, MIDDLE, BESIDE, OWN, Y, INNER, END, CORE = range(8)


class Order:
    def __init__(self, place):
        self.place = place
        self.token = None

    def call(self, kernel, inputs, outputs, grid, span=1, aliases=None, fixes=None):
        scalars = [self.place] + ([] if fixes is None else [fixes])
        tokens = [] if self.token is None else [self.token]
        before = len(scalars) + len(inputs)

        def wrapped(*refs):
            refs[-1][...] = jnp.zeros_like(refs[-1])
            kernel(*refs[:before], *refs[before + len(tokens) : -1])

        outputs = outputs + [whole(shaped(jnp.int32, 8, 128))]
        shapes = [shape for shape, _, _ in outputs]
        keep = pl.BlockSpec(memory_space=pl.ANY)
        out = pl.pallas_call(
            wrapped,
            out_shape=shapes,
            grid_spec=pltpu.PrefetchScalarGridSpec(
                num_scalar_prefetch=len(scalars),
                grid=grid,
                in_specs=[
                    keep if block is None else pl.BlockSpec(block, index)
                    for _, block, index in inputs
                ]
                + [keep] * len(tokens),
                out_specs=[pl.BlockSpec(block, index) for _, block, index in outputs],
            ),
            input_output_aliases=aliases or {},
            compiler_params=pltpu.CompilerParams(vmem_limit_bytes=vmem_bytes),
            cost_estimate=pl.CostEstimate(
                flops=int(span * 1e9), bytes_accessed=0, transcendentals=0
            ),
        )(*scalars, *[a for a, _, _ in inputs], *tokens)
        self.token = out[-1]
        return out[0] if len(out) == 2 else out[:-1]


def shaped(dtype, *shape):
    return jax.ShapeDtypeStruct(shape, dtype)


def whole(array):
    zeros = (0,) * len(array.shape)
    return (array, array.shape, lambda *_: zeros)


def rowwise(array, steps):
    return (array, (array.shape[0] // steps, array.shape[1]), lambda i, *_: (i, 0))


def columnwise(array, steps):
    return (array, (array.shape[0], array.shape[1] // steps), lambda i, *_: (0, i))


def stacked(array, k, rows):
    return (array, (rows, array.shape[1]), lambda *_: (k, 0))


def dot_t(a, b):
    return lax.dot_general(a, b, (((0,), (0,)), ((), ())), preferred_element_type=f32)


def dot_bt(a, b):
    return lax.dot_general(a, b, (((1,), (1,)), ((), ())), preferred_element_type=f32)


def dot(a, b):
    return jnp.dot(a, b, preferred_element_type=f32)


def chosen(flag, yes, no):
    return jnp.where(flag != 0, yes, no)


def halves(x_ref, rows):
    turned = x_ref[...].T
    return turned[:rows], turned[rows:]


def rounded(order, local):
    def kernel(s_ref, a_ref, out_ref):
        out_ref[...] = a_ref[...].astype(bf16)

    return order.call(
        kernel, [rowwise(local, 3)], [rowwise(shaped(bf16, *local.shape), 3)], (3,)
    )


def first_piece(order, normed, rows):
    tokens = normed.shape[0]

    def kernel(s_ref, x_ref, piece_ref):
        low, high = halves(x_ref, rows)
        piece_ref[...] = chosen(s_ref[Y], low, high)

    return order.call(
        kernel,
        [(normed, (tokens, 2 * rows), lambda i, s: (0, s[FAR]))],
        [whole(shaped(bf16, rows, tokens))],
        (1,),
    )


def split(order, normed, rows, g_pair, fixes):
    tokens = normed.shape[0]

    def kernel(s_ref, fix_ref, x_ref, g_ref, two_ref, last_ref, own_ref):
        i = pl.program_id(0)
        low, high = halves(x_ref, rows)
        own_ref[...] = chosen(s_ref[Y], high, low)

        @pl.when(i < 2)
        def _():
            two_ref[...] = chosen(s_ref[Y], low, high)

        @pl.when(i == 2)
        def _():
            last_ref[...] = chosen(s_ref[Y], low, high)

    return order.call(
        kernel,
        [
            (normed, (tokens, 2 * rows), lambda i, s, f: (0, s[(i + 1) % 4])),
            (g_pair, None, None),
        ],
        [
            (
                shaped(bf16, 2 * rows, tokens),
                (rows, tokens),
                lambda i, s, f: (jnp.minimum(i, 1), 0),
            ),
            (shaped(bf16, 3 * rows, tokens), (rows, tokens), lambda i, s, f: (0, 0)),
            (shaped(bf16, 4 * rows, tokens), (rows, tokens), lambda i, s, f: ((i + 1) % 4, 0)),
        ],
        (4,),
        expected["split"],
        fixes=fixes,
    )


def gradient_part(order, mine, k, theirs, at, key_grad, g_pair, scale, dtype, span):
    tokens, features = key_grad.shape
    rows = mine.shape[0] // 4

    def kernel(s_ref, x_ref, xp_ref, g_ref, gp_ref, out_ref):
        total = dot(x_ref[...], g_ref[...]) + dot(xp_ref[...], gp_ref[...])
        out_ref[...] = (total * scale).astype(dtype)

    return order.call(
        kernel,
        [
            stacked(mine, k, rows),
            stacked(theirs, at, rows),
            columnwise(key_grad, 2),
            columnwise(g_pair, 2),
        ],
        [columnwise(shaped(dtype, rows, features), 2)],
        (2,),
        span,
    )


def input_two(order, key_grad, g_pair, first, second, target, scale):
    tokens, features = key_grad.shape
    rows = first.shape[0]

    def kernel(s_ref, g_ref, gp_ref, a_ref, b_ref, target_ref, pair_ref, own_ref):
        weight = jnp.where(pl.program_id(0) == 0, a_ref[...], b_ref[...])
        pair_ref[...] = (dot_bt(weight, gp_ref[...]) * scale).astype(bf16)
        own_ref[...] = (dot_bt(weight, g_ref[...]) * scale).astype(bf16)

    return order.call(
        kernel,
        [whole(a) for a in (key_grad, g_pair, first, second)] + [(target, None, None)],
        [
            (target, (rows, tokens), lambda i, s: (1 + i, 0)),
            (shaped(bf16, 2 * rows, tokens), (rows, tokens), lambda i, s: (i, 0)),
        ],
        (2,),
        expected["input two"],
        {5: 0},
    )


def input_one(order, key_grad, g_pair, inner, part, end, scale, span, before=()):
    tokens, features = key_grad.shape
    rows = end.shape[0]

    def kernel(s_ref, g_ref, gp_ref, a_ref, b_ref, *rest):
        pair_ref, own_ref, w_ref = rest[len(before) :]
        weight = chosen(s_ref[INNER], a_ref[...], b_ref[...])
        w_ref[...] = weight
        pair_ref[...] = (dot_bt(weight, gp_ref[...]) * scale).astype(bf16)
        own_ref[...] = (dot_bt(weight, g_ref[...]) * scale).astype(bf16)

    out = whole(shaped(bf16, rows, tokens))
    return order.call(
        kernel,
        [whole(key_grad), whole(g_pair), stacked(inner, part, rows), whole(end)]
        + [(a, None, None) for a in before],
        [out, out, whole(shaped(bf16, rows, features))],
        (1,),
        span,
    )


def input_join(order, slots, own, others, shape, span, target=None, before=()):
    tokens = own[0][0][0].shape[1]
    tile = tokens // 3
    rows = shape[1] // 8
    flat = [
        (a, k, rows if len(piece) == 1 else a.shape[0]) for piece in own + others for a, k in piece
    ]
    kept = [a for a in (target, *before) if a is not None]

    def kernel(s_ref, *refs):
        values = iter([ref[...] for ref in refs[: len(flat)]])
        sides = [jnp.concatenate([next(values) for _ in piece], 0) for piece in own + others]
        first = pl.program_id(0) == 0
        mine = jnp.where(first, sides[0], sides[1])
        theirs = jnp.where(first, sides[2], sides[3])
        out_ref = refs[-1]

        @pl.when(s_ref[Y] == 0)
        def _():
            out_ref[...] = jnp.concatenate([mine, theirs], 0).T

        @pl.when(s_ref[Y] != 0)
        def _():
            out_ref[...] = jnp.concatenate([theirs, mine], 0).T

    def piece(array, k, height):
        return (array, (height, tile), lambda j, i, s: (k, i))

    return order.call(
        kernel,
        [piece(*p) for p in flat] + [(a, None, None) for a in kept],
        [(shaped(bf16, *shape), (tile, 2 * rows), lambda j, i, s: (i, s[slots[0] - j]))],
        (2, 3),
        span,
        None if target is None else {len(flat) + 1: 0},
    )


def key_sums(order, total, blocks, weights, span, scale=1.0, dtype=f32, before=()):
    features = weights[0].shape[1]
    tokens = blocks[0][0].shape[1]
    count = len(blocks)
    totals = [] if total is None else [columnwise(total, 2)]

    def kernel(s_ref, *refs):
        value = refs[2 * count][...] if totals else 0.0
        for x_ref, w_ref in zip(refs[:count], refs[count : 2 * count]):
            value += dot_t(x_ref[...], w_ref[...])
        refs[-1][...] = (value * scale).astype(dtype)

    return order.call(
        kernel,
        [stacked(x, k, w.shape[0]) for (x, k), w in zip(blocks, weights)]
        + [columnwise(w, 2) for w in weights]
        + totals
        + [(a, None, None) for a in before],
        [columnwise(shaped(dtype, tokens, features), 2)],
        (2,),
        span,
    )


def delta_halves(order, anchor, local):
    rows, features = local.shape

    def kernel(s_ref, a_ref, b_ref, c_ref, d_ref, own_ref, other_ref):
        own_ref[...] = a_ref[...] - b_ref[...]
        other_ref[...] = c_ref[...] - d_ref[...]

    def half(array, turned):
        def index(i, s):
            core = 1 - s[CORE] if turned else s[CORE]
            return (3 * core + i, 0)

        return (array, (rows // 6, features), index)

    out = rowwise(shaped(f32, rows // 2, features), 3)
    return order.call(
        kernel,
        [half(anchor, False), half(local, False), half(anchor, True), half(local, True)],
        [out, out],
        (3,),
    )


def total_of(order, here, there):
    def kernel(s_ref, a_ref, b_ref, out_ref):
        out_ref[...] = a_ref[...] + b_ref[...]

    return order.call(
        kernel, [rowwise(here, 3), rowwise(there, 3)], [rowwise(shaped(f32, *here.shape), 3)], (3,)
    )


def choose_sends(order, at_end, inside, beside):
    def kernel(s_ref, a_ref, b_ref, c_ref, out_ref, across_ref):
        out_ref[...] = chosen(s_ref[END], a_ref[...], b_ref[...])
        across_ref[...] = c_ref[...]

    out = rowwise(shaped(bf16, *inside.shape), 3)
    return order.call(
        kernel, [rowwise(a, 3) for a in (at_end, inside, beside)], [out, out], (3,), 0
    )


def first_handoff(order, p0, c1, p1, w_across):
    rows, features = p0.shape
    part = rows // 3

    def kernel(s_ref, p0_ref, c1_ref, p1_ref, w_ref, sum_a, send_a, sum_b, send_b):
        total = (p0_ref[...].astype(f32) + c1_ref[...].astype(f32)).astype(bf16)
        send = chosen(s_ref[END], p1_ref[...], w_ref[...])

        @pl.when(pl.program_id(0) < 2)
        def _():
            sum_a[...] = total
            send_a[...] = send

        @pl.when(pl.program_id(0) == 2)
        def _():
            sum_b[...] = total
            send_b[...] = send

    a = (
        shaped(bf16, 2 * part, features),
        (part, features),
        lambda i, s: (jnp.minimum(i, 1), 0),
    )
    b = whole(shaped(bf16, part, features))
    return order.call(
        kernel,
        [rowwise(x, 3) for x in (p0, c1, p1, w_across)],
        [a, a, b, b],
        (3,),
        expected["handoff"],
    )


def second_handoff(order, first, p1, c2, p2, q2, before, span):
    def kernel(s_ref, p1_ref, c2_ref, p2_ref, q2_ref, *rest):
        s1_ref, t_ref = rest[len(before) :]
        s1_ref[...] = (p1_ref[...].astype(f32) + c2_ref[...].astype(f32)).astype(bf16)
        t_ref[...] = (p2_ref[...] + q2_ref[...].astype(f32)).astype(bf16)

    sixth, features = p1.shape[0] // 6, p1.shape[1]
    steps = c2.shape[0] // sixth
    block = (sixth, features)
    out = rowwise(shaped(bf16, *c2.shape), steps)
    return order.call(
        kernel,
        [
            (p1, block, lambda i, s: (first + i, 0)),
            rowwise(c2, steps),
            (p2, block, lambda i, s: (first + i, 0)),
            rowwise(q2, steps),
        ]
        + [(a, None, None) for a in before],
        [out, out],
        (steps,),
        span,
    )


def nesterov_pass(order, own, other, anchor, momentum, local):
    rows, features = local.shape

    def kernel(s_ref, own_ref, other_ref, anchor_ref, momentum_ref, local_ref, *out):
        anchor_new_ref, moment_new_ref, base_ref = out
        in_own = pl.program_id(0) // 3 == s_ref[CORE]
        outer_grad = jnp.where(in_own, own_ref[...], other_ref[...]) / 4
        anchor_new, moment_new = nesterov(outer_grad, anchor_ref[...], momentum_ref[...])
        anchor_new_ref[...] = anchor_new
        moment_new_ref[...] = moment_new
        kept = mix_weight * (1.0 - inner_rate * weight_decay)
        base_ref[...] = kept * local_ref[...] + (1.0 - mix_weight) * anchor_new

    def half(array):
        return (array, (rows // 6, features), lambda i, s: (i % 3, 0))

    out = rowwise(shaped(f32, rows, features), 6)
    return order.call(
        kernel,
        [half(own), half(other)] + [rowwise(a, 6) for a in (anchor, momentum, local)],
        [out, out, out],
        (6,),
        expected["nesterov"],
    )


def final_update(order, first, fixes, p3, qa, qb, first_old, second_old, base, made=(), keys=()):
    rows, features = base.shape
    block = (rows // 6, features)
    steps = qa.shape[0] // block[0]
    scale = keys[2] if keys else None

    def kernel(s_ref, fix_ref, p_ref, a_ref, b_ref, first_ref, second_ref, base_ref, *rest):
        outs = rest[len(keys[:2]) + len(made) :]
        gradient = p_ref[...] + a_ref[...].astype(f32) + b_ref[...].astype(f32)
        first_new = beta_first * first_ref[...] + (1.0 - beta_first) * gradient
        second_new = beta_second * second_ref[...] + (1.0 - beta_second) * gradient * gradient
        root = jnp.sqrt(second_new * fix_ref[1]) + epsilon
        step = (mix_weight * inner_rate) * fix_ref[0]
        outs[0][...] = base_ref[...] - step * first_new / root
        outs[1][...] = first_new
        outs[2][...] = second_new
        if keys:
            outs[3][...] = (rest[0][...] * scale + rest[1][...].astype(f32)).astype(bf16)

    def at(array, offset):
        return (array, block, lambda i, *_: (offset + i, 0))

    out = at(shaped(f32, rows, features), first)
    inputs = [at(p3, first), rowwise(qa, steps), rowwise(qb, steps)]
    inputs += [at(a, first) for a in (first_old, second_old, base)]
    inputs += [rowwise(a, steps) for a in keys[:2]]
    aliases = {2 + len(inputs) + i: i for i in range(len(made))}
    return order.call(
        kernel,
        inputs + [(a, None, None) for a in made],
        [out] * 3 + ([rowwise(shaped(bf16, *keys[0].shape), steps)] if keys else []),
        (steps,),
        0 if keys else expected["first half"],
        aliases,
        fixes,
    )


def pair_pass(normed, key_grad, local, first_old, second_old, anchor, momentum, inner_step):
    width = normed.shape[1]
    rows = local.shape[0]
    scale = width ** (-0.5)
    me = lax.axis_index("fsdp")
    core = lax.axis_index("rep") % 2
    y, z = me % 2, me // 2
    inside = (z == 1) | (z == 2)
    far = jnp.where(z < 2, 3, 0)
    middle = jnp.where(z < 2, 2, 1)
    order = Order(jnp.stack([far, middle, z ^ 1, z, y, inside, ~inside, core]).astype(jnp.int32))

    def along(links):
        pairs = [(2 * a + c, 2 * b + c) for a, b in links for c in (0, 1)]
        return lambda value: lax.ppermute(value, "fsdp", pairs)

    outer = along([(0, 1), (1, 0), (2, 3), (3, 2)])
    inner = along([(1, 2), (2, 1)])

    def swap(value):
        return lax.ppermute(value, "fsdp", [(i, i ^ 1) for i in range(8)])

    def replica(value, bit):
        return lax.ppermute(value, "rep", [(i, i ^ bit) for i in range(4)])

    g_pair = swap(key_grad)
    weight = rounded(order, local)
    w_beside = outer(weight)
    w_inner = inner(weight)
    x0 = swap(first_piece(order, normed, rows))
    own_delta, other_delta = delta_halves(order, anchor, local)
    delta_core = replica(other_delta, 1)
    fixes = 1.0 / jnp.stack(corrections(inner_step))
    two, three, mine = split(order, normed, rows, g_pair, fixes)
    x12 = swap(two)
    delta = total_of(order, own_delta, delta_core)
    delta_there = replica(delta, 2)

    def partial(k, theirs, at, dtype, span):
        return gradient_part(order, mine, k, theirs, at, key_grad, g_pair, scale, dtype, span)

    p0 = partial(0, x0, 0, bf16, expected["first part"])
    send, across = choose_sends(order, p0, w_inner, w_beside)
    c1 = outer(send)
    w_across = inner(across)
    three, own01 = input_two(order, key_grad, g_pair, weight, w_beside, three, scale)
    x3 = swap(three)
    known = (w_beside, weight)
    own_total = key_sums(order, None, [(mine, 2), (mine, 3)], known, expected["early own"])
    total = total_of(order, delta, delta_there)
    total_there = replica(total, 1)
    p1 = partial(1, x12, 0, bf16, expected["second part"])
    p2 = partial(2, x12, 1, f32, 1)
    anchor_new, moment_new, base = nesterov_pass(
        order, total, total_there, anchor, momentum, local
    )
    pair_total = key_sums(order, None, [(x12, 1)], known[:1], expected["early pair"])

    s0a, send_a, s0b, send_b = first_handoff(order, p0, c1, p1, w_across)
    c2a, q2a = outer(send_a), inner(s0a)
    c2b, q2b = outer(send_b), inner(s0b)
    i2, own2, w_middle = input_one(
        order, key_grad, g_pair, w_inner, 0, c1, scale, expected["input middle"]
    )
    g2 = swap(i2)
    input_grad = input_join(
        order,
        (OWN, BESIDE),
        [[(own01, 0)], [(own01, 1)]],
        [[(x3, 1)], [(x3, 2)]],
        normed.shape,
        expected["join two"],
    )
    i3, own3a, w_far_a = input_one(
        order, key_grad, g_pair, w_across, 0, c2a, scale, expected["input far"], [x3]
    )
    g3a = swap(i3)
    s1, t = second_handoff(order, 0, p1, c2a, p2, q2a, [x3], expected["early sums"])
    qaa, qba = outer(t), inner(s1)
    pair_total = key_sums(
        order,
        pair_total,
        [(x12, 0), (x3, 0)],
        (w_middle, weight),
        expected["pair sums"],
        before=[g2],
    )
    p3 = partial(3, x3, 0, f32, 0)
    i3, own3b, w_far_b = input_one(
        order, key_grad, g_pair, w_across, 2, c2b, scale, expected["input last"]
    )
    g3b = swap(i3)
    w_far = (w_far_a, w_far_b)
    key_pair = swap(
        key_sums(order, pair_total, [(x0, 0), (x0, 2)], w_far, 0, scale, bf16, [q2b])
    )
    s1, t = second_handoff(order, 4, p1, c2b, p2, q2b, [g3a, g3b], expected["late sums"])
    qab, qbb = outer(t), inner(s1)
    own_total = key_sums(
        order,
        own_total,
        [(mine, 1), (mine, 0), (mine, 2)],
        (w_middle, *w_far),
        expected["own sums"],
    )
    input_grad = input_join(
        order,
        (MIDDLE, FAR),
        [[(own2, 0)], [(own3a, 0), (own3b, 0)]],
        [[(g2, 0)], [(g3a, 0), (g3b, 0)]],
        normed.shape,
        expected["join last"],
        input_grad,
    )
    state = (first_old, second_old, base)
    made = final_update(order, 0, fixes, p3, qaa, qba, *state)
    merged, first_new, second_new, keys = final_update(
        order, 4, fixes, p3, qab, qbb, *state, made, (own_total, key_pair, scale)
    )
    return (keys, input_grad, merged, first_new, second_new, anchor_new, moment_new)


def body(normed, key_grad, master, first_moment, second_moment, anchor, momentum, inner_step):
    local = master[0]
    sizes = (lax.axis_size("rep"), lax.axis_size("fsdp"))
    inner_pass = pair_pass if sizes == (4, 8) else whole_pass
    keys, input_grad, merged, first_new, second_new, anchor_new, moment_new = inner_pass(
        normed, key_grad, local, first_moment[0], second_moment[0], anchor, momentum, inner_step
    )
    return (
        keys,
        input_grad,
        merged[None],
        first_new[None],
        second_new[None],
        anchor_new,
        moment_new,
    )


def solution(mesh):
    in_specs = (
        P(("rep", "fsdp"), None),
        P(("rep", "fsdp"), None),
        P("rep", "fsdp", None),
        P("rep", "fsdp", None),
        P("rep", "fsdp", None),
        P("fsdp", None),
        P("fsdp", None),
        P(),
    )
    out_specs = (
        P(("rep", "fsdp"), None),
        P(("rep", "fsdp"), None),
        P("rep", "fsdp", None),
        P("rep", "fsdp", None),
        P("rep", "fsdp", None),
        P("fsdp", None),
        P("fsdp", None),
    )
    return jax.shard_map(body, mesh=mesh, in_specs=in_specs, out_specs=out_specs, check_vma=False)
```

```python
import jax
import jax.numpy as jnp
from jax import lax
from jax.experimental import pallas as pl
from jax.experimental.pallas import tpu as pltpu
from jax.sharding import PartitionSpec as P

beta_first = 0.9
beta_second = 0.95
inner_rate = 0.1
weight_decay = 0.1
epsilon = 1e-08
outer_rate = 0.7
outer_mu = 0.9
mix_weight = 0.5

f32 = jnp.float32
bf16 = jnp.bfloat16
vmem_bytes = 16 * 1024 * 1024

expected = {
    "split": 30,
    "first part": 0,
    "input two": 12,
    "second part": 30,
    "nesterov": 1,
    "early own": 0,
    "early pair": 0,
    "handoff": 1,
    "input middle": 0,
    "join two": 0,
    "input far": 0,
    "input last": 12,
    "early sums": 1,
    "pair sums": 0,
    "late sums": 1,
    "own sums": 0,
    "join last": 0,
    "first half": 12,
}


def corrections(inner_step):
    count_float = inner_step[0].astype(f32)
    fix_first = 1.0 - jnp.power(f32(beta_first), count_float)
    fix_second = 1.0 - jnp.power(f32(beta_second), count_float)
    return fix_first, fix_second


def adam(gradient, local, first_old, second_old, fix_first, fix_second):
    first_new = beta_first * first_old + (1.0 - beta_first) * gradient
    second_new = beta_second * second_old + (1.0 - beta_second) * gradient * gradient
    direction = first_new / fix_first / (jnp.sqrt(second_new / fix_second) + epsilon)
    stepped = local - inner_rate * (direction + weight_decay * local)
    return (stepped, first_new, second_new)


def nesterov(outer_grad, anchor_rows, moment_rows):
    moment_new = outer_mu * moment_rows + outer_grad
    anchor_new = anchor_rows - outer_rate * (outer_grad + outer_mu * moment_new)
    return (anchor_new, moment_new)


def outer_update(local, anchor, momentum):
    summed = lax.psum(anchor - local, "rep")
    return nesterov(summed / lax.axis_size("rep"), anchor, momentum)


def whole_pass(normed, key_grad, local, first_old, second_old, anchor, momentum, inner_step):
    scale = normed.shape[1] ** (-0.5)
    weight = lax.all_gather(local.astype(bf16), "fsdp", axis=0, tiled=True)
    keys = (jnp.dot(normed, weight, preferred_element_type=f32) * scale).astype(bf16)
    input_grad = (
        lax.dot_general(key_grad, weight, (((1,), (1,)), ((), ())), preferred_element_type=f32)
        * scale
    ).astype(bf16)
    gradient = lax.psum_scatter(
        lax.dot_general(normed, key_grad, (((0,), (0,)), ((), ())), preferred_element_type=f32)
        * scale,
        "fsdp",
        scatter_dimension=0,
        tiled=True,
    )
    stepped, first_new, second_new = adam(
        gradient, local, first_old, second_old, *corrections(inner_step)
    )
    anchor_new, moment_new = outer_update(local, anchor, momentum)
    merged = mix_weight * stepped + (1.0 - mix_weight) * anchor_new
    return (keys, input_grad, merged, first_new, second_new, anchor_new, moment_new)


FAR, MIDDLE, BESIDE, OWN, Y, INNER, END, CORE = range(8)


class Order:
    def __init__(self, place):
        self.place = place
        self.token = None

    def call(self, kernel, inputs, outputs, grid, span=1, aliases=None, fixes=None):
        scalars = [self.place] + ([] if fixes is None else [fixes])
        tokens = [] if self.token is None else [self.token]
        before = len(scalars) + len(inputs)

        def wrapped(*refs):
            refs[-1][...] = jnp.zeros_like(refs[-1])
            kernel(*refs[:before], *refs[before + len(tokens) : -1])

        outputs = outputs + [whole(shaped(jnp.int32, 8, 128))]
        shapes = [shape for shape, _, _ in outputs]
        keep = pl.BlockSpec(memory_space=pl.ANY)
        out = pl.pallas_call(
            wrapped,
            out_shape=shapes,
            grid_spec=pltpu.PrefetchScalarGridSpec(
                num_scalar_prefetch=len(scalars),
                grid=grid,
                in_specs=[
                    keep if block is None else pl.BlockSpec(block, index)
                    for _, block, index in inputs
                ]
                + [keep] * len(tokens),
                out_specs=[pl.BlockSpec(block, index) for _, block, index in outputs],
            ),
            input_output_aliases=aliases or {},
            compiler_params=pltpu.CompilerParams(vmem_limit_bytes=vmem_bytes),
            cost_estimate=pl.CostEstimate(
                flops=int(span * 1e9), bytes_accessed=0, transcendentals=0
            ),
        )(*scalars, *[a for a, _, _ in inputs], *tokens)
        self.token = out[-1]
        return out[0] if len(out) == 2 else out[:-1]


def shaped(dtype, *shape):
    return jax.ShapeDtypeStruct(shape, dtype)


def whole(array):
    zeros = (0,) * len(array.shape)
    return (array, array.shape, lambda *_: zeros)


def rowwise(array, steps):
    return (array, (array.shape[0] // steps, array.shape[1]), lambda i, *_: (i, 0))


def columnwise(array, steps):
    return (array, (array.shape[0], array.shape[1] // steps), lambda i, *_: (0, i))


def stacked(array, k, rows):
    return (array, (rows, array.shape[1]), lambda *_: (k, 0))


def dot_t(a, b):
    return lax.dot_general(a, b, (((0,), (0,)), ((), ())), preferred_element_type=f32)


def dot_bt(a, b):
    return lax.dot_general(a, b, (((1,), (1,)), ((), ())), preferred_element_type=f32)


def dot(a, b):
    return jnp.dot(a, b, preferred_element_type=f32)


def chosen(flag, yes, no):
    return jnp.where(flag != 0, yes, no)


def halves(x_ref, rows):
    turned = x_ref[...].T
    return turned[:rows], turned[rows:]


def rounded(order, local):
    def kernel(s_ref, a_ref, out_ref):
        out_ref[...] = a_ref[...].astype(bf16)

    return order.call(
        kernel, [rowwise(local, 3)], [rowwise(shaped(bf16, *local.shape), 3)], (3,)
    )


def first_piece(order, normed, rows):
    tokens = normed.shape[0]

    def kernel(s_ref, x_ref, piece_ref):
        low, high = halves(x_ref, rows)
        piece_ref[...] = chosen(s_ref[Y], low, high)

    return order.call(
        kernel,
        [(normed, (tokens, 2 * rows), lambda i, s: (0, s[FAR]))],
        [whole(shaped(bf16, rows, tokens))],
        (1,),
    )


def split(order, normed, rows, g_pair, fixes):
    tokens = normed.shape[0]

    def kernel(s_ref, fix_ref, x_ref, g_ref, two_ref, last_ref, own_ref):
        i = pl.program_id(0)
        low, high = halves(x_ref, rows)
        own_ref[...] = chosen(s_ref[Y], high, low)

        @pl.when(i < 2)
        def _():
            two_ref[...] = chosen(s_ref[Y], low, high)

        @pl.when(i == 2)
        def _():
            last_ref[...] = chosen(s_ref[Y], low, high)

    return order.call(
        kernel,
        [
            (normed, (tokens, 2 * rows), lambda i, s, f: (0, s[(i + 1) % 4])),
            (g_pair, None, None),
        ],
        [
            (
                shaped(bf16, 2 * rows, tokens),
                (rows, tokens),
                lambda i, s, f: (jnp.minimum(i, 1), 0),
            ),
            (shaped(bf16, 3 * rows, tokens), (rows, tokens), lambda i, s, f: (0, 0)),
            (shaped(bf16, 4 * rows, tokens), (rows, tokens), lambda i, s, f: ((i + 1) % 4, 0)),
        ],
        (4,),
        expected["split"],
        fixes=fixes,
    )


def gradient_part(order, mine, k, theirs, at, key_grad, g_pair, scale, dtype, span):
    tokens, features = key_grad.shape
    rows = mine.shape[0] // 4

    def kernel(s_ref, x_ref, xp_ref, g_ref, gp_ref, out_ref):
        total = dot(x_ref[...], g_ref[...]) + dot(xp_ref[...], gp_ref[...])
        out_ref[...] = (total * scale).astype(dtype)

    return order.call(
        kernel,
        [
            stacked(mine, k, rows),
            stacked(theirs, at, rows),
            columnwise(key_grad, 2),
            columnwise(g_pair, 2),
        ],
        [columnwise(shaped(dtype, rows, features), 2)],
        (2,),
        span,
    )


def input_two(order, key_grad, g_pair, first, second, target, scale):
    tokens, features = key_grad.shape
    rows = first.shape[0]

    def kernel(s_ref, g_ref, gp_ref, a_ref, b_ref, target_ref, pair_ref, own_ref):
        weight = jnp.where(pl.program_id(0) == 0, a_ref[...], b_ref[...])
        pair_ref[...] = (dot_bt(weight, gp_ref[...]) * scale).astype(bf16)
        own_ref[...] = (dot_bt(weight, g_ref[...]) * scale).astype(bf16)

    return order.call(
        kernel,
        [whole(a) for a in (key_grad, g_pair, first, second)] + [(target, None, None)],
        [
            (target, (rows, tokens), lambda i, s: (1 + i, 0)),
            (shaped(bf16, 2 * rows, tokens), (rows, tokens), lambda i, s: (i, 0)),
        ],
        (2,),
        expected["input two"],
        {5: 0},
    )


def input_one(order, key_grad, g_pair, inner, part, end, scale, span, before=()):
    tokens, features = key_grad.shape
    rows = end.shape[0]

    def kernel(s_ref, g_ref, gp_ref, a_ref, b_ref, *rest):
        pair_ref, own_ref, w_ref = rest[len(before) :]
        weight = chosen(s_ref[INNER], a_ref[...], b_ref[...])
        w_ref[...] = weight
        pair_ref[...] = (dot_bt(weight, gp_ref[...]) * scale).astype(bf16)
        own_ref[...] = (dot_bt(weight, g_ref[...]) * scale).astype(bf16)

    out = whole(shaped(bf16, rows, tokens))
    return order.call(
        kernel,
        [whole(key_grad), whole(g_pair), stacked(inner, part, rows), whole(end)]
        + [(a, None, None) for a in before],
        [out, out, whole(shaped(bf16, rows, features))],
        (1,),
        span,
    )


def input_join(order, slots, own, others, shape, span, target=None, before=()):
    tokens = own[0][0][0].shape[1]
    tile = tokens // 3
    rows = shape[1] // 8
    flat = [
        (a, k, rows if len(piece) == 1 else a.shape[0]) for piece in own + others for a, k in piece
    ]
    kept = [a for a in (target, *before) if a is not None]

    def kernel(s_ref, *refs):
        values = iter([ref[...] for ref in refs[: len(flat)]])
        sides = [jnp.concatenate([next(values) for _ in piece], 0) for piece in own + others]
        first = pl.program_id(0) == 0
        mine = jnp.where(first, sides[0], sides[1])
        theirs = jnp.where(first, sides[2], sides[3])
        out_ref = refs[-1]

        @pl.when(s_ref[Y] == 0)
        def _():
            out_ref[...] = jnp.concatenate([mine, theirs], 0).T

        @pl.when(s_ref[Y] != 0)
        def _():
            out_ref[...] = jnp.concatenate([theirs, mine], 0).T

    def piece(array, k, height):
        return (array, (height, tile), lambda j, i, s: (k, i))

    return order.call(
        kernel,
        [piece(*p) for p in flat] + [(a, None, None) for a in kept],
        [(shaped(bf16, *shape), (tile, 2 * rows), lambda j, i, s: (i, s[slots[0] - j]))],
        (2, 3),
        span,
        None if target is None else {len(flat) + 1: 0},
    )


def key_sums(order, total, blocks, weights, span, scale=1.0, dtype=f32, before=()):
    features = weights[0].shape[1]
    tokens = blocks[0][0].shape[1]
    count = len(blocks)
    totals = [] if total is None else [columnwise(total, 2)]

    def kernel(s_ref, *refs):
        value = refs[2 * count][...] if totals else 0.0
        for x_ref, w_ref in zip(refs[:count], refs[count : 2 * count]):
            value += dot_t(x_ref[...], w_ref[...])
        refs[-1][...] = (value * scale).astype(dtype)

    return order.call(
        kernel,
        [stacked(x, k, w.shape[0]) for (x, k), w in zip(blocks, weights)]
        + [columnwise(w, 2) for w in weights]
        + totals
        + [(a, None, None) for a in before],
        [columnwise(shaped(dtype, tokens, features), 2)],
        (2,),
        span,
    )


def delta_halves(order, anchor, local):
    rows, features = local.shape

    def kernel(s_ref, a_ref, b_ref, c_ref, d_ref, own_ref, other_ref):
        own_ref[...] = a_ref[...] - b_ref[...]
        other_ref[...] = c_ref[...] - d_ref[...]

    def half(array, turned):
        def index(i, s):
            core = 1 - s[CORE] if turned else s[CORE]
            return (3 * core + i, 0)

        return (array, (rows // 6, features), index)

    out = rowwise(shaped(f32, rows // 2, features), 3)
    return order.call(
        kernel,
        [half(anchor, False), half(local, False), half(anchor, True), half(local, True)],
        [out, out],
        (3,),
    )


def total_of(order, here, there):
    def kernel(s_ref, a_ref, b_ref, out_ref):
        out_ref[...] = a_ref[...] + b_ref[...]

    return order.call(
        kernel, [rowwise(here, 3), rowwise(there, 3)], [rowwise(shaped(f32, *here.shape), 3)], (3,)
    )


def choose_sends(order, at_end, inside, beside):
    def kernel(s_ref, a_ref, b_ref, c_ref, out_ref, across_ref):
        out_ref[...] = chosen(s_ref[END], a_ref[...], b_ref[...])
        across_ref[...] = c_ref[...]

    out = rowwise(shaped(bf16, *inside.shape), 3)
    return order.call(
        kernel, [rowwise(a, 3) for a in (at_end, inside, beside)], [out, out], (3,), 0
    )


def first_handoff(order, p0, c1, p1, w_across):
    rows, features = p0.shape
    part = rows // 3

    def kernel(s_ref, p0_ref, c1_ref, p1_ref, w_ref, sum_a, send_a, sum_b, send_b):
        total = (p0_ref[...].astype(f32) + c1_ref[...].astype(f32)).astype(bf16)
        send = chosen(s_ref[END], p1_ref[...], w_ref[...])

        @pl.when(pl.program_id(0) < 2)
        def _():
            sum_a[...] = total
            send_a[...] = send

        @pl.when(pl.program_id(0) == 2)
        def _():
            sum_b[...] = total
            send_b[...] = send

    a = (
        shaped(bf16, 2 * part, features),
        (part, features),
        lambda i, s: (jnp.minimum(i, 1), 0),
    )
    b = whole(shaped(bf16, part, features))
    return order.call(
        kernel,
        [rowwise(x, 3) for x in (p0, c1, p1, w_across)],
        [a, a, b, b],
        (3,),
        expected["handoff"],
    )


def second_handoff(order, first, p1, c2, p2, q2, before, span):
    def kernel(s_ref, p1_ref, c2_ref, p2_ref, q2_ref, *rest):
        s1_ref, t_ref = rest[len(before) :]
        s1_ref[...] = (p1_ref[...].astype(f32) + c2_ref[...].astype(f32)).astype(bf16)
        t_ref[...] = (p2_ref[...] + q2_ref[...].astype(f32)).astype(bf16)

    sixth, features = p1.shape[0] // 6, p1.shape[1]
    steps = c2.shape[0] // sixth
    block = (sixth, features)
    out = rowwise(shaped(bf16, *c2.shape), steps)
    return order.call(
        kernel,
        [
            (p1, block, lambda i, s: (first + i, 0)),
            rowwise(c2, steps),
            (p2, block, lambda i, s: (first + i, 0)),
            rowwise(q2, steps),
        ]
        + [(a, None, None) for a in before],
        [out, out],
        (steps,),
        span,
    )


def nesterov_pass(order, own, other, anchor, momentum, local):
    rows, features = local.shape

    def kernel(s_ref, own_ref, other_ref, anchor_ref, momentum_ref, local_ref, *out):
        anchor_new_ref, moment_new_ref, base_ref = out
        in_own = pl.program_id(0) // 3 == s_ref[CORE]
        outer_grad = jnp.where(in_own, own_ref[...], other_ref[...]) / 4
        anchor_new, moment_new = nesterov(outer_grad, anchor_ref[...], momentum_ref[...])
        anchor_new_ref[...] = anchor_new
        moment_new_ref[...] = moment_new
        kept = mix_weight * (1.0 - inner_rate * weight_decay)
        base_ref[...] = kept * local_ref[...] + (1.0 - mix_weight) * anchor_new

    def half(array):
        return (array, (rows // 6, features), lambda i, s: (i % 3, 0))

    out = rowwise(shaped(f32, rows, features), 6)
    return order.call(
        kernel,
        [half(own), half(other)] + [rowwise(a, 6) for a in (anchor, momentum, local)],
        [out, out, out],
        (6,),
        expected["nesterov"],
    )


def final_update(order, first, fixes, p3, qa, qb, first_old, second_old, base, made=(), keys=()):
    rows, features = base.shape
    block = (rows // 6, features)
    steps = qa.shape[0] // block[0]
    scale = keys[2] if keys else None

    def kernel(s_ref, fix_ref, p_ref, a_ref, b_ref, first_ref, second_ref, base_ref, *rest):
        outs = rest[len(keys[:2]) + len(made) :]
        gradient = p_ref[...] + a_ref[...].astype(f32) + b_ref[...].astype(f32)
        first_new = beta_first * first_ref[...] + (1.0 - beta_first) * gradient
        second_new = beta_second * second_ref[...] + (1.0 - beta_second) * gradient * gradient
        root = jnp.sqrt(second_new * fix_ref[1]) + epsilon
        step = (mix_weight * inner_rate) * fix_ref[0]
        outs[0][...] = base_ref[...] - step * first_new / root
        outs[1][...] = first_new
        outs[2][...] = second_new
        if keys:
            outs[3][...] = (rest[0][...] * scale + rest[1][...].astype(f32)).astype(bf16)

    def at(array, offset):
        return (array, block, lambda i, *_: (offset + i, 0))

    out = at(shaped(f32, rows, features), first)
    inputs = [at(p3, first), rowwise(qa, steps), rowwise(qb, steps)]
    inputs += [at(a, first) for a in (first_old, second_old, base)]
    inputs += [rowwise(a, steps) for a in keys[:2]]
    aliases = {2 + len(inputs) + i: i for i in range(len(made))}
    return order.call(
        kernel,
        inputs + [(a, None, None) for a in made],
        [out] * 3 + ([rowwise(shaped(bf16, *keys[0].shape), steps)] if keys else []),
        (steps,),
        0 if keys else expected["first half"],
        aliases,
        fixes,
    )


def pair_pass(normed, key_grad, local, first_old, second_old, anchor, momentum, inner_step):
    width = normed.shape[1]
    rows = local.shape[0]
    scale = width ** (-0.5)
    me = lax.axis_index("fsdp")
    core = lax.axis_index("rep") % 2
    y, z = me % 2, me // 2
    inside = (z == 1) | (z == 2)
    far = jnp.where(z < 2, 3, 0)
    middle = jnp.where(z < 2, 2, 1)
    order = Order(jnp.stack([far, middle, z ^ 1, z, y, inside, ~inside, core]).astype(jnp.int32))

    def along(links):
        pairs = [(2 * a + c, 2 * b + c) for a, b in links for c in (0, 1)]
        return lambda value: lax.ppermute(value, "fsdp", pairs)

    outer = along([(0, 1), (1, 0), (2, 3), (3, 2)])
    inner = along([(1, 2), (2, 1)])

    def swap(value):
        return lax.ppermute(value, "fsdp", [(i, i ^ 1) for i in range(8)])

    def replica(value, bit):
        return lax.ppermute(value, "rep", [(i, i ^ bit) for i in range(4)])

    g_pair = swap(key_grad)
    weight = rounded(order, local)
    w_beside = outer(weight)
    w_inner = inner(weight)
    x0 = swap(first_piece(order, normed, rows))
    own_delta, other_delta = delta_halves(order, anchor, local)
    delta_core = replica(other_delta, 1)
    fixes = 1.0 / jnp.stack(corrections(inner_step))
    two, three, mine = split(order, normed, rows, g_pair, fixes)
    x12 = swap(two)
    delta = total_of(order, own_delta, delta_core)
    delta_there = replica(delta, 2)

    def partial(k, theirs, at, dtype, span):
        return gradient_part(order, mine, k, theirs, at, key_grad, g_pair, scale, dtype, span)

    p0 = partial(0, x0, 0, bf16, expected["first part"])
    send, across = choose_sends(order, p0, w_inner, w_beside)
    c1 = outer(send)
    w_across = inner(across)
    three, own01 = input_two(order, key_grad, g_pair, weight, w_beside, three, scale)
    x3 = swap(three)
    known = (w_beside, weight)
    own_total = key_sums(order, None, [(mine, 2), (mine, 3)], known, expected["early own"])
    total = total_of(order, delta, delta_there)
    total_there = replica(total, 1)
    p1 = partial(1, x12, 0, bf16, expected["second part"])
    p2 = partial(2, x12, 1, f32, 1)
    anchor_new, moment_new, base = nesterov_pass(
        order, total, total_there, anchor, momentum, local
    )
    pair_total = key_sums(order, None, [(x12, 1)], known[:1], expected["early pair"])

    s0a, send_a, s0b, send_b = first_handoff(order, p0, c1, p1, w_across)
    c2a, q2a = outer(send_a), inner(s0a)
    c2b, q2b = outer(send_b), inner(s0b)
    i2, own2, w_middle = input_one(
        order, key_grad, g_pair, w_inner, 0, c1, scale, expected["input middle"]
    )
    g2 = swap(i2)
    input_grad = input_join(
        order,
        (OWN, BESIDE),
        [[(own01, 0)], [(own01, 1)]],
        [[(x3, 1)], [(x3, 2)]],
        normed.shape,
        expected["join two"],
    )
    p3 = partial(3, x3, 0, f32, 0)
    i3, own3a, w_far_a = input_one(
        order, key_grad, g_pair, w_across, 0, c2a, scale, expected["input far"], [x3]
    )
    g3a = swap(i3)
    s1, t = second_handoff(order, 0, p1, c2a, p2, q2a, [x3], expected["early sums"])
    qaa, qba = outer(t), inner(s1)
    pair_total = key_sums(
        order,
        pair_total,
        [(x12, 0), (x3, 0)],
        (w_middle, weight),
        expected["pair sums"],
        before=[g2],
    )
    i3, own3b, w_far_b = input_one(
        order, key_grad, g_pair, w_across, 2, c2b, scale, expected["input last"]
    )
    g3b = swap(i3)
    w_far = (w_far_a, w_far_b)
    key_pair = swap(
        key_sums(order, pair_total, [(x0, 0), (x0, 2)], w_far, 0, scale, bf16, [q2b])
    )
    s1, t = second_handoff(order, 4, p1, c2b, p2, q2b, [g3a, g3b], expected["late sums"])
    qab, qbb = outer(t), inner(s1)
    own_total = key_sums(
        order,
        own_total,
        [(mine, 1), (mine, 0), (mine, 2)],
        (w_middle, *w_far),
        expected["own sums"],
    )
    input_grad = input_join(
        order,
        (MIDDLE, FAR),
        [[(own2, 0)], [(own3a, 0), (own3b, 0)]],
        [[(g2, 0)], [(g3a, 0), (g3b, 0)]],
        normed.shape,
        expected["join last"],
        input_grad,
    )
    state = (first_old, second_old, base)
    made = final_update(order, 0, fixes, p3, qaa, qba, *state)
    merged, first_new, second_new, keys = final_update(
        order, 4, fixes, p3, qab, qbb, *state, made, (own_total, key_pair, scale)
    )
    return (keys, input_grad, merged, first_new, second_new, anchor_new, moment_new)


def body(normed, key_grad, master, first_moment, second_moment, anchor, momentum, inner_step):
    local = master[0]
    sizes = (lax.axis_size("rep"), lax.axis_size("fsdp"))
    inner_pass = pair_pass if sizes == (4, 8) else whole_pass
    keys, input_grad, merged, first_new, second_new, anchor_new, moment_new = inner_pass(
        normed, key_grad, local, first_moment[0], second_moment[0], anchor, momentum, inner_step
    )
    return (
        keys,
        input_grad,
        merged[None],
        first_new[None],
        second_new[None],
        anchor_new,
        moment_new,
    )


def solution(mesh):
    in_specs = (
        P(("rep", "fsdp"), None),
        P(("rep", "fsdp"), None),
        P("rep", "fsdp", None),
        P("rep", "fsdp", None),
        P("rep", "fsdp", None),
        P("fsdp", None),
        P("fsdp", None),
        P(),
    )
    out_specs = (
        P(("rep", "fsdp"), None),
        P(("rep", "fsdp"), None),
        P("rep", "fsdp", None),
        P("rep", "fsdp", None),
        P("rep", "fsdp", None),
        P("fsdp", None),
        P("fsdp", None),
    )
    return jax.shard_map(body, mesh=mesh, in_specs=in_specs, out_specs=out_specs, check_vma=False)
```

```python
import jax
import jax.numpy as jnp
from jax import lax
from jax.experimental import pallas as pl
from jax.experimental.pallas import tpu as pltpu
from jax.sharding import PartitionSpec as P

beta_first = 0.9
beta_second = 0.95
inner_rate = 0.1
weight_decay = 0.1
epsilon = 1e-08
outer_rate = 0.7
outer_mu = 0.9
mix_weight = 0.5

f32 = jnp.float32
bf16 = jnp.bfloat16
vmem_bytes = 16 * 1024 * 1024

expected = {
    "split": 30,
    "first part": 0,
    "input two": 12,
    "second part": 30,
    "nesterov": 1,
    "early own": 0,
    "early pair": 0,
    "handoff": 1,
    "input middle": 0,
    "join two": 0,
    "input far": 0,
    "input last": 12,
    "early sums": 1,
    "pair sums": 0,
    "late sums": 1,
    "own sums": 0,
    "join last": 0,
    "first half": 12,
}


def corrections(inner_step):
    count_float = inner_step[0].astype(f32)
    fix_first = 1.0 - jnp.power(f32(beta_first), count_float)
    fix_second = 1.0 - jnp.power(f32(beta_second), count_float)
    return fix_first, fix_second


def adam(gradient, local, first_old, second_old, fix_first, fix_second):
    first_new = beta_first * first_old + (1.0 - beta_first) * gradient
    second_new = beta_second * second_old + (1.0 - beta_second) * gradient * gradient
    direction = first_new / fix_first / (jnp.sqrt(second_new / fix_second) + epsilon)
    stepped = local - inner_rate * (direction + weight_decay * local)
    return (stepped, first_new, second_new)


def nesterov(outer_grad, anchor_rows, moment_rows):
    moment_new = outer_mu * moment_rows + outer_grad
    anchor_new = anchor_rows - outer_rate * (outer_grad + outer_mu * moment_new)
    return (anchor_new, moment_new)


def outer_update(local, anchor, momentum):
    summed = lax.psum(anchor - local, "rep")
    return nesterov(summed / lax.axis_size("rep"), anchor, momentum)


def whole_pass(normed, key_grad, local, first_old, second_old, anchor, momentum, inner_step):
    scale = normed.shape[1] ** (-0.5)
    weight = lax.all_gather(local.astype(bf16), "fsdp", axis=0, tiled=True)
    keys = (jnp.dot(normed, weight, preferred_element_type=f32) * scale).astype(bf16)
    input_grad = (
        lax.dot_general(key_grad, weight, (((1,), (1,)), ((), ())), preferred_element_type=f32)
        * scale
    ).astype(bf16)
    gradient = lax.psum_scatter(
        lax.dot_general(normed, key_grad, (((0,), (0,)), ((), ())), preferred_element_type=f32)
        * scale,
        "fsdp",
        scatter_dimension=0,
        tiled=True,
    )
    stepped, first_new, second_new = adam(
        gradient, local, first_old, second_old, *corrections(inner_step)
    )
    anchor_new, moment_new = outer_update(local, anchor, momentum)
    merged = mix_weight * stepped + (1.0 - mix_weight) * anchor_new
    return (keys, input_grad, merged, first_new, second_new, anchor_new, moment_new)


FAR, MIDDLE, BESIDE, OWN, Y, INNER, END, CORE = range(8)


class Order:
    def __init__(self, place):
        self.place = place
        self.token = None

    def call(self, kernel, inputs, outputs, grid, span=1, aliases=None, fixes=None):
        scalars = [self.place] + ([] if fixes is None else [fixes])
        tokens = [] if self.token is None else [self.token]
        before = len(scalars) + len(inputs)

        def wrapped(*refs):
            refs[-1][...] = jnp.zeros_like(refs[-1])
            kernel(*refs[:before], *refs[before + len(tokens) : -1])

        outputs = outputs + [whole(shaped(jnp.int32, 8, 128))]
        shapes = [shape for shape, _, _ in outputs]
        keep = pl.BlockSpec(memory_space=pl.ANY)
        out = pl.pallas_call(
            wrapped,
            out_shape=shapes,
            grid_spec=pltpu.PrefetchScalarGridSpec(
                num_scalar_prefetch=len(scalars),
                grid=grid,
                in_specs=[
                    keep if block is None else pl.BlockSpec(block, index)
                    for _, block, index in inputs
                ]
                + [keep] * len(tokens),
                out_specs=[pl.BlockSpec(block, index) for _, block, index in outputs],
            ),
            input_output_aliases=aliases or {},
            compiler_params=pltpu.CompilerParams(vmem_limit_bytes=vmem_bytes),
            cost_estimate=pl.CostEstimate(
                flops=int(span * 1e9), bytes_accessed=0, transcendentals=0
            ),
        )(*scalars, *[a for a, _, _ in inputs], *tokens)
        self.token = out[-1]
        return out[0] if len(out) == 2 else out[:-1]


def shaped(dtype, *shape):
    return jax.ShapeDtypeStruct(shape, dtype)


def whole(array):
    zeros = (0,) * len(array.shape)
    return (array, array.shape, lambda *_: zeros)


def rowwise(array, steps):
    return (array, (array.shape[0] // steps, array.shape[1]), lambda i, *_: (i, 0))


def columnwise(array, steps):
    return (array, (array.shape[0], array.shape[1] // steps), lambda i, *_: (0, i))


def stacked(array, k, rows):
    return (array, (rows, array.shape[1]), lambda *_: (k, 0))


def dot_t(a, b):
    return lax.dot_general(a, b, (((0,), (0,)), ((), ())), preferred_element_type=f32)


def dot_bt(a, b):
    return lax.dot_general(a, b, (((1,), (1,)), ((), ())), preferred_element_type=f32)


def dot(a, b):
    return jnp.dot(a, b, preferred_element_type=f32)


def chosen(flag, yes, no):
    return jnp.where(flag != 0, yes, no)


def halves(x_ref, rows):
    turned = x_ref[...].T
    return turned[:rows], turned[rows:]


def rounded(order, local):
    def kernel(s_ref, a_ref, out_ref):
        out_ref[...] = a_ref[...].astype(bf16)

    return order.call(
        kernel, [rowwise(local, 3)], [rowwise(shaped(bf16, *local.shape), 3)], (3,)
    )


def first_piece(order, normed, rows):
    tokens = normed.shape[0]

    def kernel(s_ref, x_ref, piece_ref):
        low, high = halves(x_ref, rows)
        piece_ref[...] = chosen(s_ref[Y], low, high)

    return order.call(
        kernel,
        [(normed, (tokens, 2 * rows), lambda i, s: (0, s[FAR]))],
        [whole(shaped(bf16, rows, tokens))],
        (1,),
    )


def split(order, normed, rows, g_pair, fixes):
    tokens = normed.shape[0]

    def kernel(s_ref, fix_ref, x_ref, g_ref, two_ref, last_ref, own_ref):
        i = pl.program_id(0)
        low, high = halves(x_ref, rows)
        own_ref[...] = chosen(s_ref[Y], high, low)

        @pl.when(i < 2)
        def _():
            two_ref[...] = chosen(s_ref[Y], low, high)

        @pl.when(i == 2)
        def _():
            last_ref[...] = chosen(s_ref[Y], low, high)

    return order.call(
        kernel,
        [
            (normed, (tokens, 2 * rows), lambda i, s, f: (0, s[(i + 1) % 4])),
            (g_pair, None, None),
        ],
        [
            (
                shaped(bf16, 2 * rows, tokens),
                (rows, tokens),
                lambda i, s, f: (jnp.minimum(i, 1), 0),
            ),
            (shaped(bf16, 3 * rows, tokens), (rows, tokens), lambda i, s, f: (0, 0)),
            (shaped(bf16, 4 * rows, tokens), (rows, tokens), lambda i, s, f: ((i + 1) % 4, 0)),
        ],
        (4,),
        expected["split"],
        fixes=fixes,
    )


def gradient_part(order, mine, k, theirs, at, key_grad, g_pair, scale, dtype, span):
    tokens, features = key_grad.shape
    rows = mine.shape[0] // 4

    def kernel(s_ref, x_ref, xp_ref, g_ref, gp_ref, out_ref):
        total = dot(x_ref[...], g_ref[...]) + dot(xp_ref[...], gp_ref[...])
        out_ref[...] = (total * scale).astype(dtype)

    return order.call(
        kernel,
        [
            stacked(mine, k, rows),
            stacked(theirs, at, rows),
            columnwise(key_grad, 2),
            columnwise(g_pair, 2),
        ],
        [columnwise(shaped(dtype, rows, features), 2)],
        (2,),
        span,
    )


def input_two(order, key_grad, g_pair, first, second, target, scale):
    tokens, features = key_grad.shape
    rows = first.shape[0]

    def kernel(s_ref, g_ref, gp_ref, a_ref, b_ref, target_ref, pair_ref, own_ref):
        weight = jnp.where(pl.program_id(0) == 0, a_ref[...], b_ref[...])
        pair_ref[...] = (dot_bt(weight, gp_ref[...]) * scale).astype(bf16)
        own_ref[...] = (dot_bt(weight, g_ref[...]) * scale).astype(bf16)

    return order.call(
        kernel,
        [whole(a) for a in (key_grad, g_pair, first, second)] + [(target, None, None)],
        [
            (target, (rows, tokens), lambda i, s: (1 + i, 0)),
            (shaped(bf16, 2 * rows, tokens), (rows, tokens), lambda i, s: (i, 0)),
        ],
        (2,),
        expected["input two"],
        {5: 0},
    )


def input_one(order, key_grad, g_pair, inner, part, end, scale, span, before=()):
    tokens, features = key_grad.shape
    rows = end.shape[0]

    def kernel(s_ref, g_ref, gp_ref, a_ref, b_ref, *rest):
        pair_ref, own_ref, w_ref = rest[len(before) :]
        weight = chosen(s_ref[INNER], a_ref[...], b_ref[...])
        w_ref[...] = weight
        pair_ref[...] = (dot_bt(weight, gp_ref[...]) * scale).astype(bf16)
        own_ref[...] = (dot_bt(weight, g_ref[...]) * scale).astype(bf16)

    out = whole(shaped(bf16, rows, tokens))
    return order.call(
        kernel,
        [whole(key_grad), whole(g_pair), stacked(inner, part, rows), whole(end)]
        + [(a, None, None) for a in before],
        [out, out, whole(shaped(bf16, rows, features))],
        (1,),
        span,
    )


def input_join(order, slots, own, others, shape, span, target=None, before=()):
    tokens = own[0][0][0].shape[1]
    tile = tokens // 3
    rows = shape[1] // 8
    flat = [
        (a, k, rows if len(piece) == 1 else a.shape[0]) for piece in own + others for a, k in piece
    ]
    kept = [a for a in (target, *before) if a is not None]

    def kernel(s_ref, *refs):
        values = iter([ref[...] for ref in refs[: len(flat)]])
        sides = [jnp.concatenate([next(values) for _ in piece], 0) for piece in own + others]
        first = pl.program_id(0) == 0
        mine = jnp.where(first, sides[0], sides[1])
        theirs = jnp.where(first, sides[2], sides[3])
        out_ref = refs[-1]

        @pl.when(s_ref[Y] == 0)
        def _():
            out_ref[...] = jnp.concatenate([mine, theirs], 0).T

        @pl.when(s_ref[Y] != 0)
        def _():
            out_ref[...] = jnp.concatenate([theirs, mine], 0).T

    def piece(array, k, height):
        return (array, (height, tile), lambda j, i, s: (k, i))

    return order.call(
        kernel,
        [piece(*p) for p in flat] + [(a, None, None) for a in kept],
        [(shaped(bf16, *shape), (tile, 2 * rows), lambda j, i, s: (i, s[slots[0] - j]))],
        (2, 3),
        span,
        None if target is None else {len(flat) + 1: 0},
    )


def key_sums(order, total, blocks, weights, span, scale=1.0, dtype=f32, before=()):
    features = weights[0].shape[1]
    tokens = blocks[0][0].shape[1]
    count = len(blocks)
    totals = [] if total is None else [columnwise(total, 2)]

    def kernel(s_ref, *refs):
        value = refs[2 * count][...] if totals else 0.0
        for x_ref, w_ref in zip(refs[:count], refs[count : 2 * count]):
            value += dot_t(x_ref[...], w_ref[...])
        refs[-1][...] = (value * scale).astype(dtype)

    return order.call(
        kernel,
        [stacked(x, k, w.shape[0]) for (x, k), w in zip(blocks, weights)]
        + [columnwise(w, 2) for w in weights]
        + totals
        + [(a, None, None) for a in before],
        [columnwise(shaped(dtype, tokens, features), 2)],
        (2,),
        span,
    )


def delta_halves(order, anchor, local):
    rows, features = local.shape

    def kernel(s_ref, a_ref, b_ref, c_ref, d_ref, own_ref, other_ref):
        own_ref[...] = a_ref[...] - b_ref[...]
        other_ref[...] = c_ref[...] - d_ref[...]

    def half(array, turned):
        def index(i, s):
            core = 1 - s[CORE] if turned else s[CORE]
            return (3 * core + i, 0)

        return (array, (rows // 6, features), index)

    out = rowwise(shaped(f32, rows // 2, features), 3)
    return order.call(
        kernel,
        [half(anchor, False), half(local, False), half(anchor, True), half(local, True)],
        [out, out],
        (3,),
    )


def total_of(order, here, there):
    def kernel(s_ref, a_ref, b_ref, out_ref):
        out_ref[...] = a_ref[...] + b_ref[...]

    return order.call(
        kernel, [rowwise(here, 3), rowwise(there, 3)], [rowwise(shaped(f32, *here.shape), 3)], (3,)
    )


def choose_sends(order, at_end, inside, beside):
    def kernel(s_ref, a_ref, b_ref, c_ref, out_ref, across_ref):
        out_ref[...] = chosen(s_ref[END], a_ref[...], b_ref[...])
        across_ref[...] = c_ref[...]

    out = rowwise(shaped(bf16, *inside.shape), 3)
    return order.call(
        kernel, [rowwise(a, 3) for a in (at_end, inside, beside)], [out, out], (3,), 0
    )


def first_handoff(order, p0, c1, p1, w_across):
    rows, features = p0.shape
    part = rows // 3

    def kernel(s_ref, p0_ref, c1_ref, p1_ref, w_ref, sum_a, send_a, sum_b, send_b):
        total = (p0_ref[...].astype(f32) + c1_ref[...].astype(f32)).astype(bf16)
        send = chosen(s_ref[END], p1_ref[...], w_ref[...])

        @pl.when(pl.program_id(0) < 2)
        def _():
            sum_a[...] = total
            send_a[...] = send

        @pl.when(pl.program_id(0) == 2)
        def _():
            sum_b[...] = total
            send_b[...] = send

    a = (
        shaped(bf16, 2 * part, features),
        (part, features),
        lambda i, s: (jnp.minimum(i, 1), 0),
    )
    b = whole(shaped(bf16, part, features))
    return order.call(
        kernel,
        [rowwise(x, 3) for x in (p0, c1, p1, w_across)],
        [a, a, b, b],
        (3,),
        expected["handoff"],
    )


def second_handoff(order, first, p1, c2, p2, q2, before, span):
    def kernel(s_ref, p1_ref, c2_ref, p2_ref, q2_ref, *rest):
        s1_ref, t_ref = rest[len(before) :]
        s1_ref[...] = (p1_ref[...].astype(f32) + c2_ref[...].astype(f32)).astype(bf16)
        t_ref[...] = (p2_ref[...] + q2_ref[...].astype(f32)).astype(bf16)

    sixth, features = p1.shape[0] // 6, p1.shape[1]
    steps = c2.shape[0] // sixth
    block = (sixth, features)
    out = rowwise(shaped(bf16, *c2.shape), steps)
    return order.call(
        kernel,
        [
            (p1, block, lambda i, s: (first + i, 0)),
            rowwise(c2, steps),
            (p2, block, lambda i, s: (first + i, 0)),
            rowwise(q2, steps),
        ]
        + [(a, None, None) for a in before],
        [out, out],
        (steps,),
        span,
    )


def nesterov_pass(order, own, other, anchor, momentum, local):
    rows, features = local.shape

    def kernel(s_ref, own_ref, other_ref, anchor_ref, momentum_ref, local_ref, *out):
        anchor_new_ref, moment_new_ref, base_ref = out
        in_own = pl.program_id(0) // 3 == s_ref[CORE]
        outer_grad = jnp.where(in_own, own_ref[...], other_ref[...]) / 4
        anchor_new, moment_new = nesterov(outer_grad, anchor_ref[...], momentum_ref[...])
        anchor_new_ref[...] = anchor_new
        moment_new_ref[...] = moment_new
        kept = mix_weight * (1.0 - inner_rate * weight_decay)
        base_ref[...] = kept * local_ref[...] + (1.0 - mix_weight) * anchor_new

    def half(array):
        return (array, (rows // 6, features), lambda i, s: (i % 3, 0))

    out = rowwise(shaped(f32, rows, features), 6)
    return order.call(
        kernel,
        [half(own), half(other)] + [rowwise(a, 6) for a in (anchor, momentum, local)],
        [out, out, out],
        (6,),
        expected["nesterov"],
    )


def final_update(order, first, fixes, p3, qa, qb, first_old, second_old, base, made=(), keys=()):
    rows, features = base.shape
    block = (rows // 6, features)
    steps = qa.shape[0] // block[0]
    scale = keys[2] if keys else None

    def kernel(s_ref, fix_ref, p_ref, a_ref, b_ref, first_ref, second_ref, base_ref, *rest):
        outs = rest[len(keys[:2]) + len(made) :]
        gradient = p_ref[...] + a_ref[...].astype(f32) + b_ref[...].astype(f32)
        first_new = beta_first * first_ref[...] + (1.0 - beta_first) * gradient
        second_new = beta_second * second_ref[...] + (1.0 - beta_second) * gradient * gradient
        root = jnp.sqrt(second_new * fix_ref[1]) + epsilon
        step = (mix_weight * inner_rate) * fix_ref[0]
        outs[0][...] = base_ref[...] - step * first_new / root
        outs[1][...] = first_new
        outs[2][...] = second_new
        if keys:
            outs[3][...] = (rest[0][...] * scale + rest[1][...].astype(f32)).astype(bf16)

    def at(array, offset):
        return (array, block, lambda i, *_: (offset + i, 0))

    out = at(shaped(f32, rows, features), first)
    inputs = [at(p3, first), rowwise(qa, steps), rowwise(qb, steps)]
    inputs += [at(a, first) for a in (first_old, second_old, base)]
    inputs += [rowwise(a, steps) for a in keys[:2]]
    aliases = {2 + len(inputs) + i: i for i in range(len(made))}
    return order.call(
        kernel,
        inputs + [(a, None, None) for a in made],
        [out] * 3 + ([rowwise(shaped(bf16, *keys[0].shape), steps)] if keys else []),
        (steps,),
        0 if keys else expected["first half"],
        aliases,
        fixes,
    )


def pair_pass(normed, key_grad, local, first_old, second_old, anchor, momentum, inner_step):
    width = normed.shape[1]
    rows = local.shape[0]
    scale = width ** (-0.5)
    me = lax.axis_index("fsdp")
    core = lax.axis_index("rep") % 2
    y, z = me % 2, me // 2
    inside = (z == 1) | (z == 2)
    far = jnp.where(z < 2, 3, 0)
    middle = jnp.where(z < 2, 2, 1)
    order = Order(jnp.stack([far, middle, z ^ 1, z, y, inside, ~inside, core]).astype(jnp.int32))

    def along(links):
        pairs = [(2 * a + c, 2 * b + c) for a, b in links for c in (0, 1)]
        return lambda value: lax.ppermute(value, "fsdp", pairs)

    outer = along([(0, 1), (1, 0), (2, 3), (3, 2)])
    inner = along([(1, 2), (2, 1)])

    def swap(value):
        return lax.ppermute(value, "fsdp", [(i, i ^ 1) for i in range(8)])

    def replica(value, bit):
        return lax.ppermute(value, "rep", [(i, i ^ bit) for i in range(4)])

    g_pair = swap(key_grad)
    weight = rounded(order, local)
    w_beside = outer(weight)
    w_inner = inner(weight)
    x0 = swap(first_piece(order, normed, rows))
    own_delta, other_delta = delta_halves(order, anchor, local)
    delta_core = replica(other_delta, 1)
    fixes = 1.0 / jnp.stack(corrections(inner_step))
    two, three, mine = split(order, normed, rows, g_pair, fixes)
    x12 = swap(two)
    delta = total_of(order, own_delta, delta_core)
    delta_there = replica(delta, 2)

    def partial(k, theirs, at, dtype, span):
        return gradient_part(order, mine, k, theirs, at, key_grad, g_pair, scale, dtype, span)

    p0 = partial(0, x0, 0, bf16, expected["first part"])
    send, across = choose_sends(order, p0, w_inner, w_beside)
    c1 = outer(send)
    w_across = inner(across)
    three, own01 = input_two(order, key_grad, g_pair, weight, w_beside, three, scale)
    x3 = swap(three)
    known = (w_beside, weight)
    own_total = key_sums(order, None, [(mine, 2), (mine, 3)], known, expected["early own"])
    total = total_of(order, delta, delta_there)
    total_there = replica(total, 1)
    p1 = partial(1, x12, 0, bf16, expected["second part"])
    p2 = partial(2, x12, 1, f32, 1)
    anchor_new, moment_new, base = nesterov_pass(
        order, total, total_there, anchor, momentum, local
    )

    s0a, send_a, s0b, send_b = first_handoff(order, p0, c1, p1, w_across)
    c2a, q2a = outer(send_a), inner(s0a)
    c2b, q2b = outer(send_b), inner(s0b)
    i2, own2, w_middle = input_one(
        order, key_grad, g_pair, w_inner, 0, c1, scale, expected["input middle"]
    )
    g2 = swap(i2)
    pair_total = key_sums(
        order, None, [(x12, 0), (x12, 1)], (w_middle, w_beside), expected["early pair"]
    )
    own_total = key_sums(order, own_total, [(mine, 1)], (w_middle,), expected["early pair"])
    input_grad = input_join(
        order,
        (OWN, BESIDE),
        [[(own01, 0)], [(own01, 1)]],
        [[(x3, 1)], [(x3, 2)]],
        normed.shape,
        expected["join two"],
    )
    i3, own3a, w_far_a = input_one(
        order, key_grad, g_pair, w_across, 0, c2a, scale, expected["input far"], [x3]
    )
    g3a = swap(i3)
    s1, t = second_handoff(order, 0, p1, c2a, p2, q2a, [x3], expected["early sums"])
    qaa, qba = outer(t), inner(s1)
    pair_total = key_sums(
        order,
        pair_total,
        [(x3, 0)],
        (weight,),
        expected["pair sums"],
        before=[g2],
    )
    i3, own3b, w_far_b = input_one(
        order, key_grad, g_pair, w_across, 2, c2b, scale, expected["input last"]
    )
    g3b = swap(i3)
    w_far = (w_far_a, w_far_b)
    key_pair = swap(
        key_sums(order, pair_total, [(x0, 0), (x0, 2)], w_far, 0, scale, bf16, [q2b])
    )
    s1, t = second_handoff(order, 4, p1, c2b, p2, q2b, [g3a, g3b], expected["late sums"])
    qab, qbb = outer(t), inner(s1)
    p3 = partial(3, x3, 0, f32, 0)
    own_total = key_sums(
        order,
        own_total,
        [(mine, 0), (mine, 2)],
        w_far,
        expected["own sums"],
    )
    input_grad = input_join(
        order,
        (MIDDLE, FAR),
        [[(own2, 0)], [(own3a, 0), (own3b, 0)]],
        [[(g2, 0)], [(g3a, 0), (g3b, 0)]],
        normed.shape,
        expected["join last"],
        input_grad,
    )
    state = (first_old, second_old, base)
    made = final_update(order, 0, fixes, p3, qaa, qba, *state)
    merged, first_new, second_new, keys = final_update(
        order, 4, fixes, p3, qab, qbb, *state, made, (own_total, key_pair, scale)
    )
    return (keys, input_grad, merged, first_new, second_new, anchor_new, moment_new)


def body(normed, key_grad, master, first_moment, second_moment, anchor, momentum, inner_step):
    local = master[0]
    sizes = (lax.axis_size("rep"), lax.axis_size("fsdp"))
    inner_pass = pair_pass if sizes == (4, 8) else whole_pass
    keys, input_grad, merged, first_new, second_new, anchor_new, moment_new = inner_pass(
        normed, key_grad, local, first_moment[0], second_moment[0], anchor, momentum, inner_step
    )
    return (
        keys,
        input_grad,
        merged[None],
        first_new[None],
        second_new[None],
        anchor_new,
        moment_new,
    )


def solution(mesh):
    in_specs = (
        P(("rep", "fsdp"), None),
        P(("rep", "fsdp"), None),
        P("rep", "fsdp", None),
        P("rep", "fsdp", None),
        P("rep", "fsdp", None),
        P("fsdp", None),
        P("fsdp", None),
        P(),
    )
    out_specs = (
        P(("rep", "fsdp"), None),
        P(("rep", "fsdp"), None),
        P("rep", "fsdp", None),
        P("rep", "fsdp", None),
        P("rep", "fsdp", None),
        P("fsdp", None),
        P("fsdp", None),
    )
    return jax.shard_map(body, mesh=mesh, in_specs=in_specs, out_specs=out_specs, check_vma=False)
```

```python
import jax
import jax.numpy as jnp
from jax import lax
from jax.experimental import pallas as pl
from jax.experimental.pallas import tpu as pltpu
from jax.sharding import PartitionSpec as P

beta_first = 0.9
beta_second = 0.95
inner_rate = 0.1
weight_decay = 0.1
epsilon = 1e-08
outer_rate = 0.7
outer_mu = 0.9
mix_weight = 0.5

f32 = jnp.float32
bf16 = jnp.bfloat16
vmem_bytes = 16 * 1024 * 1024

expected = {
    "split": 30,
    "first part": 0,
    "input two": 12,
    "second part": 30,
    "nesterov": 1,
    "early own": 0,
    "early pair": 0,
    "handoff": 1,
    "input middle": 0,
    "join two": 0,
    "input far": 0,
    "input last": 12,
    "early sums": 1,
    "pair sums": 0,
    "late sums": 1,
    "own sums": 0,
    "join last": 0,
    "first half": 12,
}


def corrections(inner_step):
    count_float = inner_step[0].astype(f32)
    fix_first = 1.0 - jnp.power(f32(beta_first), count_float)
    fix_second = 1.0 - jnp.power(f32(beta_second), count_float)
    return fix_first, fix_second


def adam(gradient, local, first_old, second_old, fix_first, fix_second):
    first_new = beta_first * first_old + (1.0 - beta_first) * gradient
    second_new = beta_second * second_old + (1.0 - beta_second) * gradient * gradient
    direction = first_new / fix_first / (jnp.sqrt(second_new / fix_second) + epsilon)
    stepped = local - inner_rate * (direction + weight_decay * local)
    return (stepped, first_new, second_new)


def nesterov(outer_grad, anchor_rows, moment_rows):
    moment_new = outer_mu * moment_rows + outer_grad
    anchor_new = anchor_rows - outer_rate * (outer_grad + outer_mu * moment_new)
    return (anchor_new, moment_new)


def outer_update(local, anchor, momentum):
    summed = lax.psum(anchor - local, "rep")
    return nesterov(summed / lax.axis_size("rep"), anchor, momentum)


def whole_pass(normed, key_grad, local, first_old, second_old, anchor, momentum, inner_step):
    scale = normed.shape[1] ** (-0.5)
    weight = lax.all_gather(local.astype(bf16), "fsdp", axis=0, tiled=True)
    keys = (jnp.dot(normed, weight, preferred_element_type=f32) * scale).astype(bf16)
    input_grad = (
        lax.dot_general(key_grad, weight, (((1,), (1,)), ((), ())), preferred_element_type=f32)
        * scale
    ).astype(bf16)
    gradient = lax.psum_scatter(
        lax.dot_general(normed, key_grad, (((0,), (0,)), ((), ())), preferred_element_type=f32)
        * scale,
        "fsdp",
        scatter_dimension=0,
        tiled=True,
    )
    stepped, first_new, second_new = adam(
        gradient, local, first_old, second_old, *corrections(inner_step)
    )
    anchor_new, moment_new = outer_update(local, anchor, momentum)
    merged = mix_weight * stepped + (1.0 - mix_weight) * anchor_new
    return (keys, input_grad, merged, first_new, second_new, anchor_new, moment_new)


FAR, MIDDLE, BESIDE, OWN, Y, INNER, END, CORE = range(8)


class Order:
    def __init__(self, place):
        self.place = place
        self.token = None

    def call(self, kernel, inputs, outputs, grid, span=1, aliases=None, fixes=None):
        scalars = [self.place] + ([] if fixes is None else [fixes])
        tokens = [] if self.token is None else [self.token]
        before = len(scalars) + len(inputs)

        def wrapped(*refs):
            refs[-1][...] = jnp.zeros_like(refs[-1])
            kernel(*refs[:before], *refs[before + len(tokens) : -1])

        outputs = outputs + [whole(shaped(jnp.int32, 8, 128))]
        shapes = [shape for shape, _, _ in outputs]
        keep = pl.BlockSpec(memory_space=pl.ANY)
        out = pl.pallas_call(
            wrapped,
            out_shape=shapes,
            grid_spec=pltpu.PrefetchScalarGridSpec(
                num_scalar_prefetch=len(scalars),
                grid=grid,
                in_specs=[
                    keep if block is None else pl.BlockSpec(block, index)
                    for _, block, index in inputs
                ]
                + [keep] * len(tokens),
                out_specs=[pl.BlockSpec(block, index) for _, block, index in outputs],
            ),
            input_output_aliases=aliases or {},
            compiler_params=pltpu.CompilerParams(vmem_limit_bytes=vmem_bytes),
            cost_estimate=pl.CostEstimate(
                flops=int(span * 1e9), bytes_accessed=0, transcendentals=0
            ),
        )(*scalars, *[a for a, _, _ in inputs], *tokens)
        self.token = out[-1]
        return out[0] if len(out) == 2 else out[:-1]


def shaped(dtype, *shape):
    return jax.ShapeDtypeStruct(shape, dtype)


def whole(array):
    zeros = (0,) * len(array.shape)
    return (array, array.shape, lambda *_: zeros)


def rowwise(array, steps):
    return (array, (array.shape[0] // steps, array.shape[1]), lambda i, *_: (i, 0))


def columnwise(array, steps):
    return (array, (array.shape[0], array.shape[1] // steps), lambda i, *_: (0, i))


def stacked(array, k, rows):
    return (array, (rows, array.shape[1]), lambda *_: (k, 0))


def dot_t(a, b):
    return lax.dot_general(a, b, (((0,), (0,)), ((), ())), preferred_element_type=f32)


def dot_bt(a, b):
    return lax.dot_general(a, b, (((1,), (1,)), ((), ())), preferred_element_type=f32)


def dot(a, b):
    return jnp.dot(a, b, preferred_element_type=f32)


def chosen(flag, yes, no):
    return jnp.where(flag != 0, yes, no)


def halves(x_ref, rows):
    turned = x_ref[...].T
    return turned[:rows], turned[rows:]


def rounded(order, local):
    def kernel(s_ref, a_ref, out_ref):
        out_ref[...] = a_ref[...].astype(bf16)

    return order.call(
        kernel, [rowwise(local, 3)], [rowwise(shaped(bf16, *local.shape), 3)], (3,)
    )


def first_piece(order, normed, rows):
    tokens = normed.shape[0]

    def kernel(s_ref, x_ref, piece_ref):
        low, high = halves(x_ref, rows)
        piece_ref[...] = chosen(s_ref[Y], low, high)

    return order.call(
        kernel,
        [(normed, (tokens, 2 * rows), lambda i, s: (0, s[FAR]))],
        [whole(shaped(bf16, rows, tokens))],
        (1,),
    )


def split(order, normed, rows, g_pair, fixes):
    tokens = normed.shape[0]

    def kernel(s_ref, fix_ref, x_ref, g_ref, two_ref, last_ref, own_ref):
        i = pl.program_id(0)
        low, high = halves(x_ref, rows)
        own_ref[...] = chosen(s_ref[Y], high, low)

        @pl.when(i < 2)
        def _():
            two_ref[...] = chosen(s_ref[Y], low, high)

        @pl.when(i == 2)
        def _():
            last_ref[...] = chosen(s_ref[Y], low, high)

    return order.call(
        kernel,
        [
            (normed, (tokens, 2 * rows), lambda i, s, f: (0, s[(i + 1) % 4])),
            (g_pair, None, None),
        ],
        [
            (
                shaped(bf16, 2 * rows, tokens),
                (rows, tokens),
                lambda i, s, f: (jnp.minimum(i, 1), 0),
            ),
            (shaped(bf16, 3 * rows, tokens), (rows, tokens), lambda i, s, f: (0, 0)),
            (shaped(bf16, 4 * rows, tokens), (rows, tokens), lambda i, s, f: ((i + 1) % 4, 0)),
        ],
        (4,),
        expected["split"],
        fixes=fixes,
    )


def gradient_part(order, mine, k, theirs, at, key_grad, g_pair, scale, dtype, span):
    tokens, features = key_grad.shape
    rows = mine.shape[0] // 4

    def kernel(s_ref, x_ref, xp_ref, g_ref, gp_ref, out_ref):
        total = dot(x_ref[...], g_ref[...]) + dot(xp_ref[...], gp_ref[...])
        out_ref[...] = (total * scale).astype(dtype)

    return order.call(
        kernel,
        [
            stacked(mine, k, rows),
            stacked(theirs, at, rows),
            columnwise(key_grad, 2),
            columnwise(g_pair, 2),
        ],
        [columnwise(shaped(dtype, rows, features), 2)],
        (2,),
        span,
    )


def input_two(order, key_grad, g_pair, first, second, target, scale):
    tokens, features = key_grad.shape
    rows = first.shape[0]

    def kernel(s_ref, g_ref, gp_ref, a_ref, b_ref, target_ref, pair_ref, own_ref):
        weight = jnp.where(pl.program_id(0) == 0, a_ref[...], b_ref[...])
        pair_ref[...] = (dot_bt(weight, gp_ref[...]) * scale).astype(bf16)
        own_ref[...] = (dot_bt(weight, g_ref[...]) * scale).astype(bf16)

    return order.call(
        kernel,
        [whole(a) for a in (key_grad, g_pair, first, second)] + [(target, None, None)],
        [
            (target, (rows, tokens), lambda i, s: (1 + i, 0)),
            (shaped(bf16, 2 * rows, tokens), (rows, tokens), lambda i, s: (i, 0)),
        ],
        (2,),
        expected["input two"],
        {5: 0},
    )


def input_one(order, key_grad, g_pair, inner, part, end, scale, span, before=()):
    tokens, features = key_grad.shape
    rows = end.shape[0]

    def kernel(s_ref, g_ref, gp_ref, a_ref, b_ref, *rest):
        pair_ref, own_ref, w_ref = rest[len(before) :]
        weight = chosen(s_ref[INNER], a_ref[...], b_ref[...])
        w_ref[...] = weight
        pair_ref[...] = (dot_bt(weight, gp_ref[...]) * scale).astype(bf16)
        own_ref[...] = (dot_bt(weight, g_ref[...]) * scale).astype(bf16)

    out = whole(shaped(bf16, rows, tokens))
    return order.call(
        kernel,
        [whole(key_grad), whole(g_pair), stacked(inner, part, rows), whole(end)]
        + [(a, None, None) for a in before],
        [out, out, whole(shaped(bf16, rows, features))],
        (1,),
        span,
    )


def input_join(order, slots, own, others, shape, span, target=None, before=()):
    tokens = own[0][0][0].shape[1]
    tile = tokens // 3
    rows = shape[1] // 8
    flat = [
        (a, k, rows if len(piece) == 1 else a.shape[0]) for piece in own + others for a, k in piece
    ]
    kept = [a for a in (target, *before) if a is not None]

    def kernel(s_ref, *refs):
        values = iter([ref[...] for ref in refs[: len(flat)]])
        sides = [jnp.concatenate([next(values) for _ in piece], 0) for piece in own + others]
        first = pl.program_id(0) == 0
        mine = jnp.where(first, sides[0], sides[1])
        theirs = jnp.where(first, sides[2], sides[3])
        out_ref = refs[-1]

        @pl.when(s_ref[Y] == 0)
        def _():
            out_ref[...] = jnp.concatenate([mine, theirs], 0).T

        @pl.when(s_ref[Y] != 0)
        def _():
            out_ref[...] = jnp.concatenate([theirs, mine], 0).T

    def piece(array, k, height):
        return (array, (height, tile), lambda j, i, s: (k, i))

    return order.call(
        kernel,
        [piece(*p) for p in flat] + [(a, None, None) for a in kept],
        [(shaped(bf16, *shape), (tile, 2 * rows), lambda j, i, s: (i, s[slots[0] - j]))],
        (2, 3),
        span,
        None if target is None else {len(flat) + 1: 0},
    )


def key_sums(order, total, blocks, weights, span, scale=1.0, dtype=f32, before=()):
    features = weights[0].shape[1]
    tokens = blocks[0][0].shape[1]
    count = len(blocks)
    totals = [] if total is None else [columnwise(total, 2)]

    def kernel(s_ref, *refs):
        value = refs[2 * count][...] if totals else 0.0
        for x_ref, w_ref in zip(refs[:count], refs[count : 2 * count]):
            value += dot_t(x_ref[...], w_ref[...])
        refs[-1][...] = (value * scale).astype(dtype)

    return order.call(
        kernel,
        [stacked(x, k, w.shape[0]) for (x, k), w in zip(blocks, weights)]
        + [columnwise(w, 2) for w in weights]
        + totals
        + [(a, None, None) for a in before],
        [columnwise(shaped(dtype, tokens, features), 2)],
        (2,),
        span,
    )


def delta_halves(order, anchor, local):
    rows, features = local.shape

    def kernel(s_ref, a_ref, b_ref, c_ref, d_ref, own_ref, other_ref):
        own_ref[...] = a_ref[...] - b_ref[...]
        other_ref[...] = c_ref[...] - d_ref[...]

    def half(array, turned):
        def index(i, s):
            core = 1 - s[CORE] if turned else s[CORE]
            return (3 * core + i, 0)

        return (array, (rows // 6, features), index)

    out = rowwise(shaped(f32, rows // 2, features), 3)
    return order.call(
        kernel,
        [half(anchor, False), half(local, False), half(anchor, True), half(local, True)],
        [out, out],
        (3,),
    )


def total_of(order, here, there):
    def kernel(s_ref, a_ref, b_ref, out_ref):
        out_ref[...] = a_ref[...] + b_ref[...]

    return order.call(
        kernel, [rowwise(here, 3), rowwise(there, 3)], [rowwise(shaped(f32, *here.shape), 3)], (3,)
    )


def choose_sends(order, at_end, inside, beside):
    def kernel(s_ref, a_ref, b_ref, c_ref, out_ref, across_ref):
        out_ref[...] = chosen(s_ref[END], a_ref[...], b_ref[...])
        across_ref[...] = c_ref[...]

    out = rowwise(shaped(bf16, *inside.shape), 3)
    return order.call(
        kernel, [rowwise(a, 3) for a in (at_end, inside, beside)], [out, out], (3,), 0
    )


def first_handoff(order, p0, c1, p1, w_across):
    rows, features = p0.shape
    part = rows // 3

    def kernel(s_ref, p0_ref, c1_ref, p1_ref, w_ref, sum_a, send_a, sum_b, send_b):
        total = (p0_ref[...].astype(f32) + c1_ref[...].astype(f32)).astype(bf16)
        send = chosen(s_ref[END], p1_ref[...], w_ref[...])

        @pl.when(pl.program_id(0) < 2)
        def _():
            sum_a[...] = total
            send_a[...] = send

        @pl.when(pl.program_id(0) == 2)
        def _():
            sum_b[...] = total
            send_b[...] = send

    a = (
        shaped(bf16, 2 * part, features),
        (part, features),
        lambda i, s: (jnp.minimum(i, 1), 0),
    )
    b = whole(shaped(bf16, part, features))
    return order.call(
        kernel,
        [rowwise(x, 3) for x in (p0, c1, p1, w_across)],
        [a, a, b, b],
        (3,),
        expected["handoff"],
    )


def second_handoff(order, first, p1, c2, p2, q2, before, span):
    def kernel(s_ref, p1_ref, c2_ref, p2_ref, q2_ref, *rest):
        s1_ref, t_ref = rest[len(before) :]
        s1_ref[...] = (p1_ref[...].astype(f32) + c2_ref[...].astype(f32)).astype(bf16)
        t_ref[...] = (p2_ref[...] + q2_ref[...].astype(f32)).astype(bf16)

    sixth, features = p1.shape[0] // 6, p1.shape[1]
    steps = c2.shape[0] // sixth
    block = (sixth, features)
    out = rowwise(shaped(bf16, *c2.shape), steps)
    return order.call(
        kernel,
        [
            (p1, block, lambda i, s: (first + i, 0)),
            rowwise(c2, steps),
            (p2, block, lambda i, s: (first + i, 0)),
            rowwise(q2, steps),
        ]
        + [(a, None, None) for a in before],
        [out, out],
        (steps,),
        span,
    )


def nesterov_pass(order, own, other, anchor, momentum, local):
    rows, features = local.shape

    def kernel(s_ref, own_ref, other_ref, anchor_ref, momentum_ref, local_ref, *out):
        anchor_new_ref, moment_new_ref, base_ref = out
        in_own = pl.program_id(0) // 3 == s_ref[CORE]
        outer_grad = jnp.where(in_own, own_ref[...], other_ref[...]) / 4
        anchor_new, moment_new = nesterov(outer_grad, anchor_ref[...], momentum_ref[...])
        anchor_new_ref[...] = anchor_new
        moment_new_ref[...] = moment_new
        kept = mix_weight * (1.0 - inner_rate * weight_decay)
        base_ref[...] = kept * local_ref[...] + (1.0 - mix_weight) * anchor_new

    def half(array):
        return (array, (rows // 6, features), lambda i, s: (i % 3, 0))

    out = rowwise(shaped(f32, rows, features), 6)
    return order.call(
        kernel,
        [half(own), half(other)] + [rowwise(a, 6) for a in (anchor, momentum, local)],
        [out, out, out],
        (6,),
        expected["nesterov"],
    )


def final_update(order, first, fixes, p3, qa, qb, first_old, second_old, base, made=(), keys=()):
    rows, features = base.shape
    block = (rows // 6, features)
    steps = qa.shape[0] // block[0]
    scale = keys[2] if keys else None

    def kernel(s_ref, fix_ref, p_ref, a_ref, b_ref, first_ref, second_ref, base_ref, *rest):
        outs = rest[len(keys[:2]) + len(made) :]
        gradient = p_ref[...] + a_ref[...].astype(f32) + b_ref[...].astype(f32)
        first_new = beta_first * first_ref[...] + (1.0 - beta_first) * gradient
        second_new = beta_second * second_ref[...] + (1.0 - beta_second) * gradient * gradient
        root = jnp.sqrt(second_new * fix_ref[1]) + epsilon
        step = (mix_weight * inner_rate) * fix_ref[0]
        outs[0][...] = base_ref[...] - step * first_new / root
        outs[1][...] = first_new
        outs[2][...] = second_new
        if keys:
            outs[3][...] = (rest[0][...] * scale + rest[1][...].astype(f32)).astype(bf16)

    def at(array, offset):
        return (array, block, lambda i, *_: (offset + i, 0))

    out = at(shaped(f32, rows, features), first)
    inputs = [at(p3, first), rowwise(qa, steps), rowwise(qb, steps)]
    inputs += [at(a, first) for a in (first_old, second_old, base)]
    inputs += [rowwise(a, steps) for a in keys[:2]]
    aliases = {2 + len(inputs) + i: i for i in range(len(made))}
    return order.call(
        kernel,
        inputs + [(a, None, None) for a in made],
        [out] * 3 + ([rowwise(shaped(bf16, *keys[0].shape), steps)] if keys else []),
        (steps,),
        0 if keys else expected["first half"],
        aliases,
        fixes,
    )


def pair_pass(normed, key_grad, local, first_old, second_old, anchor, momentum, inner_step):
    width = normed.shape[1]
    rows = local.shape[0]
    scale = width ** (-0.5)
    me = lax.axis_index("fsdp")
    core = lax.axis_index("rep") % 2
    y, z = me % 2, me // 2
    inside = (z == 1) | (z == 2)
    far = jnp.where(z < 2, 3, 0)
    middle = jnp.where(z < 2, 2, 1)
    order = Order(jnp.stack([far, middle, z ^ 1, z, y, inside, ~inside, core]).astype(jnp.int32))

    def along(links):
        pairs = [(2 * a + c, 2 * b + c) for a, b in links for c in (0, 1)]
        return lambda value: lax.ppermute(value, "fsdp", pairs)

    outer = along([(0, 1), (1, 0), (2, 3), (3, 2)])
    inner = along([(1, 2), (2, 1)])

    def swap(value):
        return lax.ppermute(value, "fsdp", [(i, i ^ 1) for i in range(8)])

    def replica(value, bit):
        return lax.ppermute(value, "rep", [(i, i ^ bit) for i in range(4)])

    g_pair = swap(key_grad)
    weight = rounded(order, local)
    w_beside = outer(weight)
    w_inner = inner(weight)
    x0 = swap(first_piece(order, normed, rows))
    own_delta, other_delta = delta_halves(order, anchor, local)
    delta_core = replica(other_delta, 1)
    fixes = 1.0 / jnp.stack(corrections(inner_step))
    two, three, mine = split(order, normed, rows, g_pair, fixes)
    x12 = swap(two)
    delta = total_of(order, own_delta, delta_core)
    delta_there = replica(delta, 2)

    def partial(k, theirs, at, dtype, span):
        return gradient_part(order, mine, k, theirs, at, key_grad, g_pair, scale, dtype, span)

    p0 = partial(0, x0, 0, bf16, expected["first part"])
    send, across = choose_sends(order, p0, w_inner, w_beside)
    c1 = outer(send)
    w_across = inner(across)
    three, own01 = input_two(order, key_grad, g_pair, weight, w_beside, three, scale)
    x3 = swap(three)
    known = (w_beside, weight)
    own_total = key_sums(order, None, [(mine, 2), (mine, 3)], known, expected["early own"])
    total = total_of(order, delta, delta_there)
    total_there = replica(total, 1)
    p1 = partial(1, x12, 0, bf16, expected["second part"])
    p2 = partial(2, x12, 1, f32, 1)
    anchor_new, moment_new, base = nesterov_pass(
        order, total, total_there, anchor, momentum, local
    )

    s0a, send_a, s0b, send_b = first_handoff(order, p0, c1, p1, w_across)
    c2a, q2a = outer(send_a), inner(s0a)
    c2b, q2b = outer(send_b), inner(s0b)
    i2, own2, w_middle = input_one(
        order, key_grad, g_pair, w_inner, 0, c1, scale, expected["input middle"]
    )
    g2 = swap(i2)
    pair_total = key_sums(
        order, None, [(x12, 0), (x12, 1)], (w_middle, w_beside), expected["early pair"]
    )
    own_total = key_sums(order, own_total, [(mine, 1)], (w_middle,), expected["early pair"])
    input_grad = input_join(
        order,
        (OWN, BESIDE),
        [[(own01, 0)], [(own01, 1)]],
        [[(x3, 1)], [(x3, 2)]],
        normed.shape,
        expected["join two"],
    )
    i3, own3a, w_far_a = input_one(
        order, key_grad, g_pair, w_across, 0, c2a, scale, expected["input far"], [x3]
    )
    g3a = swap(i3)
    s1, t = second_handoff(order, 0, p1, c2a, p2, q2a, [x3], expected["early sums"])
    qaa, qba = outer(t), inner(s1)
    pair_total = key_sums(
        order,
        pair_total,
        [(x3, 0)],
        (weight,),
        expected["pair sums"],
        before=[g2],
    )
    i3, own3b, w_far_b = input_one(
        order, key_grad, g_pair, w_across, 2, c2b, scale, expected["input last"]
    )
    g3b = swap(i3)
    w_far = (w_far_a, w_far_b)
    key_pair = swap(
        key_sums(order, pair_total, [(x0, 0), (x0, 2)], w_far, 0, scale, bf16, [q2b])
    )
    p3 = partial(3, x3, 0, f32, 0)
    s1, t = second_handoff(order, 4, p1, c2b, p2, q2b, [g3a, g3b], expected["late sums"])
    qab, qbb = outer(t), inner(s1)
    own_total = key_sums(
        order,
        own_total,
        [(mine, 0), (mine, 2)],
        w_far,
        expected["own sums"],
    )
    input_grad = input_join(
        order,
        (MIDDLE, FAR),
        [[(own2, 0)], [(own3a, 0), (own3b, 0)]],
        [[(g2, 0)], [(g3a, 0), (g3b, 0)]],
        normed.shape,
        expected["join last"],
        input_grad,
    )
    state = (first_old, second_old, base)
    made = final_update(order, 0, fixes, p3, qaa, qba, *state)
    merged, first_new, second_new, keys = final_update(
        order, 4, fixes, p3, qab, qbb, *state, made, (own_total, key_pair, scale)
    )
    return (keys, input_grad, merged, first_new, second_new, anchor_new, moment_new)


def body(normed, key_grad, master, first_moment, second_moment, anchor, momentum, inner_step):
    local = master[0]
    sizes = (lax.axis_size("rep"), lax.axis_size("fsdp"))
    inner_pass = pair_pass if sizes == (4, 8) else whole_pass
    keys, input_grad, merged, first_new, second_new, anchor_new, moment_new = inner_pass(
        normed, key_grad, local, first_moment[0], second_moment[0], anchor, momentum, inner_step
    )
    return (
        keys,
        input_grad,
        merged[None],
        first_new[None],
        second_new[None],
        anchor_new,
        moment_new,
    )


def solution(mesh):
    in_specs = (
        P(("rep", "fsdp"), None),
        P(("rep", "fsdp"), None),
        P("rep", "fsdp", None),
        P("rep", "fsdp", None),
        P("rep", "fsdp", None),
        P("fsdp", None),
        P("fsdp", None),
        P(),
    )
    out_specs = (
        P(("rep", "fsdp"), None),
        P(("rep", "fsdp"), None),
        P("rep", "fsdp", None),
        P("rep", "fsdp", None),
        P("rep", "fsdp", None),
        P("fsdp", None),
        P("fsdp", None),
    )
    return jax.shard_map(body, mesh=mesh, in_specs=in_specs, out_specs=out_specs, check_vma=False)
```

```python
import jax
import jax.numpy as jnp
from jax import lax
from jax.experimental import pallas as pl
from jax.experimental.pallas import tpu as pltpu
from jax.sharding import PartitionSpec as P

beta_first = 0.9
beta_second = 0.95
inner_rate = 0.1
weight_decay = 0.1
epsilon = 1e-08
outer_rate = 0.7
outer_mu = 0.9
mix_weight = 0.5

f32 = jnp.float32
bf16 = jnp.bfloat16
vmem_bytes = 16 * 1024 * 1024

expected = {
    "split": 30,
    "first part": 0,
    "input two": 12,
    "second part": 30,
    "nesterov": 1,
    "early own": 0,
    "early pair": 0,
    "handoff": 1,
    "input middle": 0,
    "join two": 0,
    "input far": 0,
    "input last": 12,
    "early sums": 1,
    "pair sums": 0,
    "late sums": 1,
    "own sums": 0,
    "join last": 0,
    "first half": 12,
}


def corrections(inner_step):
    count_float = inner_step[0].astype(f32)
    fix_first = 1.0 - jnp.power(f32(beta_first), count_float)
    fix_second = 1.0 - jnp.power(f32(beta_second), count_float)
    return fix_first, fix_second


def adam(gradient, local, first_old, second_old, fix_first, fix_second):
    first_new = beta_first * first_old + (1.0 - beta_first) * gradient
    second_new = beta_second * second_old + (1.0 - beta_second) * gradient * gradient
    direction = first_new / fix_first / (jnp.sqrt(second_new / fix_second) + epsilon)
    stepped = local - inner_rate * (direction + weight_decay * local)
    return (stepped, first_new, second_new)


def nesterov(outer_grad, anchor_rows, moment_rows):
    moment_new = outer_mu * moment_rows + outer_grad
    anchor_new = anchor_rows - outer_rate * (outer_grad + outer_mu * moment_new)
    return (anchor_new, moment_new)


def outer_update(local, anchor, momentum):
    summed = lax.psum(anchor - local, "rep")
    return nesterov(summed / lax.axis_size("rep"), anchor, momentum)


def whole_pass(normed, key_grad, local, first_old, second_old, anchor, momentum, inner_step):
    scale = normed.shape[1] ** (-0.5)
    weight = lax.all_gather(local.astype(bf16), "fsdp", axis=0, tiled=True)
    keys = (jnp.dot(normed, weight, preferred_element_type=f32) * scale).astype(bf16)
    input_grad = (
        lax.dot_general(key_grad, weight, (((1,), (1,)), ((), ())), preferred_element_type=f32)
        * scale
    ).astype(bf16)
    gradient = lax.psum_scatter(
        lax.dot_general(normed, key_grad, (((0,), (0,)), ((), ())), preferred_element_type=f32)
        * scale,
        "fsdp",
        scatter_dimension=0,
        tiled=True,
    )
    stepped, first_new, second_new = adam(
        gradient, local, first_old, second_old, *corrections(inner_step)
    )
    anchor_new, moment_new = outer_update(local, anchor, momentum)
    merged = mix_weight * stepped + (1.0 - mix_weight) * anchor_new
    return (keys, input_grad, merged, first_new, second_new, anchor_new, moment_new)


FAR, MIDDLE, BESIDE, OWN, Y, INNER, END, CORE = range(8)


class Order:
    def __init__(self, place):
        self.place = place
        self.token = None

    def call(self, kernel, inputs, outputs, grid, span=1, aliases=None, fixes=None):
        scalars = [self.place] + ([] if fixes is None else [fixes])
        tokens = [] if self.token is None else [self.token]
        before = len(scalars) + len(inputs)

        def wrapped(*refs):
            refs[-1][...] = jnp.zeros_like(refs[-1])
            kernel(*refs[:before], *refs[before + len(tokens) : -1])

        outputs = outputs + [whole(shaped(jnp.int32, 8, 128))]
        shapes = [shape for shape, _, _ in outputs]
        keep = pl.BlockSpec(memory_space=pl.ANY)
        out = pl.pallas_call(
            wrapped,
            out_shape=shapes,
            grid_spec=pltpu.PrefetchScalarGridSpec(
                num_scalar_prefetch=len(scalars),
                grid=grid,
                in_specs=[
                    keep if block is None else pl.BlockSpec(block, index)
                    for _, block, index in inputs
                ]
                + [keep] * len(tokens),
                out_specs=[pl.BlockSpec(block, index) for _, block, index in outputs],
            ),
            input_output_aliases=aliases or {},
            compiler_params=pltpu.CompilerParams(vmem_limit_bytes=vmem_bytes),
            cost_estimate=pl.CostEstimate(
                flops=int(span * 1e9), bytes_accessed=0, transcendentals=0
            ),
        )(*scalars, *[a for a, _, _ in inputs], *tokens)
        self.token = out[-1]
        return out[0] if len(out) == 2 else out[:-1]


def shaped(dtype, *shape):
    return jax.ShapeDtypeStruct(shape, dtype)


def whole(array):
    zeros = (0,) * len(array.shape)
    return (array, array.shape, lambda *_: zeros)


def rowwise(array, steps):
    return (array, (array.shape[0] // steps, array.shape[1]), lambda i, *_: (i, 0))


def columnwise(array, steps):
    return (array, (array.shape[0], array.shape[1] // steps), lambda i, *_: (0, i))


def stacked(array, k, rows):
    return (array, (rows, array.shape[1]), lambda *_: (k, 0))


def dot_t(a, b):
    return lax.dot_general(a, b, (((0,), (0,)), ((), ())), preferred_element_type=f32)


def dot_bt(a, b):
    return lax.dot_general(a, b, (((1,), (1,)), ((), ())), preferred_element_type=f32)


def dot(a, b):
    return jnp.dot(a, b, preferred_element_type=f32)


def chosen(flag, yes, no):
    return jnp.where(flag != 0, yes, no)


def halves(x_ref, rows):
    turned = x_ref[...].T
    return turned[:rows], turned[rows:]


def first_piece(order, normed, rows):
    tokens = normed.shape[0]

    def kernel(s_ref, x_ref, piece_ref):
        low, high = halves(x_ref, rows)
        piece_ref[...] = chosen(s_ref[Y], low, high)

    return order.call(
        kernel,
        [(normed, (tokens, 2 * rows), lambda i, s: (0, s[FAR]))],
        [whole(shaped(bf16, rows, tokens))],
        (1,),
    )


def split(order, normed, rows, g_pair, fixes):
    tokens = normed.shape[0]

    def kernel(s_ref, fix_ref, x_ref, g_ref, two_ref, last_ref, own_ref):
        i = pl.program_id(0)
        low, high = halves(x_ref, rows)
        own_ref[...] = chosen(s_ref[Y], high, low)

        @pl.when(i < 2)
        def _():
            two_ref[...] = chosen(s_ref[Y], low, high)

        @pl.when(i == 2)
        def _():
            last_ref[...] = chosen(s_ref[Y], low, high)

    return order.call(
        kernel,
        [
            (normed, (tokens, 2 * rows), lambda i, s, f: (0, s[(i + 1) % 4])),
            (g_pair, None, None),
        ],
        [
            (
                shaped(bf16, 2 * rows, tokens),
                (rows, tokens),
                lambda i, s, f: (jnp.minimum(i, 1), 0),
            ),
            (shaped(bf16, 3 * rows, tokens), (rows, tokens), lambda i, s, f: (0, 0)),
            (shaped(bf16, 4 * rows, tokens), (rows, tokens), lambda i, s, f: ((i + 1) % 4, 0)),
        ],
        (4,),
        expected["split"],
        fixes=fixes,
    )


def gradient_part(order, mine, k, theirs, at, key_grad, g_pair, scale, dtype, span):
    tokens, features = key_grad.shape
    rows = mine.shape[0] // 4

    def kernel(s_ref, x_ref, xp_ref, g_ref, gp_ref, out_ref):
        total = dot(x_ref[...], g_ref[...]) + dot(xp_ref[...], gp_ref[...])
        out_ref[...] = (total * scale).astype(dtype)

    return order.call(
        kernel,
        [
            stacked(mine, k, rows),
            stacked(theirs, at, rows),
            columnwise(key_grad, 2),
            columnwise(g_pair, 2),
        ],
        [columnwise(shaped(dtype, rows, features), 2)],
        (2,),
        span,
    )


def input_two(order, key_grad, g_pair, first, second, target, scale):
    tokens, features = key_grad.shape
    rows = first.shape[0]

    def kernel(s_ref, g_ref, gp_ref, a_ref, b_ref, target_ref, pair_ref, own_ref):
        weight = jnp.where(pl.program_id(0) == 0, a_ref[...], b_ref[...])
        pair_ref[...] = (dot_bt(weight, gp_ref[...]) * scale).astype(bf16)
        own_ref[...] = (dot_bt(weight, g_ref[...]) * scale).astype(bf16)

    return order.call(
        kernel,
        [whole(a) for a in (key_grad, g_pair, first, second)] + [(target, None, None)],
        [
            (target, (rows, tokens), lambda i, s: (1 + i, 0)),
            (shaped(bf16, 2 * rows, tokens), (rows, tokens), lambda i, s: (i, 0)),
        ],
        (2,),
        expected["input two"],
        {5: 0},
    )


def input_one(order, key_grad, g_pair, inner, part, end, scale, span, before=()):
    tokens, features = key_grad.shape
    rows = end.shape[0]

    def kernel(s_ref, g_ref, gp_ref, a_ref, b_ref, *rest):
        pair_ref, own_ref, w_ref = rest[len(before) :]
        weight = chosen(s_ref[INNER], a_ref[...], b_ref[...])
        w_ref[...] = weight
        pair_ref[...] = (dot_bt(weight, gp_ref[...]) * scale).astype(bf16)
        own_ref[...] = (dot_bt(weight, g_ref[...]) * scale).astype(bf16)

    out = whole(shaped(bf16, rows, tokens))
    return order.call(
        kernel,
        [whole(key_grad), whole(g_pair), stacked(inner, part, rows), whole(end)]
        + [(a, None, None) for a in before],
        [out, out, whole(shaped(bf16, rows, features))],
        (1,),
        span,
    )


def input_join(order, slots, own, others, shape, span, target=None, before=()):
    tokens = own[0][0][0].shape[1]
    tile = tokens // 3
    rows = shape[1] // 8
    flat = [
        (a, k, rows if len(piece) == 1 else a.shape[0]) for piece in own + others for a, k in piece
    ]
    kept = [a for a in (target, *before) if a is not None]

    def kernel(s_ref, *refs):
        values = iter([ref[...] for ref in refs[: len(flat)]])
        sides = [jnp.concatenate([next(values) for _ in piece], 0) for piece in own + others]
        first = pl.program_id(0) == 0
        mine = jnp.where(first, sides[0], sides[1])
        theirs = jnp.where(first, sides[2], sides[3])
        out_ref = refs[-1]

        @pl.when(s_ref[Y] == 0)
        def _():
            out_ref[...] = jnp.concatenate([mine, theirs], 0).T

        @pl.when(s_ref[Y] != 0)
        def _():
            out_ref[...] = jnp.concatenate([theirs, mine], 0).T

    def piece(array, k, height):
        return (array, (height, tile), lambda j, i, s: (k, i))

    return order.call(
        kernel,
        [piece(*p) for p in flat] + [(a, None, None) for a in kept],
        [(shaped(bf16, *shape), (tile, 2 * rows), lambda j, i, s: (i, s[slots[0] - j]))],
        (2, 3),
        span,
        None if target is None else {len(flat) + 1: 0},
    )


def key_sums(order, total, blocks, weights, span, scale=1.0, dtype=f32, before=()):
    features = weights[0].shape[1]
    tokens = blocks[0][0].shape[1]
    count = len(blocks)
    totals = [] if total is None else [columnwise(total, 2)]

    def kernel(s_ref, *refs):
        value = refs[2 * count][...] if totals else 0.0
        for x_ref, w_ref in zip(refs[:count], refs[count : 2 * count]):
            value += dot_t(x_ref[...], w_ref[...])
        refs[-1][...] = (value * scale).astype(dtype)

    return order.call(
        kernel,
        [stacked(x, k, w.shape[0]) for (x, k), w in zip(blocks, weights)]
        + [columnwise(w, 2) for w in weights]
        + totals
        + [(a, None, None) for a in before],
        [columnwise(shaped(dtype, tokens, features), 2)],
        (2,),
        span,
    )


def delta_halves(order, anchor, local):
    rows, features = local.shape

    def kernel(s_ref, a_ref, b_ref, c_ref, d_ref, own_ref, other_ref):
        own_ref[...] = a_ref[...] - b_ref[...]
        other_ref[...] = c_ref[...] - d_ref[...]

    def half(array, turned):
        def index(i, s):
            core = 1 - s[CORE] if turned else s[CORE]
            return (3 * core + i, 0)

        return (array, (rows // 6, features), index)

    out = rowwise(shaped(f32, rows // 2, features), 3)
    return order.call(
        kernel,
        [half(anchor, False), half(local, False), half(anchor, True), half(local, True)],
        [out, out],
        (3,),
    )


def total_of(order, here, there):
    def kernel(s_ref, a_ref, b_ref, out_ref):
        out_ref[...] = a_ref[...] + b_ref[...]

    return order.call(
        kernel, [rowwise(here, 3), rowwise(there, 3)], [rowwise(shaped(f32, *here.shape), 3)], (3,)
    )


def choose_sends(order, at_end, inside, beside):
    def kernel(s_ref, a_ref, b_ref, c_ref, out_ref, across_ref):
        out_ref[...] = chosen(s_ref[END], a_ref[...], b_ref[...])
        across_ref[...] = c_ref[...]

    out = rowwise(shaped(bf16, *inside.shape), 3)
    return order.call(
        kernel, [rowwise(a, 3) for a in (at_end, inside, beside)], [out, out], (3,), 0
    )


def first_handoff(order, p0, c1, p1, w_across):
    rows, features = p0.shape
    part = rows // 3

    def kernel(s_ref, p0_ref, c1_ref, p1_ref, w_ref, sum_a, send_a, sum_b, send_b):
        total = (p0_ref[...].astype(f32) + c1_ref[...].astype(f32)).astype(bf16)
        send = chosen(s_ref[END], p1_ref[...], w_ref[...])

        @pl.when(pl.program_id(0) < 2)
        def _():
            sum_a[...] = total
            send_a[...] = send

        @pl.when(pl.program_id(0) == 2)
        def _():
            sum_b[...] = total
            send_b[...] = send

    a = (
        shaped(bf16, 2 * part, features),
        (part, features),
        lambda i, s: (jnp.minimum(i, 1), 0),
    )
    b = whole(shaped(bf16, part, features))
    return order.call(
        kernel,
        [rowwise(x, 3) for x in (p0, c1, p1, w_across)],
        [a, a, b, b],
        (3,),
        expected["handoff"],
    )


def second_handoff(order, first, p1, c2, p2, q2, before, span):
    def kernel(s_ref, p1_ref, c2_ref, p2_ref, q2_ref, *rest):
        s1_ref, t_ref = rest[len(before) :]
        s1_ref[...] = (p1_ref[...].astype(f32) + c2_ref[...].astype(f32)).astype(bf16)
        t_ref[...] = (p2_ref[...] + q2_ref[...].astype(f32)).astype(bf16)

    sixth, features = p1.shape[0] // 6, p1.shape[1]
    steps = c2.shape[0] // sixth
    block = (sixth, features)
    out = rowwise(shaped(bf16, *c2.shape), steps)
    return order.call(
        kernel,
        [
            (p1, block, lambda i, s: (first + i, 0)),
            rowwise(c2, steps),
            (p2, block, lambda i, s: (first + i, 0)),
            rowwise(q2, steps),
        ]
        + [(a, None, None) for a in before],
        [out, out],
        (steps,),
        span,
    )


def nesterov_pass(order, own, other, anchor, momentum, local):
    rows, features = local.shape

    def kernel(s_ref, own_ref, other_ref, anchor_ref, momentum_ref, local_ref, *out):
        anchor_new_ref, moment_new_ref, base_ref = out
        in_own = pl.program_id(0) // 3 == s_ref[CORE]
        outer_grad = jnp.where(in_own, own_ref[...], other_ref[...]) / 4
        anchor_new, moment_new = nesterov(outer_grad, anchor_ref[...], momentum_ref[...])
        anchor_new_ref[...] = anchor_new
        moment_new_ref[...] = moment_new
        kept = mix_weight * (1.0 - inner_rate * weight_decay)
        base_ref[...] = kept * local_ref[...] + (1.0 - mix_weight) * anchor_new

    def half(array):
        return (array, (rows // 6, features), lambda i, s: (i % 3, 0))

    out = rowwise(shaped(f32, rows, features), 6)
    return order.call(
        kernel,
        [half(own), half(other)] + [rowwise(a, 6) for a in (anchor, momentum, local)],
        [out, out, out],
        (6,),
        expected["nesterov"],
    )


def final_update(order, first, fixes, p3, qa, qb, first_old, second_old, base, made=(), keys=()):
    rows, features = base.shape
    block = (rows // 6, features)
    steps = qa.shape[0] // block[0]
    scale = keys[2] if keys else None

    def kernel(s_ref, fix_ref, p_ref, a_ref, b_ref, first_ref, second_ref, base_ref, *rest):
        outs = rest[len(keys[:2]) + len(made) :]
        gradient = p_ref[...] + a_ref[...].astype(f32) + b_ref[...].astype(f32)
        first_new = beta_first * first_ref[...] + (1.0 - beta_first) * gradient
        second_new = beta_second * second_ref[...] + (1.0 - beta_second) * gradient * gradient
        root = jnp.sqrt(second_new * fix_ref[1]) + epsilon
        step = (mix_weight * inner_rate) * fix_ref[0]
        outs[0][...] = base_ref[...] - step * first_new / root
        outs[1][...] = first_new
        outs[2][...] = second_new
        if keys:
            outs[3][...] = (rest[0][...] * scale + rest[1][...].astype(f32)).astype(bf16)

    def at(array, offset):
        return (array, block, lambda i, *_: (offset + i, 0))

    out = at(shaped(f32, rows, features), first)
    inputs = [at(p3, first), rowwise(qa, steps), rowwise(qb, steps)]
    inputs += [at(a, first) for a in (first_old, second_old, base)]
    inputs += [rowwise(a, steps) for a in keys[:2]]
    aliases = {2 + len(inputs) + i: i for i in range(len(made))}
    return order.call(
        kernel,
        inputs + [(a, None, None) for a in made],
        [out] * 3 + ([rowwise(shaped(bf16, *keys[0].shape), steps)] if keys else []),
        (steps,),
        0 if keys else expected["first half"],
        aliases,
        fixes,
    )


def pair_pass(normed, key_grad, local, first_old, second_old, anchor, momentum, inner_step):
    width = normed.shape[1]
    rows = local.shape[0]
    scale = width ** (-0.5)
    me = lax.axis_index("fsdp")
    core = lax.axis_index("rep") % 2
    y, z = me % 2, me // 2
    inside = (z == 1) | (z == 2)
    far = jnp.where(z < 2, 3, 0)
    middle = jnp.where(z < 2, 2, 1)
    order = Order(jnp.stack([far, middle, z ^ 1, z, y, inside, ~inside, core]).astype(jnp.int32))

    def along(links):
        pairs = [(2 * a + c, 2 * b + c) for a, b in links for c in (0, 1)]
        return lambda value: lax.ppermute(value, "fsdp", pairs)

    outer = along([(0, 1), (1, 0), (2, 3), (3, 2)])
    inner = along([(1, 2), (2, 1)])

    def swap(value):
        return lax.ppermute(value, "fsdp", [(i, i ^ 1) for i in range(8)])

    def replica(value, bit):
        return lax.ppermute(value, "rep", [(i, i ^ bit) for i in range(4)])

    g_pair = swap(key_grad)
    weight = local.astype(bf16)
    w_beside = outer(weight)
    w_inner = inner(weight)
    x0 = swap(first_piece(order, normed, rows))
    own_delta, other_delta = delta_halves(order, anchor, local)
    delta_core = replica(other_delta, 1)
    fixes = 1.0 / jnp.stack(corrections(inner_step))
    two, three, mine = split(order, normed, rows, g_pair, fixes)
    x12 = swap(two)
    delta = total_of(order, own_delta, delta_core)
    delta_there = replica(delta, 2)

    def partial(k, theirs, at, dtype, span):
        return gradient_part(order, mine, k, theirs, at, key_grad, g_pair, scale, dtype, span)

    p0 = partial(0, x0, 0, bf16, expected["first part"])
    send, across = choose_sends(order, p0, w_inner, w_beside)
    c1 = outer(send)
    w_across = inner(across)
    three, own01 = input_two(order, key_grad, g_pair, weight, w_beside, three, scale)
    x3 = swap(three)
    known = (w_beside, weight)
    own_total = key_sums(order, None, [(mine, 2), (mine, 3)], known, expected["early own"])
    total = total_of(order, delta, delta_there)
    total_there = replica(total, 1)
    p1 = partial(1, x12, 0, bf16, expected["second part"])
    p2 = partial(2, x12, 1, f32, 1)
    anchor_new, moment_new, base = nesterov_pass(
        order, total, total_there, anchor, momentum, local
    )

    s0a, send_a, s0b, send_b = first_handoff(order, p0, c1, p1, w_across)
    c2a, q2a = outer(send_a), inner(s0a)
    c2b, q2b = outer(send_b), inner(s0b)
    i2, own2, w_middle = input_one(
        order, key_grad, g_pair, w_inner, 0, c1, scale, expected["input middle"]
    )
    g2 = swap(i2)
    pair_total = key_sums(
        order, None, [(x12, 0), (x12, 1)], (w_middle, w_beside), expected["early pair"]
    )
    own_total = key_sums(order, own_total, [(mine, 1)], (w_middle,), expected["early pair"])
    input_grad = input_join(
        order,
        (OWN, BESIDE),
        [[(own01, 0)], [(own01, 1)]],
        [[(x3, 1)], [(x3, 2)]],
        normed.shape,
        expected["join two"],
    )
    i3, own3a, w_far_a = input_one(
        order, key_grad, g_pair, w_across, 0, c2a, scale, expected["input far"], [x3]
    )
    g3a = swap(i3)
    s1, t = second_handoff(order, 0, p1, c2a, p2, q2a, [x3], expected["early sums"])
    qaa, qba = outer(t), inner(s1)
    pair_total = key_sums(
        order,
        pair_total,
        [(x3, 0)],
        (weight,),
        expected["pair sums"],
        before=[g2],
    )
    i3, own3b, w_far_b = input_one(
        order, key_grad, g_pair, w_across, 2, c2b, scale, expected["input last"]
    )
    g3b = swap(i3)
    w_far = (w_far_a, w_far_b)
    key_pair = swap(
        key_sums(order, pair_total, [(x0, 0), (x0, 2)], w_far, 0, scale, bf16, [q2b])
    )
    p3 = partial(3, x3, 0, f32, 0)
    s1, t = second_handoff(order, 4, p1, c2b, p2, q2b, [g3a, g3b], expected["late sums"])
    qab, qbb = outer(t), inner(s1)
    own_total = key_sums(
        order,
        own_total,
        [(mine, 0), (mine, 2)],
        w_far,
        expected["own sums"],
    )
    input_grad = input_join(
        order,
        (MIDDLE, FAR),
        [[(own2, 0)], [(own3a, 0), (own3b, 0)]],
        [[(g2, 0)], [(g3a, 0), (g3b, 0)]],
        normed.shape,
        expected["join last"],
        input_grad,
    )
    state = (first_old, second_old, base)
    made = final_update(order, 0, fixes, p3, qaa, qba, *state)
    merged, first_new, second_new, keys = final_update(
        order, 4, fixes, p3, qab, qbb, *state, made, (own_total, key_pair, scale)
    )
    return (keys, input_grad, merged, first_new, second_new, anchor_new, moment_new)


def body(normed, key_grad, master, first_moment, second_moment, anchor, momentum, inner_step):
    local = master[0]
    sizes = (lax.axis_size("rep"), lax.axis_size("fsdp"))
    inner_pass = pair_pass if sizes == (4, 8) else whole_pass
    keys, input_grad, merged, first_new, second_new, anchor_new, moment_new = inner_pass(
        normed, key_grad, local, first_moment[0], second_moment[0], anchor, momentum, inner_step
    )
    return (
        keys,
        input_grad,
        merged[None],
        first_new[None],
        second_new[None],
        anchor_new,
        moment_new,
    )


def solution(mesh):
    in_specs = (
        P(("rep", "fsdp"), None),
        P(("rep", "fsdp"), None),
        P("rep", "fsdp", None),
        P("rep", "fsdp", None),
        P("rep", "fsdp", None),
        P("fsdp", None),
        P("fsdp", None),
        P(),
    )
    out_specs = (
        P(("rep", "fsdp"), None),
        P(("rep", "fsdp"), None),
        P("rep", "fsdp", None),
        P("rep", "fsdp", None),
        P("rep", "fsdp", None),
        P("fsdp", None),
        P("fsdp", None),
    )
    return jax.shard_map(body, mesh=mesh, in_specs=in_specs, out_specs=out_specs, check_vma=False)
```
